32 devices in a mesh: dp: 4 (over y, x), row: 4 (over z), col: 2 (over core).
Axes of the slice: x: 2, y: 2, z: 4, core: 2. Of those that a mesh axis runs over, the one named last changes fastest.
Arguments:
- activations: bfloat16 [2048, 2048], P(('dp', 'row'), 'col'), may hold values from -6 to 6
- cotangent: bfloat16 [2048, 2048], P(('dp', 'row'), 'col'), may hold values from -6 to 6
- routing: int32 [2048, 6], P(('dp', 'row')), may hold values from 0 to 15, all different within a row; in each aligned block of 128 rows (0 to 127, 128 to 255, ...) at most 64 rows name the same one
- segments: int32 [2048], P('dp'), may hold values from 0 to 15, never falling along the last dimension, each value on 1 to 256 neighbouring positions
- scaling: float32 [2048], P('col'), may hold values from 0.25 to 1.75
- queries: bfloat16 [2048, 3072], P('col', 'row'), may hold values from -0.1875 to 0.1875
- compress: bfloat16 [2048, 576], P('col', 'row'), may hold values from -0.125 to 0.125
- rescale: float32 [512], replicated, may hold values from 0.25 to 1.75
- expand: bfloat16 [512, 4096], P(None, 'row'), may hold values from -0.25 to 0.25
- combine: bfloat16 [2048, 2048], P('row', 'col'), may hold values from -1.5 to 1.5
- premix: float32 [2048], P('col'), may hold values from 0.25 to 1.75
- router: bfloat16 [2048, 16], P('col'), may hold values from -0.0625 to 0.0625
- widening: bfloat16 [2, 2048, 2816], P(None, 'col', 'row'), may hold values from -0.125 to 0.125
- narrowing: bfloat16 [2816, 2048], P('row', 'col'), may hold values from -0.109375 to 0.109375
- fanout: bfloat16 [16, 2, 2048, 1408], P(('dp', 'row'), None, None, 'col'), may hold values from -0.125 to 0.125
- funnel: bfloat16 [16, 1408, 2048], P(('dp', 'row'), 'col'), may hold values from -2.5 to 2.5
Outputs:
- layer_output: bfloat16 [2048, 2048], P(('dp', 'row'), 'col')
- input_grad: float32 [2048, 2048], P(('dp', 'row'), 'col')
- scaling_grad: float32 [2048], P('col')
- queries_grad: float32 [2048, 3072], P('col', 'row')
- compress_grad: float32 [2048, 576], P('col', 'row')
- rescale_grad: float32 [512], replicated
- expand_grad: float32 [512, 4096], P(None, 'row')
- combine_grad: float32 [2048, 2048], P('row', 'col')
- premix_grad: float32 [2048], P('col')
- router_grad: float32 [2048, 16], P('col')
- widening_grad: float32 [2, 2048, 2816], P(None, 'col', 'row')
- narrowing_grad: float32 [2816, 2048], P('row', 'col')
- fanout_grad: float32 [16, 2, 2048, 1408], P(('dp', 'row'), None, None, 'col')
- funnel_grad: float32 [16, 1408, 2048], P(('dp', 'row'), 'col')
The draws below stay inside these ranges and needn't reach their ends.
Inputs may be any that keep to these rules, and one draw needn't show every extreme that they name: `routing`: each row names 6 different experts. In each aligned block of 128 rows (the tokens of one index of dp and row) no expert is named by more than 64 rows, a bound that some block reaches. `segments`: never falling along the tokens; each value covers 1 to 256 consecutive tokens, and some value covers exactly 256.
All inputs are finite; a program needn't handle non-finite values.
Results may differ from the reference program's by a relative error of at most 0.03.
Values may be sent and summed in bfloat16 or wider, within the bound.
A program may use at most 256 MiB of HBM per device.

```python
import math
import jax
import jax.numpy as jnp
import numpy as np
from jax import lax

D = 2048
HEADS = 16
NOPE = 128
ROPE = 64
HEADV = 128
RANK = 512
FE = 1408
SHARED = 2816
TOP = 6
BLK = 256
TOK_ROW = 128
EXPERTS = 16
TOKENS = 2048
SEQ = 512
CAP = 64
N_DP = 4
N_ROW = 4


def levels(own_key, dims, shards, low, high):
    def one(dim, shards_of):
        steps = jax.random.uniform(jax.random.fold_in(jax.random.fold_in(own_key, 6), dim), (shards_of,), jnp.float32, low / len(shards), high / len(shards))
        return jnp.repeat(jnp.exp(steps), dims[dim] // shards_of).reshape((-1,) + (1,) * (len(dims) - dim - 1))

    level = one(*shards[0])
    for cut in shards[1:]:
        level = level * one(*cut)
    return level


def split_up(amount, total, reach, slope):
    loads = [(1 << 20) // math.isqrt(grade ** slope) + 1 for grade in range(2, amount + 1)]
    rest, counts = total - reach - (amount - 1), [1] * (amount - 1)
    while rest > 0:
        candidates = [i for i in range(amount - 1) if counts[i] < reach]
        pool, budget = sum([loads[i] for i in candidates]), rest
        for i in candidates:
            extra = min(reach - counts[i], max(1, budget * loads[i] // pool), rest)
            counts[i] = counts[i] + extra
            rest = rest - extra
    return np.array([reach] + counts)


def ragged(key, amount, total, most, skew):
    if amount == 2:
        one = jax.random.randint(key, (), max(1, total - most), min(most, total - 1) + 1)
        return jnp.stack([one, total - one])
    sizes = jnp.asarray(split_up(amount, total, most, skew), jnp.int32)
    couples = (amount - 1) // 2
    source_of, receiver = sizes[1:1 + 2 * couples:2], sizes[2:2 + 2 * couples:2]
    margin = jnp.minimum(source_of - 1, most - receiver)
    passed = jax.random.randint(jax.random.fold_in(key, 1), (couples,), 0, 1 << 20) % (margin + 1)
    sizes = sizes.at[1:1 + 2 * couples:2].set(source_of - passed).at[2:2 + 2 * couples:2].set(receiver + passed)
    return sizes[jax.random.permutation(jax.random.fold_in(key, 2), amount)]


def deal_out(stream_key, own, number, rows, number_of, top, limit, skew):
    ranking = jax.random.permutation(stream_key, number_of)
    crowded, usual = portions_of(number_of, rows * top, limit, skew, True), portions_of(number_of, rows * top, limit, skew, False)
    places = jnp.arange(number_of)

    def named(sizes, turn):
        used = int((sizes > 0).sum())
        fixed = max(1, used // 4)
        shifted = fixed + (places - fixed + turn * (used - fixed)) % max(1, number_of - fixed)
        return jnp.zeros((number_of,), jnp.int32).at[ranking[jnp.where(places < fixed, places, shifted)]].set(jnp.asarray(sizes, jnp.int32))

    sizes = jnp.where(number % 4 == 0, named(crowded, number // 4), named(usual, number - number // 4 - 1))
    mixed = jax.random.permutation(jax.random.fold_in(own, 3), number_of)
    giver, taker = mixed[0:number_of // 2 * 2:2], mixed[1:number_of // 2 * 2:2]
    slack = jnp.minimum(sizes[giver] - 1, limit - sizes[taker]) // 2
    slack = jnp.where((giver == ranking[0]) | (taker == ranking[0]) | (sizes[taker] == 0), 0, jnp.maximum(slack, 0))
    shifted = jax.random.randint(jax.random.fold_in(own, 4), (number_of // 2,), 0, 1 << 20) % (slack + 1)
    sizes = sizes.at[giver].add(-shifted).at[taker].add(shifted)
    members = jnp.searchsorted(jnp.cumsum(sizes), jnp.arange(rows * top), side="right").astype(jnp.int32)
    table = members.reshape(top, rows).T
    table = table[jax.random.permutation(jax.random.fold_in(own, 1), rows)]
    turn = jax.random.randint(jax.random.fold_in(own, 2), (rows, 1), 0, top)
    return jnp.take_along_axis(table, (jnp.arange(top)[None, :] + turn) % top, axis=1)


def portions_of(amount, total, limit, slope, full):
    weights = [(1 << 20) // math.isqrt(standing ** slope) + 1 for standing in range(1, amount + 1)]
    largest = limit if full else min(limit, max(-(-total // amount), total * weights[0] // sum(weights)))
    least = 1 if total - largest >= amount - 1 else 0
    counts, rest = [largest] + [least] * (amount - 1), total - largest - least * (amount - 1)
    while rest > 0:
        free = [i for i in range(1, amount) if counts[i] < largest] or [i for i in range(1, amount) if counts[i] < limit]
        pool, left = sum([weights[i] for i in free]), rest
        for i in free:
            extra = min(limit - counts[i], max(1, left * weights[i] // pool), rest)
            counts[i] = counts[i] + extra
            rest = rest - extra
    return np.array(counts)


def gaussian(own_key, dims, scale, most, shards=(), held_as=jnp.bfloat16):
    loudness = levels(own_key, dims, shards, -0.22, 0.18) if shards else 1.0
    array = jax.random.normal(own_key, dims, jnp.float32) * scale * loudness
    return jnp.minimum(jnp.maximum(array, -most), most).astype(held_as)


def setup_inputs(seed: int = 0) -> dict:
    key_list = jax.random.split(jax.random.key(seed), 17)
    activations = gaussian(key_list[0], (TOKENS, D), 1.0, 6.0, ((0, 16), (1, 2)))
    cotangent = gaussian(key_list[1], (TOKENS, D), 1.0, 6.0, ((0, 16), (1, 2)))
    routing_keys = jax.random.split(jax.random.fold_in(key_list[2], 1), TOKENS // TOK_ROW)
    routing_turns = jax.random.permutation(jax.random.fold_in(key_list[2], 3), TOKENS // TOK_ROW)
    routing = jax.vmap(lambda own, number: deal_out(jax.random.fold_in(key_list[2], 2), own, number, TOK_ROW, EXPERTS, TOP, CAP, 2))(routing_keys, routing_turns).reshape((TOKENS, TOP))
    segments = jnp.searchsorted(jnp.cumsum(ragged(key_list[3], 2 * TOKENS // BLK, TOKENS, BLK, 1)), jnp.arange(TOKENS), side="right").astype(jnp.int32)
    scaling = jnp.clip(1.0 + 0.15 * jax.random.normal(key_list[4], (D,), jnp.float32), 0.25, 1.75)
    queries = gaussian(key_list[5], (D, HEADS * (NOPE + ROPE)), (D // 2) ** -0.5, 0.1875, ((0, 2), (1, 4)))
    compress = gaussian(key_list[6], (D, RANK + ROPE), D ** -0.5, 0.125, ((0, 2), (1, 4)))
    rescale = jnp.clip(1.0 + 0.15 * jax.random.normal(key_list[7], (RANK,), jnp.float32), 0.25, 1.75)
    expand = gaussian(key_list[8], (RANK, HEADS * (NOPE + HEADV)), RANK ** -0.5, 0.25, ((1, 4),))
    combine = gaussian(key_list[9], (HEADS * HEADV, D), 16 ** -0.5, 1.5, ((0, 4), (1, 2)))
    premix = jnp.clip(1.0 + 0.15 * jax.random.normal(key_list[10], (D,), jnp.float32), 0.25, 1.75)
    router = gaussian(key_list[11], (D, EXPERTS), (4 * D) ** -0.5, 0.0625, ((0, 2),))
    widening = gaussian(key_list[12], (2, D, SHARED), D ** -0.5, 0.125, ((1, 2), (2, 4)))
    narrowing = gaussian(key_list[13], (SHARED, D), SHARED ** -0.5, 0.109375, ((0, 4), (1, 2)))
    fanout = gaussian(key_list[14], (EXPERTS, 2, D, FE), D ** -0.5, 0.125, ((0, 16), (3, 2)))
    funnel = gaussian(key_list[15], (EXPERTS, FE, D), (max(FE // 256, 1)) ** -0.5, 2.5, ((0, 16), (1, 2)))
    return dict(activations=activations, cotangent=cotangent, routing=routing, segments=segments, scaling=scaling, queries=queries, compress=compress, rescale=rescale, expand=expand, combine=combine, premix=premix, router=router, widening=widening, narrowing=narrowing, fanout=fanout, funnel=funnel)


@jax.custom_vjp
def low(v):
    return lax.optimization_barrier(v.astype(jnp.bfloat16)).astype(jnp.float32)

@jax.custom_vjp
def low_back(v):
    return v

def low_keep(v):
    return (low(v), None)

def low_pass(kept, grad):
    return (grad,)

def back_keep(v):
    return (v, None)

def back_low(kept, grad):
    return (low(grad),)
low.defvjp(low_keep, low_pass)
low_back.defvjp(back_keep, back_low)
epsilon = 1e-06
masked_score = -1e+30
highest = lax.Precision.HIGHEST

def product(left, right):
    return jnp.dot(left, right, precision=highest)

def rms_norm(values, gain_vector):
    return values * lax.rsqrt(lax.optimization_barrier(jnp.mean(values * values, axis=-1, keepdims=True)) + epsilon) * gain_vector

def rotation(positions, rope_width):
    half_width = rope_width // 2
    frequency = 10000.0 ** (-jnp.arange(half_width, dtype=jnp.float32) * 2.0 / rope_width)
    angles = positions.astype(jnp.float32)[:, None] * frequency[None, :]
    return (jnp.cos(angles), jnp.sin(angles))

def rotate(values, cosine, sine_table, direction):
    half_width = values.shape[-1] // 2
    first_half = values[..., :half_width]
    second_half = values[..., half_width:]
    return jnp.concatenate([first_half * cosine - direction * second_half * sine_table, second_half * cosine + direction * first_half * sine_table], axis=-1)

def attend(query_heads, key_heads, value_heads, block_marks):
    length = query_heads.shape[0]
    block_rows = min(512, length)
    score_scale = query_heads.shape[-1] ** (-0.5)

    def one_block(start_row):
        query_block = lax.dynamic_slice_in_dim(query_heads, start_row, block_rows, 0)
        mark_block = lax.dynamic_slice_in_dim(block_marks, start_row, block_rows, 0)
        scores = low_back(jnp.einsum('qhd,khd->hqk', query_block, key_heads, precision=highest) * score_scale)
        visible = block_marks[None, None, :] <= mark_block[None, :, None]
        scores = jnp.where(visible, scores, masked_score)
        weight = jnp.exp(scores - lax.optimization_barrier(jnp.max(scores, axis=2, keepdims=True)))
        probability = weight / lax.optimization_barrier(jnp.sum(weight, axis=2, keepdims=True))
        return low(low_back(jnp.einsum('hqk,khd->qhd', low(probability), value_heads, precision=highest)))
    starts = (jnp.arange(length // block_rows) * block_rows).astype(jnp.int32)
    result = lax.map(jax.checkpoint(one_block), starts)
    return result.reshape(length, key_heads.shape[1], value_heads.shape[2])

def attend_packed(packed):
    return attend(packed[0], packed[1], packed[2], packed[3])

def reference(activations, cotangent, routing, segments, scaling, queries, compress, rescale, expand, combine, premix, router, widening, narrowing, fanout, funnel):
    token_count = activations.shape[0]
    source_count = N_DP * N_ROW
    pair_rows = TOK_ROW * TOP
    expert_range = jnp.arange(EXPERTS).astype(jnp.int32)
    chosen = routing[:, :, None] == expert_range[None, None, :]
    grouped = routing.reshape(source_count, pair_rows)
    matches = (grouped[:, :, None] == expert_range[None, None, :]).astype(jnp.int32)
    earlier = jnp.cumsum(matches, axis=1) - matches
    slot_index = lax.optimization_barrier(jnp.sum(earlier * matches, axis=2)).astype(jnp.int32)
    sources = jnp.arange(source_count).astype(jnp.int32)[:, None]
    places = (grouped * (source_count * CAP) + sources * CAP + slot_index).reshape(-1).astype(jnp.int32)
    owners = jnp.repeat(jnp.arange(token_count).astype(jnp.int32), TOP)
    owner_rows = jnp.zeros((EXPERTS * source_count * CAP,), jnp.int32).at[places].set(owners).reshape(EXPERTS, source_count * CAP)
    filled = jnp.zeros((EXPERTS * source_count * CAP,), jnp.float32).at[places].set(1.0).reshape(EXPERTS, source_count * CAP)
    positions = jnp.tile(jnp.arange(SEQ).astype(jnp.int32), N_DP)
    cosine, sine_table = rotation(positions, ROPE)
    block_marks = segments.reshape(N_DP, SEQ)

    def forward(inputs, scaling, queries, compress, rescale, expand, combine, premix, router, widening, narrowing, fanout, funnel):
        normed_one = low(rms_norm(inputs, scaling))
        query_raw = low_back(product(normed_one, queries)).reshape(token_count, HEADS, NOPE + ROPE)
        latent_raw = low_back(product(normed_one, compress))
        latent_normed = low(rms_norm(latent_raw[:, :RANK], rescale))
        expanded = low_back(product(latent_normed, expand)).reshape(token_count, HEADS, NOPE + HEADV)
        query_all = low(jnp.concatenate([query_raw[..., :NOPE], rotate(query_raw[..., NOPE:], cosine[:, None, :], sine_table[:, None, :], 1.0)], axis=2))
        key_shared = rotate(latent_raw[:, RANK:], cosine, sine_table, 1.0)
        key_all = low(jnp.concatenate([expanded[..., :NOPE], jnp.broadcast_to(key_shared[:, None, :], (token_count, HEADS, ROPE))], axis=2))
        value_all = low(expanded[..., NOPE:])
        attended = lax.map(attend_packed, (query_all.reshape(N_DP, SEQ, HEADS, NOPE + ROPE), key_all.reshape(N_DP, SEQ, HEADS, NOPE + ROPE), value_all.reshape(N_DP, SEQ, HEADS, HEADV), block_marks))
        attended = attended.reshape(token_count, HEADS * HEADV)
        residual = inputs + low_back(product(attended, combine))
        normed_two = low(rms_norm(residual, premix))
        router_probs = jax.nn.softmax(product(normed_two, router), axis=1)
        gate_values = lax.optimization_barrier(jnp.sum(jnp.where(chosen, router_probs[:, None, :], 0.0), axis=2))
        shared_gate_up = low_back(jnp.einsum('td,gdf->gtf', normed_two, widening, precision=highest))
        shared_hidden = low(jax.nn.silu(shared_gate_up[0]) * shared_gate_up[1])
        shared_out = low_back(product(shared_hidden, narrowing))

        def one_expert(packed):
            rows_index, rows_filled, inner_weight, outer_weight = packed
            expert_rows = low_back(normed_two[rows_index] * rows_filled[:, None])
            gate_up = low_back(jnp.einsum('rd,gdf->grf', expert_rows, inner_weight, precision=highest))
            hidden = low(jax.nn.silu(gate_up[0]) * gate_up[1])
            return low(low_back(product(hidden, outer_weight)))
        replies = lax.map(jax.checkpoint(one_expert), (owner_rows, filled, fanout, funnel))
        reply_rows = replies.reshape(-1, D)[places].reshape(token_count, TOP, D)
        routed = lax.optimization_barrier(jnp.sum(gate_values[:, :, None] * reply_rows, axis=1))
        return residual + shared_out + routed
    primals = (activations, scaling, queries, compress, rescale, expand, combine, premix, router, widening, narrowing, fanout, funnel)
    primals = tuple((argument.astype(jnp.float32) for argument in primals))
    output, pullback = jax.vjp(forward, *primals)
    gradients = pullback(cotangent.astype(jnp.float32))
    return (output.astype(jnp.bfloat16), gradients[0], gradients[1], gradients[2], gradients[3], gradients[4], gradients[5], gradients[6], gradients[7], gradients[8], gradients[9], gradients[10], gradients[11], gradients[12])
```

```python
import jax
import jax.numpy as jnp
import numpy as np
from jax import lax
from jax.experimental import pallas as pl
from jax.experimental.pallas import tpu as pltpu
from jax.sharding import PartitionSpec as P

D = 2048
NOPE = 128
ROPE = 64
HEADV = 128
RANK = 512
TOP = 6


epsilon = 1e-06
masked_score = -1e30
f32 = jnp.float32
bf16 = jnp.bfloat16


def after(value, *earlier):
    return lax.optimization_barrier((value,) + earlier)[0]


def silu_slope(values):
    sigmoid = jax.nn.sigmoid(values)
    return sigmoid * (1.0 + values * (1.0 - sigmoid))


def rotation(positions, rope_width):
    half_width = rope_width // 2
    frequency = 10000.0 ** (-jnp.arange(half_width, dtype=jnp.float32) * 2.0 / rope_width)
    angles = positions.astype(jnp.float32)[:, None] * frequency[None, :]
    return (jnp.cos(angles), jnp.sin(angles))


def rotate(values, cosine, sine_table, direction):
    half_width = values.shape[-1] // 2
    first_half = values[..., :half_width]
    second_half = values[..., half_width:]
    return jnp.concatenate(
        [
            first_half * cosine - direction * second_half * sine_table,
            second_half * cosine + direction * first_half * sine_table,
        ],
        axis=-1,
    )


def dot(left, right):
    return jnp.dot(left, right, preferred_element_type=f32)


def dot_tn(left, right):
    return lax.dot_general(left, right, (((0,), (0,)), ((), ())), preferred_element_type=f32)


def dot_nt(left, right):
    return lax.dot_general(left, right, (((1,), (1,)), ((), ())), preferred_element_type=f32)


def col_totals(values):
    return lax.psum(values, "col")


def row_gather(values):
    return lax.all_gather(values, "row", axis=0, tiled=True)


def col_gather(values, axis=0):
    return lax.all_gather(values, "col", axis=axis, tiled=True)


def col_scatter(values, axis=0):
    return lax.psum_scatter(values, "col", scatter_dimension=axis, tiled=True)


def row_scatter(values):
    return lax.psum_scatter(
        values.astype(bf16), "row", scatter_dimension=0, tiled=True
    ).astype(f32)


def send_out(parts):
    count = len(parts)
    return [parts[0]] + [
        lax.ppermute(parts[k], "dp", [(i, (i + k) % count) for i in range(count)])
        for k in range(1, count)
    ]


def send_back(parts):
    count = len(parts)
    return [parts[0]] + [
        lax.ppermute(parts[k], "dp", [(i, (i - k) % count) for i in range(count)])
        for k in range(1, count)
    ]


def norm_scale(values):
    square_sum = col_totals(jnp.sum(values * values, axis=1))
    return lax.rsqrt(square_sum / D + epsilon)


def norm_back(values, row_scale, gain_vector, upstream):
    weighted = upstream * gain_vector
    inner_mean = col_totals(jnp.sum(weighted * values, axis=1)) / D
    return weighted * row_scale[:, None] - values * (row_scale**3 * inner_mean)[:, None]


MESH = pl.DeviceIdType.MESH
VMEM = pltpu.VMEM
DMA = pltpu.SemaphoreType.DMA
MIB = 1024 * 1024
ROWS = 4
SQUARE = 4
COLS = 2
SPLIT = 2


def nn(left, right):
    return lax.dot_general(left, right, (((1,), (0,)), ((), ())), preferred_element_type=f32)


def tn(left, right):
    return lax.dot_general(left, right, (((0,), (0,)), ((), ())), preferred_element_type=f32)


def nt(left, right):
    return lax.dot_general(left, right, (((1,), (1,)), ((), ())), preferred_element_type=f32)


def block_at(row, turn):
    swapped = jnp.where(turn < 2, 1 - turn, turn)
    inner = jnp.logical_or(row == 1, row == 2)
    near = jnp.where(inner, swapped, turn)
    return jnp.where(row < 2, near, ROWS - 1 - near)


def partner(place, step):
    across, along = lax.rem(place, 2), lax.div(place, 2)
    across = lax.rem(across + step % 2, 2)
    along = lax.rem(along + step // 2, 2)
    return along * 2 + across


def remote(source, target, sent, arrived, where):
    return pltpu.make_async_remote_copy(
        src_ref=source,
        dst_ref=target,
        send_sem=sent,
        recv_sem=arrived,
        device_id=where,
        device_id_type=MESH,
    )


def greet(row, place, col, square=True):
    barrier = pltpu.get_barrier_semaphore()
    if square:

        @pl.when(row > 0)
        def _():
            pl.semaphore_signal(barrier, inc=1, device_id={"row": row - 1}, device_id_type=MESH)

        @pl.when(row < ROWS - 1)
        def _():
            pl.semaphore_signal(barrier, inc=1, device_id={"row": row + 1}, device_id_type=MESH)

        for step in range(1, SQUARE):
            pl.semaphore_signal(
                barrier, inc=1, device_id={"dp": partner(place, step)}, device_id_type=MESH
            )
        met = (
            SQUARE - 1 + (row > 0).astype(jnp.int32) + (row < ROWS - 1).astype(jnp.int32)
        )
    else:
        for step in range(1, ROWS):
            pl.semaphore_signal(
                barrier,
                inc=1,
                device_id={"row": lax.rem(row + step, ROWS)},
                device_id_type=MESH,
            )
        met = ROWS - 1
    pl.semaphore_signal(barrier, inc=1, device_id={"col": 1 - col}, device_id_type=MESH)
    pl.semaphore_wait(barrier, met + 1)


class Line:
    def __init__(self, row, buffer, sent, arrived):
        self.row, self.buffer, self.sent, self.arrived = row, buffer, sent, arrived

    def copy(self, block, way):
        to = self.row + 1 if way == 0 else self.row - 1
        here = self.buffer.at[block]
        return remote(here, here, self.sent.at[block, way], self.arrived.at[block], {"row": to})

    def each(self, block, act):
        @pl.when(jnp.logical_and(block <= self.row, self.row < ROWS - 1))
        def _():
            act(self.copy(block, 0))

        @pl.when(jnp.logical_and(block >= self.row, self.row > 0))
        def _():
            act(self.copy(block, 1))

    def wait(self, block):
        self.copy(block, 0).wait_recv()

    def pass_on(self, block):
        self.each(block, lambda copy: copy.start())

    def finish(self):
        def one(block, carried):
            self.each(block, lambda copy: copy.wait_send())
            return carried

        lax.fori_loop(0, ROWS, one, 0)


class SumLine:
    def __init__(self, row, part, leaving, coming, sent, arrived):
        self.row, self.part, self.leaving, self.coming = row, part, leaving, coming
        self.sent, self.arrived = sent, arrived
        self.lines = part.shape[1] // SPLIT

    def piece(self, index):
        return pl.ds(index * self.lines, self.lines)

    def copy(self, block, index, way):
        return remote(
            self.leaving.at[block, self.piece(index)],
            self.coming.at[way, block, self.piece(index)],
            self.sent.at[block, index],
            self.arrived.at[way, block, index],
            {"row": self.row + 1 - 2 * way},
        )

    def send(self, block, index):
        @pl.when(block > self.row)
        def _():
            self.copy(block, index, 0).start()

        @pl.when(block < self.row)
        def _():
            self.copy(block, index, 1).start()

    def chained(self, block):
        return jnp.logical_or(
            jnp.logical_and(block > self.row, self.row > 0),
            jnp.logical_and(block < self.row, self.row < ROWS - 1),
        )

    def begin(self, block):
        @pl.when(jnp.logical_and(block != self.row, jnp.logical_not(self.chained(block))))
        def _():
            self.leaving[block] = self.part[block].astype(bf16)
            for index in range(SPLIT):
                self.send(block, index)

    def pass_on(self, block):
        @pl.when(self.chained(block))
        def _():
            way = (block < self.row).astype(jnp.int32)
            for index in range(SPLIT):
                self.copy(block, index, way).wait_recv()
                piece = self.piece(index)
                self.leaving[block, piece] = (
                    self.part[block, piece] + self.coming[way, block, piece].astype(f32)
                ).astype(bf16)
                self.send(block, index)

    def total(self, target):
        target[...] = self.part[self.row]
        for way, there in ((0, self.row > 0), (1, self.row < ROWS - 1)):

            @pl.when(there)
            def _(way=way):
                for index in range(SPLIT):
                    self.copy(self.row, index, way).wait_recv()
                    target[self.piece(index)] += self.coming[
                        way, self.row, self.piece(index)
                    ].astype(f32)

    def finish(self):
        def one(block, carried):
            @pl.when(block != self.row)
            def _():
                for index in range(SPLIT):
                    self.copy(block, index, 0).wait_send()

            return carried

        lax.fori_loop(0, ROWS, one, 0)


def swap_halves(values):
    lanes = values.shape[1]
    lane = lax.broadcasted_iota(jnp.int32, values.shape, 1)
    return jnp.where(
        lane % ROPE < ROPE // 2,
        pltpu.roll(values, lanes - ROPE // 2, 1),
        pltpu.roll(values, ROPE // 2, 1),
    )


def attend_kernel(
    act_ref,
    scaling_ref,
    compress_ref,
    rescale_ref,
    premix_ref,
    cos_ref,
    sin_ref,
    key_cos_ref,
    key_sin_ref,
    mark_rows_ref,
    mark_ref,
    cot_ref,
    route_ref,
    queries_ref,
    expand_ref,
    combine_ref,
    one_ref,
    query_ref,
    key_ref,
    value_ref,
    probs_ref,
    latent_ref,
    normed_latent_ref,
    attended_ref,
    compress_all,
    residual_ref,
    two_ref,
    scale_one_ref,
    scale_two_ref,
    cot_all,
    pick_ref,
    back_ref,
    rows_ref,
    queries,
    expand,
    combine,
    stat_to,
    stat_from,
    query_own,
    query_to,
    query_from,
    latent_to,
    latent_from,
    part,
    leaving,
    coming,
    routes,
    staged,
    load_sem,
    stat_sent,
    stat_arrived,
    line_sent,
    line_arrived,
    comp_sent,
    comp_arrived,
    comp_out_sent,
    comp_out_arrived,
    query_sent,
    query_arrived,
    latent_sent,
    latent_arrived,
    att_sent,
    att_arrived,
    sum_sent,
    sum_arrived,
    cot_sent,
    cot_arrived,
    route_sent,
    route_arrived,
    out_sent,
    out_arrived,
    pair_sent,
    pair_arrived,
):
    place, row, col = lax.axis_index("dp"), lax.axis_index("row"), lax.axis_index("col")
    other = 1 - col
    sibling = {"col": other}
    tokens, width = act_ref.shape
    slots = pick_ref.shape[1] // SQUARE
    mine = query_own.shape[2]
    sliced = compress_ref.shape[0]
    quarter = width // SQUARE
    score_scale = (NOPE + ROPE) ** (-0.5)
    loads = [
        pltpu.make_async_copy(source, target, load_sem.at[i])
        for i, (source, target) in enumerate(
            [(queries_ref, queries), (expand_ref, expand), (combine_ref, combine)]
        )
    ]
    for load in loads:
        load.start()

    def stat_copy(index):
        return remote(
            stat_to.at[index],
            stat_from.at[index],
            stat_sent.at[index],
            stat_arrived.at[index],
            sibling,
        )

    def scale_of(values, index):
        own = jnp.sum(values * values, axis=1, keepdims=True)
        stat_to[index] = jnp.broadcast_to(own, (tokens, 128))
        stat_copy(index).start()
        stat_copy(index).wait_recv()
        return lax.rsqrt((own + stat_from[index][:, 0:1]) / D + epsilon)

    def comp_piece(block, member):
        return compress_all.at[
            pl.ds(pl.multiple_of(block * sliced, 16), sliced),
            pl.ds(pl.multiple_of(member * quarter, 128), quarter),
        ]

    def comp_copy(block, way):
        here = comp_piece(block, place)
        return remote(
            here,
            here,
            comp_sent.at[block, way],
            comp_arrived.at[block],
            {"row": row + 1 - 2 * way},
        )

    def comp_each(block, act):
        @pl.when(jnp.logical_and(block <= row, row < ROWS - 1))
        def _():
            act(comp_copy(block, 0))

        @pl.when(jnp.logical_and(block >= row, row > 0))
        def _():
            act(comp_copy(block, 1))

    def comp_out(block, step, member):
        here = comp_piece(block, member)
        return remote(
            here,
            here,
            comp_out_sent.at[block, step],
            comp_out_arrived.at[block, step],
            {"dp": partner(place, step)},
        )

    line = Line(row, one_ref, line_sent, line_arrived)
    cot_line = Line(row, cot_all, cot_sent, cot_arrived)
    route_line = Line(row, routes, route_sent, route_arrived)
    sums = SumLine(row, part, leaving, coming, sum_sent, sum_arrived)

    greet(row, place, col)
    compress_all[pl.ds(pl.multiple_of(row * sliced, 16), sliced)] = compress_ref[...]
    compress_all[ROWS * sliced :] = jnp.zeros(
        (compress_all.shape[0] - ROWS * sliced, width), bf16
    )
    comp_each(row, lambda copy: copy.start())
    inputs = act_ref[...].astype(f32)
    scale_one = scale_of(inputs, 0)
    scale_one_ref[...] = scale_one
    one_ref[pl.ds(row, 1)] = (
        (inputs * scale_one * scaling_ref[...]).astype(bf16).reshape(1, tokens, width)
    )
    cot_all[pl.ds(row, 1)] = cot_ref[...].reshape(1, tokens, width)
    routes[pl.ds(row, 1)] = route_ref[...].reshape((1,) + route_ref.shape)
    line.pass_on(row)
    loads[0].wait()

    def query_copy(block):
        return remote(
            query_to.at[block],
            query_from.at[block],
            query_sent.at[block],
            query_arrived.at[block],
            sibling,
        )

    def latent_copy(block):
        return remote(
            latent_to.at[block],
            latent_from.at[block],
            latent_sent.at[block],
            latent_arrived.at[block],
            sibling,
        )

    def att_copy(block, half):
        here = attended_ref.at[block, :, pl.ds(pl.multiple_of(half * 2 * HEADV, 128), 2 * HEADV)]
        return remote(here, here, att_sent.at[block], att_arrived.at[block], sibling)

    def gather(step, carried):
        block = block_at(row, step)

        @pl.when(step > 0)
        def _():
            comp_copy(block, 0).wait_recv()
            comp_each(block, lambda copy: copy.start())
            for shift in (3, 2, 1):
                comp_out(block, shift, place).start()
            line.wait(block)
            line.pass_on(block)

        tokens_here = one_ref[block]
        query_to[block] = nn(
            tokens_here, queries[:, pl.ds(pl.multiple_of(other * mine, 128), mine)]
        ).astype(bf16)
        query_copy(block).start()
        query_own[block] = nn(tokens_here, queries[:, pl.ds(pl.multiple_of(col * mine, 128), mine)])
        return carried

    lax.fori_loop(0, ROWS, gather, 0)

    cot_line.pass_on(row)
    route_line.pass_on(row)

    def out_copy(block, step):
        piece = pl.ds(step * slots, slots)
        return remote(
            staged.at[block, piece],
            rows_ref.at[col, block, piece],
            out_sent.at[block, step],
            out_arrived.at[block, step],
            {"dp": partner(place, step)},
        )

    def pair_copy(block, half):
        here = rows_ref.at[half, block]
        return remote(here, here, pair_sent.at[block], pair_arrived.at[block], sibling)

    def take(step):
        block = block_at(row, step)

        @pl.when(step > 0)
        def _():
            route_line.wait(block)
            cot_line.wait(block)
            route_line.pass_on(block)
            cot_line.pass_on(block)

        before = (
            lax.broadcasted_iota(jnp.int32, (tokens, tokens), 0)
            < lax.broadcasted_iota(jnp.int32, (tokens, tokens), 1)
        ).astype(bf16)
        routing = routes[block]
        chosen = []
        for shift in range(SQUARE):
            expert = partner(place, shift) * ROWS + row
            hit = (routing[:TOP] == expert).astype(f32)
            chosen.append(jnp.max(hit, axis=0, keepdims=True))
        goes = jnp.concatenate(chosen + chosen, axis=0)
        rank = nn(goes.astype(bf16), before)
        for shift in range(SQUARE):
            slot = lax.broadcasted_iota(jnp.int32, (slots, tokens), 0).astype(f32)
            here = jnp.logical_and(slot == rank[shift : shift + 1], goes[shift : shift + 1] > 0.5)
            pick = here.astype(f32)
            pick_ref[block, shift * slots : (shift + 1) * slots] = pick.astype(bf16)
            back_ref[block, :, shift * slots : (shift + 1) * slots] = pick.T.astype(bf16)
        staged[block] = nn(pick_ref[block], cot_all[block]).astype(bf16)
        for shift in (3, 2, 1):
            out_copy(block, shift).start()
        rows_ref[col, block, 0:slots] = staged[block, 0:slots]

    def forward(step):
        block = block_at(row, step)
        for shift in range(1, SQUARE):
            out_copy(block, shift).wait_recv()
        pair_copy(block, col).start()

    def comp_arrive(block, carried):
        @pl.when(block != row)
        def _():
            for shift in range(1, SQUARE):
                comp_out(block, shift, partner(place, shift)).wait_recv()

        return carried

    lax.fori_loop(0, ROWS, comp_arrive, 0)

    def latents(block, carried):
        value = nt(one_ref[block], compress_all[...])
        latent_to[block] = value
        latent_copy(block).start()
        latent_ref[block] = value
        return carried

    lax.fori_loop(0, ROWS, latents, 0)
    take(0)
    loads[1].wait()

    def keys(block, carried):
        latent_copy(block).wait_recv()
        latent = latent_ref[block] + latent_from[block]
        latent_ref[block] = latent
        plain = latent[:, :RANK]
        scale = lax.rsqrt(jnp.mean(plain * plain, axis=1, keepdims=True) + epsilon)
        normed = (plain * scale * rescale_ref[...]).astype(bf16)
        normed_latent_ref[block] = normed
        own = 2 * (NOPE + HEADV)
        expanded = nn(normed, expand[:, pl.ds(pl.multiple_of(col * own, 128), own)])
        rope = latent[:, RANK:]
        rope = rope * key_cos_ref[block] + swap_halves(rope) * key_sin_ref[block]
        first = jnp.concatenate([expanded[:, :NOPE], rope], axis=1)
        second = jnp.concatenate([expanded[:, 2 * NOPE : 3 * NOPE], rope], axis=1)
        key_ref[0, block] = first.astype(bf16)
        key_ref[1, block] = pltpu.roll(second, ROPE, 1).astype(bf16)
        value_ref[0, block] = expanded[:, NOPE : 2 * NOPE].astype(bf16)
        value_ref[1, block] = expanded[:, 3 * NOPE :].astype(bf16)
        query_copy(block).wait_recv()
        query = query_own[block] + query_from[block].astype(f32)
        query_ref[block] = (
            query * cos_ref[block] + swap_halves(query) * sin_ref[block]
        ).astype(bf16)
        return carried

    lax.fori_loop(0, ROWS, keys, 0)
    seq = ROWS * tokens
    lanes = NOPE + 2 * ROPE

    def attend(turn, carried):
        block = block_at(row, ROWS - 1 - turn)
        visible = mark_ref[...] <= mark_rows_ref[block]
        for head in range(2):
            query = query_ref[block, :, head * NOPE : head * NOPE + lanes]
            scores = nt(query, key_ref[head].reshape(seq, lanes)) * score_scale
            scores = jnp.where(visible, scores, masked_score)
            weight = jnp.exp(scores - jnp.max(scores, axis=1, keepdims=True))
            probs = (weight / jnp.sum(weight, axis=1, keepdims=True)).astype(bf16)
            probs_ref[head, block] = probs
            result = nn(probs, value_ref[head].reshape(seq, HEADV)).astype(bf16)
            at = pl.multiple_of((col * 2 + head) * HEADV, 128)
            attended_ref[block, :, pl.ds(at, HEADV)] = result
        att_copy(block, col).start()

        @pl.when(jnp.logical_or(turn == 1, turn == 2))
        def _():
            take(turn)

        return carried

    lax.fori_loop(0, ROWS, attend, 0)
    loads[2].wait()

    def mix(turn, carried):
        block = block_at(row, ROWS - 1 - turn)
        att_copy(block, other).wait_recv()
        part[block] = nn(attended_ref[block], combine[...])
        sums.begin(block)
        return carried

    lax.fori_loop(0, ROWS, mix, 0)

    def hand_on(turn, carried):
        sums.pass_on(block_at(row, jnp.where(turn == 0, 3, turn)))

        @pl.when(turn == 0)
        def _():
            take(3)

        forward(turn)
        return carried

    lax.fori_loop(0, 3, hand_on, 0)
    sums.total(residual_ref)
    residual = residual_ref[...] + inputs
    residual_ref[...] = residual
    scale_two = scale_of(residual, 1)
    scale_two_ref[...] = scale_two
    two_ref[...] = (residual * scale_two * premix_ref[...]).astype(bf16)
    forward(3)

    def ended(block, carried):
        pair_copy(block, other).wait_recv()
        pair_copy(block, col).wait_send()
        for shift in range(1, SQUARE):
            out_copy(block, shift).wait_send()

            @pl.when(block != row)
            def _(shift=shift):
                comp_out(block, shift, place).wait_send()

        comp_each(block, lambda copy: copy.wait_send())
        query_copy(block).wait_send()
        latent_copy(block).wait_send()
        att_copy(block, col).wait_send()
        return carried

    lax.fori_loop(0, ROWS, ended, 0)
    stat_copy(0).wait_send()
    stat_copy(1).wait_send()
    sums.finish()
    line.finish()
    cot_line.finish()
    route_line.finish()


def turning_tables(length):
    half = ROPE // 2
    frequency = 10000.0 ** (-np.arange(half, dtype=np.float32) * 2.0 / ROPE)
    angles = np.arange(length, dtype=np.float32)[:, None] * frequency[None, :].astype(np.float32)
    cosine, sine = np.cos(angles), np.sin(angles)
    cosine, sine = np.concatenate([cosine, cosine], 1), np.concatenate([-sine, sine], 1)
    ones, zeros = np.ones((length, NOPE)), np.zeros((length, NOPE))
    gap = np.zeros((length, 128 - ROPE))
    tables = (
        np.concatenate([ones, cosine, ones, cosine], 1),
        np.concatenate([zeros, sine, zeros, sine], 1),
        np.concatenate([cosine, gap], 1),
        np.concatenate([sine, gap], 1),
    )
    return [
        jnp.asarray(table.reshape(ROWS, length // ROWS, -1).astype(np.float32))
        for table in tables
    ]


def pair_sems():
    return [DMA((ROWS,)), DMA((ROWS,))]


def line_sems():
    return [DMA((ROWS, 2)), DMA((ROWS,))]


def square_sems():
    return [DMA((ROWS, SQUARE)), DMA((ROWS, SQUARE))]


def sum_sems():
    return [DMA((ROWS, SPLIT)), DMA((2, ROWS, SPLIT))]


def run_attention(
    activations,
    scaling,
    queries,
    compress,
    rescale,
    expand,
    combine,
    premix,
    segments,
    cotangent,
    routing,
    tables,
    slots,
):
    tokens, width = activations.shape
    seq = ROWS * tokens
    mine = queries.shape[1] // COLS
    sliced = compress.shape[1]
    latent_width = RANK + 128
    picked = SQUARE * slots
    lanes = NOPE + 2 * ROPE
    routes = jnp.pad(routing.T, ((0, 8 - routing.shape[1]), (0, 0)), constant_values=-1)
    whole = pl.BlockSpec(memory_space=VMEM)
    far = pl.BlockSpec(memory_space=pl.ANY)

    def shape(*dims, dtype=bf16):
        return jax.ShapeDtypeStruct(dims, dtype)

    return pl.pallas_call(
        attend_kernel,
        name="attend",
        out_shape=(
            shape(ROWS, tokens, width),
            shape(ROWS, tokens, mine),
            shape(2, ROWS, tokens, lanes),
            shape(2, ROWS, tokens, HEADV),
            shape(2, ROWS, tokens, seq),
            shape(ROWS, tokens, latent_width, dtype=f32),
            shape(ROWS, tokens, RANK),
            shape(ROWS, tokens, COLS * 2 * HEADV),
            shape(latent_width, width),
            shape(tokens, width, dtype=f32),
            shape(tokens, width),
            shape(tokens, 1, dtype=f32),
            shape(tokens, 1, dtype=f32),
            shape(ROWS, tokens, width),
            shape(ROWS, picked, tokens),
            shape(ROWS, tokens, picked),
            shape(COLS, ROWS, picked, width),
        ),
        in_specs=[whole] * 13 + [far] * 3,
        out_specs=(whole,) * 17,
        scratch_shapes=[
            VMEM(queries.shape, bf16),
            VMEM(expand.shape, bf16),
            VMEM(combine.shape, bf16),
            VMEM((2, tokens, 128), f32),
            VMEM((2, tokens, 128), f32),
            VMEM((ROWS, tokens, mine), f32),
            VMEM((ROWS, tokens, mine), bf16),
            VMEM((ROWS, tokens, mine), bf16),
            VMEM((ROWS, tokens, latent_width), f32),
            VMEM((ROWS, tokens, latent_width), f32),
            VMEM((ROWS, tokens, width), f32),
            VMEM((ROWS, tokens, width), bf16),
            VMEM((2, ROWS, tokens, width), bf16),
            VMEM((ROWS,) + routes.shape, jnp.int32),
            VMEM((ROWS, picked, width), bf16),
            DMA((3,)),
            DMA((2,)),
            DMA((2,)),
            *line_sems(),
            *line_sems(),
            *square_sems(),
            *pair_sems(),
            *pair_sems(),
            *pair_sems(),
            *sum_sems(),
            *line_sems(),
            *line_sems(),
            *square_sems(),
            *pair_sems(),
        ],
        compiler_params=pltpu.CompilerParams(
            collective_id=1, has_side_effects=True, vmem_limit_bytes=56 * MIB
        ),
        cost_estimate=pl.CostEstimate(
            flops=40 * 1024**3, bytes_accessed=32 * MIB, transcendentals=0
        ),
    )(
        activations,
        scaling.reshape(1, width),
        compress.T,
        rescale.reshape(1, RANK),
        premix.reshape(1, width),
        *tables,
        segments.reshape(ROWS, tokens, 1),
        segments.reshape(1, seq),
        cotangent,
        routes,
        queries,
        expand,
        combine,
    )


def attend_back_kernel(
    normed_grad_ref,
    residual_ref,
    scale_two_ref,
    premix_ref,
    cot_ref,
    act_ref,
    scale_one_ref,
    scaling_ref,
    one_ref,
    query_ref,
    key_ref,
    value_ref,
    probs_ref,
    latent_ref,
    rescale_ref,
    cos_ref,
    sin_ref,
    key_cos_ref,
    key_sin_ref,
    compress_all,
    queries_ref,
    expand_ref,
    combine_ref,
    input_grad_ref,
    branch_ref,
    query_grad_ref,
    expanded_ref,
    own_latent_ref,
    scaling_rows,
    rescale_rows,
    queries,
    expand,
    combine,
    stat_to,
    stat_from,
    grad_own,
    grad_to,
    grad_from,
    key_grad,
    value_grad,
    latent_own,
    latent_to,
    latent_from,
    turned,
    turned_from,
    part,
    leaving,
    coming,
    total,
    load_sem,
    stat_sent,
    stat_arrived,
    line_sent,
    line_arrived,
    grad_sent,
    grad_arrived,
    query_sent,
    query_arrived,
    latent_sent,
    latent_arrived,
    turned_sent,
    turned_arrived,
    own_sent,
    own_arrived,
    sum_sent,
    sum_arrived,
):
    place, row, col = lax.axis_index("dp"), lax.axis_index("row"), lax.axis_index("col")
    other = 1 - col
    sibling = {"col": other}
    tokens, width = act_ref.shape
    seq = ROWS * tokens
    mine = query_ref.shape[2]
    lanes = key_ref.shape[3]
    both = 2 * HEADV
    sliced = own_latent_ref.shape[0]
    score_scale = (NOPE + ROPE) ** (-0.5)
    loads = [
        pltpu.make_async_copy(source, target, load_sem.at[i])
        for i, (source, target) in enumerate(
            [(combine_ref, combine), (queries_ref, queries), (expand_ref, expand)]
        )
    ]
    for load in loads:
        load.start()
    line = Line(row, branch_ref, line_sent, line_arrived)
    sums = SumLine(row, part, leaving, coming, sum_sent, sum_arrived)
    greet(row, place, col, square=False)

    def stat_copy(index):
        return remote(
            stat_to.at[index],
            stat_from.at[index],
            stat_sent.at[index],
            stat_arrived.at[index],
            sibling,
        )

    def norm_grad(values, scale, gain, upstream, index):
        weighted = upstream * gain
        own = jnp.sum(weighted * values, axis=1, keepdims=True)
        stat_to[index] = jnp.broadcast_to(own, (tokens, 128))
        stat_copy(index).start()
        stat_copy(index).wait_recv()
        inner = (own + stat_from[index][:, 0:1]) / D
        return weighted * scale - values * (scale * scale * scale * inner)

    residual_grad = cot_ref[...].astype(f32) + norm_grad(
        residual_ref[...], scale_two_ref[...], premix_ref[...], normed_grad_ref[...], 0
    )
    input_grad_ref[...] = residual_grad
    branch_ref[pl.ds(row, 1)] = residual_grad.astype(bf16).reshape(1, tokens, width)
    key_grad[...] = jnp.zeros_like(key_grad)
    value_grad[...] = jnp.zeros_like(value_grad)
    scaling_rows[...] = jnp.zeros_like(scaling_rows)
    rescale_rows[...] = jnp.zeros_like(rescale_rows)

    def grad_copy(block):
        return remote(
            grad_to.at[block],
            grad_from.at[block],
            grad_sent.at[block],
            grad_arrived.at[block],
            sibling,
        )

    def query_copy(block, half):
        here = query_grad_ref.at[block, :, pl.ds(pl.multiple_of(half * mine, 128), mine)]
        return remote(here, here, query_sent.at[block], query_arrived.at[block], sibling)

    def latent_copy(block):
        return remote(
            latent_to.at[block],
            latent_from.at[block],
            latent_sent.at[block],
            latent_arrived.at[block],
            sibling,
        )

    def arrive(step):
        block = block_at(row, step)

        @pl.when(step > 0)
        def _():
            line.wait(block)

        line.pass_on(block)

        @pl.when(step == 0)
        def _():
            loads[0].wait()

        grads = branch_ref[block]
        grad_to[block] = nt(
            grads, combine[pl.ds(pl.multiple_of(other * both, 16), both)]
        ).astype(bf16)
        grad_copy(block).start()
        grad_own[block] = nt(grads, combine[pl.ds(pl.multiple_of(col * both, 16), both)])

    def heads(step):
        block = block_at(row, step)
        grad_copy(block).wait_recv()
        grads = (grad_own[block] + grad_from[block].astype(f32)).astype(bf16)
        pieces = []
        for head in range(2):
            upstream = grads[:, head * HEADV : (head + 1) * HEADV]
            query = query_ref[block, :, head * NOPE : head * NOPE + lanes]
            probs = probs_ref[head, block]
            weight = probs.astype(f32)
            probs_back = nt(upstream, value_ref[head].reshape(seq, HEADV))
            inner = jnp.sum(weight * probs_back, axis=1, keepdims=True)
            score_grad = (weight * (probs_back - inner)).astype(bf16)
            pieces.append(nn(score_grad, key_ref[head].reshape(seq, lanes)) * score_scale)
            key_grad[head] += tn(score_grad, query)
            value_grad[head] += tn(probs, upstream)
        first, second = pieces
        grad = jnp.concatenate(
            [first[:, :NOPE], first[:, NOPE:] + second[:, :NOPE], second[:, NOPE:]], axis=1
        )
        grad = grad * cos_ref[block] - swap_halves(grad) * sin_ref[block]
        query_grad_ref[block, :, pl.ds(pl.multiple_of(col * mine, 128), mine)] = grad.astype(bf16)
        query_copy(block, col).start()

    def project(step):
        block = block_at(row, step)

        @pl.when(step == 0)
        def _():
            loads[1].wait()

        query_copy(block, other).wait_recv()
        part[block] = nt(query_grad_ref[block], queries[...])

    def turn(step, carried):
        for delay, stage in ((0, arrive), (1, heads), (2, project)):

            @pl.when(jnp.logical_and(step >= delay, step < delay + ROWS))
            def _(delay=delay, stage=stage):
                stage(step - delay)

        return carried

    lax.fori_loop(0, ROWS + 1, turn, 0)
    loads[2].wait()

    def latents(turn, carried):
        block = block_at(row, ROWS - 1 - turn)
        here = pl.ds(pl.multiple_of(block * tokens, 128), tokens)
        first = key_grad[0, here] * score_scale
        second = pltpu.roll(key_grad[1, here] * score_scale, lanes - ROPE, 1)
        grad = jnp.concatenate(
            [first[:, :NOPE], value_grad[0, here], second[:, :NOPE], value_grad[1, here]], axis=1
        ).astype(bf16)
        expanded_ref[block] = grad
        own = 2 * (NOPE + HEADV)
        upstream = nt(grad, expand[:, pl.ds(pl.multiple_of(col * own, 128), own)])
        plain = latent_ref[block][:, :RANK]
        scale = lax.rsqrt(jnp.mean(plain * plain, axis=1, keepdims=True) + epsilon)
        rescale_rows[...] += jnp.sum(
            (upstream * plain * scale).reshape(tokens // 8, 8, RANK), axis=0
        )
        weighted = upstream * rescale_ref[...]
        inner = jnp.mean(weighted * plain, axis=1, keepdims=True)
        plain_grad = weighted * scale - plain * (scale * scale * scale * inner)
        rope = first[:, NOPE:] + second[:, NOPE:]
        lane = lax.broadcasted_iota(jnp.int32, rope.shape, 1)
        rope = jnp.where(lane < ROPE, rope, 0.0)
        rope = rope * key_cos_ref[block] - swap_halves(rope) * key_sin_ref[block]
        value = jnp.concatenate([plain_grad, rope], axis=1)
        latent_own[block] = value
        latent_to[block] = value.astype(bf16)
        latent_copy(block).start()
        return carried

    lax.fori_loop(0, ROWS, latents, 0)
    project(ROWS - 1)

    def turned_piece(member):
        return turned.at[
            pl.ds(pl.multiple_of(member * sliced, 16), sliced),
            pl.ds(pl.multiple_of(col * (seq // COLS), 128), seq // COLS),
        ]

    def turned_copy(step):
        to = lax.rem(row + step, ROWS)
        return remote(
            turned_piece(to),
            turned_from.at[step],
            turned_sent.at[step],
            turned_arrived.at[step],
            {"row": to},
        )

    def mix(turn, carried):
        block = block_at(row, ROWS - 1 - turn)
        latent_copy(block).wait_recv()
        latent = latent_own[block] + latent_from[block].astype(f32)
        here = pl.ds(pl.multiple_of(block * tokens, 128), tokens)
        total_here = part[block] + nn(latent.astype(bf16), compress_all[...])
        part[block] = total_here
        sums.begin(block)
        turned[:, here] = latent.T.astype(bf16)
        scaling_rows[...] += jnp.sum(
            (total_here * one_ref[block].astype(f32)).reshape(tokens // 8, 8, width), axis=0
        )
        return carried

    lax.fori_loop(0, ROWS, mix, 0)
    for step in range(1, ROWS):
        turned_copy(step).start()

    def hand_on(turn, carried):
        sums.pass_on(block_at(row, jnp.where(turn == 0, 3, turn)))
        return carried

    lax.fori_loop(0, 3, hand_on, 0)
    for step in range(1, ROWS):
        turned_copy(step).wait_recv()
    half = pl.ds(pl.multiple_of(col * (seq // COLS), 128), seq // COLS)
    own_sum = turned[pl.ds(pl.multiple_of(row * sliced, 16), sliced), half].astype(f32)
    for step in range(1, ROWS):
        own_sum = own_sum + turned_from[step].astype(f32)
    own_latent_ref[:, half] = own_sum.astype(bf16)

    def own_copy(part_of):
        here = own_latent_ref.at[
            :, pl.ds(pl.multiple_of(part_of * (seq // COLS), 128), seq // COLS)
        ]
        return remote(here, here, own_sent.at[0], own_arrived.at[0], sibling)

    own_copy(col).start()
    sums.total(total)
    input_grad_ref[...] += norm_grad(
        act_ref[...].astype(f32), scale_one_ref[...], scaling_ref[...], total[...], 1
    )
    own_copy(other).wait_recv()
    own_copy(col).wait_send()

    def ended(block, carried):
        grad_copy(block).wait_send()
        query_copy(block, col).wait_send()
        latent_copy(block).wait_send()
        return carried

    lax.fori_loop(0, ROWS, ended, 0)
    for step in range(1, ROWS):
        turned_copy(step).wait_send()
    stat_copy(0).wait_send()
    stat_copy(1).wait_send()
    sums.finish()
    line.finish()


def run_attention_back(
    normed_grad,
    residual,
    scale_two,
    premix,
    cotangent,
    activations,
    scale_one,
    scaling,
    one,
    query,
    key,
    value,
    probs,
    latent,
    rescale,
    tables,
    compress_all,
    queries,
    expand,
    combine,
):
    tokens, width = activations.shape
    seq = ROWS * tokens
    mine = query.shape[2]
    lanes = key.shape[3]
    latent_width = latent.shape[2]
    sliced = (RANK + ROPE) // ROWS
    whole = pl.BlockSpec(memory_space=VMEM)
    far = pl.BlockSpec(memory_space=pl.ANY)

    def shape(*dims, dtype=bf16):
        return jax.ShapeDtypeStruct(dims, dtype)

    return pl.pallas_call(
        attend_back_kernel,
        name="attend_back",
        out_shape=(
            shape(tokens, width, dtype=f32),
            shape(ROWS, tokens, width),
            shape(ROWS, tokens, COLS * mine),
            shape(ROWS, tokens, 2 * (NOPE + HEADV)),
            shape(sliced, seq),
            shape(8, width, dtype=f32),
            shape(8, RANK, dtype=f32),
        ),
        in_specs=[whole] * 20 + [far] * 3,
        out_specs=(whole,) * 7,
        scratch_shapes=[
            VMEM(queries.shape, bf16),
            VMEM(expand.shape, bf16),
            VMEM(combine.shape, bf16),
            VMEM((2, tokens, 128), f32),
            VMEM((2, tokens, 128), f32),
            VMEM((ROWS, tokens, 2 * HEADV), f32),
            VMEM((ROWS, tokens, 2 * HEADV), bf16),
            VMEM((ROWS, tokens, 2 * HEADV), bf16),
            VMEM((2, seq, lanes), f32),
            VMEM((2, seq, HEADV), f32),
            VMEM((ROWS, tokens, latent_width), f32),
            VMEM((ROWS, tokens, latent_width), bf16),
            VMEM((ROWS, tokens, latent_width), bf16),
            VMEM((latent_width, seq), bf16),
            VMEM((ROWS, sliced, seq // COLS), bf16),
            VMEM((ROWS, tokens, width), f32),
            VMEM((ROWS, tokens, width), bf16),
            VMEM((2, ROWS, tokens, width), bf16),
            VMEM((tokens, width), f32),
            DMA((3,)),
            DMA((2,)),
            DMA((2,)),
            *line_sems(),
            *pair_sems(),
            *pair_sems(),
            *pair_sems(),
            *pair_sems(),
            *pair_sems(),
            *sum_sems(),
        ],
        compiler_params=pltpu.CompilerParams(
            collective_id=3, has_side_effects=True, vmem_limit_bytes=56 * MIB
        ),
        cost_estimate=pl.CostEstimate(
            flops=40 * 1024**3, bytes_accessed=32 * MIB, transcendentals=0
        ),
    )(
        normed_grad,
        residual,
        scale_two,
        premix.reshape(1, width),
        cotangent,
        activations,
        scale_one,
        scaling.reshape(1, width),
        one,
        query,
        key,
        value,
        probs,
        latent,
        rescale.reshape(1, RANK),
        *tables,
        compress_all,
        queries,
        expand,
        combine,
    )


def silu_pair(values):
    sigmoid = 1.0 / (1.0 + jnp.exp(-values))
    return values * sigmoid, sigmoid * (1.0 + values * (1.0 - sigmoid))


def expert_kernel(
    normed_ref,
    pick_ref,
    back_ref,
    cot_rows_ref,
    cot_ref,
    fan_ref,
    fun_ref,
    wide_ref,
    narrow_ref,
    router_ref,
    sum_ref,
    gathered_ref,
    rows_out,
    gu_out,
    hidden_out,
    logit_out,
    shared_out,
    shared_gu_out,
    premix_ref,
    fan,
    fun,
    wide,
    narrow,
    cot_rows,
    rows,
    staged,
    gu,
    hidden,
    pair_own,
    pair_to,
    pair_from,
    home,
    shared_own,
    shared_to,
    shared_from,
    part,
    passed_to,
    passed_from,
    load_sem,
    store_sem,
    line_sent,
    line_arrived,
    out_sent,
    out_arrived,
    fwd_sent,
    fwd_arrived,
    shared_sent,
    shared_arrived,
    half_sent,
    half_arrived,
    home_sent,
    home_arrived,
    sum_sent,
    sum_arrived,
):
    place, row, col = lax.axis_index("dp"), lax.axis_index("row"), lax.axis_index("col")
    other = 1 - col
    tokens, width = normed_ref.shape
    picked = pick_ref.shape[1]
    slots = picked // SQUARE
    hid = fun.shape[0]
    share = narrow.shape[0]
    experts = router_ref.shape[1]
    loads = [
        pltpu.make_async_copy(source, target, load_sem.at[i])
        for i, (source, target) in enumerate(
            [
                (wide_ref, wide),
                (narrow_ref, narrow),
                (fan_ref, fan),
                (cot_rows_ref, cot_rows),
                (fun_ref, fun),
            ]
        )
    ]
    for load in loads:
        load.start()
    greet(row, place, col)
    gathered_ref[pl.ds(row, 1)] = normed_ref[...].reshape(1, tokens, width)
    premix_ref[...] = jnp.zeros_like(premix_ref)
    line = Line(row, gathered_ref, line_sent, line_arrived)
    sums = SumLine(row, part, passed_to, passed_from, sum_sent, sum_arrived)
    sibling = {"col": other}

    def out_copy(block, step):
        piece = pl.ds(step * slots, slots)
        return remote(
            staged.at[block, piece],
            rows.at[col, block, piece],
            out_sent.at[block, step],
            out_arrived.at[block, step],
            {"dp": partner(place, step)},
        )

    def home_copy(block, step):
        piece = pl.ds(step * slots, slots)
        return remote(
            staged.at[block, piece],
            home.at[block, piece],
            home_sent.at[block, step],
            home_arrived.at[block, step],
            {"dp": partner(place, step)},
        )

    def fwd_copy(block, half):
        here = rows.at[half, block]
        return remote(here, here, fwd_sent.at[block], fwd_arrived.at[block], sibling)

    def shared_copy(block):
        return remote(
            shared_to.at[block],
            shared_from.at[block],
            shared_sent.at[block],
            shared_arrived.at[block],
            sibling,
        )

    def half_copy(block):
        return remote(
            pair_to.at[block],
            pair_from.at[block],
            half_sent.at[block],
            half_arrived.at[block],
            sibling,
        )

    def stores(block):
        return [
            pltpu.make_async_copy(source, target, store_sem.at[index, block])
            for index, (source, target) in enumerate(
                [
                    (rows.at[:, block], rows_out.at[:, block]),
                    (gu.at[:, block], gu_out.at[:, block]),
                    (hidden.at[block], hidden_out.at[block]),
                ]
            )
        ]

    def take(step):
        block = block_at(row, step)

        @pl.when(step > 0)
        def _():
            line.wait(block)

        line.pass_on(block)
        staged[block] = nn(pick_ref[block], gathered_ref[block]).astype(bf16)
        for shift in (3, 2, 1):
            out_copy(block, shift).start()
        rows[col, block, 0:slots] = staged[block, 0:slots]

        @pl.when(step == 0)
        def _():
            loads[0].wait()
            loads[1].wait()

        slot = lax.rem(step, 2)
        for index, value in enumerate(
            (
                nn(gathered_ref[block], wide[0]),
                nn(gathered_ref[block], wide[1]),
                nt(cot_ref[block], narrow[...]),
            )
        ):
            shared_own[slot, index] = value
            shared_to[block, index] = value.astype(bf16)
        shared_copy(block).start()

    def forward(step):
        block = block_at(row, step)
        for shift in range(1, SQUARE):
            out_copy(block, shift).wait_recv()
        fwd_copy(block, col).start()

    def shared(step):
        block = block_at(row, step)
        slot = lax.rem(step, 2)
        shared_copy(block).wait_recv()
        gate, up, grad = [
            shared_own[slot, index] + shared_from[block, index].astype(f32) for index in range(3)
        ]
        act, slope = silu_pair(gate)
        shared_out[block] = (act * up).astype(bf16)
        gate_grad = (grad * up * slope).astype(bf16)
        up_grad = (grad * act).astype(bf16)
        shared_gu_out[0, block] = gate_grad
        shared_gu_out[1, block] = up_grad
        part[block] = nt(gate_grad, wide[0]) + nt(up_grad, wide[1])

    def experts_of(step):
        block = block_at(row, step)
        fwd_copy(block, other).wait_recv()

        @pl.when(step == 0)
        def _():
            for load in loads[2:]:
                load.wait()

        left, right = rows[0, block], rows[1, block]
        logits = nn(left, router_ref[0:width]) + nn(right, router_ref[width:])
        logits = logits - jnp.max(logits, axis=1, keepdims=True)
        weight = jnp.exp(logits)
        probs = weight / jnp.sum(weight, axis=1, keepdims=True)
        own = (
            lax.broadcasted_iota(jnp.int32, (picked, experts), 1) == place * ROWS + row
        ).astype(f32)
        gates = jnp.sum(probs * own, axis=1, keepdims=True)
        raw = nt(cot_rows[0, block], fun[:, 0:width]) + nt(cot_rows[1, block], fun[:, width:])
        gate = nn(left, fan[0, 0:width]) + nn(right, fan[0, width:])
        up = nn(left, fan[1, 0:width]) + nn(right, fan[1, width:])
        act, slope = silu_pair(gate)
        value = act * up
        hidden[block] = value.astype(bf16)
        gate_sum = gates * jnp.sum(value * raw, axis=1, keepdims=True)
        logit_grad = gate_sum * (own - probs)
        logit_out[block, :, 0:experts] = logit_grad
        logit_out[block, :, experts : experts + 1] = gates
        raw = raw * gates
        gu[0, block] = (raw * up * slope).astype(bf16)
        gu[1, block] = (raw * act).astype(bf16)
        logit_grad = logit_grad.astype(bf16)

        def half_of(half):
            lines = pl.ds(pl.multiple_of(half * width, width), width)
            return (
                nt(gu[0, block], fan[0, lines])
                + nt(gu[1, block], fan[1, lines])
                + nt(logit_grad, router_ref[lines])
            )

        pair_to[block] = half_of(other).astype(bf16)
        half_copy(block).start()
        pair_own[...] = half_of(col)
        for copy in stores(block):
            copy.start()

    def send_home(step):
        block = block_at(row, step)
        for shift in range(1, SQUARE):
            out_copy(block, shift).wait_send()
        half_copy(block).wait_recv()
        staged[block] = (pair_own[...] + pair_from[block].astype(f32)).astype(bf16)
        for shift in (3, 2, 1):
            home_copy(block, shift).start()
        home[block, 0:slots] = staged[block, 0:slots]

    def add_up(step):
        block = block_at(row, step)
        for shift in range(1, SQUARE):
            home_copy(block, shift).wait_recv()
        total = part[block] + nn(back_ref[block], home[block])
        part[block] = total
        premix_ref[...] += jnp.sum(
            (total * gathered_ref[block].astype(f32)).reshape(tokens // 8, 8, width), axis=0
        )

        sums.begin(block)

    stages = (
        (0, take),
        (1, forward),
        (1, shared),
        (3, send_home),
        (2, experts_of),
        (4, add_up),
    )

    def turn(step, carried):
        for delay, stage in stages:

            @pl.when(jnp.logical_and(step >= delay, step < delay + ROWS))
            def _(delay=delay, stage=stage):
                stage(step - delay)

        @pl.when(step >= ROWS + 3)
        def _():
            sums.pass_on(block_at(row, jnp.where(step == ROWS + 5, 1, step - 5)))

        return carried

    lax.fori_loop(0, ROWS + 6, turn, 0)
    sums.total(sum_ref)

    def ended(block, carried):
        shared_copy(block).wait_send()
        fwd_copy(block, col).wait_send()
        half_copy(block).wait_send()
        for shift in range(1, SQUARE):
            home_copy(block, shift).wait_send()
        for copy in stores(block):
            copy.wait()
        return carried

    lax.fori_loop(0, ROWS, ended, 0)
    sums.finish()
    line.finish()


def run_experts(
    normed, pick, back, cot_rows, cot_all, fan, fun, wide, narrow, router_all
):
    tokens, width = normed.shape
    picked = pick.shape[1]
    hid = fun.shape[0]
    share = narrow.shape[0]
    experts = router_all.shape[1]
    whole = pl.BlockSpec(memory_space=VMEM)
    far = pl.BlockSpec(memory_space=pl.ANY)

    def shape(*dims, dtype=bf16):
        return jax.ShapeDtypeStruct(dims, dtype)

    return pl.pallas_call(
        expert_kernel,
        name="experts",
        out_shape=(
            shape(tokens, width, dtype=f32),
            shape(ROWS, tokens, width),
            shape(COLS, ROWS, picked, width),
            shape(2, ROWS, picked, hid),
            shape(ROWS, picked, hid),
            shape(ROWS, picked, experts + 1, dtype=f32),
            shape(ROWS, tokens, share),
            shape(2, ROWS, tokens, share),
            shape(8, width, dtype=f32),
        ),
        in_specs=[whole, whole, whole, far, whole, far, far, far, far, whole],
        out_specs=(whole, whole, far, far, far, whole, whole, whole, whole),
        scratch_shapes=[
            VMEM(fan.shape, bf16),
            VMEM(fun.shape, bf16),
            VMEM(wide.shape, bf16),
            VMEM(narrow.shape, bf16),
            VMEM(cot_rows.shape, bf16),
            VMEM((COLS, ROWS, picked, width), bf16),
            VMEM((ROWS, picked, width), bf16),
            VMEM((2, ROWS, picked, hid), bf16),
            VMEM((ROWS, picked, hid), bf16),
            VMEM((picked, width), f32),
            VMEM((ROWS, picked, width), bf16),
            VMEM((ROWS, picked, width), bf16),
            VMEM((ROWS, picked, width), bf16),
            VMEM((2, 3, tokens, share), f32),
            VMEM((ROWS, 3, tokens, share), bf16),
            VMEM((ROWS, 3, tokens, share), bf16),
            VMEM((ROWS, tokens, width), f32),
            VMEM((ROWS, tokens, width), bf16),
            VMEM((2, ROWS, tokens, width), bf16),
            DMA((5,)),
            DMA((3, ROWS)),
            DMA((ROWS, 2)),
            DMA((ROWS,)),
            DMA((ROWS, SQUARE)),
            DMA((ROWS, SQUARE)),
            DMA((ROWS,)),
            DMA((ROWS,)),
            DMA((ROWS,)),
            DMA((ROWS,)),
            DMA((ROWS,)),
            DMA((ROWS,)),
            DMA((ROWS, SQUARE)),
            DMA((ROWS, SQUARE)),
            DMA((ROWS, SPLIT)),
            DMA((2, ROWS, SPLIT)),
        ],
        compiler_params=pltpu.CompilerParams(
            collective_id=2, has_side_effects=True, vmem_limit_bytes=62 * MIB
        ),
        cost_estimate=pl.CostEstimate(
            flops=60 * 1024**3, bytes_accessed=64 * MIB, transcendentals=0
        ),
    )(normed, pick, back, cot_rows, cot_all, fan, fun, wide, narrow, router_all)


def swap_back(parts):
    moves = [[(i, i ^ step) for i in range(SQUARE)] for step in range(SQUARE)]
    return [parts[0]] + [
        lax.ppermute(parts[step], "dp", moves[step]) for step in range(1, SQUARE)
    ]


def local_square(
    activations,
    cotangent,
    routing,
    segments,
    scaling,
    queries,
    compress,
    rescale,
    expand,
    combine,
    premix,
    router,
    widening,
    narrowing,
    fanout,
    funnel,
):
    dp_count = lax.axis_size("dp")
    row_count = lax.axis_size("row")
    col_count = lax.axis_size("col")
    col_index = lax.axis_index("col")
    local_rows, col_width = activations.shape
    seq_length = local_rows * row_count
    expert_total = router.shape[1]
    capacity = local_rows * TOP * 4 // (3 * expert_total)
    slot_total = capacity * row_count * dp_count
    tables = turning_tables(seq_length)
    router_all = col_gather(router)
    (
        one,
        query,
        key,
        value,
        probs,
        latent,
        latent_normed,
        attended,
        compress_all,
        residual,
        normed_two,
        scale_one,
        scale_two,
        cot_blocks,
        pick,
        back,
        cot_rows,
    ) = run_attention(
        activations,
        scaling,
        queries,
        compress,
        rescale,
        expand,
        combine,
        premix,
        segments,
        cotangent,
        routing,
        tables,
        capacity,
    )
    (
        normed_grad,
        two_blocks,
        expert_rows,
        expert_gu_grad,
        expert_hidden,
        slot_values,
        hidden_blocks,
        gu_blocks,
        premix_rows,
    ) = run_experts(
        normed_two,
        pick,
        back,
        cot_rows,
        cot_blocks,
        fanout[0],
        funnel[0],
        widening,
        narrowing,
        router_all,
    )
    cotangent_all = cot_blocks.reshape(seq_length, col_width)
    gathered_two = two_blocks.reshape(seq_length, col_width)
    hidden_all = hidden_blocks.reshape(seq_length, -1)
    gu_grad_all = gu_blocks.reshape(2, seq_length, -1)
    slot_rows = expert_rows.reshape(col_count, slot_total, col_width)
    reply_grad_rows = cot_rows.reshape(col_count, slot_total, col_width)
    slot_hidden = expert_hidden.reshape(slot_total, -1)
    slot_gu_grad = expert_gu_grad.reshape(2, slot_total, -1)
    slot_values = slot_values.reshape(slot_total, -1)
    logit_grad = slot_values[:, :expert_total].astype(bf16)
    slot_gates = slot_values[:, expert_total]

    narrowing_grad = dot_tn(hidden_all, cotangent_all)
    widening_grad = jnp.stack([dot_tn(gathered_two, gu_grad_all[i]) for i in range(2)])
    shared_sums = lax.psum((narrowing_grad.astype(bf16), widening_grad.astype(bf16)), "dp")
    (
        input_grad,
        branch_blocks,
        query_grad,
        expanded_grad,
        own_latent_grad,
        scaling_rows,
        rescale_rows,
    ) = run_attention_back(
        normed_grad,
        residual,
        scale_two,
        premix,
        cotangent,
        activations,
        scale_one,
        scaling,
        one,
        query,
        key,
        value,
        probs,
        latent,
        rescale,
        tables,
        compress_all,
        queries,
        expand,
        combine,
    )
    gathered_one = one.reshape(seq_length, col_width)
    attended_all = attended.reshape(seq_length, -1)
    late_parts = (
        dot_tn(gathered_one, query_grad.reshape(seq_length, -1)).astype(bf16),
        dot_tn(
            latent_normed.reshape(seq_length, -1), expanded_grad.reshape(seq_length, -1)
        ).astype(bf16),
        dot(own_latent_grad, gathered_one).astype(bf16),
        dot_tn(attended_all, branch_blocks.reshape(seq_length, col_width)).astype(bf16),
    )
    late_parts = (after(late_parts[0], *shared_sums),) + late_parts[1:]
    queries_sum, expand_sum, compress_sum, combine_sum = lax.psum(late_parts, "dp")

    scaled_hidden = (slot_hidden.astype(f32) * slot_gates[:, None]).astype(bf16)
    reply_part = dot(scaled_hidden, funnel[0])
    summed = col_scatter(reply_part.astype(bf16), axis=1)
    summed = summed.reshape(row_count, dp_count, capacity, col_width)
    returned = jnp.stack(swap_back([summed[:, k] for k in range(dp_count)]), axis=1)
    routed = jnp.einsum(
        "bts,bsd->btd",
        back,
        returned.reshape(row_count, dp_count * capacity, col_width),
        preferred_element_type=f32,
    ).reshape(seq_length, col_width)
    shared_out = row_scatter(routed + dot(hidden_all, narrowing))
    layer_output = (residual + shared_out).astype(bf16)

    funnel_grad = jnp.concatenate(
        [dot_tn(scaled_hidden, reply_grad_rows[i]) for i in range(col_count)], axis=1
    )[None]
    fanout_grad = jnp.stack(
        [
            jnp.concatenate([dot_tn(slot_rows[i], slot_gu_grad[j]) for i in range(col_count)])
            for j in range(2)
        ]
    )[None]

    router_part = jnp.concatenate([dot_tn(slot_rows[i], logit_grad) for i in range(col_count)])
    router_part = col_scatter(router_part)
    premix_part = jnp.sum(premix_rows, axis=0) / premix
    scaling_part = jnp.sum(scaling_rows, axis=0) / scaling
    rescale_part = col_totals(jnp.sum(rescale_rows, axis=0))
    small = jnp.concatenate(
        [premix_part, scaling_part, rescale_part, router_part.reshape(-1)]
    )
    small = lax.psum(small, ("dp", "row"))
    return (
        layer_output,
        input_grad,
        small[col_width : 2 * col_width],
        queries_sum.astype(f32),
        compress_sum.T.astype(f32),
        small[2 * col_width : 2 * col_width + RANK],
        col_gather(expand_sum, axis=1).astype(f32),
        combine_sum.astype(f32),
        small[:col_width],
        small[2 * col_width + RANK :].reshape(col_width, expert_total),
        shared_sums[1].astype(f32),
        shared_sums[0].astype(f32),
        fanout_grad,
        funnel_grad,
    )


def local(
    activations,
    cotangent,
    routing,
    segments,
    scaling,
    queries,
    compress,
    rescale,
    expand,
    combine,
    premix,
    router,
    widening,
    narrowing,
    fanout,
    funnel,
):
    dp_count = lax.axis_size("dp")
    row_count = lax.axis_size("row")
    col_count = lax.axis_size("col")
    dp_index = lax.axis_index("dp")
    row_index = lax.axis_index("row")
    col_index = lax.axis_index("col")
    local_rows = activations.shape[0]
    col_width = activations.shape[1]
    seq_length = local_rows * row_count
    half_length = seq_length // col_count
    head_width = NOPE + ROPE
    pair_width = NOPE + HEADV
    local_heads = queries.shape[1] // head_width
    slice_width = compress.shape[1]
    expert_total = router.shape[1]
    capacity = local_rows * TOP * 4 // (3 * expert_total)
    slots = capacity * row_count
    slot_total = slots * dp_count
    block_rows = min(512, half_length)
    block_count = half_length // block_rows
    score_scale = head_width ** (-0.5)

    inputs = activations.astype(f32)
    scale_one = norm_scale(inputs)
    normed_one = (inputs * scale_one[:, None] * scaling).astype(bf16)
    gathered_one = row_gather(normed_one)
    compress_all = lax.all_gather(compress, "row", axis=1, tiled=True)

    routing_all = row_gather(routing)
    cotangent_all = row_gather(after(cotangent, gathered_one))
    offsets = jnp.arange(dp_count, dtype=jnp.int32)
    my_experts = ((dp_index + offsets) % dp_count) * row_count + row_index
    goes = jnp.any(routing_all[None, :, :] == my_experts[:, None, None], axis=2)
    token_range = jnp.arange(seq_length, dtype=jnp.int32)
    earlier = (token_range[:, None] < token_range[None, :]).astype(bf16)
    rank = dot(goes.astype(bf16), earlier).astype(jnp.int32)
    slot_range = jnp.arange(slots, dtype=jnp.int32)
    pick = (
        ((rank[:, None, :] == slot_range[None, :, None]) & goes[:, None, :])
        .astype(bf16)
        .reshape(slot_total, seq_length)
    )

    def dispatch(tokens):
        rows = dot(pick, tokens).astype(bf16).reshape(dp_count, slots, col_width)
        arrived = send_out([rows[k] for k in range(dp_count)])
        return col_gather(jnp.concatenate(arrived, axis=0), axis=1)

    def bring_back(part):
        summed = col_scatter(part.astype(bf16), axis=1).reshape(dp_count, slots, col_width)
        arrived = send_back([summed[k] for k in range(dp_count)])
        return dot_tn(pick, jnp.concatenate(arrived, axis=0))

    query_part = dot(gathered_one, queries)
    latent_part = dot(gathered_one, compress_all)
    query_raw, latent_raw = col_scatter((query_part, latent_part))
    latent_plain = latent_raw[:, :RANK]
    latent_scale = lax.rsqrt(jnp.mean(latent_plain * latent_plain, axis=1) + epsilon)
    latent_normed = (latent_plain * latent_scale[:, None] * rescale).astype(bf16)
    expanded = dot(latent_normed, expand).reshape(half_length, local_heads, pair_width)
    positions = col_index * half_length + jnp.arange(half_length, dtype=jnp.int32)
    cosine, sine_table = rotation(positions, ROPE)
    key_shared = rotate(latent_raw[:, RANK:], cosine, sine_table, 1.0)
    query_heads = query_raw.reshape(half_length, local_heads, head_width)
    query_local = jnp.concatenate(
        [
            query_heads[..., :NOPE],
            rotate(query_heads[..., NOPE:], cosine[:, None, :], sine_table[:, None, :], 1.0),
        ],
        axis=2,
    ).astype(bf16)
    key_local = jnp.concatenate(
        [
            expanded[..., :NOPE],
            jnp.broadcast_to(key_shared[:, None, :], (half_length, local_heads, ROPE)),
        ],
        axis=2,
    ).astype(bf16)
    value_local = expanded[..., NOPE:].astype(bf16)
    key_flat, value_flat = (
        col_gather(key_local.reshape(half_length, local_heads * head_width)),
        col_gather(value_local.reshape(half_length, local_heads * HEADV)),
    )
    key_heads = key_flat.reshape(seq_length, local_heads, head_width)
    value_heads = value_flat.reshape(seq_length, local_heads, HEADV)
    own_segments = lax.dynamic_slice_in_dim(
        segments, col_index * half_length, half_length, 0
    ).reshape(block_count, block_rows)
    query_blocks = query_local.reshape(block_count, block_rows, local_heads, head_width)

    def attend_block(inputs_block):
        query_block, segment_block = inputs_block
        scores = (
            jnp.einsum("qhd,khd->hqk", query_block, key_heads, preferred_element_type=f32)
            * score_scale
        )
        visible = segments[None, None, :] <= segment_block[None, :, None]
        scores = jnp.where(visible, scores, masked_score)
        largest = jnp.max(scores, axis=2, keepdims=True)
        weight = jnp.exp(scores - largest)
        totals = jnp.sum(weight, axis=2, keepdims=True)
        probability = (weight / totals).astype(bf16)
        result = jnp.einsum("hqk,khd->qhd", probability, value_heads, preferred_element_type=f32)
        return (result.astype(bf16), (largest + jnp.log(totals))[..., 0])

    attended_blocks, log_totals = lax.map(attend_block, (query_blocks, own_segments))
    attended = attended_blocks.reshape(half_length, local_heads * HEADV)
    attended_all = col_gather(attended)
    branch = row_scatter(dot(attended_all, combine))

    reply_grad_rows = dispatch(cotangent_all)
    inner_weight = fanout[0]
    outer_weight = funnel[0]
    hidden_raw = dot_nt(reply_grad_rows, outer_weight)
    shared_hidden_grad = col_scatter(dot_nt(cotangent_all, narrowing))

    residual = inputs + branch
    scale_two = norm_scale(residual)
    normed_two = (residual * scale_two[:, None] * premix).astype(bf16)
    gathered_two = row_gather(normed_two)

    expert_rows = dispatch(gathered_two)
    expert_range = jnp.arange(expert_total, dtype=jnp.int32)
    router_all = lax.all_gather(router, "col", axis=0, tiled=True)
    own_expert = dp_index * row_count + row_index
    slot_probs = jax.nn.softmax(dot(expert_rows, router_all), axis=1)
    slot_gates = jnp.sum(jnp.where(expert_range == own_expert, slot_probs, 0.0), axis=1)
    gate_up = jnp.einsum("rd,gdf->grf", expert_rows, inner_weight, preferred_element_type=f32)
    gate_input, up_input = gate_up[0], gate_up[1]
    hidden = jax.nn.silu(gate_input) * up_input
    expert_hidden = hidden.astype(bf16)
    slot_gate_grad = col_totals(jnp.sum(hidden * hidden_raw, axis=1))
    hidden_grad = hidden_raw * slot_gates[:, None]
    expert_gu_grad = jnp.stack(
        [hidden_grad * up_input * silu_slope(gate_input), hidden_grad * jax.nn.silu(gate_input)]
    ).astype(bf16)
    input_part = jnp.einsum(
        "grf,gdf->rd", expert_gu_grad, inner_weight, preferred_element_type=f32
    )
    routed_grad = bring_back(input_part)
    gate_grad_parts = send_back(
        [slot_gate_grad.reshape(dp_count, slots)[k] for k in range(dp_count)]
    )

    logits = col_totals(dot(gathered_two, router))
    router_probs = jax.nn.softmax(logits, axis=1)
    gate_grad = jnp.sum(
        pick.reshape(dp_count, slots, seq_length).astype(f32)
        * jnp.stack(gate_grad_parts)[:, :, None],
        axis=1,
    )
    mine = (my_experts[:, None] == expert_range[None, :]).astype(f32)
    probs_grad = jnp.sum(gate_grad[:, :, None] * mine[:, None, :], axis=0)
    logit_grad = router_probs * (
        probs_grad - jnp.sum(router_probs * probs_grad, axis=1, keepdims=True)
    )
    router_part = dot_tn(gathered_two, logit_grad)

    shared_gate_up = col_scatter(
        jnp.einsum("td,gdf->tgf", gathered_two, widening, preferred_element_type=f32)
    )
    shared_hidden = (jax.nn.silu(shared_gate_up[:, 0]) * shared_gate_up[:, 1]).astype(bf16)
    hidden_all = col_gather(shared_hidden)
    narrowing_grad = dot_tn(hidden_all, cotangent_all)
    shared_gu_grad = jnp.stack(
        [
            shared_hidden_grad * shared_gate_up[:, 1] * silu_slope(shared_gate_up[:, 0]),
            shared_hidden_grad * jax.nn.silu(shared_gate_up[:, 0]),
        ],
        axis=1,
    ).astype(bf16)
    gu_grad_all = col_gather(shared_gu_grad)
    widening_grad = jnp.einsum(
        "td,tgf->gdf", gathered_two, gu_grad_all, preferred_element_type=f32
    )
    shared_input_part = jnp.einsum(
        "tgf,gdf->td", gu_grad_all, widening, preferred_element_type=f32
    )
    shared_sums = lax.psum((narrowing_grad.astype(bf16), widening_grad.astype(bf16)), "dp")

    grad_part = routed_grad + shared_input_part + dot_nt(logit_grad, router)
    premix_part = jnp.sum(grad_part * gathered_two.astype(f32), axis=0) / premix
    normed_grad = row_scatter(grad_part)

    upstream = cotangent.astype(f32)
    residual_grad = upstream + norm_back(residual, scale_two, premix, normed_grad)
    branch_all = row_gather(residual_grad.astype(bf16))

    funnel_grad = dot_tn((hidden * slot_gates[:, None]).astype(bf16), reply_grad_rows)[None]
    fanout_grad = jnp.einsum(
        "rd,grf->gdf", expert_rows, expert_gu_grad, preferred_element_type=f32
    )[None]
    reply_part = dot(expert_hidden, outer_weight) * slot_gates[:, None]
    routed = bring_back(reply_part)
    shared_out = row_scatter(routed + dot(hidden_all, narrowing))
    layer_output = (residual + shared_out).astype(bf16)

    combine_grad = dot_tn(attended_all, branch_all)
    combine_sum = lax.psum(after(combine_grad.astype(bf16), *shared_sums), "dp")
    attended_grad = col_scatter(dot_nt(branch_all, combine))
    attended_grad_blocks = attended_grad.astype(bf16).reshape(
        block_count, block_rows, local_heads, HEADV
    )

    def attend_back(carried, inputs_block):
        key_sum, value_sum = carried
        query_block, grad_block, log_block, segment_block = inputs_block
        scores = (
            jnp.einsum("qhd,khd->hqk", query_block, key_heads, preferred_element_type=f32)
            * score_scale
        )
        visible = segments[None, None, :] <= segment_block[None, :, None]
        probability = jnp.where(visible, jnp.exp(scores - log_block[..., None]), 0.0)
        weight_grad = jnp.einsum(
            "qhd,khd->hqk", grad_block, value_heads, preferred_element_type=f32
        )
        inner_sum = jnp.sum(probability * weight_grad, axis=2, keepdims=True)
        score_grad = (probability * (weight_grad - inner_sum)).astype(bf16)
        query_grad_block = (
            jnp.einsum("hqk,khd->qhd", score_grad, key_heads, preferred_element_type=f32)
            * score_scale
        )
        key_sum = (
            key_sum
            + jnp.einsum("hqk,qhd->khd", score_grad, query_block, preferred_element_type=f32)
            * score_scale
        )
        value_sum = value_sum + jnp.einsum(
            "hqk,qhd->khd", probability.astype(bf16), grad_block, preferred_element_type=f32
        )
        return ((key_sum, value_sum), query_grad_block)

    key_start = jnp.zeros((seq_length, local_heads, head_width), f32)
    value_start = jnp.zeros((seq_length, local_heads, HEADV), f32)
    (key_grad_all, value_grad_all), query_grad_blocks = lax.scan(
        attend_back,
        (key_start, value_start),
        (query_blocks, attended_grad_blocks, log_totals, own_segments),
    )
    key_grad, value_grad = col_scatter(
        (
            key_grad_all.reshape(seq_length, local_heads * head_width),
            value_grad_all.reshape(seq_length, local_heads * HEADV),
        )
    )
    key_grad = key_grad.reshape(half_length, local_heads, head_width)
    value_grad = value_grad.reshape(half_length, local_heads, HEADV)
    query_grad = query_grad_blocks.reshape(half_length, local_heads, head_width)
    query_raw_grad = (
        jnp.concatenate(
            [
                query_grad[..., :NOPE],
                rotate(query_grad[..., NOPE:], cosine[:, None, :], sine_table[:, None, :], -1.0),
            ],
            axis=2,
        )
        .astype(bf16)
        .reshape(half_length, local_heads * head_width)
    )
    expanded_grad = (
        jnp.concatenate([key_grad[..., :NOPE], value_grad], axis=2)
        .astype(bf16)
        .reshape(half_length, local_heads * pair_width)
    )
    shared_rope_grad = rotate(jnp.sum(key_grad[..., NOPE:], axis=1), cosine, sine_table, -1.0)

    latent_grad = dot_nt(expanded_grad, expand)
    latent_weighted = latent_grad * rescale
    latent_inner = jnp.mean(latent_weighted * latent_plain, axis=1)
    rescale_part = jnp.sum(latent_grad * latent_plain * latent_scale[:, None], axis=0)
    plain_grad = (
        latent_weighted * latent_scale[:, None]
        - latent_plain * (latent_scale**3 * latent_inner)[:, None]
    )
    latent_raw_grad = jnp.concatenate([plain_grad, shared_rope_grad], axis=1).astype(bf16)
    query_grad_all = col_gather(query_raw_grad)
    latent_grad_all = col_gather(latent_raw_grad)
    first_part = dot_nt(query_grad_all, queries) + dot_nt(latent_grad_all, compress_all)
    first_grad = row_scatter(first_part)
    input_grad = residual_grad + norm_back(inputs, scale_one, scaling, first_grad)

    queries_part = dot_tn(gathered_one, query_grad_all)
    own_latent_grad = lax.psum_scatter(
        latent_raw_grad, "row", scatter_dimension=1, tiled=True
    )
    compress_part = dot_tn(gathered_one, col_gather(own_latent_grad))
    half_rank = RANK // col_count
    latent_normed_all = col_gather(latent_normed)
    expanded_grad_all = col_gather(expanded_grad)
    expand_half = dot_tn(
        lax.dynamic_slice_in_dim(latent_normed_all, col_index * half_rank, half_rank, 1),
        expanded_grad_all,
    )
    scaling_part = jnp.sum(first_part * gathered_one.astype(f32), axis=0) / scaling
    queries_sum, expand_sum, compress_sum = lax.psum(
        (
            after(queries_part.astype(bf16), combine_sum),
            expand_half.astype(bf16),
            compress_part.astype(bf16),
        ),
        "dp",
    )
    premix_sum, router_sum = lax.psum((premix_part, router_part), ("dp", "row"))
    rescale_sum = lax.psum(rescale_part, ("dp", "row", "col"))
    scaling_sum = lax.psum(scaling_part, ("dp", "row"))
    return (
        layer_output,
        input_grad,
        scaling_sum,
        queries_sum.astype(f32),
        compress_sum.astype(f32),
        rescale_sum,
        col_gather(expand_sum).astype(f32),
        combine_sum.astype(f32),
        premix_sum,
        router_sum,
        shared_sums[1].astype(f32),
        shared_sums[0].astype(f32),
        fanout_grad,
        funnel_grad,
    )


def solution(mesh):
    placed = (
        P(("dp", "row"), "col"),
        P(("dp", "row"), "col"),
        P(("dp", "row"), None),
        P("dp"),
        P("col"),
        P("col", "row"),
        P("col", "row"),
        P(),
        P(None, "row"),
        P("row", "col"),
        P("col"),
        P("col", None),
        P(None, "col", "row"),
        P("row", "col"),
        P(("dp", "row"), None, None, "col"),
        P(("dp", "row"), "col", None),
    )
    squared = mesh.shape["dp"] == SQUARE and mesh.shape["row"] == ROWS
    return jax.shard_map(
        local_square if squared else local,
        mesh=mesh,
        in_specs=placed,
        out_specs=(
            P(("dp", "row"), "col"),
            P(("dp", "row"), "col"),
            P("col"),
            P("col", "row"),
            P("col", "row"),
            P(),
            P(None, "row"),
            P("row", "col"),
            P("col"),
            P("col", None),
            P(None, "col", "row"),
            P("row", "col"),
            P(("dp", "row"), None, None, "col"),
            P(("dp", "row"), "col", None),
        ),
        check_vma=False,
    )
```

```python
import jax
import jax.numpy as jnp
import numpy as np
from jax import lax
from jax.experimental import pallas as pl
from jax.experimental.pallas import tpu as pltpu
from jax.sharding import PartitionSpec as P

D = 2048
NOPE = 128
ROPE = 64
HEADV = 128
RANK = 512
TOP = 6


epsilon = 1e-06
masked_score = -1e30
f32 = jnp.float32
bf16 = jnp.bfloat16


def after(value, *earlier):
    return lax.optimization_barrier((value,) + earlier)[0]


def silu_slope(values):
    sigmoid = jax.nn.sigmoid(values)
    return sigmoid * (1.0 + values * (1.0 - sigmoid))


def rotation(positions, rope_width):
    half_width = rope_width // 2
    frequency = 10000.0 ** (-jnp.arange(half_width, dtype=jnp.float32) * 2.0 / rope_width)
    angles = positions.astype(jnp.float32)[:, None] * frequency[None, :]
    return (jnp.cos(angles), jnp.sin(angles))


def rotate(values, cosine, sine_table, direction):
    half_width = values.shape[-1] // 2
    first_half = values[..., :half_width]
    second_half = values[..., half_width:]
    return jnp.concatenate(
        [
            first_half * cosine - direction * second_half * sine_table,
            second_half * cosine + direction * first_half * sine_table,
        ],
        axis=-1,
    )


def dot(left, right):
    return jnp.dot(left, right, preferred_element_type=f32)


def dot_tn(left, right):
    return lax.dot_general(left, right, (((0,), (0,)), ((), ())), preferred_element_type=f32)


def dot_nt(left, right):
    return lax.dot_general(left, right, (((1,), (1,)), ((), ())), preferred_element_type=f32)


def col_totals(values):
    return lax.psum(values, "col")


def row_gather(values):
    return lax.all_gather(values, "row", axis=0, tiled=True)


def col_gather(values, axis=0):
    return lax.all_gather(values, "col", axis=axis, tiled=True)


def col_scatter(values, axis=0):
    return lax.psum_scatter(values, "col", scatter_dimension=axis, tiled=True)


def row_scatter(values):
    return lax.psum_scatter(
        values.astype(bf16), "row", scatter_dimension=0, tiled=True
    ).astype(f32)


def send_out(parts):
    count = len(parts)
    return [parts[0]] + [
        lax.ppermute(parts[k], "dp", [(i, (i + k) % count) for i in range(count)])
        for k in range(1, count)
    ]


def send_back(parts):
    count = len(parts)
    return [parts[0]] + [
        lax.ppermute(parts[k], "dp", [(i, (i - k) % count) for i in range(count)])
        for k in range(1, count)
    ]


def norm_scale(values):
    square_sum = col_totals(jnp.sum(values * values, axis=1))
    return lax.rsqrt(square_sum / D + epsilon)


def norm_back(values, row_scale, gain_vector, upstream):
    weighted = upstream * gain_vector
    inner_mean = col_totals(jnp.sum(weighted * values, axis=1)) / D
    return weighted * row_scale[:, None] - values * (row_scale**3 * inner_mean)[:, None]


MESH = pl.DeviceIdType.MESH
VMEM = pltpu.VMEM
DMA = pltpu.SemaphoreType.DMA
MIB = 1024 * 1024
ROWS = 4
SQUARE = 4
COLS = 2
SPLIT = 2


def nn(left, right):
    return lax.dot_general(left, right, (((1,), (0,)), ((), ())), preferred_element_type=f32)


def tn(left, right):
    return lax.dot_general(left, right, (((0,), (0,)), ((), ())), preferred_element_type=f32)


def nt(left, right):
    return lax.dot_general(left, right, (((1,), (1,)), ((), ())), preferred_element_type=f32)


def block_at(row, turn):
    swapped = jnp.where(turn < 2, 1 - turn, turn)
    inner = jnp.logical_or(row == 1, row == 2)
    near = jnp.where(inner, swapped, turn)
    return jnp.where(row < 2, near, ROWS - 1 - near)


def partner(place, step):
    across, along = lax.rem(place, 2), lax.div(place, 2)
    across = lax.rem(across + step % 2, 2)
    along = lax.rem(along + step // 2, 2)
    return along * 2 + across


def remote(source, target, sent, arrived, where):
    return pltpu.make_async_remote_copy(
        src_ref=source,
        dst_ref=target,
        send_sem=sent,
        recv_sem=arrived,
        device_id=where,
        device_id_type=MESH,
    )


def greet(row, place, col, line=False, square=True):
    barrier = pltpu.get_barrier_semaphore()
    met = 1
    if line:
        for step in range(1, ROWS):
            pl.semaphore_signal(
                barrier,
                inc=1,
                device_id={"row": lax.rem(row + step, ROWS)},
                device_id_type=MESH,
            )
        met = met + ROWS - 1
    else:

        @pl.when(row > 0)
        def _():
            pl.semaphore_signal(barrier, inc=1, device_id={"row": row - 1}, device_id_type=MESH)

        @pl.when(row < ROWS - 1)
        def _():
            pl.semaphore_signal(barrier, inc=1, device_id={"row": row + 1}, device_id_type=MESH)

        met = met + (row > 0).astype(jnp.int32) + (row < ROWS - 1).astype(jnp.int32)
    if square:
        for step in range(1, SQUARE):
            pl.semaphore_signal(
                barrier, inc=1, device_id={"dp": partner(place, step)}, device_id_type=MESH
            )
        met = met + SQUARE - 1
    pl.semaphore_signal(barrier, inc=1, device_id={"col": 1 - col}, device_id_type=MESH)
    pl.semaphore_wait(barrier, met)


class Line:
    def __init__(self, row, buffer, sent, arrived):
        self.row, self.buffer, self.sent, self.arrived = row, buffer, sent, arrived

    def copy(self, block, way):
        to = self.row + 1 if way == 0 else self.row - 1
        here = self.buffer.at[block]
        return remote(here, here, self.sent.at[block, way], self.arrived.at[block], {"row": to})

    def each(self, block, act):
        @pl.when(jnp.logical_and(block <= self.row, self.row < ROWS - 1))
        def _():
            act(self.copy(block, 0))

        @pl.when(jnp.logical_and(block >= self.row, self.row > 0))
        def _():
            act(self.copy(block, 1))

    def wait(self, block):
        self.copy(block, 0).wait_recv()

    def pass_on(self, block):
        self.each(block, lambda copy: copy.start())

    def finish(self):
        def one(block, carried):
            self.each(block, lambda copy: copy.wait_send())
            return carried

        lax.fori_loop(0, ROWS, one, 0)


class SumLine:
    def __init__(self, row, part, leaving, coming, sent, arrived):
        self.row, self.part, self.leaving, self.coming = row, part, leaving, coming
        self.sent, self.arrived = sent, arrived
        self.lines = part.shape[1] // SPLIT

    def piece(self, index):
        return pl.ds(index * self.lines, self.lines)

    def copy(self, block, index, way):
        return remote(
            self.leaving.at[block, self.piece(index)],
            self.coming.at[way, block, self.piece(index)],
            self.sent.at[block, index],
            self.arrived.at[way, block, index],
            {"row": self.row + 1 - 2 * way},
        )

    def send(self, block, index):
        @pl.when(block > self.row)
        def _():
            self.copy(block, index, 0).start()

        @pl.when(block < self.row)
        def _():
            self.copy(block, index, 1).start()

    def chained(self, block):
        return jnp.logical_or(
            jnp.logical_and(block > self.row, self.row > 0),
            jnp.logical_and(block < self.row, self.row < ROWS - 1),
        )

    def begin(self, block):
        @pl.when(jnp.logical_and(block != self.row, jnp.logical_not(self.chained(block))))
        def _():
            self.leaving[block] = self.part[block].astype(bf16)
            for index in range(SPLIT):
                self.send(block, index)

    def pass_on(self, block):
        @pl.when(self.chained(block))
        def _():
            way = (block < self.row).astype(jnp.int32)
            for index in range(SPLIT):
                self.copy(block, index, way).wait_recv()
                piece = self.piece(index)
                self.leaving[block, piece] = (
                    self.part[block, piece] + self.coming[way, block, piece].astype(f32)
                ).astype(bf16)
                self.send(block, index)

    def total(self, target):
        target[...] = self.part[self.row]
        for way, there in ((0, self.row > 0), (1, self.row < ROWS - 1)):

            @pl.when(there)
            def _(way=way):
                for index in range(SPLIT):
                    self.copy(self.row, index, way).wait_recv()
                    target[self.piece(index)] += self.coming[
                        way, self.row, self.piece(index)
                    ].astype(f32)

    def finish(self):
        def one(block, carried):
            @pl.when(block != self.row)
            def _():
                for index in range(SPLIT):
                    self.copy(block, index, 0).wait_send()

            return carried

        lax.fori_loop(0, ROWS, one, 0)


def swap_halves(values):
    lanes = values.shape[1]
    lane = lax.broadcasted_iota(jnp.int32, values.shape, 1)
    return jnp.where(
        lane % ROPE < ROPE // 2,
        pltpu.roll(values, lanes - ROPE // 2, 1),
        pltpu.roll(values, ROPE // 2, 1),
    )


def attend_kernel(
    act_ref,
    scaling_ref,
    compress_ref,
    rescale_ref,
    premix_ref,
    cos_ref,
    sin_ref,
    key_cos_ref,
    key_sin_ref,
    mark_ref,
    cot_ref,
    route_ref,
    router_ref,
    queries_ref,
    expand_ref,
    combine_ref,
    one_ref,
    query_ref,
    key_ref,
    value_ref,
    probs_ref,
    latent_ref,
    normed_latent_ref,
    attended_ref,
    compress_all,
    residual_ref,
    two_ref,
    scale_one_ref,
    scale_two_ref,
    cot_all,
    pick_ref,
    back_ref,
    rows_ref,
    router_all,
    queries,
    expand,
    combine,
    stat_to,
    stat_from,
    query_own,
    query_to,
    query_from,
    latent_to,
    latent_from,
    part,
    leaving,
    coming,
    routes,
    staged,
    marks,
    load_sem,
    stat_sent,
    stat_arrived,
    line_sent,
    line_arrived,
    comp_sent,
    comp_arrived,
    comp_out_sent,
    comp_out_arrived,
    query_sent,
    query_arrived,
    latent_sent,
    latent_arrived,
    att_sent,
    att_arrived,
    sum_sent,
    sum_arrived,
    cot_sent,
    cot_arrived,
    route_sent,
    route_arrived,
    out_sent,
    out_arrived,
    pair_sent,
    pair_arrived,
    router_sent,
    router_arrived,
):
    place, row, col = lax.axis_index("dp"), lax.axis_index("row"), lax.axis_index("col")
    other = 1 - col
    sibling = {"col": other}
    tokens, width = act_ref.shape
    slots = pick_ref.shape[1] // SQUARE
    mine = query_own.shape[2]
    sliced = compress_ref.shape[0]
    quarter = width // SQUARE
    score_scale = (NOPE + ROPE) ** (-0.5)
    loads = [
        pltpu.make_async_copy(source, target, load_sem.at[i])
        for i, (source, target) in enumerate(
            [(queries_ref, queries), (expand_ref, expand), (combine_ref, combine)]
        )
    ]
    for load in loads:
        load.start()

    def stat_copy(index):
        return remote(
            stat_to.at[index],
            stat_from.at[index],
            stat_sent.at[index],
            stat_arrived.at[index],
            sibling,
        )

    def scale_of(values, index):
        own = jnp.sum(values * values, axis=1, keepdims=True)
        stat_to[index] = jnp.broadcast_to(own, (tokens, 128))
        stat_copy(index).start()
        stat_copy(index).wait_recv()
        return lax.rsqrt((own + stat_from[index][:, 0:1]) / D + epsilon)

    def comp_piece(block, member):
        return compress_all.at[
            pl.ds(pl.multiple_of(block * sliced, 16), sliced),
            pl.ds(pl.multiple_of(member * quarter, 128), quarter),
        ]

    def comp_copy(block, way):
        here = comp_piece(block, place)
        return remote(
            here,
            here,
            comp_sent.at[block, way],
            comp_arrived.at[block],
            {"row": row + 1 - 2 * way},
        )

    def comp_each(block, act):
        @pl.when(jnp.logical_and(block <= row, row < ROWS - 1))
        def _():
            act(comp_copy(block, 0))

        @pl.when(jnp.logical_and(block >= row, row > 0))
        def _():
            act(comp_copy(block, 1))

    def comp_out(block, step, member):
        here = comp_piece(block, member)
        return remote(
            here,
            here,
            comp_out_sent.at[block, step],
            comp_out_arrived.at[block, step],
            {"dp": partner(place, step)},
        )

    line = Line(row, one_ref, line_sent, line_arrived)
    cot_line = Line(row, cot_all, cot_sent, cot_arrived)
    route_line = Line(row, routes, route_sent, route_arrived)
    sums = SumLine(row, part, leaving, coming, sum_sent, sum_arrived)

    greet(row, place, col)
    compress_all[pl.ds(pl.multiple_of(row * sliced, 16), sliced)] = compress_ref[...]
    compress_all[ROWS * sliced :] = jnp.zeros(
        (compress_all.shape[0] - ROWS * sliced, width), bf16
    )
    comp_each(row, lambda copy: copy.start())

    def router_copy(half):
        here = router_all.at[:, pl.ds(pl.multiple_of(half * width, width), width)]
        return remote(here, here, router_sent.at[0], router_arrived.at[0], sibling)

    router_all[:, pl.ds(pl.multiple_of(col * width, width), width)] = router_ref[...]
    inputs = act_ref[...].astype(f32)
    scale_one = scale_of(inputs, 0)
    scale_one_ref[...] = scale_one
    one_ref[pl.ds(row, 1)] = (
        (inputs * scale_one * scaling_ref[...]).astype(bf16).reshape(1, tokens, width)
    )
    cot_all[pl.ds(row, 1)] = cot_ref[...].reshape(1, tokens, width)
    routes[pl.ds(row, 1)] = route_ref[...].reshape((1,) + route_ref.shape)
    line.pass_on(row)
    router_copy(col).start()
    for block in range(ROWS):
        mark = mark_ref[:, block * tokens : (block + 1) * tokens].astype(f32)
        marks[block] = jnp.broadcast_to(mark, (8, tokens)).T
    loads[0].wait()

    def query_copy(block):
        return remote(
            query_to.at[block],
            query_from.at[block],
            query_sent.at[block],
            query_arrived.at[block],
            sibling,
        )

    def latent_copy(block):
        return remote(
            latent_to.at[block],
            latent_from.at[block],
            latent_sent.at[block],
            latent_arrived.at[block],
            sibling,
        )

    def att_copy(block, half):
        here = attended_ref.at[block, :, pl.ds(pl.multiple_of(half * 2 * HEADV, 128), 2 * HEADV)]
        return remote(here, here, att_sent.at[block], att_arrived.at[block], sibling)

    def gather(step, carried):
        block = block_at(row, step)

        @pl.when(step > 0)
        def _():
            comp_copy(block, 0).wait_recv()
            comp_each(block, lambda copy: copy.start())
            for shift in (3, 2, 1):
                comp_out(block, shift, place).start()
            line.wait(block)
            line.pass_on(block)

        tokens_here = one_ref[block]
        query_to[block] = nn(
            tokens_here, queries[:, pl.ds(pl.multiple_of(other * mine, 128), mine)]
        ).astype(bf16)
        query_copy(block).start()
        query_own[block] = nn(tokens_here, queries[:, pl.ds(pl.multiple_of(col * mine, 128), mine)])
        return carried

    lax.fori_loop(0, ROWS, gather, 0)

    cot_line.pass_on(row)
    route_line.pass_on(row)

    def out_copy(block, step):
        piece = pl.ds(step * slots, slots)
        return remote(
            staged.at[block, piece],
            rows_ref.at[col, block, piece],
            out_sent.at[block, step],
            out_arrived.at[block, step],
            {"dp": partner(place, step)},
        )

    def pair_copy(block, half):
        here = rows_ref.at[half, block]
        return remote(here, here, pair_sent.at[block], pair_arrived.at[block], sibling)

    def take(step):
        block = block_at(row, step)

        @pl.when(step > 0)
        def _():
            route_line.wait(block)
            cot_line.wait(block)
            route_line.pass_on(block)
            cot_line.pass_on(block)

        before = (
            lax.broadcasted_iota(jnp.int32, (tokens, tokens), 0)
            < lax.broadcasted_iota(jnp.int32, (tokens, tokens), 1)
        ).astype(bf16)
        routing = routes[block]
        chosen = []
        for shift in range(SQUARE):
            expert = partner(place, shift) * ROWS + row
            hit = (routing == expert).astype(f32)
            chosen.append(jnp.max(hit, axis=0, keepdims=True))
        goes = jnp.concatenate(chosen + chosen, axis=0)
        rank = nn(goes.astype(bf16), before)
        for shift in range(SQUARE):
            slot = lax.broadcasted_iota(jnp.int32, (slots, tokens), 0).astype(f32)
            here = jnp.logical_and(slot == rank[shift : shift + 1], goes[shift : shift + 1] > 0.5)
            pick = here.astype(f32)
            pick_ref[block, shift * slots : (shift + 1) * slots] = pick.astype(bf16)
            back_ref[block, :, shift * slots : (shift + 1) * slots] = pick.T.astype(bf16)
        staged[block] = nn(pick_ref[block], cot_all[block]).astype(bf16)
        for shift in (3, 2, 1):
            out_copy(block, shift).start()
        rows_ref[col, block, 0:slots] = staged[block, 0:slots]

    def forward(step):
        block = block_at(row, step)
        for shift in range(1, SQUARE):
            out_copy(block, shift).wait_recv()
        pair_copy(block, col).start()

    def comp_arrive(block, carried):
        @pl.when(block != row)
        def _():
            for shift in range(1, SQUARE):
                comp_out(block, shift, partner(place, shift)).wait_recv()

        return carried

    lax.fori_loop(0, ROWS, comp_arrive, 0)

    def latents(block, carried):
        value = nt(one_ref[block], compress_all[...])
        latent_to[block] = value
        latent_copy(block).start()
        latent_ref[block] = value
        return carried

    lax.fori_loop(0, ROWS, latents, 0)
    take(0)
    loads[1].wait()

    def keys(block, carried):
        latent_copy(block).wait_recv()
        latent = latent_ref[block] + latent_from[block]
        latent_ref[block] = latent
        plain = latent[:, :RANK]
        scale = lax.rsqrt(jnp.mean(plain * plain, axis=1, keepdims=True) + epsilon)
        normed = (plain * scale * rescale_ref[...]).astype(bf16)
        normed_latent_ref[block] = normed
        own = 2 * (NOPE + HEADV)
        expanded = nn(normed, expand[:, pl.ds(pl.multiple_of(col * own, 128), own)])
        rope = latent[:, RANK:]
        rope = rope * key_cos_ref[block] + swap_halves(rope) * key_sin_ref[block]
        first = jnp.concatenate([expanded[:, :NOPE], rope], axis=1)
        second = jnp.concatenate([expanded[:, 2 * NOPE : 3 * NOPE], rope], axis=1)
        key_ref[0, block] = first.astype(bf16)
        key_ref[1, block] = pltpu.roll(second, ROPE, 1).astype(bf16)
        value_ref[0, block] = expanded[:, NOPE : 2 * NOPE].astype(bf16)
        value_ref[1, block] = expanded[:, 3 * NOPE :].astype(bf16)
        query_copy(block).wait_recv()
        query = query_own[block] + query_from[block].astype(f32)
        query_ref[block] = (
            query * cos_ref[block] + swap_halves(query) * sin_ref[block]
        ).astype(bf16)
        return carried

    lax.fori_loop(0, ROWS, keys, 0)
    seq = ROWS * tokens
    lanes = NOPE + 2 * ROPE

    def attend(turn, carried):
        block = block_at(row, ROWS - 1 - turn)
        visible = mark_ref[...].astype(f32) <= marks[block][:, 0:1]
        for head in range(2):
            query = query_ref[block, :, head * NOPE : head * NOPE + lanes]
            scores = nt(query, key_ref[head].reshape(seq, lanes)) * score_scale
            scores = jnp.where(visible, scores, masked_score)
            weight = jnp.exp(scores - jnp.max(scores, axis=1, keepdims=True))
            probs = (weight / jnp.sum(weight, axis=1, keepdims=True)).astype(bf16)
            probs_ref[head, block] = probs
            result = nn(probs, value_ref[head].reshape(seq, HEADV)).astype(bf16)
            at = pl.multiple_of((col * 2 + head) * HEADV, 128)
            attended_ref[block, :, pl.ds(at, HEADV)] = result
        att_copy(block, col).start()

        @pl.when(jnp.logical_or(turn == 1, turn == 2))
        def _():
            take(turn)

        return carried

    lax.fori_loop(0, ROWS, attend, 0)
    loads[2].wait()

    def mix(turn, carried):
        block = block_at(row, ROWS - 1 - turn)
        att_copy(block, other).wait_recv()
        part[block] = nn(attended_ref[block], combine[...])
        sums.begin(block)
        return carried

    lax.fori_loop(0, ROWS, mix, 0)

    def hand_on(turn, carried):
        sums.pass_on(block_at(row, jnp.where(turn == 0, 3, turn)))

        @pl.when(turn == 0)
        def _():
            take(3)

        forward(turn)
        return carried

    lax.fori_loop(0, 3, hand_on, 0)
    sums.total(residual_ref)
    residual = residual_ref[...] + inputs
    residual_ref[...] = residual
    scale_two = scale_of(residual, 1)
    scale_two_ref[...] = scale_two
    two_ref[...] = (residual * scale_two * premix_ref[...]).astype(bf16)
    forward(3)

    def ended(block, carried):
        pair_copy(block, other).wait_recv()
        pair_copy(block, col).wait_send()
        for shift in range(1, SQUARE):
            out_copy(block, shift).wait_send()

            @pl.when(block != row)
            def _(shift=shift):
                comp_out(block, shift, place).wait_send()

        comp_each(block, lambda copy: copy.wait_send())
        query_copy(block).wait_send()
        latent_copy(block).wait_send()
        att_copy(block, col).wait_send()
        return carried

    lax.fori_loop(0, ROWS, ended, 0)
    router_copy(other).wait_recv()
    router_copy(col).wait_send()
    stat_copy(0).wait_send()
    stat_copy(1).wait_send()
    sums.finish()
    line.finish()
    cot_line.finish()
    route_line.finish()


def turning_tables(length):
    half = ROPE // 2
    frequency = 10000.0 ** (-np.arange(half, dtype=np.float32) * 2.0 / ROPE)
    angles = np.arange(length, dtype=np.float32)[:, None] * frequency[None, :].astype(np.float32)
    cosine, sine = np.cos(angles), np.sin(angles)
    cosine, sine = np.concatenate([cosine, cosine], 1), np.concatenate([-sine, sine], 1)
    ones, zeros = np.ones((length, NOPE)), np.zeros((length, NOPE))
    gap = np.zeros((length, 128 - ROPE))
    tables = (
        np.concatenate([ones, cosine, ones, cosine], 1),
        np.concatenate([zeros, sine, zeros, sine], 1),
        np.concatenate([cosine, gap], 1),
        np.concatenate([sine, gap], 1),
    )
    return [
        jnp.asarray(table.reshape(ROWS, length // ROWS, -1).astype(np.float32))
        for table in tables
    ]


def pair_sems():
    return [DMA((ROWS,)), DMA((ROWS,))]


def line_sems():
    return [DMA((ROWS, 2)), DMA((ROWS,))]


def square_sems():
    return [DMA((ROWS, SQUARE)), DMA((ROWS, SQUARE))]


def sum_sems():
    return [DMA((ROWS, SPLIT)), DMA((2, ROWS, SPLIT))]


def run_attention(
    activations,
    scaling,
    queries,
    compress,
    rescale,
    expand,
    combine,
    premix,
    segments,
    cotangent,
    routing,
    router,
    tables,
    slots,
):
    tokens, width = activations.shape
    seq = ROWS * tokens
    mine = queries.shape[1] // COLS
    sliced = compress.shape[1]
    latent_width = RANK + 128
    picked = SQUARE * slots
    lanes = NOPE + 2 * ROPE
    routes = routing.T
    whole = pl.BlockSpec(memory_space=VMEM)
    far = pl.BlockSpec(memory_space=pl.ANY)

    def shape(*dims, dtype=bf16):
        return jax.ShapeDtypeStruct(dims, dtype)

    return pl.pallas_call(
        attend_kernel,
        name="attend",
        out_shape=(
            shape(ROWS, tokens, width),
            shape(ROWS, tokens, mine),
            shape(2, ROWS, tokens, lanes),
            shape(2, ROWS, tokens, HEADV),
            shape(2, ROWS, tokens, seq),
            shape(ROWS, tokens, latent_width, dtype=f32),
            shape(ROWS, tokens, RANK),
            shape(ROWS, tokens, COLS * 2 * HEADV),
            shape(latent_width, width),
            shape(tokens, width, dtype=f32),
            shape(tokens, width),
            shape(tokens, 1, dtype=f32),
            shape(tokens, 1, dtype=f32),
            shape(ROWS, tokens, width),
            shape(ROWS, picked, tokens),
            shape(ROWS, tokens, picked),
            shape(COLS, ROWS, picked, width),
            shape(router.shape[1], COLS * width),
        ),
        in_specs=[whole] * 13 + [far] * 3,
        out_specs=(whole,) * 18,
        scratch_shapes=[
            VMEM(queries.shape, bf16),
            VMEM(expand.shape, bf16),
            VMEM(combine.shape, bf16),
            VMEM((2, tokens, 128), f32),
            VMEM((2, tokens, 128), f32),
            VMEM((ROWS, tokens, mine), f32),
            VMEM((ROWS, tokens, mine), bf16),
            VMEM((ROWS, tokens, mine), bf16),
            VMEM((ROWS, tokens, latent_width), f32),
            VMEM((ROWS, tokens, latent_width), f32),
            VMEM((ROWS, tokens, width), f32),
            VMEM((ROWS, tokens, width), bf16),
            VMEM((2, ROWS, tokens, width), bf16),
            VMEM((ROWS,) + routes.shape, jnp.int32),
            VMEM((ROWS, picked, width), bf16),
            VMEM((ROWS, tokens, 8), f32),
            DMA((3,)),
            DMA((2,)),
            DMA((2,)),
            *line_sems(),
            *line_sems(),
            *square_sems(),
            *pair_sems(),
            *pair_sems(),
            *pair_sems(),
            *sum_sems(),
            *line_sems(),
            *line_sems(),
            *square_sems(),
            *pair_sems(),
            DMA((1,)),
            DMA((1,)),
        ],
        compiler_params=pltpu.CompilerParams(
            collective_id=1, has_side_effects=True, vmem_limit_bytes=56 * MIB
        ),
        cost_estimate=pl.CostEstimate(
            flops=40 * 1024**3, bytes_accessed=32 * MIB, transcendentals=0
        ),
    )(
        activations,
        scaling.reshape(1, width),
        compress.T,
        rescale.reshape(1, RANK),
        premix.reshape(1, width),
        *tables,
        segments.reshape(1, seq),
        cotangent,
        routes,
        router.T,
        queries,
        expand,
        combine,
    )


def attend_back_kernel(
    normed_grad_ref,
    residual_ref,
    scale_two_ref,
    premix_ref,
    cot_ref,
    act_ref,
    scale_one_ref,
    scaling_ref,
    one_ref,
    query_ref,
    key_ref,
    value_ref,
    probs_ref,
    latent_ref,
    rescale_ref,
    cos_ref,
    sin_ref,
    key_cos_ref,
    key_sin_ref,
    compress_all,
    queries_ref,
    expand_ref,
    combine_ref,
    input_grad_ref,
    branch_ref,
    query_grad_ref,
    expanded_ref,
    own_latent_ref,
    scaling_rows,
    rescale_rows,
    queries,
    expand,
    combine,
    stat_to,
    stat_from,
    grad_own,
    grad_to,
    grad_from,
    key_grad,
    value_grad,
    latent_own,
    latent_to,
    latent_from,
    turned,
    turned_from,
    part,
    leaving,
    coming,
    total,
    load_sem,
    stat_sent,
    stat_arrived,
    line_sent,
    line_arrived,
    grad_sent,
    grad_arrived,
    query_sent,
    query_arrived,
    latent_sent,
    latent_arrived,
    turned_sent,
    turned_arrived,
    own_sent,
    own_arrived,
    sum_sent,
    sum_arrived,
):
    place, row, col = lax.axis_index("dp"), lax.axis_index("row"), lax.axis_index("col")
    other = 1 - col
    sibling = {"col": other}
    tokens, width = act_ref.shape
    seq = ROWS * tokens
    mine = query_ref.shape[2]
    lanes = key_ref.shape[3]
    both = 2 * HEADV
    sliced = own_latent_ref.shape[0]
    score_scale = (NOPE + ROPE) ** (-0.5)
    loads = [
        pltpu.make_async_copy(source, target, load_sem.at[i])
        for i, (source, target) in enumerate(
            [(combine_ref, combine), (queries_ref, queries), (expand_ref, expand)]
        )
    ]
    for load in loads:
        load.start()
    line = Line(row, branch_ref, line_sent, line_arrived)
    sums = SumLine(row, part, leaving, coming, sum_sent, sum_arrived)
    greet(row, place, col, line=True, square=False)

    def stat_copy(index):
        return remote(
            stat_to.at[index],
            stat_from.at[index],
            stat_sent.at[index],
            stat_arrived.at[index],
            sibling,
        )

    def norm_grad(values, scale, gain, upstream, index):
        weighted = upstream * gain
        own = jnp.sum(weighted * values, axis=1, keepdims=True)
        stat_to[index] = jnp.broadcast_to(own, (tokens, 128))
        stat_copy(index).start()
        stat_copy(index).wait_recv()
        inner = (own + stat_from[index][:, 0:1]) / D
        return weighted * scale - values * (scale * scale * scale * inner)

    residual_grad = cot_ref[...].astype(f32) + norm_grad(
        residual_ref[...], scale_two_ref[...], premix_ref[...], normed_grad_ref[...], 0
    )
    input_grad_ref[...] = residual_grad
    branch_ref[pl.ds(row, 1)] = residual_grad.astype(bf16).reshape(1, tokens, width)
    key_grad[...] = jnp.zeros_like(key_grad)
    value_grad[...] = jnp.zeros_like(value_grad)
    scaling_rows[...] = jnp.zeros_like(scaling_rows)
    rescale_rows[...] = jnp.zeros_like(rescale_rows)

    def grad_copy(block):
        return remote(
            grad_to.at[block],
            grad_from.at[block],
            grad_sent.at[block],
            grad_arrived.at[block],
            sibling,
        )

    def query_copy(block, half):
        here = query_grad_ref.at[block, :, pl.ds(pl.multiple_of(half * mine, 128), mine)]
        return remote(here, here, query_sent.at[block], query_arrived.at[block], sibling)

    def latent_copy(block):
        return remote(
            latent_to.at[block],
            latent_from.at[block],
            latent_sent.at[block],
            latent_arrived.at[block],
            sibling,
        )

    def arrive(step):
        block = block_at(row, step)

        @pl.when(step > 0)
        def _():
            line.wait(block)

        line.pass_on(block)

        @pl.when(step == 0)
        def _():
            loads[0].wait()

        grads = branch_ref[block]
        grad_to[block] = nt(
            grads, combine[pl.ds(pl.multiple_of(other * both, 16), both)]
        ).astype(bf16)
        grad_copy(block).start()
        grad_own[block] = nt(grads, combine[pl.ds(pl.multiple_of(col * both, 16), both)])

    def heads(step):
        block = block_at(row, step)
        grad_copy(block).wait_recv()
        grads = (grad_own[block] + grad_from[block].astype(f32)).astype(bf16)
        pieces = []
        for head in range(2):
            upstream = grads[:, head * HEADV : (head + 1) * HEADV]
            query = query_ref[block, :, head * NOPE : head * NOPE + lanes]
            probs = probs_ref[head, block]
            weight = probs.astype(f32)
            probs_back = nt(upstream, value_ref[head].reshape(seq, HEADV))
            inner = jnp.sum(weight * probs_back, axis=1, keepdims=True)
            score_grad = (weight * (probs_back - inner)).astype(bf16)
            pieces.append(nn(score_grad, key_ref[head].reshape(seq, lanes)) * score_scale)
            key_grad[head] += tn(score_grad, query)
            value_grad[head] += tn(probs, upstream)
        first, second = pieces
        grad = jnp.concatenate(
            [first[:, :NOPE], first[:, NOPE:] + second[:, :NOPE], second[:, NOPE:]], axis=1
        )
        grad = grad * cos_ref[block] - swap_halves(grad) * sin_ref[block]
        query_grad_ref[block, :, pl.ds(pl.multiple_of(col * mine, 128), mine)] = grad.astype(bf16)
        query_copy(block, col).start()

    def project(step):
        block = block_at(row, step)

        @pl.when(step == 0)
        def _():
            loads[1].wait()

        query_copy(block, other).wait_recv()
        part[block] = nt(query_grad_ref[block], queries[...])

    def turn(step, carried):
        for delay, stage in ((0, arrive), (1, heads), (2, project)):

            @pl.when(jnp.logical_and(step >= delay, step < delay + ROWS))
            def _(delay=delay, stage=stage):
                stage(step - delay)

        return carried

    lax.fori_loop(0, ROWS + 1, turn, 0)
    loads[2].wait()

    def latents(turn, carried):
        block = block_at(row, ROWS - 1 - turn)
        here = pl.ds(pl.multiple_of(block * tokens, 128), tokens)
        first = key_grad[0, here] * score_scale
        second = pltpu.roll(key_grad[1, here] * score_scale, lanes - ROPE, 1)
        grad = jnp.concatenate(
            [first[:, :NOPE], value_grad[0, here], second[:, :NOPE], value_grad[1, here]], axis=1
        ).astype(bf16)
        expanded_ref[block] = grad
        own = 2 * (NOPE + HEADV)
        upstream = nt(grad, expand[:, pl.ds(pl.multiple_of(col * own, 128), own)])
        plain = latent_ref[block][:, :RANK]
        scale = lax.rsqrt(jnp.mean(plain * plain, axis=1, keepdims=True) + epsilon)
        rescale_rows[...] += jnp.sum(
            (upstream * plain * scale).reshape(tokens // 8, 8, RANK), axis=0
        )
        weighted = upstream * rescale_ref[...]
        inner = jnp.mean(weighted * plain, axis=1, keepdims=True)
        plain_grad = weighted * scale - plain * (scale * scale * scale * inner)
        rope = first[:, NOPE:] + second[:, NOPE:]
        lane = lax.broadcasted_iota(jnp.int32, rope.shape, 1)
        rope = jnp.where(lane < ROPE, rope, 0.0)
        rope = rope * key_cos_ref[block] - swap_halves(rope) * key_sin_ref[block]
        value = jnp.concatenate([plain_grad, rope], axis=1)
        latent_own[block] = value
        latent_to[block] = value.astype(bf16)
        latent_copy(block).start()
        return carried

    lax.fori_loop(0, ROWS, latents, 0)
    project(ROWS - 1)

    def turned_piece(member):
        return turned.at[
            pl.ds(pl.multiple_of(member * sliced, 16), sliced),
            pl.ds(pl.multiple_of(col * (seq // COLS), 128), seq // COLS),
        ]

    def turned_copy(step):
        to = lax.rem(row + step, ROWS)
        return remote(
            turned_piece(to),
            turned_from.at[step],
            turned_sent.at[step],
            turned_arrived.at[step],
            {"row": to},
        )

    def mix(turn, carried):
        block = block_at(row, ROWS - 1 - turn)
        latent_copy(block).wait_recv()
        latent = latent_own[block] + latent_from[block].astype(f32)
        here = pl.ds(pl.multiple_of(block * tokens, 128), tokens)
        total_here = part[block] + nn(latent.astype(bf16), compress_all[...])
        part[block] = total_here
        sums.begin(block)
        turned[:, here] = latent.T.astype(bf16)
        scaling_rows[...] += jnp.sum(
            (total_here * one_ref[block].astype(f32)).reshape(tokens // 8, 8, width), axis=0
        )
        return carried

    lax.fori_loop(0, ROWS, mix, 0)
    for step in range(1, ROWS):
        turned_copy(step).start()

    def hand_on(turn, carried):
        sums.pass_on(block_at(row, jnp.where(turn == 0, 3, turn)))
        return carried

    lax.fori_loop(0, 3, hand_on, 0)
    for step in range(1, ROWS):
        turned_copy(step).wait_recv()
    half = pl.ds(pl.multiple_of(col * (seq // COLS), 128), seq // COLS)
    own_sum = turned[pl.ds(pl.multiple_of(row * sliced, 16), sliced), half].astype(f32)
    for step in range(1, ROWS):
        own_sum = own_sum + turned_from[step].astype(f32)
    own_latent_ref[:, half] = own_sum.astype(bf16)

    def own_copy(part_of):
        here = own_latent_ref.at[
            :, pl.ds(pl.multiple_of(part_of * (seq // COLS), 128), seq // COLS)
        ]
        return remote(here, here, own_sent.at[0], own_arrived.at[0], sibling)

    own_copy(col).start()
    sums.total(total)
    input_grad_ref[...] += norm_grad(
        act_ref[...].astype(f32), scale_one_ref[...], scaling_ref[...], total[...], 1
    )
    own_copy(other).wait_recv()
    own_copy(col).wait_send()

    def ended(block, carried):
        grad_copy(block).wait_send()
        query_copy(block, col).wait_send()
        latent_copy(block).wait_send()
        return carried

    lax.fori_loop(0, ROWS, ended, 0)
    for step in range(1, ROWS):
        turned_copy(step).wait_send()
    stat_copy(0).wait_send()
    stat_copy(1).wait_send()
    sums.finish()
    line.finish()


def run_attention_back(
    normed_grad,
    residual,
    scale_two,
    premix,
    cotangent,
    activations,
    scale_one,
    scaling,
    one,
    query,
    key,
    value,
    probs,
    latent,
    rescale,
    tables,
    compress_all,
    queries,
    expand,
    combine,
):
    tokens, width = activations.shape
    seq = ROWS * tokens
    mine = query.shape[2]
    lanes = key.shape[3]
    latent_width = latent.shape[2]
    sliced = (RANK + ROPE) // ROWS
    whole = pl.BlockSpec(memory_space=VMEM)
    far = pl.BlockSpec(memory_space=pl.ANY)

    def shape(*dims, dtype=bf16):
        return jax.ShapeDtypeStruct(dims, dtype)

    return pl.pallas_call(
        attend_back_kernel,
        name="attend_back",
        out_shape=(
            shape(tokens, width, dtype=f32),
            shape(ROWS, tokens, width),
            shape(ROWS, tokens, COLS * mine),
            shape(ROWS, tokens, 2 * (NOPE + HEADV)),
            shape(sliced, seq),
            shape(8, width, dtype=f32),
            shape(8, RANK, dtype=f32),
        ),
        in_specs=[whole] * 20 + [far] * 3,
        out_specs=(whole,) * 7,
        scratch_shapes=[
            VMEM(queries.shape, bf16),
            VMEM(expand.shape, bf16),
            VMEM(combine.shape, bf16),
            VMEM((2, tokens, 128), f32),
            VMEM((2, tokens, 128), f32),
            VMEM((ROWS, tokens, 2 * HEADV), f32),
            VMEM((ROWS, tokens, 2 * HEADV), bf16),
            VMEM((ROWS, tokens, 2 * HEADV), bf16),
            VMEM((2, seq, lanes), f32),
            VMEM((2, seq, HEADV), f32),
            VMEM((ROWS, tokens, latent_width), f32),
            VMEM((ROWS, tokens, latent_width), bf16),
            VMEM((ROWS, tokens, latent_width), bf16),
            VMEM((latent_width, seq), bf16),
            VMEM((ROWS, sliced, seq // COLS), bf16),
            VMEM((ROWS, tokens, width), f32),
            VMEM((ROWS, tokens, width), bf16),
            VMEM((2, ROWS, tokens, width), bf16),
            VMEM((tokens, width), f32),
            DMA((3,)),
            DMA((2,)),
            DMA((2,)),
            *line_sems(),
            *pair_sems(),
            *pair_sems(),
            *pair_sems(),
            *pair_sems(),
            *pair_sems(),
            *sum_sems(),
        ],
        compiler_params=pltpu.CompilerParams(
            collective_id=3, has_side_effects=True, vmem_limit_bytes=56 * MIB
        ),
        cost_estimate=pl.CostEstimate(
            flops=40 * 1024**3, bytes_accessed=32 * MIB, transcendentals=0
        ),
    )(
        normed_grad,
        residual,
        scale_two,
        premix.reshape(1, width),
        cotangent,
        activations,
        scale_one,
        scaling.reshape(1, width),
        one,
        query,
        key,
        value,
        probs,
        latent,
        rescale.reshape(1, RANK),
        *tables,
        compress_all,
        queries,
        expand,
        combine,
    )


def silu_pair(values):
    sigmoid = 1.0 / (1.0 + jnp.exp(-values))
    return values * sigmoid, sigmoid * (1.0 + values * (1.0 - sigmoid))


def expert_kernel(
    normed_ref,
    pick_ref,
    back_ref,
    cot_rows_ref,
    cot_ref,
    fan_ref,
    fun_ref,
    wide_ref,
    narrow_ref,
    router_ref,
    sum_ref,
    gathered_ref,
    rows_out,
    gu_out,
    hidden_out,
    shared_out,
    shared_gu_out,
    premix_ref,
    router_rows,
    fan,
    fun,
    wide,
    narrow,
    cot_rows,
    rows,
    staged,
    gu,
    hidden,
    pair_own,
    pair_to,
    pair_from,
    home,
    shared_own,
    shared_to,
    shared_from,
    part,
    passed_to,
    passed_from,
    load_sem,
    store_sem,
    line_sent,
    line_arrived,
    out_sent,
    out_arrived,
    fwd_sent,
    fwd_arrived,
    shared_sent,
    shared_arrived,
    half_sent,
    half_arrived,
    home_sent,
    home_arrived,
    sum_sent,
    sum_arrived,
):
    place, row, col = lax.axis_index("dp"), lax.axis_index("row"), lax.axis_index("col")
    other = 1 - col
    tokens, width = normed_ref.shape
    picked = pick_ref.shape[1]
    slots = picked // SQUARE
    hid = fun.shape[0]
    share = narrow.shape[0]
    experts = router_ref.shape[0]
    loads = [
        pltpu.make_async_copy(source, target, load_sem.at[i])
        for i, (source, target) in enumerate(
            [
                (wide_ref, wide),
                (narrow_ref, narrow),
                (fan_ref, fan),
                (cot_rows_ref, cot_rows),
                (fun_ref, fun),
            ]
        )
    ]
    for load in loads:
        load.start()
    greet(row, place, col)
    gathered_ref[pl.ds(row, 1)] = normed_ref[...].reshape(1, tokens, width)
    premix_ref[...] = jnp.zeros_like(premix_ref)
    router_rows[...] = jnp.zeros_like(router_rows)
    line = Line(row, gathered_ref, line_sent, line_arrived)
    sums = SumLine(row, part, passed_to, passed_from, sum_sent, sum_arrived)
    sibling = {"col": other}

    def out_copy(block, step):
        piece = pl.ds(step * slots, slots)
        return remote(
            staged.at[block, piece],
            rows.at[col, block, piece],
            out_sent.at[block, step],
            out_arrived.at[block, step],
            {"dp": partner(place, step)},
        )

    def home_copy(block, step):
        piece = pl.ds(step * slots, slots)
        return remote(
            staged.at[block, piece],
            home.at[block, piece],
            home_sent.at[block, step],
            home_arrived.at[block, step],
            {"dp": partner(place, step)},
        )

    def fwd_copy(block, half):
        here = rows.at[half, block]
        return remote(here, here, fwd_sent.at[block], fwd_arrived.at[block], sibling)

    def shared_copy(block):
        return remote(
            shared_to.at[block],
            shared_from.at[block],
            shared_sent.at[block],
            shared_arrived.at[block],
            sibling,
        )

    def half_copy(block):
        return remote(
            pair_to.at[block],
            pair_from.at[block],
            half_sent.at[block],
            half_arrived.at[block],
            sibling,
        )

    def stores(block):
        return [
            pltpu.make_async_copy(source, target, store_sem.at[index, block])
            for index, (source, target) in enumerate(
                [
                    (rows.at[:, block], rows_out.at[:, block]),
                    (gu.at[:, block], gu_out.at[:, block]),
                    (hidden.at[block], hidden_out.at[block]),
                ]
            )
        ]

    def take(step):
        block = block_at(row, step)

        @pl.when(step > 0)
        def _():
            line.wait(block)

        line.pass_on(block)
        staged[block] = nn(pick_ref[block], gathered_ref[block]).astype(bf16)
        for shift in (3, 2, 1):
            out_copy(block, shift).start()
        rows[col, block, 0:slots] = staged[block, 0:slots]

        @pl.when(step == 0)
        def _():
            loads[0].wait()
            loads[1].wait()

        slot = lax.rem(step, 2)
        for index, value in enumerate(
            (
                nt(gathered_ref[block], wide[0]),
                nt(gathered_ref[block], wide[1]),
                nt(cot_ref[block], narrow[...]),
            )
        ):
            shared_own[slot, index] = value
            shared_to[block, index] = value.astype(bf16)
        shared_copy(block).start()

    def forward(step):
        block = block_at(row, step)
        for shift in range(1, SQUARE):
            out_copy(block, shift).wait_recv()
        fwd_copy(block, col).start()

    def shared(step):
        block = block_at(row, step)
        slot = lax.rem(step, 2)
        shared_copy(block).wait_recv()
        gate, up, grad = [
            shared_own[slot, index] + shared_from[block, index].astype(f32) for index in range(3)
        ]
        act, slope = silu_pair(gate)
        shared_out[block] = (act * up).astype(bf16)
        gate_grad = (grad * up * slope).astype(bf16)
        up_grad = (grad * act).astype(bf16)
        shared_gu_out[0, block] = gate_grad
        shared_gu_out[1, block] = up_grad
        part[block] = nn(gate_grad, wide[0]) + nn(up_grad, wide[1])

    def experts_of(step):
        block = block_at(row, step)
        fwd_copy(block, other).wait_recv()

        @pl.when(step == 0)
        def _():
            for load in loads[2:]:
                load.wait()

        left, right = rows[0, block], rows[1, block]
        logits = nt(left, router_ref[:, 0:width]) + nt(right, router_ref[:, width:])
        logits = logits - jnp.max(logits, axis=1, keepdims=True)
        weight = jnp.exp(logits)
        probs = weight / jnp.sum(weight, axis=1, keepdims=True)
        own = (
            lax.broadcasted_iota(jnp.int32, (picked, experts), 1) == place * ROWS + row
        ).astype(f32)
        gates = jnp.sum(probs * own, axis=1, keepdims=True)
        raw = nt(cot_rows[0, block], fun[:, 0:width]) + nt(cot_rows[1, block], fun[:, width:])
        gate = nt(left, fan[0, :, 0:width]) + nt(right, fan[0, :, width:])
        up = nt(left, fan[1, :, 0:width]) + nt(right, fan[1, :, width:])
        act, slope = silu_pair(gate)
        value = act * up
        hidden[block] = (value * gates).astype(bf16)
        gate_sum = gates * jnp.sum(value * raw, axis=1, keepdims=True)
        logit_grad = gate_sum * (own - probs)
        raw = raw * gates
        gu[0, block] = (raw * up * slope).astype(bf16)
        gu[1, block] = (raw * act).astype(bf16)
        logit_grad = logit_grad.astype(bf16)
        router_rows[:, 0:width] += tn(logit_grad, left)
        router_rows[:, width:] += tn(logit_grad, right)

        def half_of(half):
            lines = pl.ds(pl.multiple_of(half * width, width), width)
            return (
                nn(gu[0, block], fan[0, :, lines])
                + nn(gu[1, block], fan[1, :, lines])
                + nn(logit_grad, router_ref[:, lines])
            )

        pair_to[block] = half_of(other).astype(bf16)
        half_copy(block).start()
        pair_own[...] = half_of(col)
        for copy in stores(block):
            copy.start()

    def send_home(step):
        block = block_at(row, step)
        for shift in range(1, SQUARE):
            out_copy(block, shift).wait_send()
        half_copy(block).wait_recv()
        staged[block] = (pair_own[...] + pair_from[block].astype(f32)).astype(bf16)
        for shift in (3, 2, 1):
            home_copy(block, shift).start()
        home[block, 0:slots] = staged[block, 0:slots]

    def add_up(step):
        block = block_at(row, step)
        for shift in range(1, SQUARE):
            home_copy(block, shift).wait_recv()
        total = part[block] + nn(back_ref[block], home[block])
        part[block] = total
        premix_ref[...] += jnp.sum(
            (total * gathered_ref[block].astype(f32)).reshape(tokens // 8, 8, width), axis=0
        )

        sums.begin(block)

    stages = (
        (0, take),
        (1, forward),
        (1, shared),
        (3, send_home),
        (2, experts_of),
        (4, add_up),
    )

    def turn(step, carried):
        for delay, stage in stages:

            @pl.when(jnp.logical_and(step >= delay, step < delay + ROWS))
            def _(delay=delay, stage=stage):
                stage(step - delay)

        @pl.when(step >= ROWS + 3)
        def _():
            sums.pass_on(block_at(row, jnp.where(step == ROWS + 5, 1, step - 5)))

        return carried

    lax.fori_loop(0, ROWS + 6, turn, 0)
    sums.total(sum_ref)

    def ended(block, carried):
        shared_copy(block).wait_send()
        fwd_copy(block, col).wait_send()
        half_copy(block).wait_send()
        for shift in range(1, SQUARE):
            home_copy(block, shift).wait_send()
        for copy in stores(block):
            copy.wait()
        return carried

    lax.fori_loop(0, ROWS, ended, 0)
    sums.finish()
    line.finish()


def run_experts(
    normed, pick, back, cot_rows, cot_all, fan, fun, wide, narrow, router_all
):
    tokens, width = normed.shape
    picked = pick.shape[1]
    hid = fun.shape[0]
    share = narrow.shape[0]
    experts = router_all.shape[0]
    whole = pl.BlockSpec(memory_space=VMEM)
    far = pl.BlockSpec(memory_space=pl.ANY)

    def shape(*dims, dtype=bf16):
        return jax.ShapeDtypeStruct(dims, dtype)

    return pl.pallas_call(
        expert_kernel,
        name="experts",
        out_shape=(
            shape(tokens, width, dtype=f32),
            shape(ROWS, tokens, width),
            shape(COLS, ROWS, picked, width),
            shape(2, ROWS, picked, hid),
            shape(ROWS, picked, hid),
            shape(ROWS, tokens, share),
            shape(2, ROWS, tokens, share),
            shape(8, width, dtype=f32),
            shape(experts, COLS * width, dtype=f32),
        ),
        in_specs=[whole, whole, whole, far, whole, far, far, far, far, whole],
        out_specs=(whole, whole, far, far, far, whole, whole, whole, whole),
        scratch_shapes=[
            VMEM(fan.shape, bf16),
            VMEM(fun.shape, bf16),
            VMEM(wide.shape, bf16),
            VMEM(narrow.shape, bf16),
            VMEM(cot_rows.shape, bf16),
            VMEM((COLS, ROWS, picked, width), bf16),
            VMEM((ROWS, picked, width), bf16),
            VMEM((2, ROWS, picked, hid), bf16),
            VMEM((ROWS, picked, hid), bf16),
            VMEM((picked, width), f32),
            VMEM((ROWS, picked, width), bf16),
            VMEM((ROWS, picked, width), bf16),
            VMEM((ROWS, picked, width), bf16),
            VMEM((2, 3, tokens, share), f32),
            VMEM((ROWS, 3, tokens, share), bf16),
            VMEM((ROWS, 3, tokens, share), bf16),
            VMEM((ROWS, tokens, width), f32),
            VMEM((ROWS, tokens, width), bf16),
            VMEM((2, ROWS, tokens, width), bf16),
            DMA((5,)),
            DMA((3, ROWS)),
            DMA((ROWS, 2)),
            DMA((ROWS,)),
            DMA((ROWS, SQUARE)),
            DMA((ROWS, SQUARE)),
            DMA((ROWS,)),
            DMA((ROWS,)),
            DMA((ROWS,)),
            DMA((ROWS,)),
            DMA((ROWS,)),
            DMA((ROWS,)),
            DMA((ROWS, SQUARE)),
            DMA((ROWS, SQUARE)),
            DMA((ROWS, SPLIT)),
            DMA((2, ROWS, SPLIT)),
        ],
        compiler_params=pltpu.CompilerParams(
            collective_id=2, has_side_effects=True, vmem_limit_bytes=62 * MIB
        ),
        cost_estimate=pl.CostEstimate(
            flops=60 * 1024**3, bytes_accessed=64 * MIB, transcendentals=0
        ),
    )(normed, pick, back, cot_rows, cot_all, fan, fun, wide, narrow, router_all)


class SquareSum:
    def __init__(self, place, part, first, second, middle, result, sent, arrived):
        self.x, self.y = lax.rem(place, 2), lax.div(place, 2)
        self.to_x, self.to_y = {"dp": partner(place, 1)}, {"dp": partner(place, 2)}
        self.part, self.first, self.second = part, first, second
        self.middle, self.result = middle, result
        self.sent, self.arrived = sent, arrived

    def copies(self, phase):
        x, y = self.x, self.y
        if phase == 0:
            plan = (
                (self.part.at[pl.ds(2 - 2 * x, 2)], self.first.at[0:2], self.to_x),
                (self.part.at[pl.ds(6 - 2 * y, 2)], self.first.at[2:4], self.to_y),
            )
        elif phase == 1:
            plan = (
                (self.middle.at[0], self.second.at[0], self.to_y),
                (self.middle.at[1], self.second.at[1], self.to_x),
            )
        elif phase == 2:
            one, two = self.result.at[2 * x + y], self.result.at[4 + 2 * y + x]
            plan = ((one, one, self.to_y), (two, two, self.to_x))
        else:
            one, two = self.result.at[pl.ds(2 * x, 2)], self.result.at[pl.ds(4 + 2 * y, 2)]
            plan = ((one, one, self.to_x), (two, two, self.to_y))
        return [
            remote(source, target, self.sent.at[2 * phase + i], self.arrived.at[2 * phase + i], to)
            for i, (source, target, to) in enumerate(plan)
        ]

    def start(self, phase):
        for copy in self.copies(phase):
            copy.start()

    def arrive(self, phase):
        for copy in self.copies(phase):
            copy.wait_recv()

    def run(self, phase):
        x, y = self.x, self.y
        if phase > 0:
            self.arrive(phase - 1)
        if phase == 1:
            for slot, piece, came in (
                (0, 2 * x + 1 - y, 1 - y),
                (1, 4 + 2 * y + 1 - x, 3 - x),
            ):
                self.middle[slot] = (
                    self.part[piece].astype(f32) + self.first[came].astype(f32)
                ).astype(bf16)
        if phase == 2:
            for slot, piece, came in ((0, 2 * x + y, y), (1, 4 + 2 * y + x, 2 + x)):
                self.result[piece] = (
                    self.part[piece].astype(f32)
                    + self.first[came].astype(f32)
                    + self.second[slot].astype(f32)
                ).astype(bf16)
        if phase < 4:
            self.start(phase)

    def finish(self):
        for phase in range(4):
            for copy in self.copies(phase):
                copy.wait_send()


def square_scratch(dims):
    count, rows, lanes = dims
    return [
        VMEM((count, 8, rows, lanes), bf16),
        VMEM((count, 4, rows, lanes), bf16),
        VMEM((count, 2, rows, lanes), bf16),
        VMEM((count, 2, rows, lanes), bf16),
        VMEM((count, 8, rows, lanes), bf16),
        DMA((count, 8)),
        DMA((count, 8)),
    ]


def finish_kernel(
    own_latent_ref,
    back_ref,
    shared_ref,
    residual_ref,
    premix_rows,
    scaling_rows,
    rescale_rows,
    router_rows,
    premix_ref,
    scaling_ref,
    hidden_ref,
    funnel_ref,
    one_ref,
    query_grad_ref,
    attended_ref,
    branch_ref,
    latent_ref,
    expanded_ref,
    narrow_ref,
    output_ref,
    queries_out,
    combine_out,
    expand_out,
    compress_out,
    small_ref,
    hidden,
    funnel,
    one,
    query_grad,
    attended,
    branch,
    latent,
    expanded,
    narrow,
    reply_own,
    reply_to,
    reply_from,
    staged,
    home,
    part,
    leaving,
    coming,
    total,
    queries_wide,
    combine_wide,
    expand_wide,
    compress_wide,
    small_to,
    small_from,
    small_line,
    small_square,
    small_own,
    load_sem,
    store_sem,
    reply_sent,
    reply_arrived,
    home_sent,
    home_arrived,
    sum_sent,
    sum_arrived,
    pair_sent,
    pair_arrived,
    small_sent,
    small_arrived,
    *sums_scratch,
):
    place, row, col = lax.axis_index("dp"), lax.axis_index("row"), lax.axis_index("col")
    other = 1 - col
    sibling = {"col": other}
    tokens, width = output_ref.shape
    seq = ROWS * tokens
    picked = back_ref.shape[2]
    slots = picked // SQUARE
    experts = router_rows.shape[0]
    loads = [
        pltpu.make_async_copy(source, target, load_sem.at[i])
        for i, (source, target) in enumerate(
            [
                (funnel_ref, funnel),
                (hidden_ref, hidden),
                (one_ref, one),
                (query_grad_ref, query_grad),
                (attended_ref, attended),
                (branch_ref, branch),
                (latent_ref, latent),
                (expanded_ref, expanded),
                (narrow_ref, narrow),
            ]
        )
    ]
    for load in loads:
        load.start()
    greet(row, place, col, line=True, square=True)
    line_sums = SumLine(row, part, leaving, coming, sum_sent, sum_arrived)

    def reply_copy(block):
        return remote(
            reply_to.at[block],
            reply_from.at[block],
            reply_sent.at[block],
            reply_arrived.at[block],
            sibling,
        )

    def home_copy(block, step):
        piece = pl.ds(step * slots, slots)
        return remote(
            staged.at[block, piece],
            home.at[block, piece],
            home_sent.at[block, step],
            home_arrived.at[block, step],
            {"dp": partner(place, step)},
        )

    def reply(turn):
        block = block_at(row, ROWS - 1 - turn)
        value = hidden[block]
        reply_to[block] = nn(
            value, funnel[:, pl.ds(pl.multiple_of(other * width, width), width)]
        ).astype(bf16)
        reply_copy(block).start()
        reply_own[lax.rem(turn, 2)] = nn(
            value, funnel[:, pl.ds(pl.multiple_of(col * width, width), width)]
        )

    def reply_home(turn):
        block = block_at(row, ROWS - 1 - turn)
        reply_copy(block).wait_recv()
        staged[block] = (
            reply_own[lax.rem(turn, 2)] + reply_from[block].astype(f32)
        ).astype(bf16)
        for shift in (3, 2, 1):
            home_copy(block, shift).start()
        home[block, 0:slots] = staged[block, 0:slots]

    def reply_add(turn, carried):
        block = block_at(row, ROWS - 1 - turn)
        for shift in range(1, SQUARE):
            home_copy(block, shift).wait_recv()
        part[block] = nn(back_ref[block], home[block]) + nn(shared_ref[block], narrow[...])
        line_sums.begin(block)
        return carried

    loads[0].wait()
    loads[1].wait()

    def replies(turn, carried):
        @pl.when(turn < ROWS)
        def _():
            reply(turn)

        @pl.when(turn > 0)
        def _():
            reply_home(turn - 1)

        return carried

    lax.fori_loop(0, ROWS + 1, replies, 0)

    kinds = [sums_scratch[7 * i : 7 * i + 7] for i in range(4)]
    sums = []
    for scratch in kinds:
        for index in range(scratch[0].shape[0]):
            sums.append(SquareSum(place, *[ref.at[index] for ref in scratch]))
    parts = [scratch[0] for scratch in kinds]
    counts = [ref.shape[0] for ref in parts]
    for load in loads[2:4]:
        load.wait()
    index = 0
    for chunk in range(counts[0]):
        height = 8 * parts[0].shape[2]
        tokens_here = one[:, :, chunk * height : (chunk + 1) * height].reshape(seq, height)
        grad = tn(tokens_here, query_grad[...].reshape(seq, query_grad.shape[2]))
        parts[0][chunk] = grad.astype(bf16).reshape(parts[0].shape[1:])
        sums[index].run(0)
        index += 1
    loads[4].wait()
    loads[5].wait()
    for chunk in range(counts[1]):
        height = 8 * parts[1].shape[2]
        tokens_here = attended[:, :, chunk * height : (chunk + 1) * height].reshape(seq, height)
        grad = tn(tokens_here, branch[...].reshape(seq, width))
        parts[1][chunk] = grad.astype(bf16).reshape(parts[1].shape[1:])
        sums[index].run(0)
        index += 1
    loads[6].wait()
    loads[7].wait()
    grad = tn(latent[...].reshape(seq, RANK), expanded[...].reshape(seq, expanded.shape[2]))
    parts[2][0] = grad.astype(bf16).reshape(parts[2].shape[1:])
    sums[index].run(0)
    index += 1
    grad = nn(own_latent_ref[...], one[...].reshape(seq, width)).astype(bf16)
    for piece in range(8):
        parts[3][0, piece] = grad[:, piece * (width // 8) : (piece + 1) * (width // 8)]
    sums[index].run(0)

    def small_copy(step):
        if step == 0:
            return remote(small_to, small_from, small_sent.at[0], small_arrived.at[0], sibling)
        if step < ROWS:
            return remote(
                small_own,
                small_line.at[step],
                small_sent.at[step],
                small_arrived.at[step],
                {"row": lax.rem(row + step, ROWS)},
            )
        shift = step - ROWS + 1
        return remote(
            small_ref,
            small_square.at[shift],
            small_sent.at[step],
            small_arrived.at[step],
            {"dp": partner(place, shift)},
        )

    rescale_row = jnp.sum(rescale_rows[...], axis=0, keepdims=True)
    empty = jnp.zeros((small_own.shape[0] - experts, width), f32)
    small_to[0:experts] = router_rows[:, pl.ds(pl.multiple_of(other * width, width), width)]
    small_to[experts:] = empty
    small_to[experts + 2 : experts + 3, 0:RANK] = rescale_row
    small_copy(0).start()
    small_own[0:experts] = router_rows[:, pl.ds(pl.multiple_of(col * width, width), width)]
    small_own[experts:] = empty
    small_own[experts : experts + 1] = (
        jnp.sum(premix_rows[...], axis=0, keepdims=True) / premix_ref[...]
    )
    small_own[experts + 1 : experts + 2] = (
        jnp.sum(scaling_rows[...], axis=0, keepdims=True) / scaling_ref[...]
    )
    small_own[experts + 2 : experts + 3, 0:RANK] = rescale_row
    small_copy(0).wait_recv()
    small_own[...] += small_from[...]
    for step in range(1, ROWS):
        small_copy(step).start()

    loads[8].wait()
    lax.fori_loop(0, ROWS, reply_add, 0)

    def line_pass(turn, carried):
        line_sums.pass_on(block_at(row, jnp.where(turn == 0, 3, turn)))
        return carried

    stores = []

    def store(source, target):
        copy = pltpu.make_async_copy(source, target, store_sem.at[len(stores)])
        copy.start()
        stores.append(copy)

    def pair_copy(half):
        here = expand_wide.at[half]
        return remote(here, here, pair_sent.at[0], pair_arrived.at[0], sibling)

    def put(index):
        kind, chunk = 0, index
        while chunk >= counts[kind]:
            chunk -= counts[kind]
            kind += 1
        result = kinds[kind][4][chunk]
        pieces, rows, lanes = result.shape
        if kind < 2:
            wide, out = ((queries_wide, queries_out), (combine_wide, combine_out))[kind]
            here = pl.ds(chunk * pieces * rows, pieces * rows)
            wide[here] = result.astype(f32).reshape(pieces * rows, lanes)
            store(wide.at[here], out.at[here])
        elif kind == 2:
            expand_wide[col] = result.astype(f32).reshape(pieces * rows, lanes)
            pair_copy(col).start()
        else:
            for piece in range(pieces):
                compress_wide[:, piece * lanes : (piece + 1) * lanes] = result[piece].astype(f32)
            store(compress_wide, compress_out)

    count = len(sums)
    small_steps = {
        2: "line",
        count + 2: "square",
    }
    for turn in range(count + 6):
        if turn < count:
            sums[turn].run(1)
        if turn == 1:
            lax.fori_loop(0, 3, line_pass, 0)
        if 0 <= turn - 2 < count:
            sums[turn - 2].run(2)
        if 0 <= turn - 4 < count:
            sums[turn - 4].run(3)
        if 0 <= turn - 6 < count:
            sums[turn - 6].run(4)
            put(turn - 6)
        if small_steps.get(turn) == "line":
            for step in range(1, ROWS):
                small_copy(step).wait_recv()
            small_ref[...] = (
                small_own[...] + small_line[1] + small_line[2] + small_line[3]
            )
            for step in range(ROWS, ROWS + SQUARE - 1):
                small_copy(step).start()
            line_sums.total(total)
            output_ref[...] = (total[...] + residual_ref[...]).astype(bf16)
        if small_steps.get(turn) == "square":
            for step in range(ROWS, ROWS + SQUARE - 1):
                small_copy(step).wait_recv()
            for step in range(ROWS, ROWS + SQUARE - 1):
                small_copy(step).wait_send()
            small_ref[...] += small_square[1] + small_square[2] + small_square[3]

    pair_copy(other).wait_recv()
    store(expand_wide.at[0], expand_out.at[:, 0 : expand_wide.shape[2]])
    store(expand_wide.at[1], expand_out.at[:, expand_wide.shape[2] :])
    for copy in stores:
        copy.wait()
    pair_copy(col).wait_send()
    for step in range(ROWS):
        small_copy(step).wait_send()
    for one_sum in sums:
        one_sum.finish()
    line_sums.finish()

    def ended(block, carried):
        reply_copy(block).wait_send()
        for shift in range(1, SQUARE):
            home_copy(block, shift).wait_send()
        return carried

    lax.fori_loop(0, ROWS, ended, 0)


def run_finish(
    own_latent,
    back,
    shared,
    residual,
    premix_rows,
    scaling_rows,
    rescale_rows,
    router_rows,
    premix,
    scaling,
    hidden,
    funnel,
    one,
    query_grad,
    attended,
    branch,
    latent,
    expanded,
    narrow,
):
    tokens, width = residual.shape
    picked = back.shape[2]
    sliced = own_latent.shape[0]
    wide = query_grad.shape[2]
    heads = attended.shape[2]
    own_heads = expanded.shape[2]
    small = (24, width)
    whole = pl.BlockSpec(memory_space=VMEM)
    far = pl.BlockSpec(memory_space=pl.ANY)

    def shape(*dims, dtype=f32):
        return jax.ShapeDtypeStruct(dims, dtype)

    loaded = (hidden, funnel, one, query_grad, attended, branch, latent, expanded, narrow)
    return pl.pallas_call(
        finish_kernel,
        name="finish",
        out_shape=(
            shape(tokens, width, dtype=bf16),
            shape(width, wide),
            shape(heads, width),
            shape(RANK, COLS * own_heads),
            shape(sliced, width),
            shape(*small),
        ),
        in_specs=[whole] * 10 + [far] * 9,
        out_specs=(whole, far, far, far, far, whole),
        scratch_shapes=[
            *[VMEM(value.shape, bf16) for value in loaded],
            VMEM((2, picked, width), f32),
            VMEM((ROWS, picked, width), bf16),
            VMEM((ROWS, picked, width), bf16),
            VMEM((ROWS, picked, width), bf16),
            VMEM((ROWS, picked, width), bf16),
            VMEM((ROWS, tokens, width), f32),
            VMEM((ROWS, tokens, width), bf16),
            VMEM((2, ROWS, tokens, width), bf16),
            VMEM((tokens, width), f32),
            VMEM((width, wide), f32),
            VMEM((heads, width), f32),
            VMEM((COLS, RANK, own_heads), f32),
            VMEM((sliced, width), f32),
            VMEM(small, f32),
            VMEM(small, f32),
            VMEM((ROWS,) + small, f32),
            VMEM((SQUARE,) + small, f32),
            VMEM(small, f32),
            DMA((len(loaded),)),
            DMA((10,)),
            *pair_sems(),
            *square_sems(),
            *sum_sems(),
            DMA((1,)),
            DMA((1,)),
            DMA((ROWS + SQUARE - 1,)),
            DMA((ROWS + SQUARE - 1,)),
            *square_scratch((4, width // 32, wide)),
            *square_scratch((2, heads // 16, width)),
            *square_scratch((1, RANK // 8, own_heads)),
            *square_scratch((1, sliced, width // 8)),
        ],
        compiler_params=pltpu.CompilerParams(
            collective_id=4, has_side_effects=True, vmem_limit_bytes=60 * MIB
        ),
        cost_estimate=pl.CostEstimate(
            flops=40 * 1024**3, bytes_accessed=64 * MIB, transcendentals=0
        ),
    )(
        own_latent,
        back,
        shared,
        residual,
        premix_rows,
        scaling_rows,
        rescale_rows,
        router_rows,
        premix.reshape(1, width),
        scaling.reshape(1, width),
        *loaded,
    )


def product_kernel(left_ref, right_ref, out_ref):
    wide = 256

    def one(index, carried):
        lanes = pl.ds(pl.multiple_of(index * wide, 128), wide)
        out_ref[0, :, lanes] = tn(left_ref[0], right_ref[0, :, lanes])
        return carried

    lax.fori_loop(0, right_ref.shape[2] // wide, one, 0)


def slot_products(left, right):
    kinds, slots, tall = left.shape
    halves, _, wide = right.shape
    return pl.pallas_call(
        product_kernel,
        name="slot_products",
        grid=(kinds, halves),
        out_shape=jax.ShapeDtypeStruct((kinds, tall, halves * wide), f32),
        in_specs=[
            pl.BlockSpec((1, slots, tall), lambda kind, half: (kind, 0, 0)),
            pl.BlockSpec((1, slots, wide), lambda kind, half: (half, 0, 0)),
        ],
        out_specs=pl.BlockSpec((1, tall, wide), lambda kind, half: (kind, 0, half)),
        compiler_params=pltpu.CompilerParams(vmem_limit_bytes=40 * MIB),
        cost_estimate=pl.CostEstimate(
            flops=2 * kinds * halves * slots * tall * wide,
            bytes_accessed=4 * kinds * halves * tall * wide,
            transcendentals=0,
        ),
    )(left, right)


def local_square(
    activations,
    cotangent,
    routing,
    segments,
    scaling,
    queries,
    compress,
    rescale,
    expand,
    combine,
    premix,
    router,
    widening,
    narrowing,
    fanout,
    funnel,
):
    dp_count = lax.axis_size("dp")
    row_count = lax.axis_size("row")
    col_count = lax.axis_size("col")
    col_index = lax.axis_index("col")
    local_rows, col_width = activations.shape
    seq_length = local_rows * row_count
    expert_total = router.shape[1]
    capacity = local_rows * TOP * 4 // (3 * expert_total)
    slot_total = capacity * row_count * dp_count
    tables = turning_tables(seq_length)
    (
        one,
        query,
        key,
        value,
        probs,
        latent,
        latent_normed,
        attended,
        compress_all,
        residual,
        normed_two,
        scale_one,
        scale_two,
        cot_blocks,
        pick,
        back,
        cot_rows,
        router_all,
    ) = run_attention(
        activations,
        scaling,
        queries,
        compress,
        rescale,
        expand,
        combine,
        premix,
        segments,
        cotangent,
        routing,
        router,
        tables,
        capacity,
    )
    (
        normed_grad,
        two_blocks,
        expert_rows,
        expert_gu_grad,
        expert_hidden,
        hidden_blocks,
        gu_blocks,
        premix_rows,
        router_rows,
    ) = run_experts(
        normed_two,
        pick,
        back,
        cot_rows,
        cot_blocks,
        fanout[0].transpose(0, 2, 1),
        funnel[0],
        widening.transpose(0, 2, 1),
        narrowing,
        router_all,
    )
    cotangent_all = cot_blocks.reshape(seq_length, col_width)
    gathered_two = two_blocks.reshape(seq_length, col_width)
    hidden_all = hidden_blocks.reshape(seq_length, -1)
    gu_grad_all = gu_blocks.reshape(2, seq_length, -1)
    slot_rows = expert_rows.reshape(col_count, slot_total, col_width)
    reply_grad_rows = cot_rows.reshape(col_count, slot_total, col_width)
    slot_hidden = expert_hidden.reshape(slot_total, -1)
    slot_gu_grad = expert_gu_grad.reshape(2, slot_total, -1)
    narrowing_grad = dot_tn(hidden_all, cotangent_all)
    widening_grad = jnp.einsum(
        "gtf,td->gfd", gu_grad_all, gathered_two, preferred_element_type=f32
    )
    shared_sums = lax.psum((narrowing_grad.astype(bf16), widening_grad.astype(bf16)), "dp")
    (
        input_grad,
        branch_blocks,
        query_grad,
        expanded_grad,
        own_latent_grad,
        scaling_rows,
        rescale_rows,
    ) = run_attention_back(
        normed_grad,
        residual,
        scale_two,
        premix,
        cotangent,
        activations,
        scale_one,
        scaling,
        one,
        query,
        key,
        value,
        probs,
        latent,
        rescale,
        tables,
        compress_all,
        queries,
        expand,
        combine,
    )
    fanout_grad = slot_products(slot_gu_grad, slot_rows)
    funnel_grad = slot_products(slot_hidden[None], reply_grad_rows)
    own_latent_grad, fanout_grad, funnel_grad = lax.optimization_barrier(
        (own_latent_grad, fanout_grad, funnel_grad)
    )
    layer_output, queries_sum, combine_sum, expand_sum, compress_sum, small = run_finish(
        own_latent_grad,
        back,
        hidden_blocks,
        residual,
        premix_rows,
        scaling_rows,
        rescale_rows,
        router_rows,
        premix,
        scaling,
        expert_hidden,
        funnel[0],
        one,
        query_grad,
        attended,
        branch_blocks,
        latent_normed,
        expanded_grad,
        narrowing,
    )
    return (
        layer_output,
        input_grad,
        small[expert_total + 1],
        queries_sum,
        compress_sum.T,
        small[expert_total + 2, :RANK],
        expand_sum,
        combine_sum,
        small[expert_total],
        small[:expert_total].T,
        shared_sums[1].astype(f32).transpose(0, 2, 1),
        shared_sums[0].astype(f32),
        fanout_grad.transpose(0, 2, 1)[None],
        funnel_grad,
    )


def local(
    activations,
    cotangent,
    routing,
    segments,
    scaling,
    queries,
    compress,
    rescale,
    expand,
    combine,
    premix,
    router,
    widening,
    narrowing,
    fanout,
    funnel,
):
    dp_count = lax.axis_size("dp")
    row_count = lax.axis_size("row")
    col_count = lax.axis_size("col")
    dp_index = lax.axis_index("dp")
    row_index = lax.axis_index("row")
    col_index = lax.axis_index("col")
    local_rows = activations.shape[0]
    col_width = activations.shape[1]
    seq_length = local_rows * row_count
    half_length = seq_length // col_count
    head_width = NOPE + ROPE
    pair_width = NOPE + HEADV
    local_heads = queries.shape[1] // head_width
    slice_width = compress.shape[1]
    expert_total = router.shape[1]
    capacity = local_rows * TOP * 4 // (3 * expert_total)
    slots = capacity * row_count
    slot_total = slots * dp_count
    block_rows = min(512, half_length)
    block_count = half_length // block_rows
    score_scale = head_width ** (-0.5)

    inputs = activations.astype(f32)
    scale_one = norm_scale(inputs)
    normed_one = (inputs * scale_one[:, None] * scaling).astype(bf16)
    gathered_one = row_gather(normed_one)
    compress_all = lax.all_gather(compress, "row", axis=1, tiled=True)

    routing_all = row_gather(routing)
    cotangent_all = row_gather(after(cotangent, gathered_one))
    offsets = jnp.arange(dp_count, dtype=jnp.int32)
    my_experts = ((dp_index + offsets) % dp_count) * row_count + row_index
    goes = jnp.any(routing_all[None, :, :] == my_experts[:, None, None], axis=2)
    token_range = jnp.arange(seq_length, dtype=jnp.int32)
    earlier = (token_range[:, None] < token_range[None, :]).astype(bf16)
    rank = dot(goes.astype(bf16), earlier).astype(jnp.int32)
    slot_range = jnp.arange(slots, dtype=jnp.int32)
    pick = (
        ((rank[:, None, :] == slot_range[None, :, None]) & goes[:, None, :])
        .astype(bf16)
        .reshape(slot_total, seq_length)
    )

    def dispatch(tokens):
        rows = dot(pick, tokens).astype(bf16).reshape(dp_count, slots, col_width)
        arrived = send_out([rows[k] for k in range(dp_count)])
        return col_gather(jnp.concatenate(arrived, axis=0), axis=1)

    def bring_back(part):
        summed = col_scatter(part.astype(bf16), axis=1).reshape(dp_count, slots, col_width)
        arrived = send_back([summed[k] for k in range(dp_count)])
        return dot_tn(pick, jnp.concatenate(arrived, axis=0))

    query_part = dot(gathered_one, queries)
    latent_part = dot(gathered_one, compress_all)
    query_raw, latent_raw = col_scatter((query_part, latent_part))
    latent_plain = latent_raw[:, :RANK]
    latent_scale = lax.rsqrt(jnp.mean(latent_plain * latent_plain, axis=1) + epsilon)
    latent_normed = (latent_plain * latent_scale[:, None] * rescale).astype(bf16)
    expanded = dot(latent_normed, expand).reshape(half_length, local_heads, pair_width)
    positions = col_index * half_length + jnp.arange(half_length, dtype=jnp.int32)
    cosine, sine_table = rotation(positions, ROPE)
    key_shared = rotate(latent_raw[:, RANK:], cosine, sine_table, 1.0)
    query_heads = query_raw.reshape(half_length, local_heads, head_width)
    query_local = jnp.concatenate(
        [
            query_heads[..., :NOPE],
            rotate(query_heads[..., NOPE:], cosine[:, None, :], sine_table[:, None, :], 1.0),
        ],
        axis=2,
    ).astype(bf16)
    key_local = jnp.concatenate(
        [
            expanded[..., :NOPE],
            jnp.broadcast_to(key_shared[:, None, :], (half_length, local_heads, ROPE)),
        ],
        axis=2,
    ).astype(bf16)
    value_local = expanded[..., NOPE:].astype(bf16)
    key_flat, value_flat = (
        col_gather(key_local.reshape(half_length, local_heads * head_width)),
        col_gather(value_local.reshape(half_length, local_heads * HEADV)),
    )
    key_heads = key_flat.reshape(seq_length, local_heads, head_width)
    value_heads = value_flat.reshape(seq_length, local_heads, HEADV)
    own_segments = lax.dynamic_slice_in_dim(
        segments, col_index * half_length, half_length, 0
    ).reshape(block_count, block_rows)
    query_blocks = query_local.reshape(block_count, block_rows, local_heads, head_width)

    def attend_block(inputs_block):
        query_block, segment_block = inputs_block
        scores = (
            jnp.einsum("qhd,khd->hqk", query_block, key_heads, preferred_element_type=f32)
            * score_scale
        )
        visible = segments[None, None, :] <= segment_block[None, :, None]
        scores = jnp.where(visible, scores, masked_score)
        largest = jnp.max(scores, axis=2, keepdims=True)
        weight = jnp.exp(scores - largest)
        totals = jnp.sum(weight, axis=2, keepdims=True)
        probability = (weight / totals).astype(bf16)
        result = jnp.einsum("hqk,khd->qhd", probability, value_heads, preferred_element_type=f32)
        return (result.astype(bf16), (largest + jnp.log(totals))[..., 0])

    attended_blocks, log_totals = lax.map(attend_block, (query_blocks, own_segments))
    attended = attended_blocks.reshape(half_length, local_heads * HEADV)
    attended_all = col_gather(attended)
    branch = row_scatter(dot(attended_all, combine))

    reply_grad_rows = dispatch(cotangent_all)
    inner_weight = fanout[0]
    outer_weight = funnel[0]
    hidden_raw = dot_nt(reply_grad_rows, outer_weight)
    shared_hidden_grad = col_scatter(dot_nt(cotangent_all, narrowing))

    residual = inputs + branch
    scale_two = norm_scale(residual)
    normed_two = (residual * scale_two[:, None] * premix).astype(bf16)
    gathered_two = row_gather(normed_two)

    expert_rows = dispatch(gathered_two)
    expert_range = jnp.arange(expert_total, dtype=jnp.int32)
    router_all = lax.all_gather(router, "col", axis=0, tiled=True)
    own_expert = dp_index * row_count + row_index
    slot_probs = jax.nn.softmax(dot(expert_rows, router_all), axis=1)
    slot_gates = jnp.sum(jnp.where(expert_range == own_expert, slot_probs, 0.0), axis=1)
    gate_up = jnp.einsum("rd,gdf->grf", expert_rows, inner_weight, preferred_element_type=f32)
    gate_input, up_input = gate_up[0], gate_up[1]
    hidden = jax.nn.silu(gate_input) * up_input
    expert_hidden = hidden.astype(bf16)
    slot_gate_grad = col_totals(jnp.sum(hidden * hidden_raw, axis=1))
    hidden_grad = hidden_raw * slot_gates[:, None]
    expert_gu_grad = jnp.stack(
        [hidden_grad * up_input * silu_slope(gate_input), hidden_grad * jax.nn.silu(gate_input)]
    ).astype(bf16)
    input_part = jnp.einsum(
        "grf,gdf->rd", expert_gu_grad, inner_weight, preferred_element_type=f32
    )
    routed_grad = bring_back(input_part)
    gate_grad_parts = send_back(
        [slot_gate_grad.reshape(dp_count, slots)[k] for k in range(dp_count)]
    )

    logits = col_totals(dot(gathered_two, router))
    router_probs = jax.nn.softmax(logits, axis=1)
    gate_grad = jnp.sum(
        pick.reshape(dp_count, slots, seq_length).astype(f32)
        * jnp.stack(gate_grad_parts)[:, :, None],
        axis=1,
    )
    mine = (my_experts[:, None] == expert_range[None, :]).astype(f32)
    probs_grad = jnp.sum(gate_grad[:, :, None] * mine[:, None, :], axis=0)
    logit_grad = router_probs * (
        probs_grad - jnp.sum(router_probs * probs_grad, axis=1, keepdims=True)
    )
    router_part = dot_tn(gathered_two, logit_grad)

    shared_gate_up = col_scatter(
        jnp.einsum("td,gdf->tgf", gathered_two, widening, preferred_element_type=f32)
    )
    shared_hidden = (jax.nn.silu(shared_gate_up[:, 0]) * shared_gate_up[:, 1]).astype(bf16)
    hidden_all = col_gather(shared_hidden)
    narrowing_grad = dot_tn(hidden_all, cotangent_all)
    shared_gu_grad = jnp.stack(
        [
            shared_hidden_grad * shared_gate_up[:, 1] * silu_slope(shared_gate_up[:, 0]),
            shared_hidden_grad * jax.nn.silu(shared_gate_up[:, 0]),
        ],
        axis=1,
    ).astype(bf16)
    gu_grad_all = col_gather(shared_gu_grad)
    widening_grad = jnp.einsum(
        "td,tgf->gdf", gathered_two, gu_grad_all, preferred_element_type=f32
    )
    shared_input_part = jnp.einsum(
        "tgf,gdf->td", gu_grad_all, widening, preferred_element_type=f32
    )
    shared_sums = lax.psum((narrowing_grad.astype(bf16), widening_grad.astype(bf16)), "dp")

    grad_part = routed_grad + shared_input_part + dot_nt(logit_grad, router)
    premix_part = jnp.sum(grad_part * gathered_two.astype(f32), axis=0) / premix
    normed_grad = row_scatter(grad_part)

    upstream = cotangent.astype(f32)
    residual_grad = upstream + norm_back(residual, scale_two, premix, normed_grad)
    branch_all = row_gather(residual_grad.astype(bf16))

    funnel_grad = dot_tn((hidden * slot_gates[:, None]).astype(bf16), reply_grad_rows)[None]
    fanout_grad = jnp.einsum(
        "rd,grf->gdf", expert_rows, expert_gu_grad, preferred_element_type=f32
    )[None]
    reply_part = dot(expert_hidden, outer_weight) * slot_gates[:, None]
    routed = bring_back(reply_part)
    shared_out = row_scatter(routed + dot(hidden_all, narrowing))
    layer_output = (residual + shared_out).astype(bf16)

    combine_grad = dot_tn(attended_all, branch_all)
    combine_sum = lax.psum(after(combine_grad.astype(bf16), *shared_sums), "dp")
    attended_grad = col_scatter(dot_nt(branch_all, combine))
    attended_grad_blocks = attended_grad.astype(bf16).reshape(
        block_count, block_rows, local_heads, HEADV
    )

    def attend_back(carried, inputs_block):
        key_sum, value_sum = carried
        query_block, grad_block, log_block, segment_block = inputs_block
        scores = (
            jnp.einsum("qhd,khd->hqk", query_block, key_heads, preferred_element_type=f32)
            * score_scale
        )
        visible = segments[None, None, :] <= segment_block[None, :, None]
        probability = jnp.where(visible, jnp.exp(scores - log_block[..., None]), 0.0)
        weight_grad = jnp.einsum(
            "qhd,khd->hqk", grad_block, value_heads, preferred_element_type=f32
        )
        inner_sum = jnp.sum(probability * weight_grad, axis=2, keepdims=True)
        score_grad = (probability * (weight_grad - inner_sum)).astype(bf16)
        query_grad_block = (
            jnp.einsum("hqk,khd->qhd", score_grad, key_heads, preferred_element_type=f32)
            * score_scale
        )
        key_sum = (
            key_sum
            + jnp.einsum("hqk,qhd->khd", score_grad, query_block, preferred_element_type=f32)
            * score_scale
        )
        value_sum = value_sum + jnp.einsum(
            "hqk,qhd->khd", probability.astype(bf16), grad_block, preferred_element_type=f32
        )
        return ((key_sum, value_sum), query_grad_block)

    key_start = jnp.zeros((seq_length, local_heads, head_width), f32)
    value_start = jnp.zeros((seq_length, local_heads, HEADV), f32)
    (key_grad_all, value_grad_all), query_grad_blocks = lax.scan(
        attend_back,
        (key_start, value_start),
        (query_blocks, attended_grad_blocks, log_totals, own_segments),
    )
    key_grad, value_grad = col_scatter(
        (
            key_grad_all.reshape(seq_length, local_heads * head_width),
            value_grad_all.reshape(seq_length, local_heads * HEADV),
        )
    )
    key_grad = key_grad.reshape(half_length, local_heads, head_width)
    value_grad = value_grad.reshape(half_length, local_heads, HEADV)
    query_grad = query_grad_blocks.reshape(half_length, local_heads, head_width)
    query_raw_grad = (
        jnp.concatenate(
            [
                query_grad[..., :NOPE],
                rotate(query_grad[..., NOPE:], cosine[:, None, :], sine_table[:, None, :], -1.0),
            ],
            axis=2,
        )
        .astype(bf16)
        .reshape(half_length, local_heads * head_width)
    )
    expanded_grad = (
        jnp.concatenate([key_grad[..., :NOPE], value_grad], axis=2)
        .astype(bf16)
        .reshape(half_length, local_heads * pair_width)
    )
    shared_rope_grad = rotate(jnp.sum(key_grad[..., NOPE:], axis=1), cosine, sine_table, -1.0)

    latent_grad = dot_nt(expanded_grad, expand)
    latent_weighted = latent_grad * rescale
    latent_inner = jnp.mean(latent_weighted * latent_plain, axis=1)
    rescale_part = jnp.sum(latent_grad * latent_plain * latent_scale[:, None], axis=0)
    plain_grad = (
        latent_weighted * latent_scale[:, None]
        - latent_plain * (latent_scale**3 * latent_inner)[:, None]
    )
    latent_raw_grad = jnp.concatenate([plain_grad, shared_rope_grad], axis=1).astype(bf16)
    query_grad_all = col_gather(query_raw_grad)
    latent_grad_all = col_gather(latent_raw_grad)
    first_part = dot_nt(query_grad_all, queries) + dot_nt(latent_grad_all, compress_all)
    first_grad = row_scatter(first_part)
    input_grad = residual_grad + norm_back(inputs, scale_one, scaling, first_grad)

    queries_part = dot_tn(gathered_one, query_grad_all)
    own_latent_grad = lax.psum_scatter(
        latent_raw_grad, "row", scatter_dimension=1, tiled=True
    )
    compress_part = dot_tn(gathered_one, col_gather(own_latent_grad))
    half_rank = RANK // col_count
    latent_normed_all = col_gather(latent_normed)
    expanded_grad_all = col_gather(expanded_grad)
    expand_half = dot_tn(
        lax.dynamic_slice_in_dim(latent_normed_all, col_index * half_rank, half_rank, 1),
        expanded_grad_all,
    )
    scaling_part = jnp.sum(first_part * gathered_one.astype(f32), axis=0) / scaling
    queries_sum, expand_sum, compress_sum = lax.psum(
        (
            after(queries_part.astype(bf16), combine_sum),
            expand_half.astype(bf16),
            compress_part.astype(bf16),
        ),
        "dp",
    )
    premix_sum, router_sum = lax.psum((premix_part, router_part), ("dp", "row"))
    rescale_sum = lax.psum(rescale_part, ("dp", "row", "col"))
    scaling_sum = lax.psum(scaling_part, ("dp", "row"))
    return (
        layer_output,
        input_grad,
        scaling_sum,
        queries_sum.astype(f32),
        compress_sum.astype(f32),
        rescale_sum,
        col_gather(expand_sum).astype(f32),
        combine_sum.astype(f32),
        premix_sum,
        router_sum,
        shared_sums[1].astype(f32),
        shared_sums[0].astype(f32),
        fanout_grad,
        funnel_grad,
    )


def solution(mesh):
    placed = (
        P(("dp", "row"), "col"),
        P(("dp", "row"), "col"),
        P(("dp", "row"), None),
        P("dp"),
        P("col"),
        P("col", "row"),
        P("col", "row"),
        P(),
        P(None, "row"),
        P("row", "col"),
        P("col"),
        P("col", None),
        P(None, "col", "row"),
        P("row", "col"),
        P(("dp", "row"), None, None, "col"),
        P(("dp", "row"), "col", None),
    )
    squared = mesh.shape["dp"] == SQUARE and mesh.shape["row"] == ROWS
    return jax.shard_map(
        local_square if squared else local,
        mesh=mesh,
        in_specs=placed,
        out_specs=(
            P(("dp", "row"), "col"),
            P(("dp", "row"), "col"),
            P("col"),
            P("col", "row"),
            P("col", "row"),
            P(),
            P(None, "row"),
            P("row", "col"),
            P("col"),
            P("col", None),
            P(None, "col", "row"),
            P("row", "col"),
            P(("dp", "row"), None, None, "col"),
            P(("dp", "row"), "col", None),
        ),
        check_vma=False,
    )
```

```python
import jax
import jax.numpy as jnp
import numpy as np
from jax import lax
from jax.experimental import pallas as pl
from jax.experimental.pallas import tpu as pltpu
from jax.sharding import PartitionSpec as P

D = 2048
NOPE = 128
ROPE = 64
HEADV = 128
RANK = 512
TOP = 6


epsilon = 1e-06
masked_score = -1e30
f32 = jnp.float32
bf16 = jnp.bfloat16


def after(value, *earlier):
    return lax.optimization_barrier((value,) + earlier)[0]


def silu_slope(values):
    sigmoid = jax.nn.sigmoid(values)
    return sigmoid * (1.0 + values * (1.0 - sigmoid))


def rotation(positions, rope_width):
    half_width = rope_width // 2
    frequency = 10000.0 ** (-jnp.arange(half_width, dtype=jnp.float32) * 2.0 / rope_width)
    angles = positions.astype(jnp.float32)[:, None] * frequency[None, :]
    return (jnp.cos(angles), jnp.sin(angles))


def rotate(values, cosine, sine_table, direction):
    half_width = values.shape[-1] // 2
    first_half = values[..., :half_width]
    second_half = values[..., half_width:]
    return jnp.concatenate(
        [
            first_half * cosine - direction * second_half * sine_table,
            second_half * cosine + direction * first_half * sine_table,
        ],
        axis=-1,
    )


def dot(left, right):
    return jnp.dot(left, right, preferred_element_type=f32)


def dot_tn(left, right):
    return lax.dot_general(left, right, (((0,), (0,)), ((), ())), preferred_element_type=f32)


def dot_nt(left, right):
    return lax.dot_general(left, right, (((1,), (1,)), ((), ())), preferred_element_type=f32)


def col_totals(values):
    return lax.psum(values, "col")


def row_gather(values):
    return lax.all_gather(values, "row", axis=0, tiled=True)


def col_gather(values, axis=0):
    return lax.all_gather(values, "col", axis=axis, tiled=True)


def col_scatter(values, axis=0):
    return lax.psum_scatter(values, "col", scatter_dimension=axis, tiled=True)


def row_scatter(values):
    return lax.psum_scatter(
        values.astype(bf16), "row", scatter_dimension=0, tiled=True
    ).astype(f32)


def send_out(parts):
    count = len(parts)
    return [parts[0]] + [
        lax.ppermute(parts[k], "dp", [(i, (i + k) % count) for i in range(count)])
        for k in range(1, count)
    ]


def send_back(parts):
    count = len(parts)
    return [parts[0]] + [
        lax.ppermute(parts[k], "dp", [(i, (i - k) % count) for i in range(count)])
        for k in range(1, count)
    ]


def norm_scale(values):
    square_sum = col_totals(jnp.sum(values * values, axis=1))
    return lax.rsqrt(square_sum / D + epsilon)


def norm_back(values, row_scale, gain_vector, upstream):
    weighted = upstream * gain_vector
    inner_mean = col_totals(jnp.sum(weighted * values, axis=1)) / D
    return weighted * row_scale[:, None] - values * (row_scale**3 * inner_mean)[:, None]


MESH = pl.DeviceIdType.MESH
VMEM = pltpu.VMEM
DMA = pltpu.SemaphoreType.DMA
MIB = 1024 * 1024
ROWS = 4
SQUARE = 4
COLS = 2
SPLIT = 2


def nn(left, right):
    return lax.dot_general(left, right, (((1,), (0,)), ((), ())), preferred_element_type=f32)


def tn(left, right):
    return lax.dot_general(left, right, (((0,), (0,)), ((), ())), preferred_element_type=f32)


def nt(left, right):
    return lax.dot_general(left, right, (((1,), (1,)), ((), ())), preferred_element_type=f32)


def block_at(row, turn):
    swapped = jnp.where(turn < 2, 1 - turn, turn)
    inner = jnp.logical_or(row == 1, row == 2)
    near = jnp.where(inner, swapped, turn)
    return jnp.where(row < 2, near, ROWS - 1 - near)


def partner(place, step):
    across, along = lax.rem(place, 2), lax.div(place, 2)
    across = lax.rem(across + step % 2, 2)
    along = lax.rem(along + step // 2, 2)
    return along * 2 + across


def remote(source, target, sent, arrived, where):
    return pltpu.make_async_remote_copy(
        src_ref=source,
        dst_ref=target,
        send_sem=sent,
        recv_sem=arrived,
        device_id=where,
        device_id_type=MESH,
    )


def greet(row, place, col, line=False, square=True):
    barrier = pltpu.get_barrier_semaphore()
    met = 1
    if line:
        for step in range(1, ROWS):
            pl.semaphore_signal(
                barrier,
                inc=1,
                device_id={"row": lax.rem(row + step, ROWS)},
                device_id_type=MESH,
            )
        met = met + ROWS - 1
    else:

        @pl.when(row > 0)
        def _():
            pl.semaphore_signal(barrier, inc=1, device_id={"row": row - 1}, device_id_type=MESH)

        @pl.when(row < ROWS - 1)
        def _():
            pl.semaphore_signal(barrier, inc=1, device_id={"row": row + 1}, device_id_type=MESH)

        met = met + (row > 0).astype(jnp.int32) + (row < ROWS - 1).astype(jnp.int32)
    if square:
        for step in range(1, SQUARE):
            pl.semaphore_signal(
                barrier, inc=1, device_id={"dp": partner(place, step)}, device_id_type=MESH
            )
        met = met + SQUARE - 1
    pl.semaphore_signal(barrier, inc=1, device_id={"col": 1 - col}, device_id_type=MESH)
    pl.semaphore_wait(barrier, met)


class Line:
    def __init__(self, row, buffer, sent, arrived):
        self.row, self.buffer, self.sent, self.arrived = row, buffer, sent, arrived

    def copy(self, block, way):
        to = self.row + 1 if way == 0 else self.row - 1
        here = self.buffer.at[block]
        return remote(here, here, self.sent.at[block, way], self.arrived.at[block], {"row": to})

    def each(self, block, act):
        @pl.when(jnp.logical_and(block <= self.row, self.row < ROWS - 1))
        def _():
            act(self.copy(block, 0))

        @pl.when(jnp.logical_and(block >= self.row, self.row > 0))
        def _():
            act(self.copy(block, 1))

    def wait(self, block):
        self.copy(block, 0).wait_recv()

    def pass_on(self, block):
        self.each(block, lambda copy: copy.start())

    def finish(self):
        def one(block, carried):
            self.each(block, lambda copy: copy.wait_send())
            return carried

        lax.fori_loop(0, ROWS, one, 0)


class SquareRest:
    def __init__(self, place, kept, got, middle, second, result, sent, arrived):
        self.x, self.y = lax.rem(place, 2), lax.div(place, 2)
        self.to_x, self.to_y = {"dp": partner(place, 1)}, {"dp": partner(place, 2)}
        self.kept, self.got = kept, got
        self.middle, self.second, self.result = middle, second, result
        self.sent, self.arrived = sent, arrived

    def copies(self, phase):
        x, y = self.x, self.y
        if phase == 1:
            plan = (
                (self.middle.at[0], self.second.at[0], self.to_y),
                (self.middle.at[1], self.second.at[1], self.to_x),
            )
        elif phase == 2:
            one, two = self.result.at[2 * x + y], self.result.at[4 + 2 * y + x]
            plan = ((one, one, self.to_y), (two, two, self.to_x))
        else:
            one, two = self.result.at[pl.ds(2 * x, 2)], self.result.at[pl.ds(4 + 2 * y, 2)]
            plan = ((one, one, self.to_x), (two, two, self.to_y))
        return [
            remote(source, target, self.sent.at[2 * phase + i], self.arrived.at[2 * phase + i], to)
            for i, (source, target, to) in enumerate(plan)
        ]

    def sum_of(self, half, side):
        wide = self.middle.shape[3]
        lanes = pl.ds(pl.multiple_of(side * wide, 128), wide)
        return self.kept[half, :, :, lanes].astype(f32) + self.got[half, :, :, lanes].astype(f32)

    def run(self, phase):
        x, y = self.x, self.y
        if phase > 1:
            for copy in self.copies(phase - 1):
                copy.wait_recv()
        if phase == 1:
            self.middle[0] = self.sum_of(0, 1 - y).astype(bf16)
            self.middle[1] = self.sum_of(1, 1 - x).astype(bf16)
        if phase == 2:
            self.result[2 * x + y] = (self.sum_of(0, y) + self.second[0].astype(f32)).astype(bf16)
            self.result[4 + 2 * y + x] = (
                self.sum_of(1, x) + self.second[1].astype(f32)
            ).astype(bf16)
        if phase < 4:
            for copy in self.copies(phase):
                copy.start()

    def finish(self):
        for phase in (1, 2, 3):
            for copy in self.copies(phase):
                copy.wait_send()


class SumLine:
    def __init__(self, row, part, leaving, coming, sent, arrived):
        self.row, self.part, self.leaving, self.coming = row, part, leaving, coming
        self.sent, self.arrived = sent, arrived
        self.lines = part.shape[1] // SPLIT

    def piece(self, index):
        return pl.ds(index * self.lines, self.lines)

    def copy(self, block, index, way):
        return remote(
            self.leaving.at[block, self.piece(index)],
            self.coming.at[way, block, self.piece(index)],
            self.sent.at[block, index],
            self.arrived.at[way, block, index],
            {"row": self.row + 1 - 2 * way},
        )

    def send(self, block, index):
        @pl.when(block > self.row)
        def _():
            self.copy(block, index, 0).start()

        @pl.when(block < self.row)
        def _():
            self.copy(block, index, 1).start()

    def chained(self, block):
        return jnp.logical_or(
            jnp.logical_and(block > self.row, self.row > 0),
            jnp.logical_and(block < self.row, self.row < ROWS - 1),
        )

    def begin(self, block):
        @pl.when(jnp.logical_and(block != self.row, jnp.logical_not(self.chained(block))))
        def _():
            self.leaving[block] = self.part[block].astype(bf16)
            for index in range(SPLIT):
                self.send(block, index)

    def pass_on(self, block):
        @pl.when(self.chained(block))
        def _():
            way = (block < self.row).astype(jnp.int32)
            for index in range(SPLIT):
                self.copy(block, index, way).wait_recv()
                piece = self.piece(index)
                self.leaving[block, piece] = (
                    self.part[block, piece] + self.coming[way, block, piece].astype(f32)
                ).astype(bf16)
                self.send(block, index)

    def total(self, target):
        target[...] = self.part[self.row]
        for way, there in ((0, self.row > 0), (1, self.row < ROWS - 1)):

            @pl.when(there)
            def _(way=way):
                for index in range(SPLIT):
                    self.copy(self.row, index, way).wait_recv()
                    target[self.piece(index)] += self.coming[
                        way, self.row, self.piece(index)
                    ].astype(f32)

    def finish(self):
        def one(block, carried):
            @pl.when(block != self.row)
            def _():
                for index in range(SPLIT):
                    self.copy(block, index, 0).wait_send()

            return carried

        lax.fori_loop(0, ROWS, one, 0)


def swap_halves(values):
    lanes = values.shape[1]
    lane = lax.broadcasted_iota(jnp.int32, values.shape, 1)
    return jnp.where(
        lane % ROPE < ROPE // 2,
        pltpu.roll(values, lanes - ROPE // 2, 1),
        pltpu.roll(values, ROPE // 2, 1),
    )


def attend_kernel(
    act_ref,
    scaling_ref,
    compress_ref,
    rescale_ref,
    premix_ref,
    cos_ref,
    sin_ref,
    key_cos_ref,
    key_sin_ref,
    mark_ref,
    cot_ref,
    route_ref,
    router_ref,
    queries_ref,
    expand_ref,
    combine_ref,
    one_out,
    query_out,
    key_out,
    value_out,
    probs_out,
    latent_out,
    normed_latent_out,
    attended_out,
    compress_out,
    cot_out,
    pick_out,
    back_out,
    rows_out,
    residual_ref,
    two_ref,
    scale_one_ref,
    scale_two_ref,
    router_all,
    one_ref,
    query_ref,
    key_ref,
    value_ref,
    probs_ref,
    latent_ref,
    normed_latent_ref,
    attended_ref,
    compress_all,
    cot_all,
    pick_ref,
    back_ref,
    rows_ref,
    queries,
    expand,
    combine,
    stat_to,
    stat_from,
    query_own,
    query_to,
    query_from,
    latent_to,
    latent_from,
    part,
    leaving,
    coming,
    routes,
    staged,
    marks,
    load_sem,
    store_sem,
    rows_sem,
    stat_sent,
    stat_arrived,
    line_sent,
    line_arrived,
    comp_sent,
    comp_arrived,
    comp_out_sent,
    comp_out_arrived,
    query_sent,
    query_arrived,
    latent_sent,
    latent_arrived,
    att_sent,
    att_arrived,
    sum_sent,
    sum_arrived,
    cot_sent,
    cot_arrived,
    route_sent,
    route_arrived,
    out_sent,
    out_arrived,
    pair_sent,
    pair_arrived,
    router_sent,
    router_arrived,
):
    place, row, col = lax.axis_index("dp"), lax.axis_index("row"), lax.axis_index("col")
    other = 1 - col
    inner = jnp.logical_and(row > 0, row < ROWS - 1)
    sibling = {"col": other}
    tokens, width = act_ref.shape
    slots = pick_ref.shape[1] // SQUARE
    mine = query_own.shape[2]
    sliced = compress_ref.shape[0]
    quarter = width // SQUARE
    score_scale = (NOPE + ROPE) ** (-0.5)
    loads = [
        pltpu.make_async_copy(source, target, load_sem.at[i])
        for i, (source, target) in enumerate(
            [(queries_ref, queries), (expand_ref, expand), (combine_ref, combine)]
        )
    ]
    for load in loads:
        load.start()
    stores = [
        pltpu.make_async_copy(source, target, store_sem.at[i])
        for i, (source, target) in enumerate(
            [
                (one_ref, one_out),
                (query_ref, query_out),
                (key_ref, key_out),
                (value_ref, value_out),
                (latent_ref, latent_out),
                (normed_latent_ref, normed_latent_out),
                (compress_all, compress_out),
                (probs_ref, probs_out),
                (attended_ref, attended_out),
                (cot_all, cot_out),
                (pick_ref, pick_out),
                (back_ref, back_out),
            ]
        )
    ]

    def rows_store(block):
        return pltpu.make_async_copy(
            rows_ref.at[:, block], rows_out.at[:, block], rows_sem.at[block]
        )

    def stat_copy(index):
        return remote(
            stat_to.at[index],
            stat_from.at[index],
            stat_sent.at[index],
            stat_arrived.at[index],
            sibling,
        )

    def scale_of(values, index):
        own = jnp.sum(values * values, axis=1, keepdims=True)
        stat_to[index] = jnp.broadcast_to(own, (tokens, 128))
        stat_copy(index).start()
        stat_copy(index).wait_recv()
        return lax.rsqrt((own + stat_from[index][:, 0:1]) / D + epsilon)

    def comp_piece(block, member):
        return compress_all.at[
            pl.ds(pl.multiple_of(block * sliced, 16), sliced),
            pl.ds(pl.multiple_of(member * quarter, 128), quarter),
        ]

    def comp_copy(block, way):
        here = comp_piece(block, place)
        return remote(
            here,
            here,
            comp_sent.at[block, way],
            comp_arrived.at[block],
            {"row": row + 1 - 2 * way},
        )

    def comp_each(block, act):
        @pl.when(jnp.logical_and(block <= row, row < ROWS - 1))
        def _():
            act(comp_copy(block, 0))

        @pl.when(jnp.logical_and(block >= row, row > 0))
        def _():
            act(comp_copy(block, 1))

    def comp_out(block, step, member):
        here = comp_piece(block, member)
        return remote(
            here,
            here,
            comp_out_sent.at[block, step],
            comp_out_arrived.at[block, step],
            {"dp": partner(place, step)},
        )

    line = Line(row, one_ref, line_sent, line_arrived)
    cot_line = Line(row, cot_all, cot_sent, cot_arrived)
    route_line = Line(row, routes, route_sent, route_arrived)
    sums = SumLine(row, part, leaving, coming, sum_sent, sum_arrived)

    greet(row, place, col)
    compress_all[pl.ds(pl.multiple_of(row * sliced, 16), sliced)] = compress_ref[...]
    compress_all[ROWS * sliced :] = jnp.zeros(
        (compress_all.shape[0] - ROWS * sliced, width), bf16
    )
    comp_each(row, lambda copy: copy.start())

    def router_copy(half):
        here = router_all.at[:, pl.ds(pl.multiple_of(half * width, width), width)]
        return remote(here, here, router_sent.at[0], router_arrived.at[0], sibling)

    router_all[:, pl.ds(pl.multiple_of(col * width, width), width)] = router_ref[...]
    inputs = act_ref[...].astype(f32)
    scale_one = scale_of(inputs, 0)
    scale_one_ref[...] = scale_one
    one_ref[pl.ds(row, 1)] = (
        (inputs * scale_one * scaling_ref[...]).astype(bf16).reshape(1, tokens, width)
    )
    cot_all[pl.ds(row, 1)] = cot_ref[...].reshape(1, tokens, width)
    routes[pl.ds(row, 1)] = route_ref[...].reshape((1,) + route_ref.shape)
    line.pass_on(row)
    router_copy(col).start()

    @pl.when(jnp.logical_not(inner))
    def _():
        route_line.pass_on(row)
        cot_line.pass_on(row)

    for block in range(ROWS):
        mark = mark_ref[:, block * tokens : (block + 1) * tokens].astype(f32)
        marks[block] = jnp.broadcast_to(mark, (8, tokens)).T
    loads[0].wait()

    def query_copy(block):
        return remote(
            query_to.at[block],
            query_from.at[block],
            query_sent.at[block],
            query_arrived.at[block],
            sibling,
        )

    def latent_copy(block):
        return remote(
            latent_to.at[block],
            latent_from.at[block],
            latent_sent.at[block],
            latent_arrived.at[block],
            sibling,
        )

    def att_copy(block, half):
        here = attended_ref.at[block, :, pl.ds(pl.multiple_of(half * 2 * HEADV, 128), 2 * HEADV)]
        return remote(here, here, att_sent.at[block], att_arrived.at[block], sibling)

    def gather(step, carried):
        block = block_at(row, step)

        @pl.when(step > 0)
        def _():
            comp_copy(block, 0).wait_recv()
            comp_each(block, lambda copy: copy.start())
            for shift in (3, 2, 1):
                comp_out(block, shift, place).start()
            line.wait(block)
            line.pass_on(block)

        tokens_here = one_ref[block]
        query_to[block] = nn(
            tokens_here, queries[:, pl.ds(pl.multiple_of(other * mine, 128), mine)]
        ).astype(bf16)
        query_copy(block).start()
        query_own[block] = nn(tokens_here, queries[:, pl.ds(pl.multiple_of(col * mine, 128), mine)])
        return carried

    lax.fori_loop(0, ROWS, gather, 0)

    @pl.when(inner)
    def _():
        route_line.pass_on(row)
        cot_line.pass_on(row)

    def relay(step):
        block = block_at(row, step)
        route_line.wait(block)
        route_line.pass_on(block)
        cot_line.wait(block)
        cot_line.pass_on(block)

    def out_copy(block, step):
        piece = pl.ds(step * slots, slots)
        return remote(
            staged.at[block, piece],
            rows_ref.at[col, block, piece],
            out_sent.at[block, step],
            out_arrived.at[block, step],
            {"dp": partner(place, step)},
        )

    def pair_copy(block, half):
        here = rows_ref.at[half, block]
        return remote(here, here, pair_sent.at[block], pair_arrived.at[block], sibling)

    def take(step):
        block = block_at(row, step)

        @pl.when(jnp.logical_and(step > 0, jnp.logical_not(inner)))
        def _():
            relay(step)

        before = (
            lax.broadcasted_iota(jnp.int32, (tokens, tokens), 0)
            < lax.broadcasted_iota(jnp.int32, (tokens, tokens), 1)
        ).astype(bf16)
        routing = routes[block]
        chosen = []
        for shift in range(SQUARE):
            expert = partner(place, shift) * ROWS + row
            hit = (routing == expert).astype(f32)
            chosen.append(jnp.max(hit, axis=0, keepdims=True))
        goes = jnp.concatenate(chosen + chosen, axis=0)
        rank = nn(goes.astype(bf16), before)
        for shift in range(SQUARE):
            slot = lax.broadcasted_iota(jnp.int32, (slots, tokens), 0).astype(f32)
            here = jnp.logical_and(slot == rank[shift : shift + 1], goes[shift : shift + 1] > 0.5)
            pick = here.astype(f32)
            pick_ref[block, shift * slots : (shift + 1) * slots] = pick.astype(bf16)
            back_ref[block, :, shift * slots : (shift + 1) * slots] = pick.T.astype(bf16)
        staged[block] = nn(pick_ref[block], cot_all[block]).astype(bf16)
        for shift in (3, 2, 1):
            out_copy(block, shift).start()
        rows_ref[col, block, 0:slots] = staged[block, 0:slots]

    def forward(step):
        block = block_at(row, step)
        for shift in range(1, SQUARE):
            out_copy(block, shift).wait_recv()
        pair_copy(block, col).start()

    def comp_arrive(block, carried):
        @pl.when(block != row)
        def _():
            for shift in range(1, SQUARE):
                comp_out(block, shift, partner(place, shift)).wait_recv()

        return carried

    lax.fori_loop(0, ROWS, comp_arrive, 0)

    def latents(block, carried):
        value = nt(one_ref[block], compress_all[...])
        latent_to[block] = value
        latent_copy(block).start()
        latent_ref[block] = value
        return carried

    lax.fori_loop(0, ROWS, latents, 0)
    take(0)

    @pl.when(inner)
    def _():
        relay(1)
        relay(2)

    loads[1].wait()

    def keys(block, carried):
        latent_copy(block).wait_recv()
        latent = latent_ref[block] + latent_from[block]
        latent_ref[block] = latent
        plain = latent[:, :RANK]
        scale = lax.rsqrt(jnp.mean(plain * plain, axis=1, keepdims=True) + epsilon)
        normed = (plain * scale * rescale_ref[...]).astype(bf16)
        normed_latent_ref[block] = normed
        own = 2 * (NOPE + HEADV)
        expanded = nn(normed, expand[:, pl.ds(pl.multiple_of(col * own, 128), own)])
        rope = latent[:, RANK:]
        rope = rope * key_cos_ref[block] + swap_halves(rope) * key_sin_ref[block]
        first = jnp.concatenate([expanded[:, :NOPE], rope], axis=1)
        second = jnp.concatenate([expanded[:, 2 * NOPE : 3 * NOPE], rope], axis=1)
        key_ref[0, block] = first.astype(bf16)
        key_ref[1, block] = pltpu.roll(second, ROPE, 1).astype(bf16)
        value_ref[0, block] = expanded[:, NOPE : 2 * NOPE].astype(bf16)
        value_ref[1, block] = expanded[:, 3 * NOPE :].astype(bf16)
        query_copy(block).wait_recv()
        query = query_own[block] + query_from[block].astype(f32)
        query_ref[block] = (
            query * cos_ref[block] + swap_halves(query) * sin_ref[block]
        ).astype(bf16)
        return carried

    lax.fori_loop(0, ROWS, keys, 0)
    for index in range(7):
        stores[index].start()
    seq = ROWS * tokens
    lanes = NOPE + 2 * ROPE

    def attend(turn, carried):
        block = block_at(row, ROWS - 1 - turn)
        visible = mark_ref[...].astype(f32) <= marks[block][:, 0:1]
        for head in range(2):
            query = query_ref[block, :, head * NOPE : head * NOPE + lanes]
            scores = nt(query, key_ref[head].reshape(seq, lanes)) * score_scale
            scores = jnp.where(visible, scores, masked_score)
            weight = jnp.exp(scores - jnp.max(scores, axis=1, keepdims=True))
            probs = (weight / jnp.sum(weight, axis=1, keepdims=True)).astype(bf16)
            probs_ref[head, block] = probs
            result = nn(probs, value_ref[head].reshape(seq, HEADV)).astype(bf16)
            at = pl.multiple_of((col * 2 + head) * HEADV, 128)
            attended_ref[block, :, pl.ds(at, HEADV)] = result
        att_copy(block, col).start()

        @pl.when(jnp.logical_and(turn == 0, inner))
        def _():
            relay(3)

        @pl.when(turn > 0)
        def _():
            mix(turn - 1)
            take(turn)

        return carried

    def mix(turn):
        block = block_at(row, ROWS - 1 - turn)
        att_copy(block, other).wait_recv()
        part[block] = nn(attended_ref[block], combine[...])
        sums.begin(block)

    loads[2].wait()
    lax.fori_loop(0, ROWS, attend, 0)
    mix(ROWS - 1)
    for index in range(7, 12):
        stores[index].start()

    def hand_on(turn, carried):
        sums.pass_on(block_at(row, jnp.where(turn == 0, 3, turn)))
        forward(turn)
        return carried

    lax.fori_loop(0, 3, hand_on, 0)
    sums.total(residual_ref)
    residual = residual_ref[...] + inputs
    residual_ref[...] = residual
    scale_two = scale_of(residual, 1)
    scale_two_ref[...] = scale_two
    two_ref[...] = (residual * scale_two * premix_ref[...]).astype(bf16)
    forward(3)

    def ended(block, carried):
        pair_copy(block, other).wait_recv()
        rows_store(block).start()
        pair_copy(block, col).wait_send()
        for shift in range(1, SQUARE):
            out_copy(block, shift).wait_send()

            @pl.when(block != row)
            def _(shift=shift):
                comp_out(block, shift, place).wait_send()

        comp_each(block, lambda copy: copy.wait_send())
        query_copy(block).wait_send()
        latent_copy(block).wait_send()
        att_copy(block, col).wait_send()
        return carried

    lax.fori_loop(0, ROWS, ended, 0)
    for store in stores:
        store.wait()

    def stored(block, carried):
        rows_store(block).wait()
        return carried

    lax.fori_loop(0, ROWS, stored, 0)
    router_copy(other).wait_recv()
    router_copy(col).wait_send()
    stat_copy(0).wait_send()
    stat_copy(1).wait_send()
    sums.finish()
    line.finish()
    cot_line.finish()
    route_line.finish()


def turning_tables(length):
    half = ROPE // 2
    frequency = 10000.0 ** (-np.arange(half, dtype=np.float32) * 2.0 / ROPE)
    angles = np.arange(length, dtype=np.float32)[:, None] * frequency[None, :].astype(np.float32)
    cosine, sine = np.cos(angles), np.sin(angles)
    cosine, sine = np.concatenate([cosine, cosine], 1), np.concatenate([-sine, sine], 1)
    ones, zeros = np.ones((length, NOPE)), np.zeros((length, NOPE))
    gap = np.zeros((length, 128 - ROPE))
    tables = (
        np.concatenate([ones, cosine, ones, cosine], 1),
        np.concatenate([zeros, sine, zeros, sine], 1),
        np.concatenate([cosine, gap], 1),
        np.concatenate([sine, gap], 1),
    )
    return [
        jnp.asarray(table.reshape(ROWS, length // ROWS, -1).astype(np.float32))
        for table in tables
    ]


def pair_sems():
    return [DMA((ROWS,)), DMA((ROWS,))]


def line_sems():
    return [DMA((ROWS, 2)), DMA((ROWS,))]


def square_sems():
    return [DMA((ROWS, SQUARE)), DMA((ROWS, SQUARE))]


def sum_sems():
    return [DMA((ROWS, SPLIT)), DMA((2, ROWS, SPLIT))]


def run_attention(
    activations,
    scaling,
    queries,
    compress,
    rescale,
    expand,
    combine,
    premix,
    segments,
    cotangent,
    routing,
    router,
    tables,
    slots,
):
    tokens, width = activations.shape
    seq = ROWS * tokens
    mine = queries.shape[1] // COLS
    sliced = compress.shape[1]
    latent_width = RANK + 128
    picked = SQUARE * slots
    lanes = NOPE + 2 * ROPE
    routes = routing.T
    whole = pl.BlockSpec(memory_space=VMEM)
    far = pl.BlockSpec(memory_space=pl.ANY)

    def shape(*dims, dtype=bf16):
        return jax.ShapeDtypeStruct(dims, dtype)

    kept = [
        shape(ROWS, tokens, width),
        shape(ROWS, tokens, mine),
        shape(2, ROWS, tokens, lanes),
        shape(2, ROWS, tokens, HEADV),
        shape(2, ROWS, tokens, seq),
        shape(ROWS, tokens, latent_width, dtype=f32),
        shape(ROWS, tokens, RANK),
        shape(ROWS, tokens, COLS * 2 * HEADV),
        shape(latent_width, width),
        shape(ROWS, tokens, width),
        shape(ROWS, picked, tokens),
        shape(ROWS, tokens, picked),
        shape(COLS, ROWS, picked, width),
    ]
    return pl.pallas_call(
        attend_kernel,
        name="attend",
        out_shape=(
            *kept,
            shape(tokens, width, dtype=f32),
            shape(tokens, width),
            shape(tokens, 1, dtype=f32),
            shape(tokens, 1, dtype=f32),
            shape(router.shape[1], COLS * width),
        ),
        in_specs=[whole] * 13 + [far] * 3,
        out_specs=(far,) * 13 + (whole,) * 5,
        scratch_shapes=[
            *[VMEM(value.shape, value.dtype) for value in kept],
            VMEM(queries.shape, bf16),
            VMEM(expand.shape, bf16),
            VMEM(combine.shape, bf16),
            VMEM((2, tokens, 128), f32),
            VMEM((2, tokens, 128), f32),
            VMEM((ROWS, tokens, mine), f32),
            VMEM((ROWS, tokens, mine), bf16),
            VMEM((ROWS, tokens, mine), bf16),
            VMEM((ROWS, tokens, latent_width), f32),
            VMEM((ROWS, tokens, latent_width), f32),
            VMEM((ROWS, tokens, width), f32),
            VMEM((ROWS, tokens, width), bf16),
            VMEM((2, ROWS, tokens, width), bf16),
            VMEM((ROWS,) + routes.shape, jnp.int32),
            VMEM((ROWS, picked, width), bf16),
            VMEM((ROWS, tokens, 8), f32),
            DMA((3,)),
            DMA((12,)),
            DMA((ROWS,)),
            DMA((2,)),
            DMA((2,)),
            *line_sems(),
            *line_sems(),
            *square_sems(),
            *pair_sems(),
            *pair_sems(),
            *pair_sems(),
            *sum_sems(),
            *line_sems(),
            *line_sems(),
            *square_sems(),
            *pair_sems(),
            DMA((1,)),
            DMA((1,)),
        ],
        compiler_params=pltpu.CompilerParams(
            collective_id=1, has_side_effects=True, vmem_limit_bytes=56 * MIB
        ),
        cost_estimate=pl.CostEstimate(
            flops=40 * 1024**3, bytes_accessed=32 * MIB, transcendentals=0
        ),
    )(
        activations,
        scaling.reshape(1, width),
        compress.T,
        rescale.reshape(1, RANK),
        premix.reshape(1, width),
        *tables,
        segments.reshape(1, seq),
        cotangent,
        routes,
        router.T,
        queries,
        expand,
        combine,
    )


def attend_back_kernel(
    normed_grad_ref,
    residual_ref,
    scale_two_ref,
    premix_ref,
    cot_ref,
    act_ref,
    scale_one_ref,
    scaling_ref,
    rescale_ref,
    combine_far,
    query_far,
    key_far,
    value_far,
    probs_far,
    cos_far,
    sin_far,
    queries_far,
    expand_far,
    latent_far,
    key_cos_far,
    key_sin_far,
    compress_far,
    one_far,
    kept_far,
    got_x_far,
    got_y_far,
    input_grad_ref,
    branch_ref,
    query_grad_ref,
    expanded_ref,
    own_latent_ref,
    scaling_rows,
    rescale_rows,
    shared_sum,
    combine,
    query_ref,
    key_ref,
    value_ref,
    probs_ref,
    cos_ref,
    sin_ref,
    queries,
    expand,
    latent_ref,
    key_cos_ref,
    key_sin_ref,
    compress_all,
    one_ref,
    kept,
    got,
    middle,
    second,
    result,
    stat_to,
    stat_from,
    grad_own,
    grad_to,
    grad_from,
    key_grad,
    value_grad,
    latent_own,
    latent_to,
    latent_from,
    turned,
    turned_from,
    part,
    leaving,
    coming,
    total,
    load_sem,
    stat_sent,
    stat_arrived,
    line_sent,
    line_arrived,
    grad_sent,
    grad_arrived,
    query_sent,
    query_arrived,
    latent_sent,
    latent_arrived,
    turned_sent,
    turned_arrived,
    own_sent,
    own_arrived,
    sum_sent,
    sum_arrived,
    rest_sent,
    rest_arrived,
    rest_sem,
):
    place, row, col = lax.axis_index("dp"), lax.axis_index("row"), lax.axis_index("col")
    other = 1 - col
    sibling = {"col": other}
    tokens, width = act_ref.shape
    seq = ROWS * tokens
    mine = query_ref.shape[2]
    lanes = key_ref.shape[3]
    both = 2 * HEADV
    sliced = own_latent_ref.shape[0]
    score_scale = (NOPE + ROPE) ** (-0.5)
    loads = [
        pltpu.make_async_copy(source, target, load_sem.at[i])
        for i, (source, target) in enumerate(
            [
                (combine_far, combine),
                (query_far, query_ref),
                (key_far, key_ref),
                (value_far, value_ref),
                (probs_far, probs_ref),
                (cos_far, cos_ref),
                (sin_far, sin_ref),
                (queries_far, queries),
                (expand_far, expand),
                (latent_far, latent_ref),
                (key_cos_far, key_cos_ref),
                (key_sin_far, key_sin_ref),
                (compress_far, compress_all),
                (one_far, one_ref),
                (kept_far, kept),
                (got_x_far, got.at[0]),
                (got_y_far, got.at[1]),
            ]
        )
    ]
    for load in loads:
        load.start()
    line = Line(row, branch_ref, line_sent, line_arrived)
    sums = SumLine(row, part, leaving, coming, sum_sent, sum_arrived)
    greet(row, place, col, line=True)

    def stat_copy(index):
        return remote(
            stat_to.at[index],
            stat_from.at[index],
            stat_sent.at[index],
            stat_arrived.at[index],
            sibling,
        )

    def norm_grad(values, scale, gain, upstream, index):
        weighted = upstream * gain
        own = jnp.sum(weighted * values, axis=1, keepdims=True)
        stat_to[index] = jnp.broadcast_to(own, (tokens, 128))
        stat_copy(index).start()
        stat_copy(index).wait_recv()
        inner = (own + stat_from[index][:, 0:1]) / D
        return weighted * scale - values * (scale * scale * scale * inner)

    residual_grad = cot_ref[...].astype(f32) + norm_grad(
        residual_ref[...], scale_two_ref[...], premix_ref[...], normed_grad_ref[...], 0
    )
    input_grad_ref[...] = residual_grad
    branch_ref[pl.ds(row, 1)] = residual_grad.astype(bf16).reshape(1, tokens, width)
    line.pass_on(row)
    key_grad[...] = jnp.zeros_like(key_grad)
    value_grad[...] = jnp.zeros_like(value_grad)
    scaling_rows[...] = jnp.zeros_like(scaling_rows)
    rescale_rows[...] = jnp.zeros_like(rescale_rows)

    rest = SquareRest(place, kept, got, middle, second, result, rest_sent, rest_arrived)

    def grad_copy(block):
        return remote(
            grad_to.at[block],
            grad_from.at[block],
            grad_sent.at[block],
            grad_arrived.at[block],
            sibling,
        )

    def query_copy(block, half):
        here = query_grad_ref.at[block, :, pl.ds(pl.multiple_of(half * mine, 128), mine)]
        return remote(here, here, query_sent.at[block], query_arrived.at[block], sibling)

    def latent_copy(block):
        return remote(
            latent_to.at[block],
            latent_from.at[block],
            latent_sent.at[block],
            latent_arrived.at[block],
            sibling,
        )

    def arrive(step):
        block = block_at(row, step)

        @pl.when(step > 0)
        def _():
            line.wait(block)
            line.pass_on(block)

        @pl.when(step == 0)
        def _():
            for load in loads[14:]:
                load.wait()
            rest.run(1)
            loads[0].wait()

        grads = branch_ref[block]
        grad_to[block] = nt(
            grads, combine[pl.ds(pl.multiple_of(other * both, 16), both)]
        ).astype(bf16)
        grad_copy(block).start()
        grad_own[block] = nt(grads, combine[pl.ds(pl.multiple_of(col * both, 16), both)])

    def heads(step):
        block = block_at(row, step)

        @pl.when(step == 0)
        def _():
            for load in loads[1:7]:
                load.wait()

        grad_copy(block).wait_recv()
        grads = (grad_own[block] + grad_from[block].astype(f32)).astype(bf16)
        pieces = []
        for head in range(2):
            upstream = grads[:, head * HEADV : (head + 1) * HEADV]
            query = query_ref[block, :, head * NOPE : head * NOPE + lanes]
            probs = probs_ref[head, block]
            weight = probs.astype(f32)
            probs_back = nt(upstream, value_ref[head].reshape(seq, HEADV))
            inner = jnp.sum(weight * probs_back, axis=1, keepdims=True)
            score_grad = (weight * (probs_back - inner)).astype(bf16)
            pieces.append(nn(score_grad, key_ref[head].reshape(seq, lanes)) * score_scale)
            key_grad[head] += tn(score_grad, query)
            value_grad[head] += tn(probs, upstream)
        first, second = pieces
        grad = jnp.concatenate(
            [first[:, :NOPE], first[:, NOPE:] + second[:, :NOPE], second[:, NOPE:]], axis=1
        )
        grad = grad * cos_ref[block] - swap_halves(grad) * sin_ref[block]
        query_grad_ref[block, :, pl.ds(pl.multiple_of(col * mine, 128), mine)] = grad.astype(bf16)
        query_copy(block, col).start()

    def project(step):
        block = block_at(row, step)

        @pl.when(step == 0)
        def _():
            loads[7].wait()

        query_copy(block, other).wait_recv()
        part[block] = nt(query_grad_ref[block], queries[...])

    def turn(step, carried):
        for delay, stage in ((0, arrive), (1, heads), (2, project)):

            @pl.when(jnp.logical_and(step >= delay, step < delay + ROWS))
            def _(delay=delay, stage=stage):
                stage(step - delay)

        @pl.when(step == 2)
        def _():
            rest.run(2)

        return carried

    lax.fori_loop(0, ROWS + 1, turn, 0)
    for load in loads[8:14]:
        load.wait()

    def latents(turn, carried):
        block = block_at(row, ROWS - 1 - turn)
        here = pl.ds(pl.multiple_of(block * tokens, 128), tokens)
        first = key_grad[0, here] * score_scale
        second = pltpu.roll(key_grad[1, here] * score_scale, lanes - ROPE, 1)
        grad = jnp.concatenate(
            [first[:, :NOPE], value_grad[0, here], second[:, :NOPE], value_grad[1, here]], axis=1
        ).astype(bf16)
        expanded_ref[block] = grad
        own = 2 * (NOPE + HEADV)
        upstream = nt(grad, expand[:, pl.ds(pl.multiple_of(col * own, 128), own)])
        plain = latent_ref[block][:, :RANK]
        scale = lax.rsqrt(jnp.mean(plain * plain, axis=1, keepdims=True) + epsilon)
        rescale_rows[...] += jnp.sum(
            (upstream * plain * scale).reshape(tokens // 8, 8, RANK), axis=0
        )
        weighted = upstream * rescale_ref[...]
        inner = jnp.mean(weighted * plain, axis=1, keepdims=True)
        plain_grad = weighted * scale - plain * (scale * scale * scale * inner)
        rope = first[:, NOPE:] + second[:, NOPE:]
        lane = lax.broadcasted_iota(jnp.int32, rope.shape, 1)
        rope = jnp.where(lane < ROPE, rope, 0.0)
        rope = rope * key_cos_ref[block] - swap_halves(rope) * key_sin_ref[block]
        value = jnp.concatenate([plain_grad, rope], axis=1)
        latent_own[block] = value
        latent_to[block] = value.astype(bf16)
        latent_copy(block).start()
        return carried

    lax.fori_loop(0, ROWS, latents, 0)
    project(ROWS - 1)
    rest.run(3)

    def turned_piece(member):
        return turned.at[
            pl.ds(pl.multiple_of(member * sliced, 16), sliced),
            pl.ds(pl.multiple_of(col * (seq // COLS), 128), seq // COLS),
        ]

    def turned_copy(step):
        to = lax.rem(row + step, ROWS)
        return remote(
            turned_piece(to),
            turned_from.at[step],
            turned_sent.at[step],
            turned_arrived.at[step],
            {"row": to},
        )

    def mix(turn, carried):
        block = block_at(row, ROWS - 1 - turn)
        latent_copy(block).wait_recv()
        latent = latent_own[block] + latent_from[block].astype(f32)
        here = pl.ds(pl.multiple_of(block * tokens, 128), tokens)
        total_here = part[block] + nn(latent.astype(bf16), compress_all[...])
        part[block] = total_here
        sums.begin(block)
        turned[:, here] = latent.T.astype(bf16)
        scaling_rows[...] += jnp.sum(
            (total_here * one_ref[block].astype(f32)).reshape(tokens // 8, 8, width), axis=0
        )
        return carried

    lax.fori_loop(0, ROWS, mix, 0)
    for step in range(1, ROWS):
        turned_copy(step).start()

    def hand_on(turn, carried):
        sums.pass_on(block_at(row, jnp.where(turn == 0, 3, turn)))
        return carried

    lax.fori_loop(0, 3, hand_on, 0)
    for step in range(1, ROWS):
        turned_copy(step).wait_recv()
    half = pl.ds(pl.multiple_of(col * (seq // COLS), 128), seq // COLS)
    own_sum = turned[pl.ds(pl.multiple_of(row * sliced, 16), sliced), half].astype(f32)
    for step in range(1, ROWS):
        own_sum = own_sum + turned_from[step].astype(f32)
    own_latent_ref[:, half] = own_sum.astype(bf16)

    def own_copy(part_of):
        here = own_latent_ref.at[
            :, pl.ds(pl.multiple_of(part_of * (seq // COLS), 128), seq // COLS)
        ]
        return remote(here, here, own_sent.at[0], own_arrived.at[0], sibling)

    own_copy(col).start()
    sums.total(total)
    rest.run(4)
    pieces = [
        pltpu.make_async_copy(
            result.at[i], shared_sum.at[:, :, i * 128 : (i + 1) * 128], rest_sem.at[i]
        )
        for i in range(8)
    ]
    for piece in pieces:
        piece.start()
    input_grad_ref[...] += norm_grad(
        act_ref[...].astype(f32), scale_one_ref[...], scaling_ref[...], total[...], 1
    )
    own_copy(other).wait_recv()
    own_copy(col).wait_send()

    def ended(block, carried):
        grad_copy(block).wait_send()
        query_copy(block, col).wait_send()
        latent_copy(block).wait_send()
        return carried

    lax.fori_loop(0, ROWS, ended, 0)
    for step in range(1, ROWS):
        turned_copy(step).wait_send()
    stat_copy(0).wait_send()
    stat_copy(1).wait_send()
    for piece in pieces:
        piece.wait()
    rest.finish()
    sums.finish()
    line.finish()


def run_attention_back(
    normed_grad,
    residual,
    scale_two,
    premix,
    cotangent,
    activations,
    scale_one,
    scaling,
    one,
    query,
    key,
    value,
    probs,
    latent,
    rescale,
    tables,
    compress_all,
    queries,
    expand,
    combine,
    shared,
):
    tokens, width = activations.shape
    seq = ROWS * tokens
    mine = query.shape[2]
    lanes = key.shape[3]
    latent_width = latent.shape[2]
    sliced = (RANK + ROPE) // ROWS
    whole = pl.BlockSpec(memory_space=VMEM)
    far = pl.BlockSpec(memory_space=pl.ANY)

    def shape(*dims, dtype=bf16):
        return jax.ShapeDtypeStruct(dims, dtype)

    kept, got_x, got_y = shared
    piece = kept.shape[1:3] + (kept.shape[3] // 2,)
    loaded = (
        combine,
        query,
        key,
        value,
        probs,
        tables[0],
        tables[1],
        queries,
        expand,
        latent,
        tables[2],
        tables[3],
        compress_all,
        one,
    )
    return pl.pallas_call(
        attend_back_kernel,
        name="attend_back",
        out_shape=(
            shape(tokens, width, dtype=f32),
            shape(ROWS, tokens, width),
            shape(ROWS, tokens, COLS * mine),
            shape(ROWS, tokens, 2 * (NOPE + HEADV)),
            shape(sliced, seq),
            shape(8, width, dtype=f32),
            shape(8, RANK, dtype=f32),
            shape(*kept.shape[1:3], width),
        ),
        in_specs=[whole] * 9 + [far] * 17,
        out_specs=(whole,) * 7 + (far,),
        scratch_shapes=[
            *[VMEM(value.shape, value.dtype) for value in loaded],
            VMEM(kept.shape, bf16),
            VMEM(kept.shape, bf16),
            VMEM((2,) + piece, bf16),
            VMEM((2,) + piece, bf16),
            VMEM((8,) + piece, bf16),
            VMEM((2, tokens, 128), f32),
            VMEM((2, tokens, 128), f32),
            VMEM((ROWS, tokens, 2 * HEADV), f32),
            VMEM((ROWS, tokens, 2 * HEADV), bf16),
            VMEM((ROWS, tokens, 2 * HEADV), bf16),
            VMEM((2, seq, lanes), f32),
            VMEM((2, seq, HEADV), f32),
            VMEM((ROWS, tokens, latent_width), f32),
            VMEM((ROWS, tokens, latent_width), bf16),
            VMEM((ROWS, tokens, latent_width), bf16),
            VMEM((latent_width, seq), bf16),
            VMEM((ROWS, sliced, seq // COLS), bf16),
            VMEM((ROWS, tokens, width), f32),
            VMEM((ROWS, tokens, width), bf16),
            VMEM((2, ROWS, tokens, width), bf16),
            VMEM((tokens, width), f32),
            DMA((17,)),
            DMA((2,)),
            DMA((2,)),
            *line_sems(),
            *pair_sems(),
            *pair_sems(),
            *pair_sems(),
            *pair_sems(),
            *pair_sems(),
            *sum_sems(),
            DMA((8,)),
            DMA((8,)),
            DMA((8,)),
        ],
        compiler_params=pltpu.CompilerParams(
            collective_id=3, has_side_effects=True, vmem_limit_bytes=56 * MIB
        ),
        cost_estimate=pl.CostEstimate(
            flops=40 * 1024**3, bytes_accessed=32 * MIB, transcendentals=0
        ),
    )(
        normed_grad,
        residual,
        scale_two,
        premix.reshape(1, width),
        cotangent,
        activations,
        scale_one,
        scaling.reshape(1, width),
        rescale.reshape(1, RANK),
        *loaded,
        kept,
        got_x,
        got_y,
    )


def silu_pair(values):
    sigmoid = 1.0 / (1.0 + jnp.exp(-values))
    return values * sigmoid, sigmoid * (1.0 + values * (1.0 - sigmoid))


def expert_kernel(
    normed_ref,
    pick_ref,
    back_ref,
    cot_ref,
    router_ref,
    cot_rows_ref,
    fan_ref,
    fun_ref,
    wide_ref,
    narrow_ref,
    sum_ref,
    gathered_ref,
    rows_out,
    gu_out,
    hidden_out,
    shared_x,
    shared_y,
    shared_kept,
    shared_out,
    premix_ref,
    router_rows,
    reply_ref,
    fan,
    fun,
    wide,
    narrow,
    cot_rows,
    rows,
    staged,
    gu,
    hidden,
    pair_own,
    pair_to,
    pair_from,
    home,
    shared_to,
    shared_from,
    part,
    passed_to,
    passed_from,
    shared_gu,
    shared_grad,
    load_sem,
    store_sem,
    line_sent,
    line_arrived,
    out_sent,
    out_arrived,
    fwd_sent,
    fwd_arrived,
    shared_sent,
    shared_arrived,
    half_sent,
    half_arrived,
    home_sent,
    home_arrived,
    sum_sent,
    sum_arrived,
    other_sent,
    other_arrived,
    reply_sent,
    reply_arrived,
    grad_sem,
):
    place, row, col = lax.axis_index("dp"), lax.axis_index("row"), lax.axis_index("col")
    other = 1 - col
    inner = jnp.logical_and(row > 0, row < ROWS - 1)
    tokens, width = normed_ref.shape
    picked = pick_ref.shape[1]
    slots = picked // SQUARE
    experts = router_ref.shape[0]
    share = narrow.shape[0]
    loads = [
        pltpu.make_async_copy(source, target, load_sem.at[i])
        for i, (source, target) in enumerate(
            [
                (wide_ref, wide),
                (narrow_ref, narrow),
                (fan_ref, fan),
                (cot_rows_ref, cot_rows),
                (fun_ref, fun),
            ]
        )
    ]
    for load in loads:
        load.start()
    greet(row, place, col)
    gathered_ref[pl.ds(row, 1)] = normed_ref[...].reshape(1, tokens, width)
    line = Line(row, gathered_ref, line_sent, line_arrived)
    line.pass_on(row)
    premix_ref[...] = jnp.zeros_like(premix_ref)
    router_rows[...] = jnp.zeros_like(router_rows)
    sums = SumLine(row, part, passed_to, passed_from, sum_sent, sum_arrived)
    sibling = {"col": other}

    def half_lines(half):
        return pl.ds(pl.multiple_of(half * width, width), width)

    def square_copy(source, target, sent, arrived, block, step):
        piece = pl.ds(step * slots, slots)
        return remote(
            source.at[block, piece],
            target.at[block, piece],
            sent.at[block, step],
            arrived.at[block, step],
            {"dp": partner(place, step)},
        )

    def out_copy(block, step):
        return square_copy(staged, rows.at[col], out_sent, out_arrived, block, step)

    def home_copy(block, step):
        return square_copy(staged, home, home_sent, home_arrived, block, step)

    def reply_copy(block, step):
        return square_copy(staged, reply_ref, reply_sent, reply_arrived, block, step)

    def fwd_copy(block, half):
        here = rows.at[half, block]
        return remote(here, here, fwd_sent.at[block], fwd_arrived.at[block], sibling)

    def shared_copy(block):
        return remote(
            shared_to.at[block],
            shared_from.at[block],
            shared_sent.at[block],
            shared_arrived.at[block],
            sibling,
        )

    def half_copy(step):
        return remote(
            pair_to.at[lax.rem(step, 2)],
            pair_from.at[step],
            half_sent.at[step],
            half_arrived.at[step],
            sibling,
        )

    def other_copy(step):
        return remote(
            pair_to.at[lax.rem(step, 2)],
            pair_from.at[jnp.where(step == ROWS - 1, ROWS, step)],
            other_sent.at[step],
            other_arrived.at[step],
            sibling,
        )

    def stores(step):
        block = block_at(row, step)
        return [
            pltpu.make_async_copy(source, target, store_sem.at[index, step])
            for index, (source, target) in enumerate(
                [
                    (rows.at[:, block], rows_out.at[:, block]),
                    (gu.at[:, lax.rem(step, 2)], gu_out.at[:, block]),
                    (hidden.at[block], hidden_out.at[block]),
                ]
            )
        ]

    def relay(step):
        block = block_at(row, step)
        line.wait(block)
        line.pass_on(block)

    def take(step):
        block = block_at(row, step)

        @pl.when(jnp.logical_and(step > 0, jnp.logical_not(inner)))
        def _():
            relay(step)

        staged[block] = nn(pick_ref[block], gathered_ref[block]).astype(bf16)
        for shift in (3, 2, 1):
            out_copy(block, shift).start()
        rows[col, block, 0:slots] = staged[block, 0:slots]

        @pl.when(step == 0)
        def _():
            loads[0].wait()
            loads[1].wait()

        for index, value in enumerate(
            (
                nt(gathered_ref[block], wide[0]),
                nt(gathered_ref[block], wide[1]),
                nt(cot_ref[block], narrow[...]),
            )
        ):
            shared_to[block, index] = value.astype(bf16)
        shared_copy(block).start()

    def forward(step):
        block = block_at(row, step)
        for shift in range(1, SQUARE):
            out_copy(block, shift).wait_recv()
        fwd_copy(block, col).start()

    def shared(step):
        block = block_at(row, step)
        shared_copy(block).wait_recv()
        gate, up, grad = [
            shared_to[block, index].astype(f32) + shared_from[block, index].astype(f32)
            for index in range(3)
        ]
        act, slope = silu_pair(gate)
        shared_out[block] = (act * up).astype(bf16)
        gate_grad = (grad * up * slope).astype(bf16)
        up_grad = (grad * act).astype(bf16)
        shared_gu[0, block] = gate_grad
        shared_gu[1, block] = up_grad
        part[block] = nn(gate_grad, wide[0]) + nn(up_grad, wide[1])

    def experts_of(step):
        block = block_at(row, step)

        @pl.when(step == 0)
        def _():
            for load in loads[2:]:
                load.wait()

        @pl.when(step > 1)
        def _():
            stores(step - 2)[1].wait()
            half_copy(step - 2).wait_send()

        fwd_copy(block, other).wait_recv()
        left, right = rows[0, block], rows[1, block]
        logits = nt(left, router_ref[:, 0:width]) + nt(right, router_ref[:, width:])
        logits = logits - jnp.max(logits, axis=1, keepdims=True)
        weight = jnp.exp(logits)
        probs = weight / jnp.sum(weight, axis=1, keepdims=True)
        own = (
            lax.broadcasted_iota(jnp.int32, (picked, experts), 1) == place * ROWS + row
        ).astype(f32)
        gates = jnp.sum(probs * own, axis=1, keepdims=True)
        raw = nt(cot_rows[0, block], fun[:, 0:width]) + nt(cot_rows[1, block], fun[:, width:])
        gate = nt(left, fan[0, :, 0:width]) + nt(right, fan[0, :, width:])
        up = nt(left, fan[1, :, 0:width]) + nt(right, fan[1, :, width:])
        act, slope = silu_pair(gate)
        value = act * up
        hidden[block] = (value * gates).astype(bf16)
        gate_sum = gates * jnp.sum(value * raw, axis=1, keepdims=True)
        logit_grad = (gate_sum * (own - probs)).astype(bf16)
        raw = raw * gates
        slot = lax.rem(step, 2)
        gu[0, slot] = (raw * up * slope).astype(bf16)
        gu[1, slot] = (raw * act).astype(bf16)

        def half_of(half):
            lines = half_lines(half)
            return (
                nn(gu[0, slot], fan[0, :, lines])
                + nn(gu[1, slot], fan[1, :, lines])
                + nn(logit_grad, router_ref[:, lines])
            )

        pair_to[slot] = half_of(other).astype(bf16)
        half_copy(step).start()
        pair_own[...] = half_of(col)
        router_rows[:, 0:width] += tn(logit_grad, left)
        router_rows[:, width:] += tn(logit_grad, right)
        for copy in stores(step):
            copy.start()
        for shift in range(1, SQUARE):
            out_copy(block, shift).wait_send()
        half_copy(step).wait_recv()
        staged[block] = (pair_own[...] + pair_from[step].astype(f32)).astype(bf16)
        for shift in (3, 2, 1):
            home_copy(block, shift).start()
        home[block, 0:slots] = staged[block, 0:slots]

    def add_up(step):
        block = block_at(row, step)
        for shift in range(1, SQUARE):
            home_copy(block, shift).wait_recv()
        total = part[block] + nn(back_ref[block], home[block])
        part[block] = total
        premix_ref[...] += jnp.sum(
            (total * gathered_ref[block].astype(f32)).reshape(tokens // 8, 8, width), axis=0
        )
        sums.begin(block)

    def reply(step):
        block = block_at(row, step)
        slot = lax.rem(step, 2)

        @pl.when(step < 2)
        def _():
            half_copy(step + 2).wait_send()

        @pl.when(step > 1)
        def _():
            other_copy(step - 2).wait_send()

        pair_to[slot] = nn(hidden[block], fun[:, half_lines(other)]).astype(bf16)
        other_copy(step).start()

    def reply_home(step):
        block = block_at(row, step)
        own = nn(hidden[block], fun[:, half_lines(col)])
        for shift in range(1, SQUARE):
            home_copy(block, shift).wait_send()
        came = jnp.where(step == ROWS - 1, ROWS, step)
        other_copy(step).wait_recv()
        staged[block] = (own + pair_from[came].astype(f32)).astype(bf16)
        for shift in (3, 2, 1):
            reply_copy(block, shift).start()
        reply_ref[block, 0:slots] = staged[block, 0:slots]

    def turn(step, carried):
        @pl.when(step < ROWS)
        def _():
            take(step)

        @pl.when(jnp.logical_and(step == 0, inner))
        def _():
            relay(1)
            relay(2)

        @pl.when(jnp.logical_and(step >= 1, step < ROWS))
        def _():
            forward(step - 1)

        @pl.when(jnp.logical_and(step >= 2, step < ROWS + 2))
        def _():
            experts_of(step - 2)

        @pl.when(step == ROWS)
        def _():
            forward(ROWS - 1)

        @pl.when(jnp.logical_or(step == 1, step >= 3))
        def _():
            shared(jnp.where(step == 1, 0, step - 2))

        @pl.when(jnp.logical_and(step == 1, inner))
        def _():
            relay(3)

        @pl.when(step >= 3)
        def _():
            add_up(step - 3)

        return carried

    lax.fori_loop(0, ROWS + 2, turn, 0)

    def replies(step, carried):
        @pl.when(step < ROWS)
        def _():
            reply(step)

        @pl.when(step > 0)
        def _():
            reply_home(step - 1)

        return carried

    lax.fori_loop(0, ROWS + 1, replies, 0)
    add_up(ROWS - 1)

    def hand_on(turn, carried):
        sums.pass_on(block_at(row, jnp.where(turn == 2, 1, turn + 2)))
        return carried

    lax.fori_loop(0, ROWS - 1, hand_on, 0)

    seq = ROWS * tokens
    for index, (left, right) in enumerate(
        (
            (shared_out, cot_ref),
            (shared_gu.at[0], gathered_ref),
            (shared_gu.at[1], gathered_ref),
        )
    ):
        grad = tn(left[...].reshape(seq, share), right[...].reshape(seq, width))
        shared_grad[index] = grad.astype(bf16)
    x, y = lax.rem(place, 2), lax.div(place, 2)
    quarter = width // SQUARE
    grad_copies = []
    for index, (half, side, target) in enumerate(
        (
            (0, 1 - x, shared_x),
            (1, 1 - y, shared_y),
            (0, x, shared_kept.at[0]),
            (1, y, shared_kept.at[1]),
        )
    ):
        lanes = pl.ds(pl.multiple_of((2 * half + side) * quarter, 128), quarter)
        grad_copies.append(
            pltpu.make_async_copy(shared_grad.at[:, :, lanes], target, grad_sem.at[index])
        )
        grad_copies[index].start()
    sums.total(sum_ref)

    def ended(step, carried):
        block = block_at(row, step)
        shared_copy(block).wait_send()
        fwd_copy(block, col).wait_send()
        for shift in range(1, SQUARE):
            reply_copy(block, shift).wait_recv()
            reply_copy(block, shift).wait_send()
        copies = stores(step)
        copies[0].wait()
        copies[2].wait()

        @pl.when(step >= ROWS - 2)
        def _():
            copies[1].wait()
            other_copy(step).wait_send()

        return carried

    lax.fori_loop(0, ROWS, ended, 0)
    for copy in grad_copies:
        copy.wait()
    sums.finish()
    line.finish()


def run_experts(
    normed, pick, back, cot_rows, cot_all, fan, fun, wide, narrow, router_all
):
    tokens, width = normed.shape
    picked = pick.shape[1]
    hid = fun.shape[0]
    share = narrow.shape[0]
    experts = router_all.shape[0]
    whole = pl.BlockSpec(memory_space=VMEM)
    far = pl.BlockSpec(memory_space=pl.ANY)

    def shape(*dims, dtype=bf16):
        return jax.ShapeDtypeStruct(dims, dtype)

    return pl.pallas_call(
        expert_kernel,
        name="experts",
        out_shape=(
            shape(tokens, width, dtype=f32),
            shape(ROWS, tokens, width),
            shape(COLS, ROWS, picked, width),
            shape(2, ROWS, picked, hid),
            shape(ROWS, picked, hid),
            shape(3, share, width // SQUARE),
            shape(3, share, width // SQUARE),
            shape(2, 3, share, width // SQUARE),
            shape(ROWS, tokens, share),
            shape(8, width, dtype=f32),
            shape(experts, COLS * width, dtype=f32),
            shape(ROWS, picked, width),
        ),
        in_specs=[whole] * 5 + [far] * 5,
        out_specs=(whole, whole) + (far,) * 6 + (whole,) * 4,
        scratch_shapes=[
            VMEM(fan.shape, bf16),
            VMEM(fun.shape, bf16),
            VMEM(wide.shape, bf16),
            VMEM(narrow.shape, bf16),
            VMEM(cot_rows.shape, bf16),
            VMEM((COLS, ROWS, picked, width), bf16),
            VMEM((ROWS, picked, width), bf16),
            VMEM((2, 2, picked, hid), bf16),
            VMEM((ROWS, picked, hid), bf16),
            VMEM((picked, width), f32),
            VMEM((2, picked, width), bf16),
            VMEM((ROWS + 1, picked, width), bf16),
            VMEM((ROWS, picked, width), bf16),
            VMEM((ROWS, 3, tokens, share), bf16),
            VMEM((ROWS, 3, tokens, share), bf16),
            VMEM((ROWS, tokens, width), f32),
            VMEM((ROWS, tokens, width), bf16),
            VMEM((2, ROWS, tokens, width), bf16),
            VMEM((2, ROWS, tokens, share), bf16),
            VMEM((3, share, width), bf16),
            DMA((5,)),
            DMA((3, ROWS)),
            *line_sems(),
            *square_sems(),
            *pair_sems(),
            *pair_sems(),
            *pair_sems(),
            *square_sems(),
            *sum_sems(),
            *pair_sems(),
            *square_sems(),
            DMA((4,)),
        ],
        compiler_params=pltpu.CompilerParams(
            collective_id=2, has_side_effects=True, vmem_limit_bytes=62 * MIB
        ),
        cost_estimate=pl.CostEstimate(
            flops=60 * 1024**3, bytes_accessed=64 * MIB, transcendentals=0
        ),
    )(normed, pick, back, cot_all, router_all, cot_rows, fan, fun, wide, narrow)


class SquareSum:
    def __init__(self, place, part, first, second, middle, result, sent, arrived):
        self.x, self.y = lax.rem(place, 2), lax.div(place, 2)
        self.to_x, self.to_y = {"dp": partner(place, 1)}, {"dp": partner(place, 2)}
        self.part, self.first, self.second = part, first, second
        self.middle, self.result = middle, result
        self.sent, self.arrived = sent, arrived

    def copies(self, phase):
        x, y = self.x, self.y
        if phase == 0:
            plan = (
                (self.part.at[pl.ds(2 - 2 * x, 2)], self.first.at[0:2], self.to_x),
                (self.part.at[pl.ds(6 - 2 * y, 2)], self.first.at[2:4], self.to_y),
            )
        elif phase == 1:
            plan = (
                (self.middle.at[0], self.second.at[0], self.to_y),
                (self.middle.at[1], self.second.at[1], self.to_x),
            )
        elif phase == 2:
            one, two = self.result.at[2 * x + y], self.result.at[4 + 2 * y + x]
            plan = ((one, one, self.to_y), (two, two, self.to_x))
        else:
            one, two = self.result.at[pl.ds(2 * x, 2)], self.result.at[pl.ds(4 + 2 * y, 2)]
            plan = ((one, one, self.to_x), (two, two, self.to_y))
        return [
            remote(source, target, self.sent.at[2 * phase + i], self.arrived.at[2 * phase + i], to)
            for i, (source, target, to) in enumerate(plan)
        ]

    def start(self, phase):
        for copy in self.copies(phase):
            copy.start()

    def arrive(self, phase):
        for copy in self.copies(phase):
            copy.wait_recv()

    def run(self, phase):
        x, y = self.x, self.y
        if phase > 0:
            self.arrive(phase - 1)
        if phase == 1:
            for slot, piece, came in (
                (0, 2 * x + 1 - y, 1 - y),
                (1, 4 + 2 * y + 1 - x, 3 - x),
            ):
                self.middle[slot] = (
                    self.part[piece].astype(f32) + self.first[came].astype(f32)
                ).astype(bf16)
        if phase == 2:
            for slot, piece, came in ((0, 2 * x + y, y), (1, 4 + 2 * y + x, 2 + x)):
                self.result[piece] = (
                    self.part[piece].astype(f32)
                    + self.first[came].astype(f32)
                    + self.second[slot].astype(f32)
                ).astype(bf16)
        if phase < 4:
            self.start(phase)

    def finish(self):
        for phase in range(4):
            for copy in self.copies(phase):
                copy.wait_send()


def square_scratch(dims):
    count, rows, lanes = dims
    return [
        VMEM((count, 8, rows, lanes), bf16),
        VMEM((count, 4, rows, lanes), bf16),
        VMEM((count, 2, rows, lanes), bf16),
        VMEM((count, 2, rows, lanes), bf16),
        VMEM((count, 8, rows, lanes), bf16),
        DMA((count, 8)),
        DMA((count, 8)),
    ]


def finish_kernel(
    own_latent_ref,
    back_ref,
    shared_ref,
    residual_ref,
    premix_rows,
    scaling_rows,
    rescale_rows,
    router_rows,
    premix_ref,
    scaling_ref,
    home_ref,
    one_ref,
    query_grad_ref,
    attended_ref,
    branch_ref,
    latent_ref,
    expanded_ref,
    narrow_ref,
    output_ref,
    queries_out,
    combine_out,
    expand_out,
    compress_out,
    small_ref,
    home,
    one,
    query_grad,
    attended,
    branch,
    latent,
    expanded,
    narrow,
    part,
    leaving,
    coming,
    total,
    queries_wide,
    combine_wide,
    expand_wide,
    compress_wide,
    small_to,
    small_from,
    small_line,
    small_square,
    small_own,
    load_sem,
    store_sem,
    sum_sent,
    sum_arrived,
    pair_sent,
    pair_arrived,
    small_sent,
    small_arrived,
    *sums_scratch,
):
    place, row, col = lax.axis_index("dp"), lax.axis_index("row"), lax.axis_index("col")
    other = 1 - col
    sibling = {"col": other}
    tokens, width = output_ref.shape
    seq = ROWS * tokens
    experts = router_rows.shape[0]
    loads = [
        pltpu.make_async_copy(source, target, load_sem.at[i])
        for i, (source, target) in enumerate(
            [
                (narrow_ref, narrow),
                (home_ref, home),
                (one_ref, one),
                (query_grad_ref, query_grad),
                (attended_ref, attended),
                (branch_ref, branch),
                (latent_ref, latent),
                (expanded_ref, expanded),
            ]
        )
    ]
    for load in loads:
        load.start()
    greet(row, place, col, line=True, square=True)
    line_sums = SumLine(row, part, leaving, coming, sum_sent, sum_arrived)

    def reply_add(turn, carried):
        block = block_at(row, ROWS - 1 - turn)
        part[block] = nn(back_ref[block], home[block]) + nn(shared_ref[block], narrow[...])
        line_sums.begin(block)
        return carried

    kinds = [sums_scratch[7 * i : 7 * i + 7] for i in range(4)]
    sums = []
    for scratch in kinds:
        for index in range(scratch[0].shape[0]):
            sums.append(SquareSum(place, *[ref.at[index] for ref in scratch]))
    parts = [scratch[0] for scratch in kinds]
    counts = [ref.shape[0] for ref in parts]
    def begin(index):
        kind, chunk = 0, index
        while chunk >= counts[kind]:
            chunk -= counts[kind]
            kind += 1
        if chunk == 0:
            for load in loads[2 + 2 * min(kind, 3) :][: 2 if kind < 3 else 0]:
                load.wait()
        if kind < 2:
            left, right = ((one, query_grad), (attended, branch))[kind]
            height = 8 * parts[kind].shape[2]
            piece = left[:, :, chunk * height : (chunk + 1) * height].reshape(seq, height)
            grad = tn(piece, right[...].reshape(seq, right.shape[2]))
        elif kind == 2:
            grad = tn(latent[...].reshape(seq, RANK), expanded[...].reshape(seq, expanded.shape[2]))
        else:
            grad = nn(own_latent_ref[...], one[...].reshape(seq, width)).astype(bf16)
            for piece in range(8):
                parts[3][0, piece] = grad[:, piece * (width // 8) : (piece + 1) * (width // 8)]
        if kind < 3:
            parts[kind][chunk] = grad.astype(bf16).reshape(parts[kind].shape[1:])
        sums[index].run(0)

    ahead = 3
    for index in range(ahead):
        begin(index)

    def small_copy(step):
        if step == 0:
            return remote(small_to, small_from, small_sent.at[0], small_arrived.at[0], sibling)
        if step < ROWS:
            return remote(
                small_own,
                small_line.at[step],
                small_sent.at[step],
                small_arrived.at[step],
                {"row": lax.rem(row + step, ROWS)},
            )
        shift = step - ROWS + 1
        return remote(
            small_ref,
            small_square.at[shift],
            small_sent.at[step],
            small_arrived.at[step],
            {"dp": partner(place, shift)},
        )

    def small_begin():
        rescale_row = jnp.sum(rescale_rows[...], axis=0, keepdims=True)
        empty = jnp.zeros((small_own.shape[0] - experts, width), f32)
        small_to[0:experts] = router_rows[:, pl.ds(pl.multiple_of(other * width, width), width)]
        small_to[experts:] = empty
        small_to[experts + 2 : experts + 3, 0:RANK] = rescale_row
        small_copy(0).start()
        small_own[0:experts] = router_rows[:, pl.ds(pl.multiple_of(col * width, width), width)]
        small_own[experts:] = empty
        small_own[experts : experts + 1] = (
            jnp.sum(premix_rows[...], axis=0, keepdims=True) / premix_ref[...]
        )
        small_own[experts + 1 : experts + 2] = (
            jnp.sum(scaling_rows[...], axis=0, keepdims=True) / scaling_ref[...]
        )
        small_own[experts + 2 : experts + 3, 0:RANK] = rescale_row

    def small_line_begin():
        small_copy(0).wait_recv()
        small_own[...] += small_from[...]
        for step in range(1, ROWS):
            small_copy(step).start()

    def small_square_begin():
        for step in range(1, ROWS):
            small_copy(step).wait_recv()
        small_ref[...] = small_own[...] + small_line[1] + small_line[2] + small_line[3]
        for step in range(ROWS, ROWS + SQUARE - 1):
            small_copy(step).start()

    def small_end():
        for step in range(ROWS, ROWS + SQUARE - 1):
            small_copy(step).wait_recv()
        for step in range(ROWS, ROWS + SQUARE - 1):
            small_copy(step).wait_send()
        small_ref[...] += small_square[1] + small_square[2] + small_square[3]

    def reply_begin():
        loads[0].wait()
        loads[1].wait()
        lax.fori_loop(0, ROWS, reply_add, 0)

    def reply_pass():
        lax.fori_loop(0, 3, line_pass, 0)

    def reply_end():
        line_sums.total(total)
        output_ref[...] = (total[...] + residual_ref[...]).astype(bf16)

    def line_pass(turn, carried):
        line_sums.pass_on(block_at(row, jnp.where(turn == 0, 3, turn)))
        return carried

    stores = []

    def store(source, target):
        copy = pltpu.make_async_copy(source, target, store_sem.at[len(stores)])
        copy.start()
        stores.append(copy)

    def pair_copy(half):
        here = expand_wide.at[half]
        return remote(here, here, pair_sent.at[0], pair_arrived.at[0], sibling)

    def put(index):
        kind, chunk = 0, index
        while chunk >= counts[kind]:
            chunk -= counts[kind]
            kind += 1
        result = kinds[kind][4][chunk]
        pieces, rows, lanes = result.shape
        if kind < 2:
            wide, out = ((queries_wide, queries_out), (combine_wide, combine_out))[kind]
            here = pl.ds(chunk * pieces * rows, pieces * rows)
            wide[here] = result.astype(f32).reshape(pieces * rows, lanes)
            store(wide.at[here], out.at[here])
        elif kind == 2:
            expand_wide[col] = result.astype(f32).reshape(pieces * rows, lanes)
            pair_copy(col).start()
        else:
            for piece in range(pieces):
                compress_wide[:, piece * lanes : (piece + 1) * lanes] = result[piece].astype(f32)
            store(compress_wide, compress_out)

    count = len(sums)
    between = {
        0: (reply_begin, small_begin),
        1: (small_line_begin,),
        4: (reply_pass,),
        5: (small_square_begin,),
        count - 1: (reply_end,),
        count + 1: (small_end,),
    }
    for turn in range(count + 3):
        if turn < count:
            sums[turn].run(1)
        if turn + ahead < count:
            begin(turn + ahead)
        for phase in (2, 3, 4):
            index = turn + 1 - phase
            if 0 <= index < count:
                sums[index].run(phase)
                if phase == 4:
                    put(index)
        for act in between.get(turn, ()):
            act()

    pair_copy(other).wait_recv()
    store(expand_wide.at[0], expand_out.at[:, 0 : expand_wide.shape[2]])
    store(expand_wide.at[1], expand_out.at[:, expand_wide.shape[2] :])
    for copy in stores:
        copy.wait()
    pair_copy(col).wait_send()
    for step in range(ROWS):
        small_copy(step).wait_send()
    for one_sum in sums:
        one_sum.finish()
    line_sums.finish()


def run_finish(
    own_latent,
    back,
    shared,
    residual,
    premix_rows,
    scaling_rows,
    rescale_rows,
    router_rows,
    premix,
    scaling,
    home,
    one,
    query_grad,
    attended,
    branch,
    latent,
    expanded,
    narrow,
):
    tokens, width = residual.shape
    sliced = own_latent.shape[0]
    wide = query_grad.shape[2]
    heads = attended.shape[2]
    own_heads = expanded.shape[2]
    small = (24, width)
    whole = pl.BlockSpec(memory_space=VMEM)
    far = pl.BlockSpec(memory_space=pl.ANY)

    def shape(*dims, dtype=f32):
        return jax.ShapeDtypeStruct(dims, dtype)

    loaded = (home, one, query_grad, attended, branch, latent, expanded, narrow)
    return pl.pallas_call(
        finish_kernel,
        name="finish",
        out_shape=(
            shape(tokens, width, dtype=bf16),
            shape(width, wide),
            shape(heads, width),
            shape(RANK, COLS * own_heads),
            shape(sliced, width),
            shape(*small),
        ),
        in_specs=[whole] * 10 + [far] * 8,
        out_specs=(whole, far, far, far, far, whole),
        scratch_shapes=[
            *[VMEM(value.shape, bf16) for value in loaded],
            VMEM((ROWS, tokens, width), f32),
            VMEM((ROWS, tokens, width), bf16),
            VMEM((2, ROWS, tokens, width), bf16),
            VMEM((tokens, width), f32),
            VMEM((width, wide), f32),
            VMEM((heads, width), f32),
            VMEM((COLS, RANK, own_heads), f32),
            VMEM((sliced, width), f32),
            VMEM(small, f32),
            VMEM(small, f32),
            VMEM((ROWS,) + small, f32),
            VMEM((SQUARE,) + small, f32),
            VMEM(small, f32),
            DMA((len(loaded),)),
            DMA((10,)),
            *sum_sems(),
            DMA((1,)),
            DMA((1,)),
            DMA((ROWS + SQUARE - 1,)),
            DMA((ROWS + SQUARE - 1,)),
            *square_scratch((4, width // 32, wide)),
            *square_scratch((2, heads // 16, width)),
            *square_scratch((1, RANK // 8, own_heads)),
            *square_scratch((1, sliced, width // 8)),
        ],
        compiler_params=pltpu.CompilerParams(
            collective_id=4, has_side_effects=True, vmem_limit_bytes=60 * MIB
        ),
        cost_estimate=pl.CostEstimate(
            flops=40 * 1024**3, bytes_accessed=64 * MIB, transcendentals=0
        ),
    )(
        own_latent,
        back,
        shared,
        residual,
        premix_rows,
        scaling_rows,
        rescale_rows,
        router_rows,
        premix.reshape(1, width),
        scaling.reshape(1, width),
        *loaded,
    )


def product_kernel(left_ref, right_ref, out_ref, turned):
    wide = 256

    @pl.when(pl.program_id(1) == 0)
    def _():
        turned[...] = left_ref[0].T

    def one(index, carried):
        lanes = pl.ds(pl.multiple_of(index * wide, 128), wide)
        out_ref[0, :, lanes] = nn(turned[...], right_ref[0, :, lanes])
        return carried

    lax.fori_loop(0, right_ref.shape[2] // wide, one, 0)


def slot_products(left, right):
    kinds, slots, tall = left.shape
    halves, _, wide = right.shape
    return pl.pallas_call(
        product_kernel,
        name="slot_products",
        grid=(kinds, halves),
        out_shape=jax.ShapeDtypeStruct((kinds, tall, halves * wide), f32),
        in_specs=[
            pl.BlockSpec((1, slots, tall), lambda kind, half: (kind, 0, 0)),
            pl.BlockSpec((1, slots, wide), lambda kind, half: (half, 0, 0)),
        ],
        out_specs=pl.BlockSpec((1, tall, wide), lambda kind, half: (kind, 0, half)),
        scratch_shapes=[VMEM((tall, slots), bf16)],
        compiler_params=pltpu.CompilerParams(vmem_limit_bytes=40 * MIB),
        cost_estimate=pl.CostEstimate(
            flops=2 * kinds * halves * slots * tall * wide,
            bytes_accessed=4 * kinds * halves * tall * wide,
            transcendentals=0,
        ),
    )(left, right)


def local_square(
    activations,
    cotangent,
    routing,
    segments,
    scaling,
    queries,
    compress,
    rescale,
    expand,
    combine,
    premix,
    router,
    widening,
    narrowing,
    fanout,
    funnel,
):
    dp_count = lax.axis_size("dp")
    row_count = lax.axis_size("row")
    col_count = lax.axis_size("col")
    col_index = lax.axis_index("col")
    local_rows, col_width = activations.shape
    seq_length = local_rows * row_count
    expert_total = router.shape[1]
    capacity = local_rows * TOP * 4 // (3 * expert_total)
    slot_total = capacity * row_count * dp_count
    tables = turning_tables(seq_length)
    (
        one,
        query,
        key,
        value,
        probs,
        latent,
        latent_normed,
        attended,
        compress_all,
        cot_blocks,
        pick,
        back,
        cot_rows,
        residual,
        normed_two,
        scale_one,
        scale_two,
        router_all,
    ) = run_attention(
        activations,
        scaling,
        queries,
        compress,
        rescale,
        expand,
        combine,
        premix,
        segments,
        cotangent,
        routing,
        router,
        tables,
        capacity,
    )
    (
        normed_grad,
        two_blocks,
        expert_rows,
        expert_gu_grad,
        expert_hidden,
        shared_x,
        shared_y,
        shared_kept,
        hidden_blocks,
        premix_rows,
        router_rows,
        reply_blocks,
    ) = run_experts(
        normed_two,
        pick,
        back,
        cot_rows,
        cot_blocks,
        fanout[0].transpose(0, 2, 1),
        funnel[0],
        widening.transpose(0, 2, 1),
        narrowing,
        router_all,
    )
    slot_rows = expert_rows.reshape(col_count, slot_total, col_width)
    reply_grad_rows = cot_rows.reshape(col_count, slot_total, col_width)
    slot_hidden = expert_hidden.reshape(slot_total, -1)
    slot_gu_grad = expert_gu_grad.reshape(2, slot_total, -1)
    got_x = lax.ppermute(shared_x, "dp", [(i, i ^ 1) for i in range(SQUARE)])
    got_y = lax.ppermute(shared_y, "dp", [(i, i ^ 2) for i in range(SQUARE)])
    fanout_grad = slot_products(slot_gu_grad, slot_rows)
    funnel_grad = slot_products(slot_hidden[None], reply_grad_rows)
    normed_grad, fanout_grad, funnel_grad = lax.optimization_barrier(
        (normed_grad, fanout_grad, funnel_grad)
    )
    (
        input_grad,
        branch_blocks,
        query_grad,
        expanded_grad,
        own_latent_grad,
        scaling_rows,
        rescale_rows,
        shared_sum,
    ) = run_attention_back(
        normed_grad,
        residual,
        scale_two,
        premix,
        cotangent,
        activations,
        scale_one,
        scaling,
        one,
        query,
        key,
        value,
        probs,
        latent,
        rescale,
        tables,
        compress_all,
        queries,
        expand,
        combine,
        (shared_kept, got_x, got_y),
    )
    layer_output, queries_sum, combine_sum, expand_sum, compress_sum, small = run_finish(
        own_latent_grad,
        back,
        hidden_blocks,
        residual,
        premix_rows,
        scaling_rows,
        rescale_rows,
        router_rows,
        premix,
        scaling,
        reply_blocks,
        one,
        query_grad,
        attended,
        branch_blocks,
        latent_normed,
        expanded_grad,
        narrowing,
    )
    return (
        layer_output,
        input_grad,
        small[expert_total + 1],
        queries_sum,
        compress_sum.T,
        small[expert_total + 2, :RANK],
        expand_sum,
        combine_sum,
        small[expert_total],
        small[:expert_total].T,
        shared_sum[1:].astype(f32).transpose(0, 2, 1),
        shared_sum[0].astype(f32),
        fanout_grad.transpose(0, 2, 1)[None],
        funnel_grad,
    )


def local(
    activations,
    cotangent,
    routing,
    segments,
    scaling,
    queries,
    compress,
    rescale,
    expand,
    combine,
    premix,
    router,
    widening,
    narrowing,
    fanout,
    funnel,
):
    dp_count = lax.axis_size("dp")
    row_count = lax.axis_size("row")
    col_count = lax.axis_size("col")
    dp_index = lax.axis_index("dp")
    row_index = lax.axis_index("row")
    col_index = lax.axis_index("col")
    local_rows = activations.shape[0]
    col_width = activations.shape[1]
    seq_length = local_rows * row_count
    half_length = seq_length // col_count
    head_width = NOPE + ROPE
    pair_width = NOPE + HEADV
    local_heads = queries.shape[1] // head_width
    slice_width = compress.shape[1]
    expert_total = router.shape[1]
    capacity = local_rows * TOP * 4 // (3 * expert_total)
    slots = capacity * row_count
    slot_total = slots * dp_count
    block_rows = min(512, half_length)
    block_count = half_length // block_rows
    score_scale = head_width ** (-0.5)

    inputs = activations.astype(f32)
    scale_one = norm_scale(inputs)
    normed_one = (inputs * scale_one[:, None] * scaling).astype(bf16)
    gathered_one = row_gather(normed_one)
    compress_all = lax.all_gather(compress, "row", axis=1, tiled=True)

    routing_all = row_gather(routing)
    cotangent_all = row_gather(after(cotangent, gathered_one))
    offsets = jnp.arange(dp_count, dtype=jnp.int32)
    my_experts = ((dp_index + offsets) % dp_count) * row_count + row_index
    goes = jnp.any(routing_all[None, :, :] == my_experts[:, None, None], axis=2)
    token_range = jnp.arange(seq_length, dtype=jnp.int32)
    earlier = (token_range[:, None] < token_range[None, :]).astype(bf16)
    rank = dot(goes.astype(bf16), earlier).astype(jnp.int32)
    slot_range = jnp.arange(slots, dtype=jnp.int32)
    pick = (
        ((rank[:, None, :] == slot_range[None, :, None]) & goes[:, None, :])
        .astype(bf16)
        .reshape(slot_total, seq_length)
    )

    def dispatch(tokens):
        rows = dot(pick, tokens).astype(bf16).reshape(dp_count, slots, col_width)
        arrived = send_out([rows[k] for k in range(dp_count)])
        return col_gather(jnp.concatenate(arrived, axis=0), axis=1)

    def bring_back(part):
        summed = col_scatter(part.astype(bf16), axis=1).reshape(dp_count, slots, col_width)
        arrived = send_back([summed[k] for k in range(dp_count)])
        return dot_tn(pick, jnp.concatenate(arrived, axis=0))

    query_part = dot(gathered_one, queries)
    latent_part = dot(gathered_one, compress_all)
    query_raw, latent_raw = col_scatter((query_part, latent_part))
    latent_plain = latent_raw[:, :RANK]
    latent_scale = lax.rsqrt(jnp.mean(latent_plain * latent_plain, axis=1) + epsilon)
    latent_normed = (latent_plain * latent_scale[:, None] * rescale).astype(bf16)
    expanded = dot(latent_normed, expand).reshape(half_length, local_heads, pair_width)
    positions = col_index * half_length + jnp.arange(half_length, dtype=jnp.int32)
    cosine, sine_table = rotation(positions, ROPE)
    key_shared = rotate(latent_raw[:, RANK:], cosine, sine_table, 1.0)
    query_heads = query_raw.reshape(half_length, local_heads, head_width)
    query_local = jnp.concatenate(
        [
            query_heads[..., :NOPE],
            rotate(query_heads[..., NOPE:], cosine[:, None, :], sine_table[:, None, :], 1.0),
        ],
        axis=2,
    ).astype(bf16)
    key_local = jnp.concatenate(
        [
            expanded[..., :NOPE],
            jnp.broadcast_to(key_shared[:, None, :], (half_length, local_heads, ROPE)),
        ],
        axis=2,
    ).astype(bf16)
    value_local = expanded[..., NOPE:].astype(bf16)
    key_flat, value_flat = (
        col_gather(key_local.reshape(half_length, local_heads * head_width)),
        col_gather(value_local.reshape(half_length, local_heads * HEADV)),
    )
    key_heads = key_flat.reshape(seq_length, local_heads, head_width)
    value_heads = value_flat.reshape(seq_length, local_heads, HEADV)
    own_segments = lax.dynamic_slice_in_dim(
        segments, col_index * half_length, half_length, 0
    ).reshape(block_count, block_rows)
    query_blocks = query_local.reshape(block_count, block_rows, local_heads, head_width)

    def attend_block(inputs_block):
        query_block, segment_block = inputs_block
        scores = (
            jnp.einsum("qhd,khd->hqk", query_block, key_heads, preferred_element_type=f32)
            * score_scale
        )
        visible = segments[None, None, :] <= segment_block[None, :, None]
        scores = jnp.where(visible, scores, masked_score)
        largest = jnp.max(scores, axis=2, keepdims=True)
        weight = jnp.exp(scores - largest)
        totals = jnp.sum(weight, axis=2, keepdims=True)
        probability = (weight / totals).astype(bf16)
        result = jnp.einsum("hqk,khd->qhd", probability, value_heads, preferred_element_type=f32)
        return (result.astype(bf16), (largest + jnp.log(totals))[..., 0])

    attended_blocks, log_totals = lax.map(attend_block, (query_blocks, own_segments))
    attended = attended_blocks.reshape(half_length, local_heads * HEADV)
    attended_all = col_gather(attended)
    branch = row_scatter(dot(attended_all, combine))

    reply_grad_rows = dispatch(cotangent_all)
    inner_weight = fanout[0]
    outer_weight = funnel[0]
    hidden_raw = dot_nt(reply_grad_rows, outer_weight)
    shared_hidden_grad = col_scatter(dot_nt(cotangent_all, narrowing))

    residual = inputs + branch
    scale_two = norm_scale(residual)
    normed_two = (residual * scale_two[:, None] * premix).astype(bf16)
    gathered_two = row_gather(normed_two)

    expert_rows = dispatch(gathered_two)
    expert_range = jnp.arange(expert_total, dtype=jnp.int32)
    router_all = lax.all_gather(router, "col", axis=0, tiled=True)
    own_expert = dp_index * row_count + row_index
    slot_probs = jax.nn.softmax(dot(expert_rows, router_all), axis=1)
    slot_gates = jnp.sum(jnp.where(expert_range == own_expert, slot_probs, 0.0), axis=1)
    gate_up = jnp.einsum("rd,gdf->grf", expert_rows, inner_weight, preferred_element_type=f32)
    gate_input, up_input = gate_up[0], gate_up[1]
    hidden = jax.nn.silu(gate_input) * up_input
    expert_hidden = hidden.astype(bf16)
    slot_gate_grad = col_totals(jnp.sum(hidden * hidden_raw, axis=1))
    hidden_grad = hidden_raw * slot_gates[:, None]
    expert_gu_grad = jnp.stack(
        [hidden_grad * up_input * silu_slope(gate_input), hidden_grad * jax.nn.silu(gate_input)]
    ).astype(bf16)
    input_part = jnp.einsum(
        "grf,gdf->rd", expert_gu_grad, inner_weight, preferred_element_type=f32
    )
    routed_grad = bring_back(input_part)
    gate_grad_parts = send_back(
        [slot_gate_grad.reshape(dp_count, slots)[k] for k in range(dp_count)]
    )

    logits = col_totals(dot(gathered_two, router))
    router_probs = jax.nn.softmax(logits, axis=1)
    gate_grad = jnp.sum(
        pick.reshape(dp_count, slots, seq_length).astype(f32)
        * jnp.stack(gate_grad_parts)[:, :, None],
        axis=1,
    )
    mine = (my_experts[:, None] == expert_range[None, :]).astype(f32)
    probs_grad = jnp.sum(gate_grad[:, :, None] * mine[:, None, :], axis=0)
    logit_grad = router_probs * (
        probs_grad - jnp.sum(router_probs * probs_grad, axis=1, keepdims=True)
    )
    router_part = dot_tn(gathered_two, logit_grad)

    shared_gate_up = col_scatter(
        jnp.einsum("td,gdf->tgf", gathered_two, widening, preferred_element_type=f32)
    )
    shared_hidden = (jax.nn.silu(shared_gate_up[:, 0]) * shared_gate_up[:, 1]).astype(bf16)
    hidden_all = col_gather(shared_hidden)
    narrowing_grad = dot_tn(hidden_all, cotangent_all)
    shared_gu_grad = jnp.stack(
        [
            shared_hidden_grad * shared_gate_up[:, 1] * silu_slope(shared_gate_up[:, 0]),
            shared_hidden_grad * jax.nn.silu(shared_gate_up[:, 0]),
        ],
        axis=1,
    ).astype(bf16)
    gu_grad_all = col_gather(shared_gu_grad)
    widening_grad = jnp.einsum(
        "td,tgf->gdf", gathered_two, gu_grad_all, preferred_element_type=f32
    )
    shared_input_part = jnp.einsum(
        "tgf,gdf->td", gu_grad_all, widening, preferred_element_type=f32
    )
    shared_sums = lax.psum((narrowing_grad.astype(bf16), widening_grad.astype(bf16)), "dp")

    grad_part = routed_grad + shared_input_part + dot_nt(logit_grad, router)
    premix_part = jnp.sum(grad_part * gathered_two.astype(f32), axis=0) / premix
    normed_grad = row_scatter(grad_part)

    upstream = cotangent.astype(f32)
    residual_grad = upstream + norm_back(residual, scale_two, premix, normed_grad)
    branch_all = row_gather(residual_grad.astype(bf16))

    funnel_grad = dot_tn((hidden * slot_gates[:, None]).astype(bf16), reply_grad_rows)[None]
    fanout_grad = jnp.einsum(
        "rd,grf->gdf", expert_rows, expert_gu_grad, preferred_element_type=f32
    )[None]
    reply_part = dot(expert_hidden, outer_weight) * slot_gates[:, None]
    routed = bring_back(reply_part)
    shared_out = row_scatter(routed + dot(hidden_all, narrowing))
    layer_output = (residual + shared_out).astype(bf16)

    combine_grad = dot_tn(attended_all, branch_all)
    combine_sum = lax.psum(after(combine_grad.astype(bf16), *shared_sums), "dp")
    attended_grad = col_scatter(dot_nt(branch_all, combine))
    attended_grad_blocks = attended_grad.astype(bf16).reshape(
        block_count, block_rows, local_heads, HEADV
    )

    def attend_back(carried, inputs_block):
        key_sum, value_sum = carried
        query_block, grad_block, log_block, segment_block = inputs_block
        scores = (
            jnp.einsum("qhd,khd->hqk", query_block, key_heads, preferred_element_type=f32)
            * score_scale
        )
        visible = segments[None, None, :] <= segment_block[None, :, None]
        probability = jnp.where(visible, jnp.exp(scores - log_block[..., None]), 0.0)
        weight_grad = jnp.einsum(
            "qhd,khd->hqk", grad_block, value_heads, preferred_element_type=f32
        )
        inner_sum = jnp.sum(probability * weight_grad, axis=2, keepdims=True)
        score_grad = (probability * (weight_grad - inner_sum)).astype(bf16)
        query_grad_block = (
            jnp.einsum("hqk,khd->qhd", score_grad, key_heads, preferred_element_type=f32)
            * score_scale
        )
        key_sum = (
            key_sum
            + jnp.einsum("hqk,qhd->khd", score_grad, query_block, preferred_element_type=f32)
            * score_scale
        )
        value_sum = value_sum + jnp.einsum(
            "hqk,qhd->khd", probability.astype(bf16), grad_block, preferred_element_type=f32
        )
        return ((key_sum, value_sum), query_grad_block)

    key_start = jnp.zeros((seq_length, local_heads, head_width), f32)
    value_start = jnp.zeros((seq_length, local_heads, HEADV), f32)
    (key_grad_all, value_grad_all), query_grad_blocks = lax.scan(
        attend_back,
        (key_start, value_start),
        (query_blocks, attended_grad_blocks, log_totals, own_segments),
    )
    key_grad, value_grad = col_scatter(
        (
            key_grad_all.reshape(seq_length, local_heads * head_width),
            value_grad_all.reshape(seq_length, local_heads * HEADV),
        )
    )
    key_grad = key_grad.reshape(half_length, local_heads, head_width)
    value_grad = value_grad.reshape(half_length, local_heads, HEADV)
    query_grad = query_grad_blocks.reshape(half_length, local_heads, head_width)
    query_raw_grad = (
        jnp.concatenate(
            [
                query_grad[..., :NOPE],
                rotate(query_grad[..., NOPE:], cosine[:, None, :], sine_table[:, None, :], -1.0),
            ],
            axis=2,
        )
        .astype(bf16)
        .reshape(half_length, local_heads * head_width)
    )
    expanded_grad = (
        jnp.concatenate([key_grad[..., :NOPE], value_grad], axis=2)
        .astype(bf16)
        .reshape(half_length, local_heads * pair_width)
    )
    shared_rope_grad = rotate(jnp.sum(key_grad[..., NOPE:], axis=1), cosine, sine_table, -1.0)

    latent_grad = dot_nt(expanded_grad, expand)
    latent_weighted = latent_grad * rescale
    latent_inner = jnp.mean(latent_weighted * latent_plain, axis=1)
    rescale_part = jnp.sum(latent_grad * latent_plain * latent_scale[:, None], axis=0)
    plain_grad = (
        latent_weighted * latent_scale[:, None]
        - latent_plain * (latent_scale**3 * latent_inner)[:, None]
    )
    latent_raw_grad = jnp.concatenate([plain_grad, shared_rope_grad], axis=1).astype(bf16)
    query_grad_all = col_gather(query_raw_grad)
    latent_grad_all = col_gather(latent_raw_grad)
    first_part = dot_nt(query_grad_all, queries) + dot_nt(latent_grad_all, compress_all)
    first_grad = row_scatter(first_part)
    input_grad = residual_grad + norm_back(inputs, scale_one, scaling, first_grad)

    queries_part = dot_tn(gathered_one, query_grad_all)
    own_latent_grad = lax.psum_scatter(
        latent_raw_grad, "row", scatter_dimension=1, tiled=True
    )
    compress_part = dot_tn(gathered_one, col_gather(own_latent_grad))
    half_rank = RANK // col_count
    latent_normed_all = col_gather(latent_normed)
    expanded_grad_all = col_gather(expanded_grad)
    expand_half = dot_tn(
        lax.dynamic_slice_in_dim(latent_normed_all, col_index * half_rank, half_rank, 1),
        expanded_grad_all,
    )
    scaling_part = jnp.sum(first_part * gathered_one.astype(f32), axis=0) / scaling
    queries_sum, expand_sum, compress_sum = lax.psum(
        (
            after(queries_part.astype(bf16), combine_sum),
            expand_half.astype(bf16),
            compress_part.astype(bf16),
        ),
        "dp",
    )
    premix_sum, router_sum = lax.psum((premix_part, router_part), ("dp", "row"))
    rescale_sum = lax.psum(rescale_part, ("dp", "row", "col"))
    scaling_sum = lax.psum(scaling_part, ("dp", "row"))
    return (
        layer_output,
        input_grad,
        scaling_sum,
        queries_sum.astype(f32),
        compress_sum.astype(f32),
        rescale_sum,
        col_gather(expand_sum).astype(f32),
        combine_sum.astype(f32),
        premix_sum,
        router_sum,
        shared_sums[1].astype(f32),
        shared_sums[0].astype(f32),
        fanout_grad,
        funnel_grad,
    )


def solution(mesh):
    placed = (
        P(("dp", "row"), "col"),
        P(("dp", "row"), "col"),
        P(("dp", "row"), None),
        P("dp"),
        P("col"),
        P("col", "row"),
        P("col", "row"),
        P(),
        P(None, "row"),
        P("row", "col"),
        P("col"),
        P("col", None),
        P(None, "col", "row"),
        P("row", "col"),
        P(("dp", "row"), None, None, "col"),
        P(("dp", "row"), "col", None),
    )
    squared = mesh.shape["dp"] == SQUARE and mesh.shape["row"] == ROWS
    return jax.shard_map(
        local_square if squared else local,
        mesh=mesh,
        in_specs=placed,
        out_specs=(
            P(("dp", "row"), "col"),
            P(("dp", "row"), "col"),
            P("col"),
            P("col", "row"),
            P("col", "row"),
            P(),
            P(None, "row"),
            P("row", "col"),
            P("col"),
            P("col", None),
            P(None, "col", "row"),
            P("row", "col"),
            P(("dp", "row"), None, None, "col"),
            P(("dp", "row"), "col", None),
        ),
        check_vma=False,
    )
```

```python
import functools

import jax
import jax.numpy as jnp
import numpy as np
from jax import lax
from jax.experimental import pallas as pl
from jax.experimental.pallas import tpu as pltpu
from jax.sharding import PartitionSpec as P

D = 2048
NOPE = 128
ROPE = 64
HEADV = 128
RANK = 512
TOP = 6


epsilon = 1e-06
masked_score = -1e30
f32 = jnp.float32
bf16 = jnp.bfloat16


def after(value, *earlier):
    return lax.optimization_barrier((value,) + earlier)[0]


def silu_slope(values):
    sigmoid = jax.nn.sigmoid(values)
    return sigmoid * (1.0 + values * (1.0 - sigmoid))


def rotation(positions, rope_width):
    half_width = rope_width // 2
    frequency = 10000.0 ** (-jnp.arange(half_width, dtype=jnp.float32) * 2.0 / rope_width)
    angles = positions.astype(jnp.float32)[:, None] * frequency[None, :]
    return (jnp.cos(angles), jnp.sin(angles))


def rotate(values, cosine, sine_table, direction):
    half_width = values.shape[-1] // 2
    first_half = values[..., :half_width]
    second_half = values[..., half_width:]
    return jnp.concatenate(
        [
            first_half * cosine - direction * second_half * sine_table,
            second_half * cosine + direction * first_half * sine_table,
        ],
        axis=-1,
    )


def dot(left, right):
    return jnp.dot(left, right, preferred_element_type=f32)


def dot_tn(left, right):
    return lax.dot_general(left, right, (((0,), (0,)), ((), ())), preferred_element_type=f32)


def dot_nt(left, right):
    return lax.dot_general(left, right, (((1,), (1,)), ((), ())), preferred_element_type=f32)


def col_totals(values):
    return lax.psum(values, "col")


def row_gather(values):
    return lax.all_gather(values, "row", axis=0, tiled=True)


def col_gather(values, axis=0):
    return lax.all_gather(values, "col", axis=axis, tiled=True)


def col_scatter(values, axis=0):
    return lax.psum_scatter(values, "col", scatter_dimension=axis, tiled=True)


def row_scatter(values):
    return lax.psum_scatter(
        values.astype(bf16), "row", scatter_dimension=0, tiled=True
    ).astype(f32)


def send_out(parts):
    count = len(parts)
    return [parts[0]] + [
        lax.ppermute(parts[k], "dp", [(i, (i + k) % count) for i in range(count)])
        for k in range(1, count)
    ]


def send_back(parts):
    count = len(parts)
    return [parts[0]] + [
        lax.ppermute(parts[k], "dp", [(i, (i - k) % count) for i in range(count)])
        for k in range(1, count)
    ]


def norm_scale(values):
    square_sum = col_totals(jnp.sum(values * values, axis=1))
    return lax.rsqrt(square_sum / D + epsilon)


def norm_back(values, row_scale, gain_vector, upstream):
    weighted = upstream * gain_vector
    inner_mean = col_totals(jnp.sum(weighted * values, axis=1)) / D
    return weighted * row_scale[:, None] - values * (row_scale**3 * inner_mean)[:, None]


MESH = pl.DeviceIdType.MESH
VMEM = pltpu.VMEM
DMA = pltpu.SemaphoreType.DMA
MIB = 1024 * 1024
ROWS = 4
SQUARE = 4
COLS = 2
SPLIT = 2


def nn(left, right):
    return lax.dot_general(left, right, (((1,), (0,)), ((), ())), preferred_element_type=f32)


def tn(left, right):
    return lax.dot_general(left, right, (((0,), (0,)), ((), ())), preferred_element_type=f32)


def nt(left, right):
    return lax.dot_general(left, right, (((1,), (1,)), ((), ())), preferred_element_type=f32)


def block_at(row, turn):
    swapped = jnp.where(turn < 2, 1 - turn, turn)
    inner = jnp.logical_or(row == 1, row == 2)
    near = jnp.where(inner, swapped, turn)
    return jnp.where(row < 2, near, ROWS - 1 - near)


def partner(place, step):
    across, along = lax.rem(place, 2), lax.div(place, 2)
    across = lax.rem(across + step % 2, 2)
    along = lax.rem(along + step // 2, 2)
    return along * 2 + across


def remote(source, target, sent, arrived, where):
    return pltpu.make_async_remote_copy(
        src_ref=source,
        dst_ref=target,
        send_sem=sent,
        recv_sem=arrived,
        device_id=where,
        device_id_type=MESH,
    )


def greet(row, place, col, line=False, square=True):
    barrier = pltpu.get_barrier_semaphore()
    met = 1
    if line:
        for step in range(1, ROWS):
            pl.semaphore_signal(
                barrier,
                inc=1,
                device_id={"row": lax.rem(row + step, ROWS)},
                device_id_type=MESH,
            )
        met = met + ROWS - 1
    else:

        @pl.when(row > 0)
        def _():
            pl.semaphore_signal(barrier, inc=1, device_id={"row": row - 1}, device_id_type=MESH)

        @pl.when(row < ROWS - 1)
        def _():
            pl.semaphore_signal(barrier, inc=1, device_id={"row": row + 1}, device_id_type=MESH)

        met = met + (row > 0).astype(jnp.int32) + (row < ROWS - 1).astype(jnp.int32)
    if square:
        for step in range(1, SQUARE):
            pl.semaphore_signal(
                barrier, inc=1, device_id={"dp": partner(place, step)}, device_id_type=MESH
            )
        met = met + SQUARE - 1
    pl.semaphore_signal(barrier, inc=1, device_id={"col": 1 - col}, device_id_type=MESH)
    pl.semaphore_wait(barrier, met)


class Line:
    def __init__(self, row, buffer, sent, arrived):
        self.row, self.buffer, self.sent, self.arrived = row, buffer, sent, arrived

    def copy(self, block, way):
        to = self.row + 1 if way == 0 else self.row - 1
        here = self.buffer.at[block]
        return remote(here, here, self.sent.at[block, way], self.arrived.at[block], {"row": to})

    def each(self, block, act):
        @pl.when(jnp.logical_and(block <= self.row, self.row < ROWS - 1))
        def _():
            act(self.copy(block, 0))

        @pl.when(jnp.logical_and(block >= self.row, self.row > 0))
        def _():
            act(self.copy(block, 1))

    def wait(self, block):
        self.copy(block, 0).wait_recv()

    def pass_on(self, block):
        self.each(block, lambda copy: copy.start())

    def finish(self):
        def one(block, carried):
            self.each(block, lambda copy: copy.wait_send())
            return carried

        lax.fori_loop(0, ROWS, one, 0)


class SquareRest:
    def __init__(self, place, kept, got, middle, second, result, sent, arrived):
        self.x, self.y = lax.rem(place, 2), lax.div(place, 2)
        self.to_x, self.to_y = {"dp": partner(place, 1)}, {"dp": partner(place, 2)}
        self.kept, self.got = kept, got
        self.middle, self.second, self.result = middle, second, result
        self.sent, self.arrived = sent, arrived

    def copies(self, phase):
        x, y = self.x, self.y
        if phase == 1:
            plan = (
                (self.middle.at[0], self.second.at[0], self.to_y),
                (self.middle.at[1], self.second.at[1], self.to_x),
            )
        elif phase == 2:
            one, two = self.result.at[2 * x + y], self.result.at[4 + 2 * y + x]
            plan = ((one, one, self.to_y), (two, two, self.to_x))
        else:
            one, two = self.result.at[pl.ds(2 * x, 2)], self.result.at[pl.ds(4 + 2 * y, 2)]
            plan = ((one, one, self.to_x), (two, two, self.to_y))
        return [
            remote(source, target, self.sent.at[2 * phase + i], self.arrived.at[2 * phase + i], to)
            for i, (source, target, to) in enumerate(plan)
        ]

    def sum_of(self, half, side):
        wide = self.middle.shape[3]
        lanes = pl.ds(pl.multiple_of(side * wide, 128), wide)
        return self.kept[half, :, :, lanes].astype(f32) + self.got[half, :, :, lanes].astype(f32)

    def run(self, phase):
        x, y = self.x, self.y
        if phase > 1:
            for copy in self.copies(phase - 1):
                copy.wait_recv()
        if phase == 1:
            self.middle[0] = self.sum_of(0, 1 - y).astype(bf16)
            self.middle[1] = self.sum_of(1, 1 - x).astype(bf16)
        if phase == 2:
            self.result[2 * x + y] = (self.sum_of(0, y) + self.second[0].astype(f32)).astype(bf16)
            self.result[4 + 2 * y + x] = (
                self.sum_of(1, x) + self.second[1].astype(f32)
            ).astype(bf16)
        if phase < 4:
            for copy in self.copies(phase):
                copy.start()

    def finish(self):
        for phase in (1, 2, 3):
            for copy in self.copies(phase):
                copy.wait_send()


class SumLine:
    def __init__(self, row, part, leaving, coming, sent, arrived):
        self.row, self.part, self.leaving, self.coming = row, part, leaving, coming
        self.sent, self.arrived = sent, arrived
        self.lines = part.shape[1] // SPLIT

    def piece(self, index):
        return pl.ds(index * self.lines, self.lines)

    def copy(self, block, index, way):
        return remote(
            self.leaving.at[block, self.piece(index)],
            self.coming.at[way, block, self.piece(index)],
            self.sent.at[block, index],
            self.arrived.at[way, block, index],
            {"row": self.row + 1 - 2 * way},
        )

    def send(self, block, index):
        @pl.when(block > self.row)
        def _():
            self.copy(block, index, 0).start()

        @pl.when(block < self.row)
        def _():
            self.copy(block, index, 1).start()

    def chained(self, block):
        return jnp.logical_or(
            jnp.logical_and(block > self.row, self.row > 0),
            jnp.logical_and(block < self.row, self.row < ROWS - 1),
        )

    def begin(self, block):
        @pl.when(jnp.logical_and(block != self.row, jnp.logical_not(self.chained(block))))
        def _():
            self.leaving[block] = self.part[block].astype(bf16)
            for index in range(SPLIT):
                self.send(block, index)

    def pass_on(self, block):
        @pl.when(self.chained(block))
        def _():
            way = (block < self.row).astype(jnp.int32)
            for index in range(SPLIT):
                self.copy(block, index, way).wait_recv()
                piece = self.piece(index)
                self.leaving[block, piece] = (
                    self.part[block, piece] + self.coming[way, block, piece].astype(f32)
                ).astype(bf16)
                self.send(block, index)

    def total(self, target):
        target[...] = self.part[self.row]
        for way, there in ((0, self.row > 0), (1, self.row < ROWS - 1)):

            @pl.when(there)
            def _(way=way):
                for index in range(SPLIT):
                    self.copy(self.row, index, way).wait_recv()
                    target[self.piece(index)] += self.coming[
                        way, self.row, self.piece(index)
                    ].astype(f32)

    def finish(self):
        def one(block, carried):
            @pl.when(block != self.row)
            def _():
                for index in range(SPLIT):
                    self.copy(block, index, 0).wait_send()

            return carried

        lax.fori_loop(0, ROWS, one, 0)


def swap_halves(values):
    lanes = values.shape[1]
    lane = lax.broadcasted_iota(jnp.int32, values.shape, 1)
    return jnp.where(
        lane % ROPE < ROPE // 2,
        pltpu.roll(values, lanes - ROPE // 2, 1),
        pltpu.roll(values, ROPE // 2, 1),
    )


def attend_kernel(
    act_ref,
    scaling_ref,
    compress_ref,
    rescale_ref,
    premix_ref,
    cos_ref,
    sin_ref,
    key_cos_ref,
    key_sin_ref,
    mark_ref,
    cot_ref,
    route_ref,
    router_ref,
    queries_ref,
    expand_ref,
    combine_ref,
    one_out,
    query_out,
    key_out,
    value_out,
    probs_out,
    latent_out,
    normed_latent_out,
    attended_out,
    compress_out,
    cot_out,
    pick_out,
    back_out,
    rows_out,
    residual_ref,
    two_ref,
    scale_one_ref,
    scale_two_ref,
    router_all,
    one_ref,
    query_ref,
    key_ref,
    value_ref,
    probs_ref,
    latent_ref,
    normed_latent_ref,
    attended_ref,
    compress_all,
    cot_all,
    pick_ref,
    back_ref,
    rows_ref,
    queries,
    expand,
    combine,
    stat_to,
    stat_from,
    query_own,
    query_to,
    query_from,
    latent_to,
    latent_from,
    part,
    leaving,
    coming,
    routes,
    staged,
    marks,
    load_sem,
    store_sem,
    rows_sem,
    stat_sent,
    stat_arrived,
    line_sent,
    line_arrived,
    comp_sent,
    comp_arrived,
    comp_out_sent,
    comp_out_arrived,
    query_sent,
    query_arrived,
    latent_sent,
    latent_arrived,
    att_sent,
    att_arrived,
    sum_sent,
    sum_arrived,
    cot_sent,
    cot_arrived,
    route_sent,
    route_arrived,
    out_sent,
    out_arrived,
    pair_sent,
    pair_arrived,
    router_sent,
    router_arrived,
):
    place, row, col = lax.axis_index("dp"), lax.axis_index("row"), lax.axis_index("col")
    other = 1 - col
    inner = jnp.logical_and(row > 0, row < ROWS - 1)
    sibling = {"col": other}
    tokens, width = act_ref.shape
    slots = pick_ref.shape[1] // SQUARE
    mine = query_own.shape[2]
    sliced = compress_ref.shape[0]
    quarter = width // SQUARE
    score_scale = (NOPE + ROPE) ** (-0.5)
    loads = [
        pltpu.make_async_copy(source, target, load_sem.at[i])
        for i, (source, target) in enumerate(
            [(queries_ref, queries), (expand_ref, expand), (combine_ref, combine)]
        )
    ]
    for load in loads:
        load.start()
    stores = [
        pltpu.make_async_copy(source, target, store_sem.at[i])
        for i, (source, target) in enumerate(
            [
                (one_ref, one_out),
                (query_ref, query_out),
                (key_ref, key_out),
                (value_ref, value_out),
                (latent_ref, latent_out),
                (normed_latent_ref, normed_latent_out),
                (compress_all, compress_out),
                (probs_ref, probs_out),
                (attended_ref, attended_out),
                (cot_all, cot_out),
                (pick_ref, pick_out),
                (back_ref, back_out),
            ]
        )
    ]

    def rows_store(block):
        return pltpu.make_async_copy(
            rows_ref.at[:, block], rows_out.at[:, block], rows_sem.at[block]
        )

    def stat_copy(index):
        return remote(
            stat_to.at[index],
            stat_from.at[index],
            stat_sent.at[index],
            stat_arrived.at[index],
            sibling,
        )

    def scale_of(values, index):
        own = jnp.sum(values * values, axis=1, keepdims=True)
        stat_to[index] = jnp.broadcast_to(own, (tokens, 128))
        stat_copy(index).start()
        stat_copy(index).wait_recv()
        return lax.rsqrt((own + stat_from[index][:, 0:1]) / D + epsilon)

    def comp_piece(block, member):
        return compress_all.at[
            pl.ds(pl.multiple_of(block * sliced, 16), sliced),
            pl.ds(pl.multiple_of(member * quarter, 128), quarter),
        ]

    def comp_copy(block, way):
        here = comp_piece(block, place)
        return remote(
            here,
            here,
            comp_sent.at[block, way],
            comp_arrived.at[block],
            {"row": row + 1 - 2 * way},
        )

    def comp_each(block, act):
        @pl.when(jnp.logical_and(block <= row, row < ROWS - 1))
        def _():
            act(comp_copy(block, 0))

        @pl.when(jnp.logical_and(block >= row, row > 0))
        def _():
            act(comp_copy(block, 1))

    def comp_out(block, step, member):
        here = comp_piece(block, member)
        return remote(
            here,
            here,
            comp_out_sent.at[block, step],
            comp_out_arrived.at[block, step],
            {"dp": partner(place, step)},
        )

    line = Line(row, one_ref, line_sent, line_arrived)
    cot_line = Line(row, cot_all, cot_sent, cot_arrived)
    route_line = Line(row, routes, route_sent, route_arrived)
    sums = SumLine(row, part, leaving, coming, sum_sent, sum_arrived)

    greet(row, place, col)
    compress_all[pl.ds(pl.multiple_of(row * sliced, 16), sliced)] = compress_ref[...]
    compress_all[ROWS * sliced :] = jnp.zeros(
        (compress_all.shape[0] - ROWS * sliced, width), bf16
    )
    comp_each(row, lambda copy: copy.start())

    def router_copy(half):
        here = router_all.at[:, pl.ds(pl.multiple_of(half * width, width), width)]
        return remote(here, here, router_sent.at[0], router_arrived.at[0], sibling)

    router_all[:, pl.ds(pl.multiple_of(col * width, width), width)] = router_ref[...]
    inputs = act_ref[...].astype(f32)
    scale_one = scale_of(inputs, 0)
    scale_one_ref[...] = scale_one
    one_ref[pl.ds(row, 1)] = (
        (inputs * scale_one * scaling_ref[...]).astype(bf16).reshape(1, tokens, width)
    )
    cot_all[pl.ds(row, 1)] = cot_ref[...].reshape(1, tokens, width)
    routes[pl.ds(row, 1)] = route_ref[...].reshape((1,) + route_ref.shape)
    line.pass_on(row)
    router_copy(col).start()

    @pl.when(jnp.logical_not(inner))
    def _():
        route_line.pass_on(row)
        cot_line.pass_on(row)

    for block in range(ROWS):
        mark = mark_ref[:, block * tokens : (block + 1) * tokens].astype(f32)
        marks[block] = jnp.broadcast_to(mark, (8, tokens)).T
    loads[0].wait()

    def query_copy(block):
        return remote(
            query_to.at[block],
            query_from.at[block],
            query_sent.at[block],
            query_arrived.at[block],
            sibling,
        )

    def latent_copy(block):
        return remote(
            latent_to.at[block],
            latent_from.at[block],
            latent_sent.at[block],
            latent_arrived.at[block],
            sibling,
        )

    def att_copy(block, half):
        here = attended_ref.at[block, :, pl.ds(pl.multiple_of(half * 2 * HEADV, 128), 2 * HEADV)]
        return remote(here, here, att_sent.at[block], att_arrived.at[block], sibling)

    def gather(step, carried):
        block = block_at(row, step)

        @pl.when(step > 0)
        def _():
            comp_copy(block, 0).wait_recv()
            comp_each(block, lambda copy: copy.start())
            for shift in (3, 2, 1):
                comp_out(block, shift, place).start()
            line.wait(block)
            line.pass_on(block)

        tokens_here = one_ref[block]
        query_to[block] = nn(
            tokens_here, queries[:, pl.ds(pl.multiple_of(other * mine, 128), mine)]
        ).astype(bf16)
        query_copy(block).start()
        query_own[block] = nn(tokens_here, queries[:, pl.ds(pl.multiple_of(col * mine, 128), mine)])
        return carried

    lax.fori_loop(0, ROWS, gather, 0)

    @pl.when(inner)
    def _():
        route_line.pass_on(row)
        cot_line.pass_on(row)

    def relay(step):
        block = block_at(row, step)
        route_line.wait(block)
        route_line.pass_on(block)
        cot_line.wait(block)
        cot_line.pass_on(block)

    def out_copy(block, step):
        piece = pl.ds(step * slots, slots)
        return remote(
            staged.at[block, piece],
            rows_ref.at[col, block, piece],
            out_sent.at[block, step],
            out_arrived.at[block, step],
            {"dp": partner(place, step)},
        )

    def pair_copy(block, half):
        here = rows_ref.at[half, block]
        return remote(here, here, pair_sent.at[block], pair_arrived.at[block], sibling)

    def take(step):
        block = block_at(row, step)

        @pl.when(jnp.logical_and(step > 0, jnp.logical_not(inner)))
        def _():
            relay(step)

        before = (
            lax.broadcasted_iota(jnp.int32, (tokens, tokens), 0)
            < lax.broadcasted_iota(jnp.int32, (tokens, tokens), 1)
        ).astype(bf16)
        routing = routes[block]
        chosen = []
        for shift in range(SQUARE):
            expert = partner(place, shift) * ROWS + row
            hit = (routing == expert).astype(f32)
            chosen.append(jnp.max(hit, axis=0, keepdims=True))
        goes = jnp.concatenate(chosen + chosen, axis=0)
        rank = nn(goes.astype(bf16), before)
        for shift in range(SQUARE):
            slot = lax.broadcasted_iota(jnp.int32, (slots, tokens), 0).astype(f32)
            here = jnp.logical_and(slot == rank[shift : shift + 1], goes[shift : shift + 1] > 0.5)
            pick = here.astype(f32)
            pick_ref[block, shift * slots : (shift + 1) * slots] = pick.astype(bf16)
            back_ref[block, :, shift * slots : (shift + 1) * slots] = pick.T.astype(bf16)
        staged[block] = nn(pick_ref[block], cot_all[block]).astype(bf16)
        for shift in (3, 2, 1):
            out_copy(block, shift).start()
        rows_ref[col, block, 0:slots] = staged[block, 0:slots]

    def forward(step):
        block = block_at(row, step)
        for shift in range(1, SQUARE):
            out_copy(block, shift).wait_recv()
        pair_copy(block, col).start()

    def comp_arrive(block, carried):
        @pl.when(block != row)
        def _():
            for shift in range(1, SQUARE):
                comp_out(block, shift, partner(place, shift)).wait_recv()

        return carried

    lax.fori_loop(0, ROWS, comp_arrive, 0)

    def latents(block, carried):
        value = nt(one_ref[block], compress_all[...])
        latent_to[block] = value
        latent_copy(block).start()
        latent_ref[block] = value
        return carried

    lax.fori_loop(0, ROWS, latents, 0)
    take(0)

    @pl.when(inner)
    def _():
        relay(1)
        relay(2)

    loads[1].wait()

    def keys(block, carried):
        latent_copy(block).wait_recv()
        latent = latent_ref[block] + latent_from[block]
        latent_ref[block] = latent
        plain = latent[:, :RANK]
        scale = lax.rsqrt(jnp.mean(plain * plain, axis=1, keepdims=True) + epsilon)
        normed = (plain * scale * rescale_ref[...]).astype(bf16)
        normed_latent_ref[block] = normed
        own = 2 * (NOPE + HEADV)
        expanded = nn(normed, expand[:, pl.ds(pl.multiple_of(col * own, 128), own)])
        rope = latent[:, RANK:]
        rope = rope * key_cos_ref[block] + swap_halves(rope) * key_sin_ref[block]
        first = jnp.concatenate([expanded[:, :NOPE], rope], axis=1)
        second = jnp.concatenate([expanded[:, 2 * NOPE : 3 * NOPE], rope], axis=1)
        key_ref[0, block] = first.astype(bf16)
        key_ref[1, block] = pltpu.roll(second, ROPE, 1).astype(bf16)
        value_ref[0, block] = expanded[:, NOPE : 2 * NOPE].astype(bf16)
        value_ref[1, block] = expanded[:, 3 * NOPE :].astype(bf16)
        query_copy(block).wait_recv()
        query = query_own[block] + query_from[block].astype(f32)
        query_ref[block] = (
            query * cos_ref[block] + swap_halves(query) * sin_ref[block]
        ).astype(bf16)
        return carried

    lax.fori_loop(0, ROWS, keys, 0)
    for index in range(7):
        stores[index].start()
    seq = ROWS * tokens
    lanes = NOPE + 2 * ROPE

    def attend(turn, carried):
        block = block_at(row, ROWS - 1 - turn)
        visible = mark_ref[...].astype(f32) <= marks[block][:, 0:1]
        for head in range(2):
            query = query_ref[block, :, head * NOPE : head * NOPE + lanes]
            scores = nt(query, key_ref[head].reshape(seq, lanes)) * score_scale
            scores = jnp.where(visible, scores, masked_score)
            weight = jnp.exp(scores - jnp.max(scores, axis=1, keepdims=True))
            probs = (weight / jnp.sum(weight, axis=1, keepdims=True)).astype(bf16)
            probs_ref[head, block] = probs
            result = nn(probs, value_ref[head].reshape(seq, HEADV)).astype(bf16)
            at = pl.multiple_of((col * 2 + head) * HEADV, 128)
            attended_ref[block, :, pl.ds(at, HEADV)] = result
        att_copy(block, col).start()

        @pl.when(jnp.logical_and(turn == 0, inner))
        def _():
            relay(3)

        @pl.when(turn > 0)
        def _():
            mix(turn - 1)
            take(turn)

        return carried

    def mix(turn):
        block = block_at(row, ROWS - 1 - turn)
        att_copy(block, other).wait_recv()
        part[block] = nn(attended_ref[block], combine[...])
        sums.begin(block)

    loads[2].wait()
    lax.fori_loop(0, ROWS, attend, 0)
    mix(ROWS - 1)
    for index in range(7, 12):
        stores[index].start()

    def hand_on(turn, carried):
        sums.pass_on(block_at(row, jnp.where(turn == 0, 3, turn)))
        forward(turn)
        return carried

    lax.fori_loop(0, 3, hand_on, 0)
    sums.total(residual_ref)
    residual = residual_ref[...] + inputs
    residual_ref[...] = residual
    scale_two = scale_of(residual, 1)
    scale_two_ref[...] = scale_two
    two_ref[...] = (residual * scale_two * premix_ref[...]).astype(bf16)
    forward(3)

    def ended(block, carried):
        pair_copy(block, other).wait_recv()
        rows_store(block).start()
        pair_copy(block, col).wait_send()
        for shift in range(1, SQUARE):
            out_copy(block, shift).wait_send()

            @pl.when(block != row)
            def _(shift=shift):
                comp_out(block, shift, place).wait_send()

        comp_each(block, lambda copy: copy.wait_send())
        query_copy(block).wait_send()
        latent_copy(block).wait_send()
        att_copy(block, col).wait_send()
        return carried

    lax.fori_loop(0, ROWS, ended, 0)
    for store in stores:
        store.wait()

    def stored(block, carried):
        rows_store(block).wait()
        return carried

    lax.fori_loop(0, ROWS, stored, 0)
    router_copy(other).wait_recv()
    router_copy(col).wait_send()
    stat_copy(0).wait_send()
    stat_copy(1).wait_send()
    sums.finish()
    line.finish()
    cot_line.finish()
    route_line.finish()


def turning_tables(length):
    half = ROPE // 2
    frequency = 10000.0 ** (-np.arange(half, dtype=np.float32) * 2.0 / ROPE)
    angles = np.arange(length, dtype=np.float32)[:, None] * frequency[None, :].astype(np.float32)
    cosine, sine = np.cos(angles), np.sin(angles)
    cosine, sine = np.concatenate([cosine, cosine], 1), np.concatenate([-sine, sine], 1)
    ones, zeros = np.ones((length, NOPE)), np.zeros((length, NOPE))
    gap = np.zeros((length, 128 - ROPE))
    tables = (
        np.concatenate([ones, cosine, ones, cosine], 1),
        np.concatenate([zeros, sine, zeros, sine], 1),
        np.concatenate([cosine, gap], 1),
        np.concatenate([sine, gap], 1),
    )
    return [
        jnp.asarray(table.reshape(ROWS, length // ROWS, -1).astype(np.float32))
        for table in tables
    ]


def pair_sems():
    return [DMA((ROWS,)), DMA((ROWS,))]


def line_sems():
    return [DMA((ROWS, 2)), DMA((ROWS,))]


def square_sems():
    return [DMA((ROWS, SQUARE)), DMA((ROWS, SQUARE))]


def sum_sems():
    return [DMA((ROWS, SPLIT)), DMA((2, ROWS, SPLIT))]


def run_attention(
    activations,
    scaling,
    queries,
    compress,
    rescale,
    expand,
    combine,
    premix,
    segments,
    cotangent,
    routing,
    router,
    tables,
    slots,
):
    tokens, width = activations.shape
    seq = ROWS * tokens
    mine = queries.shape[1] // COLS
    sliced = compress.shape[1]
    latent_width = RANK + 128
    picked = SQUARE * slots
    lanes = NOPE + 2 * ROPE
    routes = routing.T
    whole = pl.BlockSpec(memory_space=VMEM)
    far = pl.BlockSpec(memory_space=pl.ANY)

    def shape(*dims, dtype=bf16):
        return jax.ShapeDtypeStruct(dims, dtype)

    kept = [
        shape(ROWS, tokens, width),
        shape(ROWS, tokens, mine),
        shape(2, ROWS, tokens, lanes),
        shape(2, ROWS, tokens, HEADV),
        shape(2, ROWS, tokens, seq),
        shape(ROWS, tokens, latent_width, dtype=f32),
        shape(ROWS, tokens, RANK),
        shape(ROWS, tokens, COLS * 2 * HEADV),
        shape(latent_width, width),
        shape(ROWS, tokens, width),
        shape(ROWS, picked, tokens),
        shape(ROWS, tokens, picked),
        shape(COLS, ROWS, picked, width),
    ]
    return pl.pallas_call(
        attend_kernel,
        name="attend",
        out_shape=(
            *kept,
            shape(tokens, width, dtype=f32),
            shape(tokens, width),
            shape(tokens, 1, dtype=f32),
            shape(tokens, 1, dtype=f32),
            shape(router.shape[1], COLS * width),
        ),
        in_specs=[whole] * 13 + [far] * 3,
        out_specs=(far,) * 13 + (whole,) * 5,
        scratch_shapes=[
            *[VMEM(value.shape, value.dtype) for value in kept],
            VMEM(queries.shape, bf16),
            VMEM(expand.shape, bf16),
            VMEM(combine.shape, bf16),
            VMEM((2, tokens, 128), f32),
            VMEM((2, tokens, 128), f32),
            VMEM((ROWS, tokens, mine), f32),
            VMEM((ROWS, tokens, mine), bf16),
            VMEM((ROWS, tokens, mine), bf16),
            VMEM((ROWS, tokens, latent_width), f32),
            VMEM((ROWS, tokens, latent_width), f32),
            VMEM((ROWS, tokens, width), f32),
            VMEM((ROWS, tokens, width), bf16),
            VMEM((2, ROWS, tokens, width), bf16),
            VMEM((ROWS,) + routes.shape, jnp.int32),
            VMEM((ROWS, picked, width), bf16),
            VMEM((ROWS, tokens, 8), f32),
            DMA((3,)),
            DMA((12,)),
            DMA((ROWS,)),
            DMA((2,)),
            DMA((2,)),
            *line_sems(),
            *line_sems(),
            *square_sems(),
            *pair_sems(),
            *pair_sems(),
            *pair_sems(),
            *sum_sems(),
            *line_sems(),
            *line_sems(),
            *square_sems(),
            *pair_sems(),
            DMA((1,)),
            DMA((1,)),
        ],
        compiler_params=pltpu.CompilerParams(
            collective_id=1, has_side_effects=True, vmem_limit_bytes=56 * MIB
        ),
        cost_estimate=pl.CostEstimate(
            flops=40 * 1024**3, bytes_accessed=32 * MIB, transcendentals=0
        ),
    )(
        activations,
        scaling.reshape(1, width),
        compress.T,
        rescale.reshape(1, RANK),
        premix.reshape(1, width),
        *tables,
        segments.reshape(1, seq),
        cotangent,
        routes,
        router.T,
        queries,
        expand,
        combine,
    )


def attend_back_kernel(
    normed_grad_ref,
    residual_ref,
    scale_two_ref,
    premix_ref,
    cot_ref,
    act_ref,
    scale_one_ref,
    scaling_ref,
    rescale_ref,
    combine_far,
    query_far,
    key_far,
    value_far,
    probs_far,
    cos_far,
    sin_far,
    queries_far,
    expand_far,
    latent_far,
    key_cos_far,
    key_sin_far,
    compress_far,
    one_far,
    kept_far,
    got_x_far,
    got_y_far,
    attended_far,
    normed_latent_far,
    narrow_far,
    home_far,
    back_far,
    shared_far,
    premix_far,
    router_far,
    input_grad_ref,
    output_ref,
    small_ref,
    shared_sum,
    queries_out,
    combine_out,
    expand_out,
    compress_out,
    branch_ref,
    query_grad_ref,
    expanded_ref,
    own_latent_ref,
    scaling_rows,
    rescale_rows,
    combine,
    query_ref,
    key_ref,
    value_ref,
    probs_ref,
    cos_ref,
    sin_ref,
    queries,
    expand,
    latent_ref,
    key_cos_ref,
    key_sin_ref,
    compress_all,
    one_ref,
    kept,
    got,
    middle,
    second,
    result,
    attended,
    normed_latent,
    narrow,
    home,
    back_ref,
    shared_ref,
    premix_rows,
    router_rows,
    stat_to,
    stat_from,
    grad_own,
    grad_to,
    grad_from,
    key_grad,
    value_grad,
    latent_own,
    latent_to,
    latent_from,
    turned,
    turned_from,
    part,
    leaving,
    coming,
    total,
    load_sem,
    stat_sent,
    stat_arrived,
    line_sent,
    line_arrived,
    grad_sent,
    grad_arrived,
    query_sent,
    query_arrived,
    latent_sent,
    latent_arrived,
    turned_sent,
    turned_arrived,
    own_sent,
    own_arrived,
    sum_sent,
    sum_arrived,
    rest_sent,
    rest_arrived,
    rest_sem,
    reply_coming,
    small_to,
    small_from,
    small_line,
    small_square,
    small_own,
    expand_other,
    store_sem,
    reply_sent,
    reply_arrived,
    pair_sent,
    pair_arrived,
    small_sent,
    small_arrived,
    *sums_scratch,
):
    place, row, col = lax.axis_index("dp"), lax.axis_index("row"), lax.axis_index("col")
    other = 1 - col
    sibling = {"col": other}
    tokens, width = act_ref.shape
    seq = ROWS * tokens
    mine = query_ref.shape[2]
    lanes = key_ref.shape[3]
    both = 2 * HEADV
    sliced = own_latent_ref.shape[0]
    score_scale = (NOPE + ROPE) ** (-0.5)
    loads = [
        pltpu.make_async_copy(source, target, load_sem.at[i])
        for i, (source, target) in enumerate(
            [
                (combine_far, combine),
                (query_far, query_ref),
                (key_far, key_ref),
                (value_far, value_ref),
                (probs_far, probs_ref),
                (cos_far, cos_ref),
                (sin_far, sin_ref),
                (queries_far, queries),
                (expand_far, expand),
                (latent_far, latent_ref),
                (key_cos_far, key_cos_ref),
                (key_sin_far, key_sin_ref),
                (compress_far, compress_all),
                (one_far, one_ref),
                (kept_far, kept),
                (got_x_far, got.at[0]),
                (got_y_far, got.at[1]),
                (attended_far, attended),
                (normed_latent_far, normed_latent),
                (narrow_far, narrow),
                (home_far, home),
                (back_far, back_ref),
                (shared_far, shared_ref),
                (premix_far, premix_rows),
                (router_far, router_rows),
            ]
        )
    ]
    for load in loads:
        load.start()
    line = Line(row, branch_ref, line_sent, line_arrived)
    sums = SumLine(row, part, leaving, coming, sum_sent, sum_arrived)
    greet(row, place, col, line=True)

    def stat_copy(index):
        return remote(
            stat_to.at[index],
            stat_from.at[index],
            stat_sent.at[index],
            stat_arrived.at[index],
            sibling,
        )

    def norm_grad(values, scale, gain, upstream, index):
        weighted = upstream * gain
        own = jnp.sum(weighted * values, axis=1, keepdims=True)
        stat_to[index] = jnp.broadcast_to(own, (tokens, 128))
        stat_copy(index).start()
        stat_copy(index).wait_recv()
        inner = (own + stat_from[index][:, 0:1]) / D
        return weighted * scale - values * (scale * scale * scale * inner)

    residual_grad = cot_ref[...].astype(f32) + norm_grad(
        residual_ref[...], scale_two_ref[...], premix_ref[...], normed_grad_ref[...], 0
    )
    input_grad_ref[...] = residual_grad
    branch_ref[pl.ds(row, 1)] = residual_grad.astype(bf16).reshape(1, tokens, width)
    line.pass_on(row)
    key_grad[...] = jnp.zeros_like(key_grad)
    value_grad[...] = jnp.zeros_like(value_grad)
    scaling_rows[...] = jnp.zeros_like(scaling_rows)
    rescale_rows[...] = jnp.zeros_like(rescale_rows)

    rest = SquareRest(place, kept, got, middle, second, result, rest_sent, rest_arrived)

    line_sums = SumLine(
        row, part, leaving, reply_coming, reply_sent, reply_arrived
    )
    experts = router_rows.shape[0]
    kinds = [sums_scratch[7 * i : 7 * i + 7] for i in range(4)]
    parts = [scratch[0] for scratch in kinds]
    plan = [(kind, chunk) for kind in range(4) for chunk in range(parts[kind].shape[0])]
    pieces_of = [
        SquareSum(place, *[ref.at[chunk] for ref in kinds[kind]]) for kind, chunk in plan
    ]
    count = len(plan)

    def begin(index):
        kind, chunk = plan[index]
        part_ref = parts[kind]
        if kind == 0 and chunk == 0:
            loads[17].wait()
        if kind == 2:
            loads[18].wait()
        if kind < 2:
            left, right = ((attended, branch_ref), (one_ref, query_grad_ref))[kind]
            height = 8 * part_ref.shape[2]
            piece = left[:, :, chunk * height : (chunk + 1) * height].reshape(seq, height)
            grad = tn(piece, right[...].reshape(seq, right.shape[2]))
        elif kind == 2:
            grad = tn(
                normed_latent[...].reshape(seq, RANK),
                expanded_ref[...].reshape(seq, expanded_ref.shape[2]),
            )
        else:
            grad = nn(own_latent_ref[...], one_ref[...].reshape(seq, width)).astype(bf16)
            for piece in range(8):
                part_ref[0, piece] = grad[:, piece * (width // 8) : (piece + 1) * (width // 8)]
        if kind < 3:
            part_ref[chunk] = grad.astype(bf16).reshape(part_ref.shape[1:])
        pieces_of[index].run(0)

    stores = []

    def store(source, target):
        copy = pltpu.make_async_copy(source, target, store_sem.at[len(stores)])
        copy.start()
        stores.append(copy)

    def pair_copy():
        return remote(kinds[2][4].at[0], expand_other, pair_sent.at[0], pair_arrived.at[0], sibling)

    def expand_lanes(half):
        wide = expand_other.shape[2]
        return expand_out.at[:, :, pl.ds(pl.multiple_of(half * wide, 128), wide)]

    def put(index):
        kind, chunk = plan[index]
        done = kinds[kind][4]
        if kind < 2:
            store(done.at[chunk], (combine_out, queries_out)[kind].at[chunk])
        elif kind == 2:
            store(done.at[0], expand_lanes(col))
            pair_copy().start()
        else:
            lanes = width // 8
            for piece in range(8):
                store(done.at[0, piece], compress_out.at[:, piece * lanes : (piece + 1) * lanes])

    def advance(turn):
        for phase in (1, 2, 3, 4):
            index = turn - phase
            if 0 <= index < count:
                pieces_of[index].run(phase)
                if phase == 4:
                    put(index)
        if 2 <= turn < count:
            begin(turn)

    def reply_add(turn, carried):
        block = block_at(row, ROWS - 1 - turn)
        part[block] = nn(back_ref[block], home[block]) + nn(shared_ref[block], narrow[...])
        line_sums.begin(block)
        return carried

    def small_copy(step):
        if step == 0:
            return remote(small_to, small_from, small_sent.at[0], small_arrived.at[0], sibling)
        if step < ROWS:
            return remote(
                small_own,
                small_line.at[step],
                small_sent.at[step],
                small_arrived.at[step],
                {"row": lax.rem(row + step, ROWS)},
            )
        shift = step - ROWS + 1
        return remote(
            small_ref,
            small_square.at[shift],
            small_sent.at[step],
            small_arrived.at[step],
            {"dp": partner(place, shift)},
        )

    def small_begin():
        loads[23].wait()
        loads[24].wait()
        rescale_row = jnp.sum(rescale_rows[...], axis=0, keepdims=True)
        empty = jnp.zeros((small_own.shape[0] - experts, width), f32)
        small_to[0:experts] = router_rows[:, pl.ds(pl.multiple_of(other * width, width), width)]
        small_to[experts:] = empty
        small_to[experts + 2 : experts + 3, 0:RANK] = rescale_row
        small_copy(0).start()
        small_own[0:experts] = router_rows[:, pl.ds(pl.multiple_of(col * width, width), width)]
        small_own[experts:] = empty
        small_own[experts : experts + 1] = (
            jnp.sum(premix_rows[...], axis=0, keepdims=True) / premix_ref[...]
        )
        small_own[experts + 1 : experts + 2] = (
            jnp.sum(scaling_rows[...], axis=0, keepdims=True) / scaling_ref[...]
        )
        small_own[experts + 2 : experts + 3, 0:RANK] = rescale_row

    def small_line_begin():
        small_copy(0).wait_recv()
        small_own[...] += small_from[...]
        for step in range(1, ROWS):
            small_copy(step).start()

    def small_square_begin():
        for step in range(1, ROWS):
            small_copy(step).wait_recv()
        small_ref[...] = small_own[...] + small_line[1] + small_line[2] + small_line[3]
        for step in range(ROWS, ROWS + SQUARE - 1):
            small_copy(step).start()

    def small_end():
        for step in range(ROWS, ROWS + SQUARE - 1):
            small_copy(step).wait_recv()
        for step in range(ROWS, ROWS + SQUARE - 1):
            small_copy(step).wait_send()
        small_ref[...] += small_square[1] + small_square[2] + small_square[3]

    def reply_begin():
        for load in loads[19:23]:
            load.wait()
        lax.fori_loop(0, ROWS, reply_add, 0)

    def reply_pass():
        lax.fori_loop(0, 3, line_pass, 0)

    def reply_end():
        line_sums.total(total)
        output_ref[...] = (total[...] + residual_ref[...]).astype(bf16)

    def line_pass(turn, carried):
        line_sums.pass_on(block_at(row, jnp.where(turn == 0, 3, turn)))
        return carried

    def grad_copy(block):
        return remote(
            grad_to.at[block],
            grad_from.at[block],
            grad_sent.at[block],
            grad_arrived.at[block],
            sibling,
        )

    def query_copy(block, half):
        here = query_grad_ref.at[block, :, pl.ds(pl.multiple_of(half * mine, 128), mine)]
        return remote(here, here, query_sent.at[block], query_arrived.at[block], sibling)

    def latent_copy(block):
        return remote(
            latent_to.at[block],
            latent_from.at[block],
            latent_sent.at[block],
            latent_arrived.at[block],
            sibling,
        )

    def arrive(step):
        block = block_at(row, step)

        @pl.when(step > 0)
        def _():
            line.wait(block)
            line.pass_on(block)

        @pl.when(step == 0)
        def _():
            for load in loads[14:17]:
                load.wait()
            rest.run(1)
            loads[0].wait()

        grads = branch_ref[block]
        grad_to[block] = nt(
            grads, combine[pl.ds(pl.multiple_of(other * both, 16), both)]
        ).astype(bf16)
        grad_copy(block).start()
        grad_own[block] = nt(grads, combine[pl.ds(pl.multiple_of(col * both, 16), both)])

    def heads(step):
        block = block_at(row, step)

        @pl.when(step == 0)
        def _():
            for load in loads[1:7]:
                load.wait()

        grad_copy(block).wait_recv()
        grads = (grad_own[block] + grad_from[block].astype(f32)).astype(bf16)
        pieces = []
        for head in range(2):
            upstream = grads[:, head * HEADV : (head + 1) * HEADV]
            query = query_ref[block, :, head * NOPE : head * NOPE + lanes]
            probs = probs_ref[head, block]
            weight = probs.astype(f32)
            probs_back = nt(upstream, value_ref[head].reshape(seq, HEADV))
            inner = jnp.sum(weight * probs_back, axis=1, keepdims=True)
            score_grad = (weight * (probs_back - inner)).astype(bf16)
            pieces.append(nn(score_grad, key_ref[head].reshape(seq, lanes)) * score_scale)
            key_grad[head] += tn(score_grad, query)
            value_grad[head] += tn(probs, upstream)
        first, second = pieces
        grad = jnp.concatenate(
            [first[:, :NOPE], first[:, NOPE:] + second[:, :NOPE], second[:, NOPE:]], axis=1
        )
        grad = grad * cos_ref[block] - swap_halves(grad) * sin_ref[block]
        query_grad_ref[block, :, pl.ds(pl.multiple_of(col * mine, 128), mine)] = grad.astype(bf16)
        query_copy(block, col).start()

    def project(step):
        block = block_at(row, step)

        @pl.when(step == 0)
        def _():
            loads[7].wait()

        query_copy(block, other).wait_recv()
        part[block] = nt(query_grad_ref[block], queries[...])

    def turn(step, carried):
        for delay, stage in ((0, arrive), (1, heads), (2, project)):

            @pl.when(jnp.logical_and(step >= delay, step < delay + ROWS))
            def _(delay=delay, stage=stage):
                stage(step - delay)

        @pl.when(step == 2)
        def _():
            rest.run(2)

        return carried

    lax.fori_loop(0, ROWS + 1, turn, 0)
    for load in loads[8:14]:
        load.wait()
    begin(0)
    begin(1)

    def latents(turn, carried):
        block = block_at(row, ROWS - 1 - turn)
        here = pl.ds(pl.multiple_of(block * tokens, 128), tokens)
        first = key_grad[0, here] * score_scale
        second = pltpu.roll(key_grad[1, here] * score_scale, lanes - ROPE, 1)
        grad = jnp.concatenate(
            [first[:, :NOPE], value_grad[0, here], second[:, :NOPE], value_grad[1, here]], axis=1
        ).astype(bf16)
        expanded_ref[block] = grad
        own = 2 * (NOPE + HEADV)
        upstream = nt(grad, expand[:, pl.ds(pl.multiple_of(col * own, 128), own)])
        plain = latent_ref[block][:, :RANK]
        scale = lax.rsqrt(jnp.mean(plain * plain, axis=1, keepdims=True) + epsilon)
        rescale_rows[...] += jnp.sum(
            (upstream * plain * scale).reshape(tokens // 8, 8, RANK), axis=0
        )
        weighted = upstream * rescale_ref[...]
        inner = jnp.mean(weighted * plain, axis=1, keepdims=True)
        plain_grad = weighted * scale - plain * (scale * scale * scale * inner)
        rope = first[:, NOPE:] + second[:, NOPE:]
        lane = lax.broadcasted_iota(jnp.int32, rope.shape, 1)
        rope = jnp.where(lane < ROPE, rope, 0.0)
        rope = rope * key_cos_ref[block] - swap_halves(rope) * key_sin_ref[block]
        value = jnp.concatenate([plain_grad, rope], axis=1)
        latent_own[block] = value
        latent_to[block] = value.astype(bf16)
        latent_copy(block).start()
        return carried

    lax.fori_loop(0, ROWS, latents, 0)
    project(ROWS - 1)
    rest.run(3)

    def turned_piece(member):
        return turned.at[
            pl.ds(pl.multiple_of(member * sliced, 16), sliced),
            pl.ds(pl.multiple_of(col * (seq // COLS), 128), seq // COLS),
        ]

    def turned_copy(step):
        to = lax.rem(row + step, ROWS)
        return remote(
            turned_piece(to),
            turned_from.at[step],
            turned_sent.at[step],
            turned_arrived.at[step],
            {"row": to},
        )

    def mix(turn, carried):
        block = block_at(row, ROWS - 1 - turn)
        latent_copy(block).wait_recv()
        latent = latent_own[block] + latent_from[block].astype(f32)
        here = pl.ds(pl.multiple_of(block * tokens, 128), tokens)
        total_here = part[block] + nn(latent.astype(bf16), compress_all[...])
        part[block] = total_here
        sums.begin(block)
        turned[:, here] = latent.T.astype(bf16)
        scaling_rows[...] += jnp.sum(
            (total_here * one_ref[block].astype(f32)).reshape(tokens // 8, 8, width), axis=0
        )
        return carried

    lax.fori_loop(0, ROWS, mix, 0)
    for step in range(1, ROWS):
        turned_copy(step).start()

    advance(1)
    for turn in range(3):
        sums.pass_on(block_at(row, 3 if turn == 0 else turn))
        advance(turn + 2)
    for step in range(1, ROWS):
        turned_copy(step).wait_recv()
    half = pl.ds(pl.multiple_of(col * (seq // COLS), 128), seq // COLS)
    own_sum = turned[pl.ds(pl.multiple_of(row * sliced, 16), sliced), half].astype(f32)
    for step in range(1, ROWS):
        own_sum = own_sum + turned_from[step].astype(f32)
    own_latent_ref[:, half] = own_sum.astype(bf16)

    def own_copy(part_of):
        here = own_latent_ref.at[
            :, pl.ds(pl.multiple_of(part_of * (seq // COLS), 128), seq // COLS)
        ]
        return remote(here, here, own_sent.at[0], own_arrived.at[0], sibling)

    own_copy(col).start()
    advance(5)
    sums.total(total)
    input_grad_ref[...] += norm_grad(
        act_ref[...].astype(f32), scale_one_ref[...], scaling_ref[...], total[...], 1
    )
    sums.finish()
    reply_begin()
    small_begin()
    advance(6)
    rest.run(4)
    pieces = [
        pltpu.make_async_copy(
            result.at[i], shared_sum.at[:, :, i * 128 : (i + 1) * 128], rest_sem.at[i]
        )
        for i in range(8)
    ]
    for piece in pieces:
        piece.start()
    small_line_begin()
    own_copy(other).wait_recv()
    own_copy(col).wait_send()
    advance(7)
    advance(8)
    reply_pass()
    small_square_begin()
    for turn in range(9, count + 5):
        advance(turn)
    reply_end()
    small_end()
    pair_copy().wait_recv()
    store(expand_other, expand_lanes(other))

    def ended(block, carried):
        grad_copy(block).wait_send()
        query_copy(block, col).wait_send()
        latent_copy(block).wait_send()
        return carried

    lax.fori_loop(0, ROWS, ended, 0)
    for step in range(1, ROWS):
        turned_copy(step).wait_send()
    stat_copy(0).wait_send()
    stat_copy(1).wait_send()
    for piece in pieces:
        piece.wait()
    for copy in stores:
        copy.wait()
    pair_copy().wait_send()
    for step in range(ROWS):
        small_copy(step).wait_send()
    for one_sum in pieces_of:
        one_sum.finish()
    line_sums.finish()
    rest.finish()
    line.finish()


def run_attention_back(
    normed_grad,
    residual,
    scale_two,
    premix,
    cotangent,
    activations,
    scale_one,
    scaling,
    one,
    query,
    key,
    value,
    probs,
    latent,
    rescale,
    tables,
    compress_all,
    queries,
    expand,
    combine,
    shared,
    more,
):
    tokens, width = activations.shape
    seq = ROWS * tokens
    mine = query.shape[2]
    lanes = key.shape[3]
    latent_width = latent.shape[2]
    sliced = (RANK + ROPE) // ROWS
    whole = pl.BlockSpec(memory_space=VMEM)
    far = pl.BlockSpec(memory_space=pl.ANY)

    def shape(*dims, dtype=bf16):
        return jax.ShapeDtypeStruct(dims, dtype)

    kept, got_x, got_y = shared
    heads = more[0].shape[2]
    own_heads = 2 * (NOPE + HEADV)
    small = (24, width)
    piece = kept.shape[1:3] + (kept.shape[3] // 2,)
    loaded = (
        combine,
        query,
        key,
        value,
        probs,
        tables[0],
        tables[1],
        queries,
        expand,
        latent,
        tables[2],
        tables[3],
        compress_all,
        one,
    )
    return pl.pallas_call(
        attend_back_kernel,
        name="attend_back",
        out_shape=(
            shape(tokens, width, dtype=f32),
            shape(tokens, width),
            shape(*small, dtype=f32),
            shape(*kept.shape[1:3], width),
            shape(4, 8, width // 32, COLS * mine),
            shape(2, 8, heads // 16, width),
            shape(8, RANK // 8, COLS * own_heads),
            shape(sliced, width),
        ),
        in_specs=[whole] * 9 + [far] * 25,
        out_specs=(whole,) * 3 + (far,) * 5,
        scratch_shapes=[
            VMEM((ROWS, tokens, width), bf16),
            VMEM((ROWS, tokens, COLS * mine), bf16),
            VMEM((ROWS, tokens, own_heads), bf16),
            VMEM((sliced, seq), bf16),
            VMEM((8, width), f32),
            VMEM((8, RANK), f32),
            *[VMEM(value.shape, value.dtype) for value in loaded],
            VMEM(kept.shape, bf16),
            VMEM(kept.shape, bf16),
            VMEM((2,) + piece, bf16),
            VMEM((2,) + piece, bf16),
            VMEM((8,) + piece, bf16),
            *[VMEM(value.shape, value.dtype) for value in more],
            VMEM((2, tokens, 128), f32),
            VMEM((2, tokens, 128), f32),
            VMEM((ROWS, tokens, 2 * HEADV), f32),
            VMEM((ROWS, tokens, 2 * HEADV), bf16),
            VMEM((ROWS, tokens, 2 * HEADV), bf16),
            VMEM((2, seq, lanes), f32),
            VMEM((2, seq, HEADV), f32),
            VMEM((ROWS, tokens, latent_width), f32),
            VMEM((ROWS, tokens, latent_width), bf16),
            VMEM((ROWS, tokens, latent_width), bf16),
            VMEM((latent_width, seq), bf16),
            VMEM((ROWS, sliced, seq // COLS), bf16),
            VMEM((ROWS, tokens, width), f32),
            VMEM((ROWS, tokens, width), bf16),
            VMEM((2, ROWS, tokens, width), bf16),
            VMEM((tokens, width), f32),
            DMA((25,)),
            DMA((2,)),
            DMA((2,)),
            *line_sems(),
            *pair_sems(),
            *pair_sems(),
            *pair_sems(),
            *pair_sems(),
            *pair_sems(),
            *sum_sems(),
            DMA((8,)),
            DMA((8,)),
            DMA((8,)),
            VMEM((2, ROWS, tokens, width), bf16),
            VMEM(small, f32),
            VMEM(small, f32),
            VMEM((ROWS,) + small, f32),
            VMEM((SQUARE,) + small, f32),
            VMEM(small, f32),
            VMEM((8, RANK // 8, own_heads), bf16),
            DMA((16,)),
            *sum_sems(),
            DMA((1,)),
            DMA((1,)),
            DMA((ROWS + SQUARE - 1,)),
            DMA((ROWS + SQUARE - 1,)),
            *square_scratch((2, heads // 16, width)),
            *square_scratch((4, width // 32, COLS * mine)),
            *square_scratch((1, RANK // 8, own_heads)),
            *square_scratch((1, sliced, width // 8)),
        ],
        compiler_params=pltpu.CompilerParams(
            collective_id=3, has_side_effects=True, vmem_limit_bytes=62 * MIB
        ),
        cost_estimate=pl.CostEstimate(
            flops=40 * 1024**3, bytes_accessed=32 * MIB, transcendentals=0
        ),
    )(
        normed_grad,
        residual,
        scale_two,
        premix.reshape(1, width),
        cotangent,
        activations,
        scale_one,
        scaling.reshape(1, width),
        rescale.reshape(1, RANK),
        *loaded,
        kept,
        got_x,
        got_y,
        *more,
    )


def silu_pair(values):
    sigmoid = 1.0 / (1.0 + jnp.exp(-values))
    return values * sigmoid, sigmoid * (1.0 + values * (1.0 - sigmoid))


def expert_kernel(
    normed_ref,
    pick_ref,
    back_ref,
    cot_ref,
    router_ref,
    cot_rows_ref,
    fan_ref,
    fun_ref,
    wide_ref,
    narrow_ref,
    sum_ref,
    gathered_ref,
    rows_out,
    gu_out,
    hidden_out,
    shared_x,
    shared_y,
    shared_kept,
    shared_out,
    premix_ref,
    router_rows,
    reply_ref,
    fan,
    fun,
    wide,
    narrow,
    cot_rows,
    rows,
    staged,
    gu,
    hidden,
    pair_own,
    pair_to,
    pair_from,
    home,
    shared_to,
    shared_from,
    part,
    passed_to,
    passed_from,
    shared_gu,
    shared_grad,
    load_sem,
    store_sem,
    line_sent,
    line_arrived,
    out_sent,
    out_arrived,
    fwd_sent,
    fwd_arrived,
    shared_sent,
    shared_arrived,
    half_sent,
    half_arrived,
    home_sent,
    home_arrived,
    sum_sent,
    sum_arrived,
    other_sent,
    other_arrived,
    reply_sent,
    reply_arrived,
    grad_sem,
):
    place, row, col = lax.axis_index("dp"), lax.axis_index("row"), lax.axis_index("col")
    other = 1 - col
    inner = jnp.logical_and(row > 0, row < ROWS - 1)
    tokens, width = normed_ref.shape
    picked = pick_ref.shape[1]
    slots = picked // SQUARE
    experts = router_ref.shape[0]
    share = narrow.shape[0]
    loads = [
        pltpu.make_async_copy(source, target, load_sem.at[i])
        for i, (source, target) in enumerate(
            [
                (wide_ref, wide),
                (narrow_ref, narrow),
                (fan_ref, fan),
                (cot_rows_ref, cot_rows),
                (fun_ref, fun),
            ]
        )
    ]
    for load in loads:
        load.start()
    greet(row, place, col)
    gathered_ref[pl.ds(row, 1)] = normed_ref[...].reshape(1, tokens, width)
    line = Line(row, gathered_ref, line_sent, line_arrived)
    line.pass_on(row)
    premix_ref[...] = jnp.zeros_like(premix_ref)
    router_rows[...] = jnp.zeros_like(router_rows)
    sums = SumLine(row, part, passed_to, passed_from, sum_sent, sum_arrived)
    sibling = {"col": other}

    def half_lines(half):
        return pl.ds(pl.multiple_of(half * width, width), width)

    def square_copy(source, target, sent, arrived, block, step):
        piece = pl.ds(step * slots, slots)
        return remote(
            source.at[block, piece],
            target.at[block, piece],
            sent.at[block, step],
            arrived.at[block, step],
            {"dp": partner(place, step)},
        )

    def out_copy(block, step):
        return square_copy(staged, rows.at[col], out_sent, out_arrived, block, step)

    def home_copy(block, step):
        return square_copy(staged, home, home_sent, home_arrived, block, step)

    def reply_copy(block, step):
        return square_copy(staged, reply_ref, reply_sent, reply_arrived, block, step)

    def fwd_copy(block, half):
        here = rows.at[half, block]
        return remote(here, here, fwd_sent.at[block], fwd_arrived.at[block], sibling)

    def shared_copy(block):
        return remote(
            shared_to.at[block],
            shared_from.at[block],
            shared_sent.at[block],
            shared_arrived.at[block],
            sibling,
        )

    def half_copy(step):
        return remote(
            pair_to.at[lax.rem(step, 2)],
            pair_from.at[step],
            half_sent.at[step],
            half_arrived.at[step],
            sibling,
        )

    def other_copy(step):
        return remote(
            pair_to.at[lax.rem(step, 2)],
            pair_from.at[jnp.where(step == ROWS - 1, ROWS, step)],
            other_sent.at[step],
            other_arrived.at[step],
            sibling,
        )

    def stores(step):
        block = block_at(row, step)
        return [
            pltpu.make_async_copy(source, target, store_sem.at[index, step])
            for index, (source, target) in enumerate(
                [
                    (rows.at[:, block], rows_out.at[:, block]),
                    (gu.at[:, lax.rem(step, 2)], gu_out.at[:, block]),
                    (hidden.at[block], hidden_out.at[block]),
                ]
            )
        ]

    def relay(step):
        block = block_at(row, step)
        line.wait(block)
        line.pass_on(block)

    def take(step):
        block = block_at(row, step)

        @pl.when(jnp.logical_and(step > 0, jnp.logical_not(inner)))
        def _():
            relay(step)

        staged[block] = nn(pick_ref[block], gathered_ref[block]).astype(bf16)
        for shift in (3, 2, 1):
            out_copy(block, shift).start()
        rows[col, block, 0:slots] = staged[block, 0:slots]

        @pl.when(step == 0)
        def _():
            loads[0].wait()
            loads[1].wait()

        for index, value in enumerate(
            (
                nt(gathered_ref[block], wide[0]),
                nt(gathered_ref[block], wide[1]),
                nt(cot_ref[block], narrow[...]),
            )
        ):
            shared_to[block, index] = value.astype(bf16)
        shared_copy(block).start()

    def forward(step):
        block = block_at(row, step)
        for shift in range(1, SQUARE):
            out_copy(block, shift).wait_recv()
        fwd_copy(block, col).start()

    def shared(step):
        block = block_at(row, step)
        shared_copy(block).wait_recv()
        gate, up, grad = [
            shared_to[block, index].astype(f32) + shared_from[block, index].astype(f32)
            for index in range(3)
        ]
        act, slope = silu_pair(gate)
        shared_out[block] = (act * up).astype(bf16)
        gate_grad = (grad * up * slope).astype(bf16)
        up_grad = (grad * act).astype(bf16)
        shared_gu[0, block] = gate_grad
        shared_gu[1, block] = up_grad
        part[block] = nn(gate_grad, wide[0]) + nn(up_grad, wide[1])

    def experts_of(step):
        block = block_at(row, step)

        @pl.when(step == 0)
        def _():
            for load in loads[2:]:
                load.wait()

        @pl.when(step > 1)
        def _():
            stores(step - 2)[1].wait()
            half_copy(step - 2).wait_send()

        fwd_copy(block, other).wait_recv()
        left, right = rows[0, block], rows[1, block]
        logits = nt(left, router_ref[:, 0:width]) + nt(right, router_ref[:, width:])
        logits = logits - jnp.max(logits, axis=1, keepdims=True)
        weight = jnp.exp(logits)
        probs = weight / jnp.sum(weight, axis=1, keepdims=True)
        own = (
            lax.broadcasted_iota(jnp.int32, (picked, experts), 1) == place * ROWS + row
        ).astype(f32)
        gates = jnp.sum(probs * own, axis=1, keepdims=True)
        raw = nt(cot_rows[0, block], fun[:, 0:width]) + nt(cot_rows[1, block], fun[:, width:])
        gate = nt(left, fan[0, :, 0:width]) + nt(right, fan[0, :, width:])
        up = nt(left, fan[1, :, 0:width]) + nt(right, fan[1, :, width:])
        act, slope = silu_pair(gate)
        value = act * up
        hidden[block] = (value * gates).astype(bf16)
        gate_sum = gates * jnp.sum(value * raw, axis=1, keepdims=True)
        logit_grad = (gate_sum * (own - probs)).astype(bf16)
        raw = raw * gates
        slot = lax.rem(step, 2)
        gu[0, slot] = (raw * up * slope).astype(bf16)
        gu[1, slot] = (raw * act).astype(bf16)

        def half_of(half):
            lines = half_lines(half)
            return (
                nn(gu[0, slot], fan[0, :, lines])
                + nn(gu[1, slot], fan[1, :, lines])
                + nn(logit_grad, router_ref[:, lines])
            )

        pair_to[slot] = half_of(other).astype(bf16)
        half_copy(step).start()
        pair_own[...] = half_of(col)
        router_rows[:, 0:width] += tn(logit_grad, left)
        router_rows[:, width:] += tn(logit_grad, right)
        for copy in stores(step):
            copy.start()
        for shift in range(1, SQUARE):
            out_copy(block, shift).wait_send()
        half_copy(step).wait_recv()
        staged[block] = (pair_own[...] + pair_from[step].astype(f32)).astype(bf16)
        for shift in (3, 2, 1):
            home_copy(block, shift).start()
        home[block, 0:slots] = staged[block, 0:slots]

    def add_up(step):
        block = block_at(row, step)
        for shift in range(1, SQUARE):
            home_copy(block, shift).wait_recv()
        total = part[block] + nn(back_ref[block], home[block])
        part[block] = total
        premix_ref[...] += jnp.sum(
            (total * gathered_ref[block].astype(f32)).reshape(tokens // 8, 8, width), axis=0
        )
        sums.begin(block)

    def reply(step):
        block = block_at(row, step)
        slot = lax.rem(step, 2)

        @pl.when(step < 2)
        def _():
            half_copy(step + 2).wait_send()

        @pl.when(step > 1)
        def _():
            other_copy(step - 2).wait_send()

        pair_to[slot] = nn(hidden[block], fun[:, half_lines(other)]).astype(bf16)
        other_copy(step).start()

    def reply_home(step):
        block = block_at(row, step)
        own = nn(hidden[block], fun[:, half_lines(col)])
        for shift in range(1, SQUARE):
            home_copy(block, shift).wait_send()
        came = jnp.where(step == ROWS - 1, ROWS, step)
        other_copy(step).wait_recv()
        staged[block] = (own + pair_from[came].astype(f32)).astype(bf16)
        for shift in (3, 2, 1):
            reply_copy(block, shift).start()
        reply_ref[block, 0:slots] = staged[block, 0:slots]

    def turn(step, carried):
        @pl.when(step < ROWS)
        def _():
            take(step)

        @pl.when(jnp.logical_and(step == 0, inner))
        def _():
            relay(1)
            relay(2)

        @pl.when(jnp.logical_and(step >= 1, step < ROWS))
        def _():
            forward(step - 1)

        @pl.when(jnp.logical_and(step >= 2, step < ROWS + 2))
        def _():
            experts_of(step - 2)

        @pl.when(step == ROWS)
        def _():
            forward(ROWS - 1)

        @pl.when(jnp.logical_or(step == 1, step >= 3))
        def _():
            shared(jnp.where(step == 1, 0, step - 2))

        @pl.when(jnp.logical_and(step == 1, inner))
        def _():
            relay(3)

        @pl.when(step >= 3)
        def _():
            add_up(step - 3)

        return carried

    lax.fori_loop(0, ROWS + 2, turn, 0)

    def replies(step, carried):
        @pl.when(step < ROWS)
        def _():
            reply(step)

        @pl.when(step > 0)
        def _():
            reply_home(step - 1)

        return carried

    lax.fori_loop(0, ROWS + 1, replies, 0)
    add_up(ROWS - 1)

    def hand_on(turn, carried):
        sums.pass_on(block_at(row, jnp.where(turn == 2, 1, turn + 2)))
        return carried

    lax.fori_loop(0, ROWS - 1, hand_on, 0)

    seq = ROWS * tokens
    for index, (left, right) in enumerate(
        (
            (shared_out, cot_ref),
            (shared_gu.at[0], gathered_ref),
            (shared_gu.at[1], gathered_ref),
        )
    ):
        grad = tn(left[...].reshape(seq, share), right[...].reshape(seq, width))
        shared_grad[index] = grad.astype(bf16)
    x, y = lax.rem(place, 2), lax.div(place, 2)
    quarter = width // SQUARE
    grad_copies = []
    for index, (half, side, target) in enumerate(
        (
            (0, 1 - x, shared_x),
            (1, 1 - y, shared_y),
            (0, x, shared_kept.at[0]),
            (1, y, shared_kept.at[1]),
        )
    ):
        lanes = pl.ds(pl.multiple_of((2 * half + side) * quarter, 128), quarter)
        grad_copies.append(
            pltpu.make_async_copy(shared_grad.at[:, :, lanes], target, grad_sem.at[index])
        )
        grad_copies[index].start()
    sums.total(sum_ref)

    def ended(step, carried):
        block = block_at(row, step)
        shared_copy(block).wait_send()
        fwd_copy(block, col).wait_send()
        for shift in range(1, SQUARE):
            reply_copy(block, shift).wait_recv()
            reply_copy(block, shift).wait_send()
        copies = stores(step)
        copies[0].wait()
        copies[2].wait()

        @pl.when(step >= ROWS - 2)
        def _():
            copies[1].wait()
            other_copy(step).wait_send()

        return carried

    lax.fori_loop(0, ROWS, ended, 0)
    for copy in grad_copies:
        copy.wait()
    sums.finish()
    line.finish()


def run_experts(
    normed, pick, back, cot_rows, cot_all, fan, fun, wide, narrow, router_all
):
    tokens, width = normed.shape
    picked = pick.shape[1]
    hid = fun.shape[0]
    share = narrow.shape[0]
    experts = router_all.shape[0]
    whole = pl.BlockSpec(memory_space=VMEM)
    far = pl.BlockSpec(memory_space=pl.ANY)

    def shape(*dims, dtype=bf16):
        return jax.ShapeDtypeStruct(dims, dtype)

    return pl.pallas_call(
        expert_kernel,
        name="experts",
        out_shape=(
            shape(tokens, width, dtype=f32),
            shape(ROWS, tokens, width),
            shape(COLS, ROWS, picked, width),
            shape(2, ROWS, picked, hid),
            shape(ROWS, picked, hid),
            shape(3, share, width // SQUARE),
            shape(3, share, width // SQUARE),
            shape(2, 3, share, width // SQUARE),
            shape(ROWS, tokens, share),
            shape(8, width, dtype=f32),
            shape(experts, COLS * width, dtype=f32),
            shape(ROWS, picked, width),
        ),
        in_specs=[whole] * 5 + [far] * 5,
        out_specs=(whole, whole) + (far,) * 6 + (whole,) * 4,
        scratch_shapes=[
            VMEM(fan.shape, bf16),
            VMEM(fun.shape, bf16),
            VMEM(wide.shape, bf16),
            VMEM(narrow.shape, bf16),
            VMEM(cot_rows.shape, bf16),
            VMEM((COLS, ROWS, picked, width), bf16),
            VMEM((ROWS, picked, width), bf16),
            VMEM((2, 2, picked, hid), bf16),
            VMEM((ROWS, picked, hid), bf16),
            VMEM((picked, width), f32),
            VMEM((2, picked, width), bf16),
            VMEM((ROWS + 1, picked, width), bf16),
            VMEM((ROWS, picked, width), bf16),
            VMEM((ROWS, 3, tokens, share), bf16),
            VMEM((ROWS, 3, tokens, share), bf16),
            VMEM((ROWS, tokens, width), f32),
            VMEM((ROWS, tokens, width), bf16),
            VMEM((2, ROWS, tokens, width), bf16),
            VMEM((2, ROWS, tokens, share), bf16),
            VMEM((3, share, width), bf16),
            DMA((5,)),
            DMA((3, ROWS)),
            *line_sems(),
            *square_sems(),
            *pair_sems(),
            *pair_sems(),
            *pair_sems(),
            *square_sems(),
            *sum_sems(),
            *pair_sems(),
            *square_sems(),
            DMA((4,)),
        ],
        compiler_params=pltpu.CompilerParams(
            collective_id=2, has_side_effects=True, vmem_limit_bytes=62 * MIB
        ),
        cost_estimate=pl.CostEstimate(
            flops=60 * 1024**3, bytes_accessed=64 * MIB, transcendentals=0
        ),
    )(normed, pick, back, cot_all, router_all, cot_rows, fan, fun, wide, narrow)


class SquareSum:
    def __init__(self, place, part, first, second, middle, result, sent, arrived):
        self.x, self.y = lax.rem(place, 2), lax.div(place, 2)
        self.to_x, self.to_y = {"dp": partner(place, 1)}, {"dp": partner(place, 2)}
        self.part, self.first, self.second = part, first, second
        self.middle, self.result = middle, result
        self.sent, self.arrived = sent, arrived

    def copies(self, phase):
        x, y = self.x, self.y
        if phase == 0:
            plan = (
                (self.part.at[pl.ds(2 - 2 * x, 2)], self.first.at[0:2], self.to_x),
                (self.part.at[pl.ds(6 - 2 * y, 2)], self.first.at[2:4], self.to_y),
            )
        elif phase == 1:
            plan = (
                (self.middle.at[0], self.second.at[0], self.to_y),
                (self.middle.at[1], self.second.at[1], self.to_x),
            )
        elif phase == 2:
            one, two = self.result.at[2 * x + y], self.result.at[4 + 2 * y + x]
            plan = ((one, one, self.to_y), (two, two, self.to_x))
        else:
            one, two = self.result.at[pl.ds(2 * x, 2)], self.result.at[pl.ds(4 + 2 * y, 2)]
            plan = ((one, one, self.to_x), (two, two, self.to_y))
        return [
            remote(source, target, self.sent.at[2 * phase + i], self.arrived.at[2 * phase + i], to)
            for i, (source, target, to) in enumerate(plan)
        ]

    def start(self, phase):
        for copy in self.copies(phase):
            copy.start()

    def arrive(self, phase):
        for copy in self.copies(phase):
            copy.wait_recv()

    def run(self, phase):
        x, y = self.x, self.y
        if phase > 0:
            self.arrive(phase - 1)
        if phase == 1:
            for slot, piece, came in (
                (0, 2 * x + 1 - y, 1 - y),
                (1, 4 + 2 * y + 1 - x, 3 - x),
            ):
                self.middle[slot] = (
                    self.part[piece].astype(f32) + self.first[came].astype(f32)
                ).astype(bf16)
        if phase == 2:
            for slot, piece, came in ((0, 2 * x + y, y), (1, 4 + 2 * y + x, 2 + x)):
                self.result[piece] = (
                    self.part[piece].astype(f32)
                    + self.first[came].astype(f32)
                    + self.second[slot].astype(f32)
                ).astype(bf16)
        if phase < 4:
            self.start(phase)

    def finish(self):
        for phase in range(4):
            for copy in self.copies(phase):
                copy.wait_send()


def square_scratch(dims):
    count, rows, lanes = dims
    return [
        VMEM((count, 8, rows, lanes), bf16),
        VMEM((count, 4, rows, lanes), bf16),
        VMEM((count, 2, rows, lanes), bf16),
        VMEM((count, 2, rows, lanes), bf16),
        VMEM((count, 8, rows, lanes), bf16),
        DMA((count, 8)),
        DMA((count, 8)),
    ]


def write_kernel(count, plan, *refs):
    sources, targets = refs[:count], refs[count : count + len(plan)]
    rest = refs[count + len(plan) :]
    held, wide = rest[:count], rest[count : count + len(plan)]
    load_sem, store_sem = rest[count + len(plan) :]
    loads = [
        pltpu.make_async_copy(sources[i], held[i], load_sem.at[i]) for i in range(count)
    ]
    stores = [
        pltpu.make_async_copy(wide[i], targets[i], store_sem.at[i]) for i in range(len(plan))
    ]
    for load in loads:
        load.start()
    waited = set()
    for i, (source, where) in enumerate(plan):
        if source not in waited:
            loads[source].wait()
            waited.add(source)
        wide[i][...] = held[source][where].astype(wide[i].dtype)
        stores[i].start()
    for store in stores:
        store.wait()


def write_out(arrays, plan):
    far = pl.BlockSpec(memory_space=pl.ANY)
    shapes = [jax.ShapeDtypeStruct(shape, dtype) for _, _, shape, dtype in plan]
    return pl.pallas_call(
        functools.partial(
            write_kernel, len(arrays), [(source, where) for source, where, _, _ in plan]
        ),
        name="write_out",
        out_shape=shapes,
        in_specs=[far] * len(arrays),
        out_specs=[far] * len(plan),
        scratch_shapes=[
            *[VMEM(array.shape, array.dtype) for array in arrays],
            *[VMEM(shape.shape, shape.dtype) for shape in shapes],
            DMA((len(arrays),)),
            DMA((len(plan),)),
        ],
        compiler_params=pltpu.CompilerParams(vmem_limit_bytes=62 * MIB),
        cost_estimate=pl.CostEstimate(flops=0, bytes_accessed=24 * MIB, transcendentals=0),
    )(*arrays)


def product_kernel(left_ref, right_ref, out_ref, turned):
    wide = 256

    @pl.when(pl.program_id(1) == 0)
    def _():
        turned[...] = left_ref[0].T

    def one(index, carried):
        lanes = pl.ds(pl.multiple_of(index * wide, 128), wide)
        out_ref[0, :, lanes] = nn(turned[...], right_ref[0, :, lanes])
        return carried

    lax.fori_loop(0, right_ref.shape[2] // wide, one, 0)


def slot_products(left, right):
    kinds, slots, tall = left.shape
    halves, _, wide = right.shape
    return pl.pallas_call(
        product_kernel,
        name="slot_products",
        grid=(kinds, halves),
        out_shape=jax.ShapeDtypeStruct((kinds, tall, halves * wide), f32),
        in_specs=[
            pl.BlockSpec((1, slots, tall), lambda kind, half: (kind, 0, 0)),
            pl.BlockSpec((1, slots, wide), lambda kind, half: (half, 0, 0)),
        ],
        out_specs=pl.BlockSpec((1, tall, wide), lambda kind, half: (kind, 0, half)),
        scratch_shapes=[VMEM((tall, slots), bf16)],
        compiler_params=pltpu.CompilerParams(vmem_limit_bytes=40 * MIB),
        cost_estimate=pl.CostEstimate(
            flops=2 * kinds * halves * slots * tall * wide,
            bytes_accessed=4 * kinds * halves * tall * wide,
            transcendentals=0,
        ),
    )(left, right)


def local_square(
    activations,
    cotangent,
    routing,
    segments,
    scaling,
    queries,
    compress,
    rescale,
    expand,
    combine,
    premix,
    router,
    widening,
    narrowing,
    fanout,
    funnel,
):
    dp_count = lax.axis_size("dp")
    row_count = lax.axis_size("row")
    col_count = lax.axis_size("col")
    col_index = lax.axis_index("col")
    local_rows, col_width = activations.shape
    seq_length = local_rows * row_count
    expert_total = router.shape[1]
    capacity = local_rows * TOP * 4 // (3 * expert_total)
    slot_total = capacity * row_count * dp_count
    tables = turning_tables(seq_length)
    (
        one,
        query,
        key,
        value,
        probs,
        latent,
        latent_normed,
        attended,
        compress_all,
        cot_blocks,
        pick,
        back,
        cot_rows,
        residual,
        normed_two,
        scale_one,
        scale_two,
        router_all,
    ) = run_attention(
        activations,
        scaling,
        queries,
        compress,
        rescale,
        expand,
        combine,
        premix,
        segments,
        cotangent,
        routing,
        router,
        tables,
        capacity,
    )
    (
        normed_grad,
        two_blocks,
        expert_rows,
        expert_gu_grad,
        expert_hidden,
        shared_x,
        shared_y,
        shared_kept,
        hidden_blocks,
        premix_rows,
        router_rows,
        reply_blocks,
    ) = run_experts(
        normed_two,
        pick,
        back,
        cot_rows,
        cot_blocks,
        fanout[0].transpose(0, 2, 1),
        funnel[0],
        widening.transpose(0, 2, 1),
        narrowing,
        router_all,
    )
    slot_rows = expert_rows.reshape(col_count, slot_total, col_width)
    reply_grad_rows = cot_rows.reshape(col_count, slot_total, col_width)
    slot_hidden = expert_hidden.reshape(slot_total, -1)
    slot_gu_grad = expert_gu_grad.reshape(2, slot_total, -1)
    got_x = lax.ppermute(shared_x, "dp", [(i, i ^ 1) for i in range(SQUARE)])
    got_y = lax.ppermute(shared_y, "dp", [(i, i ^ 2) for i in range(SQUARE)])
    fanout_grad = slot_products(slot_gu_grad, slot_rows)
    funnel_grad = slot_products(slot_hidden[None], reply_grad_rows)
    normed_grad, fanout_grad, funnel_grad = lax.optimization_barrier(
        (normed_grad, fanout_grad, funnel_grad)
    )
    (
        input_grad,
        layer_output,
        small,
        shared_sum,
        queries_sum,
        combine_sum,
        expand_sum,
        compress_sum,
    ) = run_attention_back(
        normed_grad,
        residual,
        scale_two,
        premix,
        cotangent,
        activations,
        scale_one,
        scaling,
        one,
        query,
        key,
        value,
        probs,
        latent,
        rescale,
        tables,
        compress_all,
        queries,
        expand,
        combine,
        (shared_kept, got_x, got_y),
        (
            attended,
            latent_normed,
            narrowing,
            reply_blocks,
            back,
            hidden_blocks,
            premix_rows,
            router_rows,
        ),
    )
    everything = slice(None)
    share = narrowing.shape[0]
    (
        widening_grad,
        narrowing_grad,
        queries_grad,
        combine_grad,
        expand_grad,
        compress_grad,
        input_grad,
        layer_output,
        router_grad,
        premix_grad,
        scaling_grad,
        rescale_grad,
    ) = write_out(
        (
            shared_sum,
            queries_sum.reshape(queries.shape),
            combine_sum.reshape(combine.shape),
            expand_sum.reshape(expand.shape),
            compress_sum,
            input_grad,
            layer_output,
            small,
        ),
        (
            (0, slice(1, 3), (2, share, col_width), f32),
            (0, 0, (share, col_width), f32),
            (1, everything, queries.shape, f32),
            (2, everything, combine.shape, f32),
            (3, everything, expand.shape, f32),
            (4, everything, compress_sum.shape, f32),
            (5, everything, input_grad.shape, f32),
            (6, everything, layer_output.shape, bf16),
            (7, slice(0, expert_total), (expert_total, col_width), f32),
            (7, slice(expert_total, expert_total + 1), (1, col_width), f32),
            (7, slice(expert_total + 1, expert_total + 2), (1, col_width), f32),
            (7, (slice(expert_total + 2, expert_total + 3), slice(0, RANK)), (1, RANK), f32),
        ),
    )
    return (
        layer_output,
        input_grad,
        scaling_grad.reshape(col_width),
        queries_grad,
        compress_grad.T,
        rescale_grad.reshape(RANK),
        expand_grad,
        combine_grad,
        premix_grad.reshape(col_width),
        router_grad.T,
        widening_grad.transpose(0, 2, 1),
        narrowing_grad,
        fanout_grad.transpose(0, 2, 1)[None],
        funnel_grad,
    )


def local(
    activations,
    cotangent,
    routing,
    segments,
    scaling,
    queries,
    compress,
    rescale,
    expand,
    combine,
    premix,
    router,
    widening,
    narrowing,
    fanout,
    funnel,
):
    dp_count = lax.axis_size("dp")
    row_count = lax.axis_size("row")
    col_count = lax.axis_size("col")
    dp_index = lax.axis_index("dp")
    row_index = lax.axis_index("row")
    col_index = lax.axis_index("col")
    local_rows = activations.shape[0]
    col_width = activations.shape[1]
    seq_length = local_rows * row_count
    half_length = seq_length // col_count
    head_width = NOPE + ROPE
    pair_width = NOPE + HEADV
    local_heads = queries.shape[1] // head_width
    slice_width = compress.shape[1]
    expert_total = router.shape[1]
    capacity = local_rows * TOP * 4 // (3 * expert_total)
    slots = capacity * row_count
    slot_total = slots * dp_count
    block_rows = min(512, half_length)
    block_count = half_length // block_rows
    score_scale = head_width ** (-0.5)

    inputs = activations.astype(f32)
    scale_one = norm_scale(inputs)
    normed_one = (inputs * scale_one[:, None] * scaling).astype(bf16)
    gathered_one = row_gather(normed_one)
    compress_all = lax.all_gather(compress, "row", axis=1, tiled=True)

    routing_all = row_gather(routing)
    cotangent_all = row_gather(after(cotangent, gathered_one))
    offsets = jnp.arange(dp_count, dtype=jnp.int32)
    my_experts = ((dp_index + offsets) % dp_count) * row_count + row_index
    goes = jnp.any(routing_all[None, :, :] == my_experts[:, None, None], axis=2)
    token_range = jnp.arange(seq_length, dtype=jnp.int32)
    earlier = (token_range[:, None] < token_range[None, :]).astype(bf16)
    rank = dot(goes.astype(bf16), earlier).astype(jnp.int32)
    slot_range = jnp.arange(slots, dtype=jnp.int32)
    pick = (
        ((rank[:, None, :] == slot_range[None, :, None]) & goes[:, None, :])
        .astype(bf16)
        .reshape(slot_total, seq_length)
    )

    def dispatch(tokens):
        rows = dot(pick, tokens).astype(bf16).reshape(dp_count, slots, col_width)
        arrived = send_out([rows[k] for k in range(dp_count)])
        return col_gather(jnp.concatenate(arrived, axis=0), axis=1)

    def bring_back(part):
        summed = col_scatter(part.astype(bf16), axis=1).reshape(dp_count, slots, col_width)
        arrived = send_back([summed[k] for k in range(dp_count)])
        return dot_tn(pick, jnp.concatenate(arrived, axis=0))

    query_part = dot(gathered_one, queries)
    latent_part = dot(gathered_one, compress_all)
    query_raw, latent_raw = col_scatter((query_part, latent_part))
    latent_plain = latent_raw[:, :RANK]
    latent_scale = lax.rsqrt(jnp.mean(latent_plain * latent_plain, axis=1) + epsilon)
    latent_normed = (latent_plain * latent_scale[:, None] * rescale).astype(bf16)
    expanded = dot(latent_normed, expand).reshape(half_length, local_heads, pair_width)
    positions = col_index * half_length + jnp.arange(half_length, dtype=jnp.int32)
    cosine, sine_table = rotation(positions, ROPE)
    key_shared = rotate(latent_raw[:, RANK:], cosine, sine_table, 1.0)
    query_heads = query_raw.reshape(half_length, local_heads, head_width)
    query_local = jnp.concatenate(
        [
            query_heads[..., :NOPE],
            rotate(query_heads[..., NOPE:], cosine[:, None, :], sine_table[:, None, :], 1.0),
        ],
        axis=2,
    ).astype(bf16)
    key_local = jnp.concatenate(
        [
            expanded[..., :NOPE],
            jnp.broadcast_to(key_shared[:, None, :], (half_length, local_heads, ROPE)),
        ],
        axis=2,
    ).astype(bf16)
    value_local = expanded[..., NOPE:].astype(bf16)
    key_flat, value_flat = (
        col_gather(key_local.reshape(half_length, local_heads * head_width)),
        col_gather(value_local.reshape(half_length, local_heads * HEADV)),
    )
    key_heads = key_flat.reshape(seq_length, local_heads, head_width)
    value_heads = value_flat.reshape(seq_length, local_heads, HEADV)
    own_segments = lax.dynamic_slice_in_dim(
        segments, col_index * half_length, half_length, 0
    ).reshape(block_count, block_rows)
    query_blocks = query_local.reshape(block_count, block_rows, local_heads, head_width)

    def attend_block(inputs_block):
        query_block, segment_block = inputs_block
        scores = (
            jnp.einsum("qhd,khd->hqk", query_block, key_heads, preferred_element_type=f32)
            * score_scale
        )
        visible = segments[None, None, :] <= segment_block[None, :, None]
        scores = jnp.where(visible, scores, masked_score)
        largest = jnp.max(scores, axis=2, keepdims=True)
        weight = jnp.exp(scores - largest)
        totals = jnp.sum(weight, axis=2, keepdims=True)
        probability = (weight / totals).astype(bf16)
        result = jnp.einsum("hqk,khd->qhd", probability, value_heads, preferred_element_type=f32)
        return (result.astype(bf16), (largest + jnp.log(totals))[..., 0])

    attended_blocks, log_totals = lax.map(attend_block, (query_blocks, own_segments))
    attended = attended_blocks.reshape(half_length, local_heads * HEADV)
    attended_all = col_gather(attended)
    branch = row_scatter(dot(attended_all, combine))

    reply_grad_rows = dispatch(cotangent_all)
    inner_weight = fanout[0]
    outer_weight = funnel[0]
    hidden_raw = dot_nt(reply_grad_rows, outer_weight)
    shared_hidden_grad = col_scatter(dot_nt(cotangent_all, narrowing))

    residual = inputs + branch
    scale_two = norm_scale(residual)
    normed_two = (residual * scale_two[:, None] * premix).astype(bf16)
    gathered_two = row_gather(normed_two)

    expert_rows = dispatch(gathered_two)
    expert_range = jnp.arange(expert_total, dtype=jnp.int32)
    router_all = lax.all_gather(router, "col", axis=0, tiled=True)
    own_expert = dp_index * row_count + row_index
    slot_probs = jax.nn.softmax(dot(expert_rows, router_all), axis=1)
    slot_gates = jnp.sum(jnp.where(expert_range == own_expert, slot_probs, 0.0), axis=1)
    gate_up = jnp.einsum("rd,gdf->grf", expert_rows, inner_weight, preferred_element_type=f32)
    gate_input, up_input = gate_up[0], gate_up[1]
    hidden = jax.nn.silu(gate_input) * up_input
    expert_hidden = hidden.astype(bf16)
    slot_gate_grad = col_totals(jnp.sum(hidden * hidden_raw, axis=1))
    hidden_grad = hidden_raw * slot_gates[:, None]
    expert_gu_grad = jnp.stack(
        [hidden_grad * up_input * silu_slope(gate_input), hidden_grad * jax.nn.silu(gate_input)]
    ).astype(bf16)
    input_part = jnp.einsum(
        "grf,gdf->rd", expert_gu_grad, inner_weight, preferred_element_type=f32
    )
    routed_grad = bring_back(input_part)
    gate_grad_parts = send_back(
        [slot_gate_grad.reshape(dp_count, slots)[k] for k in range(dp_count)]
    )

    logits = col_totals(dot(gathered_two, router))
    router_probs = jax.nn.softmax(logits, axis=1)
    gate_grad = jnp.sum(
        pick.reshape(dp_count, slots, seq_length).astype(f32)
        * jnp.stack(gate_grad_parts)[:, :, None],
        axis=1,
    )
    mine = (my_experts[:, None] == expert_range[None, :]).astype(f32)
    probs_grad = jnp.sum(gate_grad[:, :, None] * mine[:, None, :], axis=0)
    logit_grad = router_probs * (
        probs_grad - jnp.sum(router_probs * probs_grad, axis=1, keepdims=True)
    )
    router_part = dot_tn(gathered_two, logit_grad)

    shared_gate_up = col_scatter(
        jnp.einsum("td,gdf->tgf", gathered_two, widening, preferred_element_type=f32)
    )
    shared_hidden = (jax.nn.silu(shared_gate_up[:, 0]) * shared_gate_up[:, 1]).astype(bf16)
    hidden_all = col_gather(shared_hidden)
    narrowing_grad = dot_tn(hidden_all, cotangent_all)
    shared_gu_grad = jnp.stack(
        [
            shared_hidden_grad * shared_gate_up[:, 1] * silu_slope(shared_gate_up[:, 0]),
            shared_hidden_grad * jax.nn.silu(shared_gate_up[:, 0]),
        ],
        axis=1,
    ).astype(bf16)
    gu_grad_all = col_gather(shared_gu_grad)
    widening_grad = jnp.einsum(
        "td,tgf->gdf", gathered_two, gu_grad_all, preferred_element_type=f32
    )
    shared_input_part = jnp.einsum(
        "tgf,gdf->td", gu_grad_all, widening, preferred_element_type=f32
    )
    shared_sums = lax.psum((narrowing_grad.astype(bf16), widening_grad.astype(bf16)), "dp")

    grad_part = routed_grad + shared_input_part + dot_nt(logit_grad, router)
    premix_part = jnp.sum(grad_part * gathered_two.astype(f32), axis=0) / premix
    normed_grad = row_scatter(grad_part)

    upstream = cotangent.astype(f32)
    residual_grad = upstream + norm_back(residual, scale_two, premix, normed_grad)
    branch_all = row_gather(residual_grad.astype(bf16))

    funnel_grad = dot_tn((hidden * slot_gates[:, None]).astype(bf16), reply_grad_rows)[None]
    fanout_grad = jnp.einsum(
        "rd,grf->gdf", expert_rows, expert_gu_grad, preferred_element_type=f32
    )[None]
    reply_part = dot(expert_hidden, outer_weight) * slot_gates[:, None]
    routed = bring_back(reply_part)
    shared_out = row_scatter(routed + dot(hidden_all, narrowing))
    layer_output = (residual + shared_out).astype(bf16)

    combine_grad = dot_tn(attended_all, branch_all)
    combine_sum = lax.psum(after(combine_grad.astype(bf16), *shared_sums), "dp")
    attended_grad = col_scatter(dot_nt(branch_all, combine))
    attended_grad_blocks = attended_grad.astype(bf16).reshape(
        block_count, block_rows, local_heads, HEADV
    )

    def attend_back(carried, inputs_block):
        key_sum, value_sum = carried
        query_block, grad_block, log_block, segment_block = inputs_block
        scores = (
            jnp.einsum("qhd,khd->hqk", query_block, key_heads, preferred_element_type=f32)
            * score_scale
        )
        visible = segments[None, None, :] <= segment_block[None, :, None]
        probability = jnp.where(visible, jnp.exp(scores - log_block[..., None]), 0.0)
        weight_grad = jnp.einsum(
            "qhd,khd->hqk", grad_block, value_heads, preferred_element_type=f32
        )
        inner_sum = jnp.sum(probability * weight_grad, axis=2, keepdims=True)
        score_grad = (probability * (weight_grad - inner_sum)).astype(bf16)
        query_grad_block = (
            jnp.einsum("hqk,khd->qhd", score_grad, key_heads, preferred_element_type=f32)
            * score_scale
        )
        key_sum = (
            key_sum
            + jnp.einsum("hqk,qhd->khd", score_grad, query_block, preferred_element_type=f32)
            * score_scale
        )
        value_sum = value_sum + jnp.einsum(
            "hqk,qhd->khd", probability.astype(bf16), grad_block, preferred_element_type=f32
        )
        return ((key_sum, value_sum), query_grad_block)

    key_start = jnp.zeros((seq_length, local_heads, head_width), f32)
    value_start = jnp.zeros((seq_length, local_heads, HEADV), f32)
    (key_grad_all, value_grad_all), query_grad_blocks = lax.scan(
        attend_back,
        (key_start, value_start),
        (query_blocks, attended_grad_blocks, log_totals, own_segments),
    )
    key_grad, value_grad = col_scatter(
        (
            key_grad_all.reshape(seq_length, local_heads * head_width),
            value_grad_all.reshape(seq_length, local_heads * HEADV),
        )
    )
    key_grad = key_grad.reshape(half_length, local_heads, head_width)
    value_grad = value_grad.reshape(half_length, local_heads, HEADV)
    query_grad = query_grad_blocks.reshape(half_length, local_heads, head_width)
    query_raw_grad = (
        jnp.concatenate(
            [
                query_grad[..., :NOPE],
                rotate(query_grad[..., NOPE:], cosine[:, None, :], sine_table[:, None, :], -1.0),
            ],
            axis=2,
        )
        .astype(bf16)
        .reshape(half_length, local_heads * head_width)
    )
    expanded_grad = (
        jnp.concatenate([key_grad[..., :NOPE], value_grad], axis=2)
        .astype(bf16)
        .reshape(half_length, local_heads * pair_width)
    )
    shared_rope_grad = rotate(jnp.sum(key_grad[..., NOPE:], axis=1), cosine, sine_table, -1.0)

    latent_grad = dot_nt(expanded_grad, expand)
    latent_weighted = latent_grad * rescale
    latent_inner = jnp.mean(latent_weighted * latent_plain, axis=1)
    rescale_part = jnp.sum(latent_grad * latent_plain * latent_scale[:, None], axis=0)
    plain_grad = (
        latent_weighted * latent_scale[:, None]
        - latent_plain * (latent_scale**3 * latent_inner)[:, None]
    )
    latent_raw_grad = jnp.concatenate([plain_grad, shared_rope_grad], axis=1).astype(bf16)
    query_grad_all = col_gather(query_raw_grad)
    latent_grad_all = col_gather(latent_raw_grad)
    first_part = dot_nt(query_grad_all, queries) + dot_nt(latent_grad_all, compress_all)
    first_grad = row_scatter(first_part)
    input_grad = residual_grad + norm_back(inputs, scale_one, scaling, first_grad)

    queries_part = dot_tn(gathered_one, query_grad_all)
    own_latent_grad = lax.psum_scatter(
        latent_raw_grad, "row", scatter_dimension=1, tiled=True
    )
    compress_part = dot_tn(gathered_one, col_gather(own_latent_grad))
    half_rank = RANK // col_count
    latent_normed_all = col_gather(latent_normed)
    expanded_grad_all = col_gather(expanded_grad)
    expand_half = dot_tn(
        lax.dynamic_slice_in_dim(latent_normed_all, col_index * half_rank, half_rank, 1),
        expanded_grad_all,
    )
    scaling_part = jnp.sum(first_part * gathered_one.astype(f32), axis=0) / scaling
    queries_sum, expand_sum, compress_sum = lax.psum(
        (
            after(queries_part.astype(bf16), combine_sum),
            expand_half.astype(bf16),
            compress_part.astype(bf16),
        ),
        "dp",
    )
    premix_sum, router_sum = lax.psum((premix_part, router_part), ("dp", "row"))
    rescale_sum = lax.psum(rescale_part, ("dp", "row", "col"))
    scaling_sum = lax.psum(scaling_part, ("dp", "row"))
    return (
        layer_output,
        input_grad,
        scaling_sum,
        queries_sum.astype(f32),
        compress_sum.astype(f32),
        rescale_sum,
        col_gather(expand_sum).astype(f32),
        combine_sum.astype(f32),
        premix_sum,
        router_sum,
        shared_sums[1].astype(f32),
        shared_sums[0].astype(f32),
        fanout_grad,
        funnel_grad,
    )


def solution(mesh):
    placed = (
        P(("dp", "row"), "col"),
        P(("dp", "row"), "col"),
        P(("dp", "row"), None),
        P("dp"),
        P("col"),
        P("col", "row"),
        P("col", "row"),
        P(),
        P(None, "row"),
        P("row", "col"),
        P("col"),
        P("col", None),
        P(None, "col", "row"),
        P("row", "col"),
        P(("dp", "row"), None, None, "col"),
        P(("dp", "row"), "col", None),
    )
    squared = mesh.shape["dp"] == SQUARE and mesh.shape["row"] == ROWS
    return jax.shard_map(
        local_square if squared else local,
        mesh=mesh,
        in_specs=placed,
        out_specs=(
            P(("dp", "row"), "col"),
            P(("dp", "row"), "col"),
            P("col"),
            P("col", "row"),
            P("col", "row"),
            P(),
            P(None, "row"),
            P("row", "col"),
            P("col"),
            P("col", None),
            P(None, "col", "row"),
            P("row", "col"),
            P(("dp", "row"), None, None, "col"),
            P(("dp", "row"), "col", None),
        ),
        check_vma=False,
    )
```

```python
import functools

import jax
import jax.numpy as jnp
import numpy as np
from jax import lax
from jax.experimental import pallas as pl
from jax.experimental.pallas import tpu as pltpu
from jax.sharding import PartitionSpec as P

D = 2048
NOPE = 128
ROPE = 64
HEADV = 128
RANK = 512
TOP = 6


epsilon = 1e-06
masked_score = -1e30
f32 = jnp.float32
bf16 = jnp.bfloat16


def after(value, *earlier):
    return lax.optimization_barrier((value,) + earlier)[0]


def silu_slope(values):
    sigmoid = jax.nn.sigmoid(values)
    return sigmoid * (1.0 + values * (1.0 - sigmoid))


def rotation(positions, rope_width):
    half_width = rope_width // 2
    frequency = 10000.0 ** (-jnp.arange(half_width, dtype=jnp.float32) * 2.0 / rope_width)
    angles = positions.astype(jnp.float32)[:, None] * frequency[None, :]
    return (jnp.cos(angles), jnp.sin(angles))


def rotate(values, cosine, sine_table, direction):
    half_width = values.shape[-1] // 2
    first_half = values[..., :half_width]
    second_half = values[..., half_width:]
    return jnp.concatenate(
        [
            first_half * cosine - direction * second_half * sine_table,
            second_half * cosine + direction * first_half * sine_table,
        ],
        axis=-1,
    )


def dot(left, right):
    return jnp.dot(left, right, preferred_element_type=f32)


def dot_tn(left, right):
    return lax.dot_general(left, right, (((0,), (0,)), ((), ())), preferred_element_type=f32)


def dot_nt(left, right):
    return lax.dot_general(left, right, (((1,), (1,)), ((), ())), preferred_element_type=f32)


def col_totals(values):
    return lax.psum(values, "col")


def row_gather(values):
    return lax.all_gather(values, "row", axis=0, tiled=True)


def col_gather(values, axis=0):
    return lax.all_gather(values, "col", axis=axis, tiled=True)


def col_scatter(values, axis=0):
    return lax.psum_scatter(values, "col", scatter_dimension=axis, tiled=True)


def row_scatter(values):
    return lax.psum_scatter(
        values.astype(bf16), "row", scatter_dimension=0, tiled=True
    ).astype(f32)


def send_out(parts):
    count = len(parts)
    return [parts[0]] + [
        lax.ppermute(parts[k], "dp", [(i, (i + k) % count) for i in range(count)])
        for k in range(1, count)
    ]


def send_back(parts):
    count = len(parts)
    return [parts[0]] + [
        lax.ppermute(parts[k], "dp", [(i, (i - k) % count) for i in range(count)])
        for k in range(1, count)
    ]


def norm_scale(values):
    square_sum = col_totals(jnp.sum(values * values, axis=1))
    return lax.rsqrt(square_sum / D + epsilon)


def norm_back(values, row_scale, gain_vector, upstream):
    weighted = upstream * gain_vector
    inner_mean = col_totals(jnp.sum(weighted * values, axis=1)) / D
    return weighted * row_scale[:, None] - values * (row_scale**3 * inner_mean)[:, None]


MESH = pl.DeviceIdType.MESH
VMEM = pltpu.VMEM
DMA = pltpu.SemaphoreType.DMA
MIB = 1024 * 1024
ROWS = 4
SQUARE = 4
COLS = 2
SPLIT = 2


def nn(left, right):
    return lax.dot_general(left, right, (((1,), (0,)), ((), ())), preferred_element_type=f32)


def tn(left, right):
    return lax.dot_general(left, right, (((0,), (0,)), ((), ())), preferred_element_type=f32)


def nt(left, right):
    return lax.dot_general(left, right, (((1,), (1,)), ((), ())), preferred_element_type=f32)


def block_at(row, turn):
    swapped = jnp.where(turn < 2, 1 - turn, turn)
    inner = jnp.logical_or(row == 1, row == 2)
    near = jnp.where(inner, swapped, turn)
    return jnp.where(row < 2, near, ROWS - 1 - near)


def partner(place, step):
    across, along = lax.rem(place, 2), lax.div(place, 2)
    across = lax.rem(across + step % 2, 2)
    along = lax.rem(along + step // 2, 2)
    return along * 2 + across


def remote(source, target, sent, arrived, where):
    return pltpu.make_async_remote_copy(
        src_ref=source,
        dst_ref=target,
        send_sem=sent,
        recv_sem=arrived,
        device_id=where,
        device_id_type=MESH,
    )


def greet(row, place, col, line=False, square=True):
    barrier = pltpu.get_barrier_semaphore()
    met = 1
    if line:
        for step in range(1, ROWS):
            pl.semaphore_signal(
                barrier,
                inc=1,
                device_id={"row": lax.rem(row + step, ROWS)},
                device_id_type=MESH,
            )
        met = met + ROWS - 1
    else:

        @pl.when(row > 0)
        def _():
            pl.semaphore_signal(barrier, inc=1, device_id={"row": row - 1}, device_id_type=MESH)

        @pl.when(row < ROWS - 1)
        def _():
            pl.semaphore_signal(barrier, inc=1, device_id={"row": row + 1}, device_id_type=MESH)

        met = met + (row > 0).astype(jnp.int32) + (row < ROWS - 1).astype(jnp.int32)
    if square:
        for step in range(1, SQUARE):
            pl.semaphore_signal(
                barrier, inc=1, device_id={"dp": partner(place, step)}, device_id_type=MESH
            )
        met = met + SQUARE - 1
    pl.semaphore_signal(barrier, inc=1, device_id={"col": 1 - col}, device_id_type=MESH)
    pl.semaphore_wait(barrier, met)


class Line:
    def __init__(self, row, buffer, sent, arrived):
        self.row, self.buffer, self.sent, self.arrived = row, buffer, sent, arrived

    def copy(self, block, way):
        to = self.row + 1 if way == 0 else self.row - 1
        here = self.buffer.at[block]
        return remote(here, here, self.sent.at[block, way], self.arrived.at[block], {"row": to})

    def each(self, block, act):
        @pl.when(jnp.logical_and(block <= self.row, self.row < ROWS - 1))
        def _():
            act(self.copy(block, 0))

        @pl.when(jnp.logical_and(block >= self.row, self.row > 0))
        def _():
            act(self.copy(block, 1))

    def wait(self, block):
        self.copy(block, 0).wait_recv()

    def pass_on(self, block):
        self.each(block, lambda copy: copy.start())

    def finish(self):
        def one(block, carried):
            self.each(block, lambda copy: copy.wait_send())
            return carried

        lax.fori_loop(0, ROWS, one, 0)


class SquareRest:
    def __init__(self, place, which, kept, got, middle, second, result, sent, arrived):
        self.x, self.y, self.which = lax.rem(place, 2), lax.div(place, 2), which
        self.to_x, self.to_y = {"dp": partner(place, 1)}, {"dp": partner(place, 2)}
        self.kept, self.got = kept, got
        self.middle, self.second, self.result = middle, second, result
        self.sent, self.arrived = sent.at[which], arrived.at[which]

    def copies(self, phase):
        x, y, which = self.x, self.y, self.which
        if phase == 1:
            plan = (
                (self.middle.at[0, which], self.second.at[0, which], self.to_y),
                (self.middle.at[1, which], self.second.at[1, which], self.to_x),
            )
        elif phase == 2:
            one = self.result.at[2 * x + y, which]
            two = self.result.at[4 + 2 * y + x, which]
            plan = ((one, one, self.to_y), (two, two, self.to_x))
        else:
            one = self.result.at[pl.ds(2 * x, 2), which]
            two = self.result.at[pl.ds(4 + 2 * y, 2), which]
            plan = ((one, one, self.to_x), (two, two, self.to_y))
        return [
            remote(source, target, self.sent.at[2 * phase + i], self.arrived.at[2 * phase + i], to)
            for i, (source, target, to) in enumerate(plan)
        ]

    def sum_of(self, half, side):
        wide = self.middle.shape[3]
        lanes = pl.ds(pl.multiple_of(side * wide, 128), wide)
        which = self.which
        kept, got = self.kept[half, which, :, lanes], self.got[half, which, :, lanes]
        return kept.astype(f32) + got.astype(f32)

    def run(self, phase):
        x, y, which = self.x, self.y, self.which
        if phase > 1:
            for copy in self.copies(phase - 1):
                copy.wait_recv()
        if phase == 1:
            self.middle[0, which] = self.sum_of(0, 1 - y).astype(bf16)
            self.middle[1, which] = self.sum_of(1, 1 - x).astype(bf16)
        if phase == 2:
            self.result[2 * x + y, which] = (
                self.sum_of(0, y) + self.second[0, which].astype(f32)
            ).astype(bf16)
            self.result[4 + 2 * y + x, which] = (
                self.sum_of(1, x) + self.second[1, which].astype(f32)
            ).astype(bf16)
        if phase < 4:
            for copy in self.copies(phase):
                copy.start()

    def finish(self):
        for phase in (1, 2, 3):
            for copy in self.copies(phase):
                copy.wait_send()


class SumLine:
    def __init__(self, row, part, leaving, coming, sent, arrived):
        self.row, self.part, self.leaving, self.coming = row, part, leaving, coming
        self.sent, self.arrived = sent, arrived
        self.lines = part.shape[1] // SPLIT

    def piece(self, index):
        return pl.ds(index * self.lines, self.lines)

    def copy(self, block, index, way):
        return remote(
            self.leaving.at[block, self.piece(index)],
            self.coming.at[way, block, self.piece(index)],
            self.sent.at[block, index],
            self.arrived.at[way, block, index],
            {"row": self.row + 1 - 2 * way},
        )

    def send(self, block, index):
        @pl.when(block > self.row)
        def _():
            self.copy(block, index, 0).start()

        @pl.when(block < self.row)
        def _():
            self.copy(block, index, 1).start()

    def chained(self, block):
        return jnp.logical_or(
            jnp.logical_and(block > self.row, self.row > 0),
            jnp.logical_and(block < self.row, self.row < ROWS - 1),
        )

    def begin(self, block):
        @pl.when(jnp.logical_and(block != self.row, jnp.logical_not(self.chained(block))))
        def _():
            self.leaving[block] = self.part[block].astype(bf16)
            for index in range(SPLIT):
                self.send(block, index)

    def pass_on(self, block):
        @pl.when(self.chained(block))
        def _():
            way = (block < self.row).astype(jnp.int32)
            for index in range(SPLIT):
                self.copy(block, index, way).wait_recv()
                piece = self.piece(index)
                self.leaving[block, piece] = (
                    self.part[block, piece].astype(f32)
                    + self.coming[way, block, piece].astype(f32)
                ).astype(bf16)
                self.send(block, index)

    def total(self, target):
        target[...] = self.part[self.row].astype(f32)
        for way, there in ((0, self.row > 0), (1, self.row < ROWS - 1)):

            @pl.when(there)
            def _(way=way):
                for index in range(SPLIT):
                    self.copy(self.row, index, way).wait_recv()
                    target[self.piece(index)] += self.coming[
                        way, self.row, self.piece(index)
                    ].astype(f32)

    def finish(self):
        def one(block, carried):
            @pl.when(block != self.row)
            def _():
                for index in range(SPLIT):
                    self.copy(block, index, 0).wait_send()

            return carried

        lax.fori_loop(0, ROWS, one, 0)


def swap_halves(values):
    lanes = values.shape[1]
    lane = lax.broadcasted_iota(jnp.int32, values.shape, 1)
    return jnp.where(
        lane % ROPE < ROPE // 2,
        pltpu.roll(values, lanes - ROPE // 2, 1),
        pltpu.roll(values, ROPE // 2, 1),
    )


def attend_kernel(
    act_ref,
    scaling_ref,
    compress_ref,
    rescale_ref,
    premix_ref,
    cos_ref,
    sin_ref,
    key_cos_ref,
    key_sin_ref,
    mark_ref,
    cot_ref,
    route_ref,
    router_ref,
    queries_ref,
    expand_ref,
    combine_ref,
    one_out,
    query_out,
    key_out,
    value_out,
    probs_out,
    latent_out,
    normed_latent_out,
    attended_out,
    compress_out,
    cot_out,
    pick_out,
    back_out,
    rows_out,
    residual_ref,
    two_ref,
    scale_one_ref,
    scale_two_ref,
    router_all,
    one_ref,
    query_ref,
    key_ref,
    value_ref,
    probs_ref,
    latent_ref,
    normed_latent_ref,
    attended_ref,
    compress_all,
    cot_all,
    pick_ref,
    back_ref,
    rows_ref,
    queries,
    expand,
    combine,
    stat_to,
    stat_from,
    query_own,
    query_to,
    query_from,
    latent_to,
    latent_from,
    part,
    leaving,
    coming,
    routes,
    staged,
    marks,
    raw,
    scales,
    load_sem,
    store_sem,
    rows_sem,
    stat_sent,
    stat_arrived,
    line_sent,
    line_arrived,
    comp_sent,
    comp_arrived,
    comp_out_sent,
    comp_out_arrived,
    query_sent,
    query_arrived,
    latent_sent,
    latent_arrived,
    att_sent,
    att_arrived,
    sum_sent,
    sum_arrived,
    cot_sent,
    cot_arrived,
    route_sent,
    route_arrived,
    out_sent,
    out_arrived,
    pair_sent,
    pair_arrived,
    router_sent,
    router_arrived,
    scale_sent,
    scale_arrived,
):
    place, row, col = lax.axis_index("dp"), lax.axis_index("row"), lax.axis_index("col")
    other = 1 - col
    inner = jnp.logical_and(row > 0, row < ROWS - 1)
    sibling = {"col": other}
    tokens, width = act_ref.shape
    slots = pick_ref.shape[1] // SQUARE
    mine = query_own.shape[2]
    sliced = compress_ref.shape[0]
    quarter = width // SQUARE
    score_scale = (NOPE + ROPE) ** (-0.5)
    loads = [
        pltpu.make_async_copy(source, target, load_sem.at[i])
        for i, (source, target) in enumerate(
            [(queries_ref, queries), (expand_ref, expand), (combine_ref, combine)]
        )
    ]
    for load in loads:
        load.start()
    stores = [
        pltpu.make_async_copy(source, target, store_sem.at[i])
        for i, (source, target) in enumerate(
            [
                (one_ref, one_out),
                (query_ref, query_out),
                (key_ref, key_out),
                (value_ref, value_out),
                (latent_ref, latent_out),
                (normed_latent_ref, normed_latent_out),
                (compress_all, compress_out),
                (probs_ref, probs_out),
                (attended_ref, attended_out),
                (cot_all, cot_out),
                (pick_ref, pick_out),
                (back_ref, back_out),
            ]
        )
    ]

    def rows_store(block):
        return pltpu.make_async_copy(
            rows_ref.at[:, block], rows_out.at[:, block], rows_sem.at[block]
        )

    def stat_copy(index):
        return remote(
            stat_to.at[index],
            stat_from.at[index],
            stat_sent.at[index],
            stat_arrived.at[index],
            sibling,
        )

    def scale_of(values, index):
        own = jnp.sum(values * values, axis=1, keepdims=True)
        stat_to[index] = jnp.broadcast_to(own, (tokens, 128))
        stat_copy(index).start()
        stat_copy(index).wait_recv()
        return lax.rsqrt((own + stat_from[index][:, 0:1]) / D + epsilon)

    def comp_piece(block, member):
        return compress_all.at[
            pl.ds(pl.multiple_of(block * sliced, 16), sliced),
            pl.ds(pl.multiple_of(member * quarter, 128), quarter),
        ]

    def comp_copy(block, way):
        here = comp_piece(block, place)
        return remote(
            here,
            here,
            comp_sent.at[block, way],
            comp_arrived.at[block],
            {"row": row + 1 - 2 * way},
        )

    def comp_each(block, act):
        @pl.when(jnp.logical_and(block <= row, row < ROWS - 1))
        def _():
            act(comp_copy(block, 0))

        @pl.when(jnp.logical_and(block >= row, row > 0))
        def _():
            act(comp_copy(block, 1))

    def comp_out(block, step, member):
        here = comp_piece(block, member)
        return remote(
            here,
            here,
            comp_out_sent.at[block, step],
            comp_out_arrived.at[block, step],
            {"dp": partner(place, step)},
        )

    line = Line(row, raw, line_sent, line_arrived)
    scale_line = Line(row, scales, scale_sent, scale_arrived)
    cot_line = Line(row, cot_all, cot_sent, cot_arrived)
    route_line = Line(row, routes, route_sent, route_arrived)
    sums = SumLine(row, part, leaving, coming, sum_sent, sum_arrived)

    greet(row, place, col)
    compress_all[pl.ds(pl.multiple_of(row * sliced, 16), sliced)] = compress_ref[...]
    compress_all[ROWS * sliced :] = jnp.zeros(
        (compress_all.shape[0] - ROWS * sliced, width), bf16
    )
    comp_each(row, lambda copy: copy.start())
    raw[pl.ds(row, 1)] = act_ref[...].reshape(1, tokens, width)
    line.pass_on(row)

    def router_copy(half):
        here = router_all.at[:, pl.ds(pl.multiple_of(half * width, width), width)]
        return remote(here, here, router_sent.at[0], router_arrived.at[0], sibling)

    inputs = act_ref[...].astype(f32)
    scale_one = scale_of(inputs, 0)
    scale_one_ref[...] = scale_one
    scales[pl.ds(row, 1)] = jnp.broadcast_to(scale_one, (tokens, 128)).T[0:8].reshape(1, 8, tokens)
    scale_line.pass_on(row)
    router_all[:, pl.ds(pl.multiple_of(col * width, width), width)] = router_ref[...]
    router_copy(col).start()
    cot_all[pl.ds(row, 1)] = cot_ref[...].reshape(1, tokens, width)
    routes[pl.ds(row, 1)] = route_ref[...].reshape((1,) + route_ref.shape)

    @pl.when(jnp.logical_not(inner))
    def _():
        route_line.pass_on(row)
        cot_line.pass_on(row)

    for block in range(ROWS):
        mark = mark_ref[:, block * tokens : (block + 1) * tokens].astype(f32)
        marks[block] = jnp.broadcast_to(mark, (8, tokens)).T
    loads[0].wait()

    def query_copy(block):
        return remote(
            query_to.at[block],
            query_from.at[block],
            query_sent.at[block],
            query_arrived.at[block],
            sibling,
        )

    def latent_copy(block):
        return remote(
            latent_to.at[block],
            latent_from.at[block],
            latent_sent.at[block],
            latent_arrived.at[block],
            sibling,
        )

    def att_copy(block, half):
        here = attended_ref.at[block, :, pl.ds(pl.multiple_of(half * 2 * HEADV, 128), 2 * HEADV)]
        return remote(here, here, att_sent.at[block], att_arrived.at[block], sibling)

    def comp_relay(step):
        block = block_at(row, step)
        comp_copy(block, 0).wait_recv()
        comp_each(block, lambda copy: copy.start())
        for shift in (3, 2, 1):
            comp_out(block, shift, place).start()

    def relay_one(step):
        block = block_at(row, step)
        line.wait(block)
        line.pass_on(block)
        scale_line.wait(block)
        scale_line.pass_on(block)

    def normalise(step):
        block = block_at(row, step)
        scale = scales[block].T[:, 0:1]
        normed = (raw[block].astype(f32) * scale * scaling_ref[...]).astype(bf16)
        one_ref[block] = normed
        query_to[block] = nn(
            normed, queries[:, pl.ds(pl.multiple_of(other * mine, 128), mine)]
        ).astype(bf16)
        query_copy(block).start()
        query_own[block] = nn(normed, queries[:, pl.ds(pl.multiple_of(col * mine, 128), mine)])

    def latents(step):
        block = block_at(row, step)
        value = nt(one_ref[block], compress_all[...])
        latent_to[block] = value
        latent_copy(block).start()
        latent_ref[block] = value

    def keys(step):
        block = block_at(row, step)
        latent_copy(block).wait_recv()
        latent = latent_ref[block] + latent_from[block]
        latent_ref[block] = latent
        plain = latent[:, :RANK]
        scale = lax.rsqrt(jnp.mean(plain * plain, axis=1, keepdims=True) + epsilon)
        normed = (plain * scale * rescale_ref[...]).astype(bf16)
        normed_latent_ref[block] = normed
        own = 2 * (NOPE + HEADV)
        expanded = nn(normed, expand[:, pl.ds(pl.multiple_of(col * own, 128), own)])
        rope = latent[:, RANK:]
        rope = rope * key_cos_ref[block] + swap_halves(rope) * key_sin_ref[block]
        first = jnp.concatenate([expanded[:, :NOPE], rope], axis=1)
        second = jnp.concatenate([expanded[:, 2 * NOPE : 3 * NOPE], rope], axis=1)
        key_ref[0, block] = first.astype(bf16)
        key_ref[1, block] = pltpu.roll(second, ROPE, 1).astype(bf16)
        value_ref[0, block] = expanded[:, NOPE : 2 * NOPE].astype(bf16)
        value_ref[1, block] = expanded[:, 3 * NOPE :].astype(bf16)
        query_copy(block).wait_recv()
        query = query_own[block] + query_from[block].astype(f32)
        query_ref[block] = (
            query * cos_ref[block] + swap_halves(query) * sin_ref[block]
        ).astype(bf16)

    def gather(step, carried):
        @pl.when(step > 0)
        def _():
            relay_one(step)

        normalise(step)

        @pl.when(step < 2)
        def _():
            comp_relay(step + 1)

        @pl.when(step == 1)
        def _():
            comp_relay(3)

        return carried

    lax.fori_loop(0, ROWS - 1, gather, 0)

    @pl.when(inner)
    def _():
        relay_one(ROWS - 1)

    def comp_arrive(block, carried):
        @pl.when(block != row)
        def _():
            for shift in range(1, SQUARE):
                comp_out(block, shift, partner(place, shift)).wait_recv()

        return carried

    lax.fori_loop(0, ROWS, comp_arrive, 0)
    loads[1].wait()

    def middle(step, carried):
        @pl.when(jnp.logical_and(step == ROWS - 1, jnp.logical_not(inner)))
        def _():
            relay_one(step)

        @pl.when(step == ROWS - 1)
        def _():
            normalise(step)

        @pl.when(step < ROWS)
        def _():
            latents(step)

        @pl.when(step > 0)
        def _():
            keys(step - 1)

        return carried

    lax.fori_loop(0, ROWS - 1, middle, 0)

    @pl.when(inner)
    def _():
        route_line.pass_on(row)
        cot_line.pass_on(row)

    def relay(step):
        block = block_at(row, step)
        route_line.wait(block)
        route_line.pass_on(block)
        cot_line.wait(block)
        cot_line.pass_on(block)

    def out_copy(block, step):
        piece = pl.ds(step * slots, slots)
        return remote(
            staged.at[block, piece],
            rows_ref.at[col, block, piece],
            out_sent.at[block, step],
            out_arrived.at[block, step],
            {"dp": partner(place, step)},
        )

    def pair_copy(block, half):
        here = rows_ref.at[half, block]
        return remote(here, here, pair_sent.at[block], pair_arrived.at[block], sibling)

    def take(step):
        block = block_at(row, step)

        @pl.when(jnp.logical_and(step > 0, jnp.logical_not(inner)))
        def _():
            relay(step)

        before = (
            lax.broadcasted_iota(jnp.int32, (tokens, tokens), 0)
            < lax.broadcasted_iota(jnp.int32, (tokens, tokens), 1)
        ).astype(bf16)
        routing = routes[block]
        chosen = []
        for shift in range(SQUARE):
            expert = partner(place, shift) * ROWS + row
            hit = (routing == expert).astype(f32)
            chosen.append(jnp.max(hit, axis=0, keepdims=True))
        goes = jnp.concatenate(chosen + chosen, axis=0)
        rank = nn(goes.astype(bf16), before)
        for shift in range(SQUARE):
            slot = lax.broadcasted_iota(jnp.int32, (slots, tokens), 0).astype(f32)
            here = jnp.logical_and(slot == rank[shift : shift + 1], goes[shift : shift + 1] > 0.5)
            pick = here.astype(f32)
            pick_ref[block, shift * slots : (shift + 1) * slots] = pick.astype(bf16)
            back_ref[block, :, shift * slots : (shift + 1) * slots] = pick.T.astype(bf16)
        staged[block] = nn(pick_ref[block], cot_all[block]).astype(bf16)
        for shift in (3, 2, 1):
            out_copy(block, shift).start()
        rows_ref[col, block, 0:slots] = staged[block, 0:slots]

    def forward(step):
        block = block_at(row, step)
        for shift in range(1, SQUARE):
            out_copy(block, shift).wait_recv()
        pair_copy(block, col).start()

    take(0)
    lax.fori_loop(ROWS - 1, ROWS + 1, middle, 0)

    @pl.when(inner)
    def _():
        relay(1)
        relay(2)

    for index in range(7):
        stores[index].start()
    seq = ROWS * tokens
    lanes = NOPE + 2 * ROPE

    def attend(turn, carried):
        block = block_at(row, ROWS - 1 - turn)
        visible = mark_ref[...].astype(f32) <= marks[block][:, 0:1]
        for head in range(2):
            query = query_ref[block, :, head * NOPE : head * NOPE + lanes]
            scores = nt(query, key_ref[head].reshape(seq, lanes)) * score_scale
            scores = jnp.where(visible, scores, masked_score)
            weight = jnp.exp(scores - jnp.max(scores, axis=1, keepdims=True))
            probs = (weight / jnp.sum(weight, axis=1, keepdims=True)).astype(bf16)
            probs_ref[head, block] = probs
            result = nn(probs, value_ref[head].reshape(seq, HEADV)).astype(bf16)
            at = pl.multiple_of((col * 2 + head) * HEADV, 128)
            attended_ref[block, :, pl.ds(at, HEADV)] = result
        att_copy(block, col).start()

        @pl.when(jnp.logical_and(turn == 0, inner))
        def _():
            relay(3)

        @pl.when(turn > 0)
        def _():
            mix(turn - 1)
            take(turn)

        return carried

    def mix(turn):
        block = block_at(row, ROWS - 1 - turn)
        att_copy(block, other).wait_recv()
        part[block] = nn(attended_ref[block], combine[...])
        sums.begin(block)

    loads[2].wait()
    lax.fori_loop(0, ROWS, attend, 0)
    mix(ROWS - 1)
    for index in range(7, 12):
        stores[index].start()

    def hand_on(turn, carried):
        sums.pass_on(block_at(row, jnp.where(turn == 0, 3, turn)))
        forward(turn)
        return carried

    lax.fori_loop(0, 3, hand_on, 0)
    sums.total(residual_ref)
    residual = residual_ref[...] + inputs
    residual_ref[...] = residual
    scale_two = scale_of(residual, 1)
    scale_two_ref[...] = scale_two
    two_ref[...] = (residual * scale_two * premix_ref[...]).astype(bf16)
    forward(3)

    def ended(block, carried):
        pair_copy(block, other).wait_recv()
        rows_store(block).start()
        pair_copy(block, col).wait_send()
        for shift in range(1, SQUARE):
            out_copy(block, shift).wait_send()

            @pl.when(block != row)
            def _(shift=shift):
                comp_out(block, shift, place).wait_send()

        comp_each(block, lambda copy: copy.wait_send())
        query_copy(block).wait_send()
        latent_copy(block).wait_send()
        att_copy(block, col).wait_send()
        return carried

    lax.fori_loop(0, ROWS, ended, 0)
    for store in stores:
        store.wait()

    def stored(block, carried):
        rows_store(block).wait()
        return carried

    lax.fori_loop(0, ROWS, stored, 0)
    router_copy(other).wait_recv()
    router_copy(col).wait_send()
    stat_copy(0).wait_send()
    stat_copy(1).wait_send()
    sums.finish()
    line.finish()
    scale_line.finish()
    cot_line.finish()
    route_line.finish()


def turning_tables(length):
    half = ROPE // 2
    frequency = 10000.0 ** (-np.arange(half, dtype=np.float32) * 2.0 / ROPE)
    angles = np.arange(length, dtype=np.float32)[:, None] * frequency[None, :].astype(np.float32)
    cosine, sine = np.cos(angles), np.sin(angles)
    cosine, sine = np.concatenate([cosine, cosine], 1), np.concatenate([-sine, sine], 1)
    ones, zeros = np.ones((length, NOPE)), np.zeros((length, NOPE))
    gap = np.zeros((length, 128 - ROPE))
    tables = (
        np.concatenate([ones, cosine, ones, cosine], 1),
        np.concatenate([zeros, sine, zeros, sine], 1),
        np.concatenate([cosine, gap], 1),
        np.concatenate([sine, gap], 1),
    )
    return [
        jnp.asarray(table.reshape(ROWS, length // ROWS, -1).astype(np.float32))
        for table in tables
    ]


def pair_sems():
    return [DMA((ROWS,)), DMA((ROWS,))]


def line_sems():
    return [DMA((ROWS, 2)), DMA((ROWS,))]


def square_sems():
    return [DMA((ROWS, SQUARE)), DMA((ROWS, SQUARE))]


def sum_sems():
    return [DMA((ROWS, SPLIT)), DMA((2, ROWS, SPLIT))]


def run_attention(
    activations,
    scaling,
    queries,
    compress,
    rescale,
    expand,
    combine,
    premix,
    segments,
    cotangent,
    routing,
    router,
    tables,
    slots,
):
    tokens, width = activations.shape
    seq = ROWS * tokens
    mine = queries.shape[1] // COLS
    sliced = compress.shape[1]
    latent_width = RANK + 128
    picked = SQUARE * slots
    lanes = NOPE + 2 * ROPE
    routes = routing.T
    whole = pl.BlockSpec(memory_space=VMEM)
    far = pl.BlockSpec(memory_space=pl.ANY)

    def shape(*dims, dtype=bf16):
        return jax.ShapeDtypeStruct(dims, dtype)

    kept = [
        shape(ROWS, tokens, width),
        shape(ROWS, tokens, mine),
        shape(2, ROWS, tokens, lanes),
        shape(2, ROWS, tokens, HEADV),
        shape(2, ROWS, tokens, seq),
        shape(ROWS, tokens, latent_width, dtype=f32),
        shape(ROWS, tokens, RANK),
        shape(ROWS, tokens, COLS * 2 * HEADV),
        shape(latent_width, width),
        shape(ROWS, tokens, width),
        shape(ROWS, picked, tokens),
        shape(ROWS, tokens, picked),
        shape(COLS, ROWS, picked, width),
    ]
    return pl.pallas_call(
        attend_kernel,
        name="attend",
        out_shape=(
            *kept,
            shape(tokens, width, dtype=f32),
            shape(tokens, width),
            shape(tokens, 1, dtype=f32),
            shape(tokens, 1, dtype=f32),
            shape(router.shape[1], COLS * width),
        ),
        in_specs=[whole] * 13 + [far] * 3,
        out_specs=(far,) * 13 + (whole,) * 5,
        scratch_shapes=[
            *[VMEM(value.shape, value.dtype) for value in kept],
            VMEM(queries.shape, bf16),
            VMEM(expand.shape, bf16),
            VMEM(combine.shape, bf16),
            VMEM((2, tokens, 128), f32),
            VMEM((2, tokens, 128), f32),
            VMEM((ROWS, tokens, mine), f32),
            VMEM((ROWS, tokens, mine), bf16),
            VMEM((ROWS, tokens, mine), bf16),
            VMEM((ROWS, tokens, latent_width), f32),
            VMEM((ROWS, tokens, latent_width), f32),
            VMEM((ROWS, tokens, width), f32),
            VMEM((ROWS, tokens, width), bf16),
            VMEM((2, ROWS, tokens, width), bf16),
            VMEM((ROWS,) + routes.shape, jnp.int32),
            VMEM((ROWS, picked, width), bf16),
            VMEM((ROWS, tokens, 8), f32),
            VMEM((ROWS, tokens, width), bf16),
            VMEM((ROWS, 8, tokens), f32),
            DMA((3,)),
            DMA((12,)),
            DMA((ROWS,)),
            DMA((2,)),
            DMA((2,)),
            *line_sems(),
            *line_sems(),
            *square_sems(),
            *pair_sems(),
            *pair_sems(),
            *pair_sems(),
            *sum_sems(),
            *line_sems(),
            *line_sems(),
            *square_sems(),
            *pair_sems(),
            DMA((1,)),
            DMA((1,)),
            *line_sems(),
        ],
        compiler_params=pltpu.CompilerParams(
            collective_id=1, has_side_effects=True, vmem_limit_bytes=56 * MIB
        ),
        cost_estimate=pl.CostEstimate(
            flops=40 * 1024**3, bytes_accessed=32 * MIB, transcendentals=0
        ),
    )(
        activations,
        scaling.reshape(1, width),
        compress.T,
        rescale.reshape(1, RANK),
        premix.reshape(1, width),
        *tables,
        segments.reshape(1, seq),
        cotangent,
        routes,
        router.T,
        queries,
        expand,
        combine,
    )


def attend_back_kernel(
    normed_grad_ref,
    residual_ref,
    scale_two_ref,
    premix_ref,
    cot_ref,
    act_ref,
    scale_one_ref,
    scaling_ref,
    rescale_ref,
    combine_far,
    query_far,
    key_far,
    value_far,
    probs_far,
    cos_far,
    sin_far,
    queries_far,
    expand_far,
    latent_far,
    key_cos_far,
    key_sin_far,
    compress_far,
    one_far,
    kept_far,
    got_x_far,
    got_y_far,
    attended_far,
    normed_latent_far,
    narrow_far,
    home_far,
    back_far,
    shared_far,
    premix_far,
    router_far,
    input_grad_ref,
    output_ref,
    small_ref,
    shared_sum,
    queries_out,
    combine_out,
    expand_out,
    compress_out,
    branch_ref,
    query_grad_ref,
    expanded_ref,
    own_latent_ref,
    scaling_rows,
    rescale_rows,
    combine,
    query_ref,
    key_ref,
    value_ref,
    probs_ref,
    cos_ref,
    sin_ref,
    queries,
    expand,
    latent_ref,
    key_cos_ref,
    key_sin_ref,
    compress_all,
    one_ref,
    kept,
    got,
    middle,
    second,
    result,
    attended,
    normed_latent,
    narrow,
    home,
    back_ref,
    shared_ref,
    premix_rows,
    router_rows,
    stat_to,
    stat_from,
    grad_own,
    grad_to,
    grad_from,
    key_grad,
    value_grad,
    latent_own,
    latent_to,
    latent_from,
    turned,
    turned_from,
    part,
    leaving,
    coming,
    total,
    load_sem,
    stat_sent,
    stat_arrived,
    line_sent,
    line_arrived,
    grad_sent,
    grad_arrived,
    query_sent,
    query_arrived,
    latent_sent,
    latent_arrived,
    turned_sent,
    turned_arrived,
    own_sent,
    own_arrived,
    sum_sent,
    sum_arrived,
    rest_sent,
    rest_arrived,
    rest_sem,
    reply_part,
    reply_leaving,
    reply_coming,
    small_to,
    small_from,
    small_line,
    small_square,
    small_own,
    expand_other,
    store_sem,
    reply_sent,
    reply_arrived,
    pair_sent,
    pair_arrived,
    small_sent,
    small_arrived,
    *sums_scratch,
):
    place, row, col = lax.axis_index("dp"), lax.axis_index("row"), lax.axis_index("col")
    other = 1 - col
    sibling = {"col": other}
    tokens, width = act_ref.shape
    seq = ROWS * tokens
    mine = query_ref.shape[2]
    lanes = key_ref.shape[3]
    both = 2 * HEADV
    sliced = own_latent_ref.shape[0]
    score_scale = (NOPE + ROPE) ** (-0.5)
    loads = [
        pltpu.make_async_copy(source, target, load_sem.at[i])
        for i, (source, target) in enumerate(
            [
                (kept_far, kept),
                (got_x_far, got.at[0]),
                (got_y_far, got.at[1]),
                (combine_far, combine),
                (query_far, query_ref),
                (key_far, key_ref),
                (value_far, value_ref),
                (probs_far, probs_ref),
                (cos_far, cos_ref),
                (sin_far, sin_ref),
                (queries_far, queries),
                (expand_far, expand),
                (latent_far, latent_ref),
                (key_cos_far, key_cos_ref),
                (key_sin_far, key_sin_ref),
                (compress_far, compress_all),
                (one_far, one_ref),
                (attended_far, attended),
                (normed_latent_far, normed_latent),
                (narrow_far, narrow),
                (home_far, home),
                (back_far, back_ref),
                (shared_far, shared_ref),
                (premix_far, premix_rows),
                (router_far, router_rows),
            ]
        )
    ]
    for load in loads:
        load.start()
    line = Line(row, branch_ref, line_sent, line_arrived)
    sums = SumLine(row, part, leaving, coming, sum_sent, sum_arrived)
    greet(row, place, col, line=True)

    def stat_copy(index):
        return remote(
            stat_to.at[index],
            stat_from.at[index],
            stat_sent.at[index],
            stat_arrived.at[index],
            sibling,
        )

    def norm_begin(values, gain, upstream, index):
        weighted = upstream * gain
        own = jnp.sum(weighted * values, axis=1, keepdims=True)
        stat_to[index] = jnp.broadcast_to(own, (tokens, 128))
        stat_copy(index).start()

    def norm_grad(values, scale, gain, upstream, index):
        stat_copy(index).wait_recv()
        inner = (stat_to[index][:, 0:1] + stat_from[index][:, 0:1]) / D
        return upstream * gain * scale - values * (scale * scale * scale * inner)

    norm_begin(residual_ref[...], premix_ref[...], normed_grad_ref[...], 0)
    for load in loads[0:3]:
        load.wait()
    rests = [
        SquareRest(place, which, kept, got, middle, second, result, rest_sent, rest_arrived)
        for which in range(kept.shape[1])
    ]
    for rest in rests:
        rest.run(1)
    residual_grad = cot_ref[...].astype(f32) + norm_grad(
        residual_ref[...], scale_two_ref[...], premix_ref[...], normed_grad_ref[...], 0
    )
    input_grad_ref[...] = residual_grad
    branch_ref[pl.ds(row, 1)] = residual_grad.astype(bf16).reshape(1, tokens, width)
    line.pass_on(row)
    key_grad[...] = jnp.zeros_like(key_grad)
    value_grad[...] = jnp.zeros_like(value_grad)
    scaling_rows[...] = jnp.zeros_like(scaling_rows)
    rescale_rows[...] = jnp.zeros_like(rescale_rows)

    line_sums = SumLine(
        row, reply_part, reply_leaving, reply_coming, reply_sent, reply_arrived
    )
    experts = router_rows.shape[0]
    kinds = [sums_scratch[7 * i : 7 * i + 7] for i in range(4)]
    parts = [scratch[0] for scratch in kinds]
    plan = [(kind, chunk) for kind in range(4) for chunk in range(parts[kind].shape[0])]
    pieces_of = [
        SquareSum(place, *[ref.at[chunk] for ref in kinds[kind]]) for kind, chunk in plan
    ]
    count = len(plan)

    def begin(index):
        kind, chunk = plan[index]
        part_ref = parts[kind]
        if kind == 0 and chunk == 0:
            loads[17].wait()
        if kind == 2:
            loads[18].wait()
        if kind < 2:
            left, right = ((attended, branch_ref), (one_ref, query_grad_ref))[kind]
            height = 8 * part_ref.shape[2]
            piece = left[:, :, chunk * height : (chunk + 1) * height].reshape(seq, height)
            grad = tn(piece, right[...].reshape(seq, right.shape[2]))
        elif kind == 2:
            grad = tn(
                normed_latent[...].reshape(seq, RANK),
                expanded_ref[...].reshape(seq, expanded_ref.shape[2]),
            )
        else:
            grad = nn(own_latent_ref[...], one_ref[...].reshape(seq, width)).astype(bf16)
            for piece in range(8):
                part_ref[0, piece] = grad[:, piece * (width // 8) : (piece + 1) * (width // 8)]
        if kind < 3:
            part_ref[chunk] = grad.astype(bf16).reshape(part_ref.shape[1:])
        pieces_of[index].run(0)

    stores = []

    def store(source, target):
        copy = pltpu.make_async_copy(source, target, store_sem.at[len(stores)])
        copy.start()
        stores.append(copy)

    def pair_copy():
        return remote(kinds[2][4].at[0], expand_other, pair_sent.at[0], pair_arrived.at[0], sibling)

    def expand_lanes(half):
        wide = expand_other.shape[2]
        return expand_out.at[:, :, pl.ds(pl.multiple_of(half * wide, 128), wide)]

    def put(index):
        kind, chunk = plan[index]
        done = kinds[kind][4]
        if kind < 2:
            store(done.at[chunk], (combine_out, queries_out)[kind].at[chunk])
        elif kind == 2:
            store(done.at[0], expand_lanes(col))
            pair_copy().start()
        else:
            lanes = width // 8
            for piece in range(8):
                store(done.at[0, piece], compress_out.at[:, piece * lanes : (piece + 1) * lanes])

    def advance(turn):
        for phase in (1, 2, 3, 4):
            index = turn - phase
            if 0 <= index < count:
                pieces_of[index].run(phase)
                if phase == 4:
                    put(index)
        if 2 <= turn < count:
            begin(turn)

    def reply_add(turn, carried):
        block = block_at(row, ROWS - 1 - turn)
        reply_part[block] = (
            nn(back_ref[block], home[block]) + nn(shared_ref[block], narrow[...])
        ).astype(bf16)
        line_sums.begin(block)
        return carried

    def small_copy(step):
        if step == 0:
            return remote(small_to, small_from, small_sent.at[0], small_arrived.at[0], sibling)
        if step < ROWS:
            return remote(
                small_own,
                small_line.at[step],
                small_sent.at[step],
                small_arrived.at[step],
                {"row": lax.rem(row + step, ROWS)},
            )
        shift = step - ROWS + 1
        return remote(
            small_ref,
            small_square.at[shift],
            small_sent.at[step],
            small_arrived.at[step],
            {"dp": partner(place, shift)},
        )

    def small_begin():
        loads[23].wait()
        loads[24].wait()
        rescale_row = jnp.sum(rescale_rows[...], axis=0, keepdims=True)
        empty = jnp.zeros((small_own.shape[0] - experts, width), f32)
        small_to[0:experts] = router_rows[:, pl.ds(pl.multiple_of(other * width, width), width)]
        small_to[experts:] = empty
        small_to[experts + 2 : experts + 3, 0:RANK] = rescale_row
        small_copy(0).start()
        small_own[0:experts] = router_rows[:, pl.ds(pl.multiple_of(col * width, width), width)]
        small_own[experts:] = empty
        small_own[experts : experts + 1] = (
            jnp.sum(premix_rows[...], axis=0, keepdims=True) / premix_ref[...]
        )
        small_own[experts + 1 : experts + 2] = (
            jnp.sum(scaling_rows[...], axis=0, keepdims=True) / scaling_ref[...]
        )
        small_own[experts + 2 : experts + 3, 0:RANK] = rescale_row

    def small_line_begin():
        small_copy(0).wait_recv()
        small_own[...] += small_from[...]
        for step in range(1, ROWS):
            small_copy(step).start()

    def small_square_begin():
        for step in range(1, ROWS):
            small_copy(step).wait_recv()
        small_ref[...] = small_own[...] + small_line[1] + small_line[2] + small_line[3]
        for step in range(ROWS, ROWS + SQUARE - 1):
            small_copy(step).start()

    def small_end():
        for step in range(ROWS, ROWS + SQUARE - 1):
            small_copy(step).wait_recv()
        for step in range(ROWS, ROWS + SQUARE - 1):
            small_copy(step).wait_send()
        small_ref[...] += small_square[1] + small_square[2] + small_square[3]

    def reply_begin():
        for load in loads[19:23]:
            load.wait()
        lax.fori_loop(0, ROWS, reply_add, 0)

    def reply_pass():
        lax.fori_loop(0, 3, line_pass, 0)

    def reply_end():
        line_sums.total(total)
        output_ref[...] = (total[...] + residual_ref[...]).astype(bf16)

    def line_pass(turn, carried):
        line_sums.pass_on(block_at(row, jnp.where(turn == 0, 3, turn)))
        return carried

    def grad_copy(block):
        return remote(
            grad_to.at[block],
            grad_from.at[block],
            grad_sent.at[block],
            grad_arrived.at[block],
            sibling,
        )

    def query_copy(block, half):
        here = query_grad_ref.at[block, :, pl.ds(pl.multiple_of(half * mine, 128), mine)]
        return remote(here, here, query_sent.at[block], query_arrived.at[block], sibling)

    def latent_copy(block):
        return remote(
            latent_to.at[block],
            latent_from.at[block],
            latent_sent.at[block],
            latent_arrived.at[block],
            sibling,
        )

    def arrive(step):
        block = block_at(row, step)

        @pl.when(step > 0)
        def _():
            line.wait(block)
            line.pass_on(block)

        @pl.when(step == 0)
        def _():
            loads[3].wait()

        grads = branch_ref[block]
        grad_to[block] = nt(
            grads, combine[pl.ds(pl.multiple_of(other * both, 16), both)]
        ).astype(bf16)
        grad_copy(block).start()
        grad_own[block] = nt(grads, combine[pl.ds(pl.multiple_of(col * both, 16), both)])

    def heads(step):
        block = block_at(row, step)

        @pl.when(step == 0)
        def _():
            for load in loads[4:10]:
                load.wait()

        grad_copy(block).wait_recv()
        grads = (grad_own[block] + grad_from[block].astype(f32)).astype(bf16)
        pieces = []
        for head in range(2):
            upstream = grads[:, head * HEADV : (head + 1) * HEADV]
            query = query_ref[block, :, head * NOPE : head * NOPE + lanes]
            probs = probs_ref[head, block]
            weight = probs.astype(f32)
            probs_back = nt(upstream, value_ref[head].reshape(seq, HEADV))
            inner = jnp.sum(weight * probs_back, axis=1, keepdims=True)
            score_grad = (weight * (probs_back - inner)).astype(bf16)
            pieces.append(nn(score_grad, key_ref[head].reshape(seq, lanes)) * score_scale)
            key_grad[head] += tn(score_grad, query)
            value_grad[head] += tn(probs, upstream)
        first, second = pieces
        grad = jnp.concatenate(
            [first[:, :NOPE], first[:, NOPE:] + second[:, :NOPE], second[:, NOPE:]], axis=1
        )
        grad = grad * cos_ref[block] - swap_halves(grad) * sin_ref[block]
        query_grad_ref[block, :, pl.ds(pl.multiple_of(col * mine, 128), mine)] = grad.astype(bf16)
        query_copy(block, col).start()

    def project(step):
        block = block_at(row, step)

        @pl.when(step == 0)
        def _():
            loads[10].wait()

        query_copy(block, other).wait_recv()
        part[block] = nt(query_grad_ref[block], queries[...])

    def turn(step, carried):
        for delay, stage in ((0, arrive), (1, heads), (2, project)):

            @pl.when(jnp.logical_and(step >= delay, step < delay + ROWS))
            def _(delay=delay, stage=stage):
                stage(step - delay)

        @pl.when(step == 1)
        def _():
            rests[0].run(2)
            rests[1].run(2)

        @pl.when(step == 2)
        def _():
            rests[2].run(2)
            rests[0].run(3)

        @pl.when(step == 3)
        def _():
            rests[1].run(3)
            rests[2].run(3)

        return carried

    lax.fori_loop(0, ROWS + 1, turn, 0)
    for load in loads[11:17]:
        load.wait()
    begin(0)
    begin(1)
    reply_begin()

    def latents(turn, carried):
        block = block_at(row, ROWS - 1 - turn)
        here = pl.ds(pl.multiple_of(block * tokens, 128), tokens)
        first = key_grad[0, here] * score_scale
        second = pltpu.roll(key_grad[1, here] * score_scale, lanes - ROPE, 1)
        grad = jnp.concatenate(
            [first[:, :NOPE], value_grad[0, here], second[:, :NOPE], value_grad[1, here]], axis=1
        ).astype(bf16)
        expanded_ref[block] = grad
        own = 2 * (NOPE + HEADV)
        upstream = nt(grad, expand[:, pl.ds(pl.multiple_of(col * own, 128), own)])
        plain = latent_ref[block][:, :RANK]
        scale = lax.rsqrt(jnp.mean(plain * plain, axis=1, keepdims=True) + epsilon)
        rescale_rows[...] += jnp.sum(
            (upstream * plain * scale).reshape(tokens // 8, 8, RANK), axis=0
        )
        weighted = upstream * rescale_ref[...]
        inner = jnp.mean(weighted * plain, axis=1, keepdims=True)
        plain_grad = weighted * scale - plain * (scale * scale * scale * inner)
        rope = first[:, NOPE:] + second[:, NOPE:]
        lane = lax.broadcasted_iota(jnp.int32, rope.shape, 1)
        rope = jnp.where(lane < ROPE, rope, 0.0)
        rope = rope * key_cos_ref[block] - swap_halves(rope) * key_sin_ref[block]
        value = jnp.concatenate([plain_grad, rope], axis=1)
        latent_own[block] = value
        latent_to[block] = value.astype(bf16)
        latent_copy(block).start()
        return carried

    lax.fori_loop(0, ROWS, latents, 0)
    project(ROWS - 1)

    def turned_piece(member):
        return turned.at[
            pl.ds(pl.multiple_of(member * sliced, 16), sliced),
            pl.ds(pl.multiple_of(col * (seq // COLS), 128), seq // COLS),
        ]

    def turned_copy(step):
        to = lax.rem(row + step, ROWS)
        return remote(
            turned_piece(to),
            turned_from.at[step],
            turned_sent.at[step],
            turned_arrived.at[step],
            {"row": to},
        )

    def mix(turn, carried):
        block = block_at(row, ROWS - 1 - turn)
        latent_copy(block).wait_recv()
        latent = latent_own[block] + latent_from[block].astype(f32)
        here = pl.ds(pl.multiple_of(block * tokens, 128), tokens)
        total_here = part[block] + nn(latent.astype(bf16), compress_all[...])
        part[block] = total_here
        sums.begin(block)
        turned[:, here] = latent.T.astype(bf16)
        scaling_rows[...] += jnp.sum(
            (total_here * one_ref[block].astype(f32)).reshape(tokens // 8, 8, width), axis=0
        )
        return carried

    lax.fori_loop(0, ROWS, mix, 0)
    for step in range(1, ROWS):
        turned_copy(step).start()

    advance(1)
    for turn in range(3):
        sums.pass_on(block_at(row, 3 if turn == 0 else turn))
        advance(turn + 2)
    for step in range(1, ROWS):
        turned_copy(step).wait_recv()
    half = pl.ds(pl.multiple_of(col * (seq // COLS), 128), seq // COLS)
    own_sum = turned[pl.ds(pl.multiple_of(row * sliced, 16), sliced), half].astype(f32)
    for step in range(1, ROWS):
        own_sum = own_sum + turned_from[step].astype(f32)
    own_latent_ref[:, half] = own_sum.astype(bf16)

    def own_copy(part_of):
        here = own_latent_ref.at[
            :, pl.ds(pl.multiple_of(part_of * (seq // COLS), 128), seq // COLS)
        ]
        return remote(here, here, own_sent.at[0], own_arrived.at[0], sibling)

    own_copy(col).start()
    advance(5)
    sums.total(total)
    norm_begin(act_ref[...].astype(f32), scaling_ref[...], total[...], 1)
    input_grad_ref[...] += norm_grad(
        act_ref[...].astype(f32), scale_one_ref[...], scaling_ref[...], total[...], 1
    )
    small_begin()
    advance(6)
    reply_pass()
    for rest in rests:
        rest.run(4)
    pieces = [
        pltpu.make_async_copy(
            result.at[i], shared_sum.at[:, :, i * 128 : (i + 1) * 128], rest_sem.at[i]
        )
        for i in range(8)
    ]
    for piece in pieces:
        piece.start()
    small_line_begin()
    own_copy(other).wait_recv()
    own_copy(col).wait_send()
    advance(7)
    advance(8)
    small_square_begin()
    reply_end()
    for turn in range(9, count + 5):
        advance(turn)
    small_end()
    pair_copy().wait_recv()
    store(expand_other, expand_lanes(other))

    def ended(block, carried):
        grad_copy(block).wait_send()
        query_copy(block, col).wait_send()
        latent_copy(block).wait_send()
        return carried

    lax.fori_loop(0, ROWS, ended, 0)
    for step in range(1, ROWS):
        turned_copy(step).wait_send()
    stat_copy(0).wait_send()
    stat_copy(1).wait_send()
    for piece in pieces:
        piece.wait()
    for copy in stores:
        copy.wait()
    pair_copy().wait_send()
    for step in range(ROWS):
        small_copy(step).wait_send()
    for one_sum in pieces_of:
        one_sum.finish()
    line_sums.finish()
    for rest in rests:
        rest.finish()
    sums.finish()
    line.finish()


def run_attention_back(
    normed_grad,
    residual,
    scale_two,
    premix,
    cotangent,
    activations,
    scale_one,
    scaling,
    one,
    query,
    key,
    value,
    probs,
    latent,
    rescale,
    tables,
    compress_all,
    queries,
    expand,
    combine,
    shared,
    more,
):
    tokens, width = activations.shape
    seq = ROWS * tokens
    mine = query.shape[2]
    lanes = key.shape[3]
    latent_width = latent.shape[2]
    sliced = (RANK + ROPE) // ROWS
    whole = pl.BlockSpec(memory_space=VMEM)
    far = pl.BlockSpec(memory_space=pl.ANY)

    def shape(*dims, dtype=bf16):
        return jax.ShapeDtypeStruct(dims, dtype)

    kept, got_x, got_y = shared
    heads = more[0].shape[2]
    own_heads = 2 * (NOPE + HEADV)
    small = (24, width)
    piece = kept.shape[1:3] + (kept.shape[3] // 2,)
    loaded = (
        combine,
        query,
        key,
        value,
        probs,
        tables[0],
        tables[1],
        queries,
        expand,
        latent,
        tables[2],
        tables[3],
        compress_all,
        one,
    )
    return pl.pallas_call(
        attend_back_kernel,
        name="attend_back",
        out_shape=(
            shape(tokens, width, dtype=f32),
            shape(tokens, width),
            shape(*small, dtype=f32),
            shape(*kept.shape[1:3], width),
            shape(4, 8, width // 32, COLS * mine),
            shape(2, 8, heads // 16, width),
            shape(8, RANK // 8, COLS * own_heads),
            shape(sliced, width),
        ),
        in_specs=[whole] * 9 + [far] * 25,
        out_specs=(whole,) * 3 + (far,) * 5,
        scratch_shapes=[
            VMEM((ROWS, tokens, width), bf16),
            VMEM((ROWS, tokens, COLS * mine), bf16),
            VMEM((ROWS, tokens, own_heads), bf16),
            VMEM((sliced, seq), bf16),
            VMEM((8, width), f32),
            VMEM((8, RANK), f32),
            *[VMEM(value.shape, value.dtype) for value in loaded],
            VMEM(kept.shape, bf16),
            VMEM(kept.shape, bf16),
            VMEM((2,) + piece, bf16),
            VMEM((2,) + piece, bf16),
            VMEM((8,) + piece, bf16),
            *[VMEM(value.shape, value.dtype) for value in more],
            VMEM((2, tokens, 128), f32),
            VMEM((2, tokens, 128), f32),
            VMEM((ROWS, tokens, 2 * HEADV), f32),
            VMEM((ROWS, tokens, 2 * HEADV), bf16),
            VMEM((ROWS, tokens, 2 * HEADV), bf16),
            VMEM((2, seq, lanes), f32),
            VMEM((2, seq, HEADV), f32),
            VMEM((ROWS, tokens, latent_width), f32),
            VMEM((ROWS, tokens, latent_width), bf16),
            VMEM((ROWS, tokens, latent_width), bf16),
            VMEM((latent_width, seq), bf16),
            VMEM((ROWS, sliced, seq // COLS), bf16),
            VMEM((ROWS, tokens, width), f32),
            VMEM((ROWS, tokens, width), bf16),
            VMEM((2, ROWS, tokens, width), bf16),
            VMEM((tokens, width), f32),
            DMA((25,)),
            DMA((2,)),
            DMA((2,)),
            *line_sems(),
            *pair_sems(),
            *pair_sems(),
            *pair_sems(),
            *pair_sems(),
            *pair_sems(),
            *sum_sems(),
            DMA((kept.shape[1], 8)),
            DMA((kept.shape[1], 8)),
            DMA((8,)),
            VMEM((ROWS, tokens, width), bf16),
            VMEM((ROWS, tokens, width), bf16),
            VMEM((2, ROWS, tokens, width), bf16),
            VMEM(small, f32),
            VMEM(small, f32),
            VMEM((ROWS,) + small, f32),
            VMEM((SQUARE,) + small, f32),
            VMEM(small, f32),
            VMEM((8, RANK // 8, own_heads), bf16),
            DMA((16,)),
            *sum_sems(),
            DMA((1,)),
            DMA((1,)),
            DMA((ROWS + SQUARE - 1,)),
            DMA((ROWS + SQUARE - 1,)),
            *square_scratch((2, heads // 16, width)),
            *square_scratch((4, width // 32, COLS * mine)),
            *square_scratch((1, RANK // 8, own_heads)),
            *square_scratch((1, sliced, width // 8)),
        ],
        compiler_params=pltpu.CompilerParams(
            collective_id=3, has_side_effects=True, vmem_limit_bytes=62 * MIB
        ),
        cost_estimate=pl.CostEstimate(
            flops=40 * 1024**3, bytes_accessed=32 * MIB, transcendentals=0
        ),
    )(
        normed_grad,
        residual,
        scale_two,
        premix.reshape(1, width),
        cotangent,
        activations,
        scale_one,
        scaling.reshape(1, width),
        rescale.reshape(1, RANK),
        *loaded,
        kept,
        got_x,
        got_y,
        *more,
    )


def silu_pair(values):
    sigmoid = 1.0 / (1.0 + jnp.exp(-values))
    return values * sigmoid, sigmoid * (1.0 + values * (1.0 - sigmoid))


def expert_kernel(
    normed_ref,
    pick_ref,
    back_ref,
    cot_ref,
    router_ref,
    cot_rows_ref,
    fan_ref,
    fun_ref,
    wide_ref,
    narrow_ref,
    sum_ref,
    gathered_ref,
    rows_out,
    gu_out,
    hidden_out,
    shared_x,
    shared_y,
    shared_kept,
    shared_out,
    premix_ref,
    router_rows,
    reply_ref,
    fan,
    fun,
    wide,
    narrow,
    cot_rows,
    rows,
    staged,
    gu,
    hidden,
    pair_own,
    pair_to,
    pair_from,
    home,
    shared_to,
    shared_from,
    part,
    passed_to,
    passed_from,
    shared_gu,
    shared_grad,
    load_sem,
    store_sem,
    line_sent,
    line_arrived,
    out_sent,
    out_arrived,
    fwd_sent,
    fwd_arrived,
    shared_sent,
    shared_arrived,
    half_sent,
    half_arrived,
    home_sent,
    home_arrived,
    sum_sent,
    sum_arrived,
    other_sent,
    other_arrived,
    reply_sent,
    reply_arrived,
    grad_sem,
):
    place, row, col = lax.axis_index("dp"), lax.axis_index("row"), lax.axis_index("col")
    other = 1 - col
    inner = jnp.logical_and(row > 0, row < ROWS - 1)
    tokens, width = normed_ref.shape
    picked = pick_ref.shape[1]
    slots = picked // SQUARE
    experts = router_ref.shape[0]
    share = narrow.shape[0]
    loads = [
        pltpu.make_async_copy(source, target, load_sem.at[i])
        for i, (source, target) in enumerate(
            [
                (wide_ref, wide),
                (narrow_ref, narrow),
                (fan_ref, fan),
                (cot_rows_ref, cot_rows),
                (fun_ref, fun),
            ]
        )
    ]
    for load in loads:
        load.start()
    greet(row, place, col)
    gathered_ref[pl.ds(row, 1)] = normed_ref[...].reshape(1, tokens, width)
    line = Line(row, gathered_ref, line_sent, line_arrived)
    line.pass_on(row)
    premix_ref[...] = jnp.zeros_like(premix_ref)
    router_rows[...] = jnp.zeros_like(router_rows)
    sums = SumLine(row, part, passed_to, passed_from, sum_sent, sum_arrived)
    sibling = {"col": other}

    def half_lines(half):
        return pl.ds(pl.multiple_of(half * width, width), width)

    def square_copy(source, target, sent, arrived, block, step):
        piece = pl.ds(step * slots, slots)
        return remote(
            source.at[block, piece],
            target.at[block, piece],
            sent.at[block, step],
            arrived.at[block, step],
            {"dp": partner(place, step)},
        )

    def out_copy(block, step):
        return square_copy(staged, rows.at[col], out_sent, out_arrived, block, step)

    def home_copy(block, step):
        return square_copy(staged, home, home_sent, home_arrived, block, step)

    def reply_copy(block, step):
        return square_copy(staged, reply_ref, reply_sent, reply_arrived, block, step)

    def fwd_copy(block, half):
        here = rows.at[half, block]
        return remote(here, here, fwd_sent.at[block], fwd_arrived.at[block], sibling)

    def shared_copy(block):
        return remote(
            shared_to.at[block],
            shared_from.at[block],
            shared_sent.at[block],
            shared_arrived.at[block],
            sibling,
        )

    def half_copy(step):
        return remote(
            pair_to.at[lax.rem(step, 2)],
            pair_from.at[step],
            half_sent.at[step],
            half_arrived.at[step],
            sibling,
        )

    def other_copy(step):
        return remote(
            pair_to.at[lax.rem(step, 2)],
            pair_from.at[jnp.where(step == ROWS - 1, ROWS, step)],
            other_sent.at[step],
            other_arrived.at[step],
            sibling,
        )

    def stores(step):
        block = block_at(row, step)
        return [
            pltpu.make_async_copy(source, target, store_sem.at[index, step])
            for index, (source, target) in enumerate(
                [
                    (rows.at[:, block], rows_out.at[:, block]),
                    (gu.at[:, lax.rem(step, 2)], gu_out.at[:, block]),
                    (hidden.at[block], hidden_out.at[block]),
                ]
            )
        ]

    def relay(step):
        block = block_at(row, step)
        line.wait(block)
        line.pass_on(block)

    def take(step):
        block = block_at(row, step)

        @pl.when(jnp.logical_and(step > 0, jnp.logical_not(inner)))
        def _():
            relay(step)

        staged[block] = nn(pick_ref[block], gathered_ref[block]).astype(bf16)
        for shift in (3, 2, 1):
            out_copy(block, shift).start()
        rows[col, block, 0:slots] = staged[block, 0:slots]

    def shared_begin(step):
        block = block_at(row, step)

        @pl.when(step == 0)
        def _():
            loads[0].wait()
            loads[1].wait()

        for index, value in enumerate(
            (
                nt(gathered_ref[block], wide[0]),
                nt(gathered_ref[block], wide[1]),
                nt(cot_ref[block], narrow[...]),
            )
        ):
            shared_to[block, index] = value.astype(bf16)
        shared_copy(block).start()

    def forward(step):
        block = block_at(row, step)
        for shift in range(1, SQUARE):
            out_copy(block, shift).wait_recv()
        fwd_copy(block, col).start()

    def shared(step):
        block = block_at(row, step)
        shared_copy(block).wait_recv()
        gate, up, grad = [
            shared_to[block, index].astype(f32) + shared_from[block, index].astype(f32)
            for index in range(3)
        ]
        act, slope = silu_pair(gate)
        shared_out[block] = (act * up).astype(bf16)
        gate_grad = (grad * up * slope).astype(bf16)
        up_grad = (grad * act).astype(bf16)
        shared_gu[0, block] = gate_grad
        shared_gu[1, block] = up_grad
        part[block] = nn(gate_grad, wide[0]) + nn(up_grad, wide[1])

    def experts_of(step):
        block = block_at(row, step)

        @pl.when(step == 0)
        def _():
            for load in loads[2:]:
                load.wait()

        @pl.when(step > 1)
        def _():
            stores(step - 2)[1].wait()
            half_copy(step - 2).wait_send()

        fwd_copy(block, other).wait_recv()
        left, right = rows[0, block], rows[1, block]
        logits = nt(left, router_ref[:, 0:width]) + nt(right, router_ref[:, width:])
        logits = logits - jnp.max(logits, axis=1, keepdims=True)
        weight = jnp.exp(logits)
        probs = weight / jnp.sum(weight, axis=1, keepdims=True)
        own = (
            lax.broadcasted_iota(jnp.int32, (picked, experts), 1) == place * ROWS + row
        ).astype(f32)
        gates = jnp.sum(probs * own, axis=1, keepdims=True)
        raw = nt(cot_rows[0, block], fun[:, 0:width]) + nt(cot_rows[1, block], fun[:, width:])
        gate = nt(left, fan[0, :, 0:width]) + nt(right, fan[0, :, width:])
        up = nt(left, fan[1, :, 0:width]) + nt(right, fan[1, :, width:])
        act, slope = silu_pair(gate)
        value = act * up
        hidden[block] = (value * gates).astype(bf16)
        gate_sum = gates * jnp.sum(value * raw, axis=1, keepdims=True)
        logit_grad = (gate_sum * (own - probs)).astype(bf16)
        raw = raw * gates
        slot = lax.rem(step, 2)
        gu[0, slot] = (raw * up * slope).astype(bf16)
        gu[1, slot] = (raw * act).astype(bf16)

        def half_of(half):
            lines = half_lines(half)
            return (
                nn(gu[0, slot], fan[0, :, lines])
                + nn(gu[1, slot], fan[1, :, lines])
                + nn(logit_grad, router_ref[:, lines])
            )

        pair_to[slot] = half_of(other).astype(bf16)
        half_copy(step).start()
        pair_own[...] = half_of(col)
        router_rows[:, 0:width] += tn(logit_grad, left)
        router_rows[:, width:] += tn(logit_grad, right)
        for copy in stores(step):
            copy.start()

    def send_home(step):
        block = block_at(row, step)
        for shift in range(1, SQUARE):
            out_copy(block, shift).wait_send()
        half_copy(step).wait_recv()
        staged[block] = (pair_own[...] + pair_from[step].astype(f32)).astype(bf16)
        for shift in (3, 2, 1):
            home_copy(block, shift).start()
        home[block, 0:slots] = staged[block, 0:slots]

    def add_up(step):
        block = block_at(row, step)
        for shift in range(1, SQUARE):
            home_copy(block, shift).wait_recv()
        total = part[block] + nn(back_ref[block], home[block])
        part[block] = total
        premix_ref[...] += jnp.sum(
            (total * gathered_ref[block].astype(f32)).reshape(tokens // 8, 8, width), axis=0
        )
        sums.begin(block)

    def reply(step):
        block = block_at(row, step)
        slot = lax.rem(step, 2)

        @pl.when(step < 2)
        def _():
            half_copy(step + 2).wait_send()

        @pl.when(step > 1)
        def _():
            other_copy(step - 2).wait_send()

        pair_to[slot] = nn(hidden[block], fun[:, half_lines(other)]).astype(bf16)
        other_copy(step).start()

    def reply_home(step):
        block = block_at(row, step)
        own = nn(hidden[block], fun[:, half_lines(col)])
        for shift in range(1, SQUARE):
            home_copy(block, shift).wait_send()
        came = jnp.where(step == ROWS - 1, ROWS, step)
        other_copy(step).wait_recv()
        staged[block] = (own + pair_from[came].astype(f32)).astype(bf16)
        for shift in (3, 2, 1):
            reply_copy(block, shift).start()
        reply_ref[block, 0:slots] = staged[block, 0:slots]

    def turn(step, carried):
        @pl.when(jnp.logical_and(step == 2, inner))
        def _():
            relay(3)

        @pl.when(step < ROWS)
        def _():
            take(step)

        @pl.when(jnp.logical_and(step >= 1, step <= ROWS))
        def _():
            forward(step - 1)

        @pl.when(step < ROWS)
        def _():
            shared_begin(step)

        @pl.when(jnp.logical_and(step == 0, inner))
        def _():
            relay(1)
            relay(2)

        @pl.when(step >= 2)
        def _():
            shared(step - 2)
            send_home(step - 2)

        @pl.when(step == ROWS)
        def _():
            reply(0)

        @pl.when(step == ROWS + 1)
        def _():
            reply_home(0)

        @pl.when(step >= ROWS)
        def _():
            add_up(2 * step - 2 * ROWS)

        @pl.when(step == ROWS)
        def _():
            add_up(1)

        @pl.when(jnp.logical_and(step >= 1, step <= ROWS))
        def _():
            experts_of(step - 1)

        return carried

    lax.fori_loop(0, ROWS + 2, turn, 0)

    def replies(step, carried):
        @pl.when(step < ROWS)
        def _():
            reply(step)

        @pl.when(step > 1)
        def _():
            reply_home(step - 1)

        return carried

    lax.fori_loop(1, ROWS + 1, replies, 0)
    add_up(ROWS - 1)

    def hand_on(turn, carried):
        sums.pass_on(block_at(row, jnp.where(turn == 2, 1, turn + 2)))
        return carried

    lax.fori_loop(0, ROWS - 1, hand_on, 0)

    seq = ROWS * tokens
    for index, (left, right) in enumerate(
        (
            (shared_out, cot_ref),
            (shared_gu.at[0], gathered_ref),
            (shared_gu.at[1], gathered_ref),
        )
    ):
        grad = tn(left[...].reshape(seq, share), right[...].reshape(seq, width))
        shared_grad[index] = grad.astype(bf16)
    x, y = lax.rem(place, 2), lax.div(place, 2)
    quarter = width // SQUARE
    grad_copies = []
    for index, (half, side, target) in enumerate(
        (
            (0, 1 - x, shared_x),
            (1, 1 - y, shared_y),
            (0, x, shared_kept.at[0]),
            (1, y, shared_kept.at[1]),
        )
    ):
        lanes = pl.ds(pl.multiple_of((2 * half + side) * quarter, 128), quarter)
        grad_copies.append(
            pltpu.make_async_copy(shared_grad.at[:, :, lanes], target, grad_sem.at[index])
        )
        grad_copies[index].start()
    sums.total(sum_ref)

    def ended(step, carried):
        block = block_at(row, step)
        shared_copy(block).wait_send()
        fwd_copy(block, col).wait_send()
        for shift in range(1, SQUARE):
            reply_copy(block, shift).wait_recv()
            reply_copy(block, shift).wait_send()
        copies = stores(step)
        copies[0].wait()
        copies[2].wait()

        @pl.when(step >= ROWS - 2)
        def _():
            copies[1].wait()
            other_copy(step).wait_send()

        return carried

    lax.fori_loop(0, ROWS, ended, 0)
    for copy in grad_copies:
        copy.wait()
    sums.finish()
    line.finish()


def run_experts(
    normed, pick, back, cot_rows, cot_all, fan, fun, wide, narrow, router_all
):
    tokens, width = normed.shape
    picked = pick.shape[1]
    hid = fun.shape[0]
    share = narrow.shape[0]
    experts = router_all.shape[0]
    whole = pl.BlockSpec(memory_space=VMEM)
    far = pl.BlockSpec(memory_space=pl.ANY)

    def shape(*dims, dtype=bf16):
        return jax.ShapeDtypeStruct(dims, dtype)

    return pl.pallas_call(
        expert_kernel,
        name="experts",
        out_shape=(
            shape(tokens, width, dtype=f32),
            shape(ROWS, tokens, width),
            shape(COLS, ROWS, picked, width),
            shape(2, ROWS, picked, hid),
            shape(ROWS, picked, hid),
            shape(3, share, width // SQUARE),
            shape(3, share, width // SQUARE),
            shape(2, 3, share, width // SQUARE),
            shape(ROWS, tokens, share),
            shape(8, width, dtype=f32),
            shape(experts, COLS * width, dtype=f32),
            shape(ROWS, picked, width),
        ),
        in_specs=[whole] * 5 + [far] * 5,
        out_specs=(whole, whole) + (far,) * 6 + (whole,) * 4,
        scratch_shapes=[
            VMEM(fan.shape, bf16),
            VMEM(fun.shape, bf16),
            VMEM(wide.shape, bf16),
            VMEM(narrow.shape, bf16),
            VMEM(cot_rows.shape, bf16),
            VMEM((COLS, ROWS, picked, width), bf16),
            VMEM((ROWS, picked, width), bf16),
            VMEM((2, 2, picked, hid), bf16),
            VMEM((ROWS, picked, hid), bf16),
            VMEM((picked, width), f32),
            VMEM((2, picked, width), bf16),
            VMEM((ROWS + 1, picked, width), bf16),
            VMEM((ROWS, picked, width), bf16),
            VMEM((ROWS, 3, tokens, share), bf16),
            VMEM((ROWS, 3, tokens, share), bf16),
            VMEM((ROWS, tokens, width), f32),
            VMEM((ROWS, tokens, width), bf16),
            VMEM((2, ROWS, tokens, width), bf16),
            VMEM((2, ROWS, tokens, share), bf16),
            VMEM((3, share, width), bf16),
            DMA((5,)),
            DMA((3, ROWS)),
            *line_sems(),
            *square_sems(),
            *pair_sems(),
            *pair_sems(),
            *pair_sems(),
            *square_sems(),
            *sum_sems(),
            *pair_sems(),
            *square_sems(),
            DMA((4,)),
        ],
        compiler_params=pltpu.CompilerParams(
            collective_id=2, has_side_effects=True, vmem_limit_bytes=62 * MIB
        ),
        cost_estimate=pl.CostEstimate(
            flops=60 * 1024**3, bytes_accessed=64 * MIB, transcendentals=0
        ),
    )(normed, pick, back, cot_all, router_all, cot_rows, fan, fun, wide, narrow)


class SquareSum:
    def __init__(self, place, part, first, second, middle, result, sent, arrived):
        self.x, self.y = lax.rem(place, 2), lax.div(place, 2)
        self.to_x, self.to_y = {"dp": partner(place, 1)}, {"dp": partner(place, 2)}
        self.part, self.first, self.second = part, first, second
        self.middle, self.result = middle, result
        self.sent, self.arrived = sent, arrived

    def copies(self, phase):
        x, y = self.x, self.y
        if phase == 0:
            plan = (
                (self.part.at[pl.ds(2 - 2 * x, 2)], self.first.at[0:2], self.to_x),
                (self.part.at[pl.ds(6 - 2 * y, 2)], self.first.at[2:4], self.to_y),
            )
        elif phase == 1:
            plan = (
                (self.middle.at[0], self.second.at[0], self.to_y),
                (self.middle.at[1], self.second.at[1], self.to_x),
            )
        elif phase == 2:
            one, two = self.result.at[2 * x + y], self.result.at[4 + 2 * y + x]
            plan = ((one, one, self.to_y), (two, two, self.to_x))
        else:
            one, two = self.result.at[pl.ds(2 * x, 2)], self.result.at[pl.ds(4 + 2 * y, 2)]
            plan = ((one, one, self.to_x), (two, two, self.to_y))
        return [
            remote(source, target, self.sent.at[2 * phase + i], self.arrived.at[2 * phase + i], to)
            for i, (source, target, to) in enumerate(plan)
        ]

    def start(self, phase):
        for copy in self.copies(phase):
            copy.start()

    def arrive(self, phase):
        for copy in self.copies(phase):
            copy.wait_recv()

    def run(self, phase):
        x, y = self.x, self.y
        if phase > 0:
            self.arrive(phase - 1)
        if phase == 1:
            for slot, piece, came in (
                (0, 2 * x + 1 - y, 1 - y),
                (1, 4 + 2 * y + 1 - x, 3 - x),
            ):
                self.middle[slot] = (
                    self.part[piece].astype(f32) + self.first[came].astype(f32)
                ).astype(bf16)
        if phase == 2:
            for slot, piece, came in ((0, 2 * x + y, y), (1, 4 + 2 * y + x, 2 + x)):
                self.result[piece] = (
                    self.part[piece].astype(f32)
                    + self.first[came].astype(f32)
                    + self.second[slot].astype(f32)
                ).astype(bf16)
        if phase < 4:
            self.start(phase)

    def finish(self):
        for phase in range(4):
            for copy in self.copies(phase):
                copy.wait_send()


def square_scratch(dims):
    count, rows, lanes = dims
    return [
        VMEM((count, 8, rows, lanes), bf16),
        VMEM((count, 4, rows, lanes), bf16),
        VMEM((count, 2, rows, lanes), bf16),
        VMEM((count, 2, rows, lanes), bf16),
        VMEM((count, 8, rows, lanes), bf16),
        DMA((count, 8)),
        DMA((count, 8)),
    ]


def write_kernel(count, plan, *refs):
    sources, targets = refs[:count], refs[count : count + len(plan)]
    rest = refs[count + len(plan) :]
    held, wide = rest[:count], rest[count : count + len(plan)]
    load_sem, store_sem = rest[count + len(plan) :]
    loads = [
        pltpu.make_async_copy(sources[i], held[i], load_sem.at[i]) for i in range(count)
    ]
    stores = [
        pltpu.make_async_copy(wide[i], targets[i], store_sem.at[i]) for i in range(len(plan))
    ]
    for load in loads:
        load.start()
    waited = set()
    for i, (source, where) in enumerate(plan):
        if source not in waited:
            loads[source].wait()
            waited.add(source)
        wide[i][...] = held[source][where].astype(wide[i].dtype)
        stores[i].start()
    for store in stores:
        store.wait()


def write_out(arrays, plan):
    far = pl.BlockSpec(memory_space=pl.ANY)
    shapes = [jax.ShapeDtypeStruct(shape, dtype) for _, _, shape, dtype in plan]
    return pl.pallas_call(
        functools.partial(
            write_kernel, len(arrays), [(source, where) for source, where, _, _ in plan]
        ),
        name="write_out",
        out_shape=shapes,
        in_specs=[far] * len(arrays),
        out_specs=[far] * len(plan),
        scratch_shapes=[
            *[VMEM(array.shape, array.dtype) for array in arrays],
            *[VMEM(shape.shape, shape.dtype) for shape in shapes],
            DMA((len(arrays),)),
            DMA((len(plan),)),
        ],
        compiler_params=pltpu.CompilerParams(vmem_limit_bytes=62 * MIB),
        cost_estimate=pl.CostEstimate(flops=0, bytes_accessed=24 * MIB, transcendentals=0),
    )(*arrays)


def product_kernel(left_ref, right_ref, out_ref, turned):
    wide = 256

    @pl.when(pl.program_id(1) == 0)
    def _():
        turned[...] = left_ref[0].T

    def one(index, carried):
        lanes = pl.ds(pl.multiple_of(index * wide, 128), wide)
        out_ref[0, :, lanes] = nn(turned[...], right_ref[0, :, lanes])
        return carried

    lax.fori_loop(0, right_ref.shape[2] // wide, one, 0)


def slot_products(left, right):
    kinds, slots, tall = left.shape
    halves, _, wide = right.shape
    return pl.pallas_call(
        product_kernel,
        name="slot_products",
        grid=(kinds, halves),
        out_shape=jax.ShapeDtypeStruct((kinds, tall, halves * wide), f32),
        in_specs=[
            pl.BlockSpec((1, slots, tall), lambda kind, half: (kind, 0, 0)),
            pl.BlockSpec((1, slots, wide), lambda kind, half: (half, 0, 0)),
        ],
        out_specs=pl.BlockSpec((1, tall, wide), lambda kind, half: (kind, 0, half)),
        scratch_shapes=[VMEM((tall, slots), bf16)],
        compiler_params=pltpu.CompilerParams(vmem_limit_bytes=40 * MIB),
        cost_estimate=pl.CostEstimate(
            flops=2 * kinds * halves * slots * tall * wide,
            bytes_accessed=4 * kinds * halves * tall * wide,
            transcendentals=0,
        ),
    )(left, right)


def local_square(
    activations,
    cotangent,
    routing,
    segments,
    scaling,
    queries,
    compress,
    rescale,
    expand,
    combine,
    premix,
    router,
    widening,
    narrowing,
    fanout,
    funnel,
):
    dp_count = lax.axis_size("dp")
    row_count = lax.axis_size("row")
    col_count = lax.axis_size("col")
    col_index = lax.axis_index("col")
    local_rows, col_width = activations.shape
    seq_length = local_rows * row_count
    expert_total = router.shape[1]
    capacity = local_rows * TOP * 4 // (3 * expert_total)
    slot_total = capacity * row_count * dp_count
    tables = turning_tables(seq_length)
    (
        one,
        query,
        key,
        value,
        probs,
        latent,
        latent_normed,
        attended,
        compress_all,
        cot_blocks,
        pick,
        back,
        cot_rows,
        residual,
        normed_two,
        scale_one,
        scale_two,
        router_all,
    ) = run_attention(
        activations,
        scaling,
        queries,
        compress,
        rescale,
        expand,
        combine,
        premix,
        segments,
        cotangent,
        routing,
        router,
        tables,
        capacity,
    )
    (
        normed_grad,
        two_blocks,
        expert_rows,
        expert_gu_grad,
        expert_hidden,
        shared_x,
        shared_y,
        shared_kept,
        hidden_blocks,
        premix_rows,
        router_rows,
        reply_blocks,
    ) = run_experts(
        normed_two,
        pick,
        back,
        cot_rows,
        cot_blocks,
        fanout[0].transpose(0, 2, 1),
        funnel[0],
        widening.transpose(0, 2, 1),
        narrowing,
        router_all,
    )
    slot_rows = expert_rows.reshape(col_count, slot_total, col_width)
    reply_grad_rows = cot_rows.reshape(col_count, slot_total, col_width)
    slot_hidden = expert_hidden.reshape(slot_total, -1)
    slot_gu_grad = expert_gu_grad.reshape(2, slot_total, -1)
    got_x = lax.ppermute(shared_x, "dp", [(i, i ^ 1) for i in range(SQUARE)])
    got_y = lax.ppermute(shared_y, "dp", [(i, i ^ 2) for i in range(SQUARE)])
    fanout_grad = slot_products(slot_gu_grad, slot_rows)
    funnel_grad = slot_products(slot_hidden[None], reply_grad_rows)
    normed_grad, fanout_grad, funnel_grad = lax.optimization_barrier(
        (normed_grad, fanout_grad, funnel_grad)
    )
    (
        input_grad,
        layer_output,
        small,
        shared_sum,
        queries_sum,
        combine_sum,
        expand_sum,
        compress_sum,
    ) = run_attention_back(
        normed_grad,
        residual,
        scale_two,
        premix,
        cotangent,
        activations,
        scale_one,
        scaling,
        one,
        query,
        key,
        value,
        probs,
        latent,
        rescale,
        tables,
        compress_all,
        queries,
        expand,
        combine,
        (shared_kept, got_x, got_y),
        (
            attended,
            latent_normed,
            narrowing,
            reply_blocks,
            back,
            hidden_blocks,
            premix_rows,
            router_rows,
        ),
    )
    everything = slice(None)
    share = narrowing.shape[0]
    (
        widening_grad,
        narrowing_grad,
        queries_grad,
        combine_grad,
        expand_grad,
        compress_grad,
        input_grad,
        layer_output,
        router_grad,
        premix_grad,
        scaling_grad,
        rescale_grad,
    ) = write_out(
        (
            shared_sum,
            queries_sum.reshape(queries.shape),
            combine_sum.reshape(combine.shape),
            expand_sum.reshape(expand.shape),
            compress_sum,
            input_grad,
            layer_output,
            small,
        ),
        (
            (0, slice(1, 3), (2, share, col_width), f32),
            (0, 0, (share, col_width), f32),
            (1, everything, queries.shape, f32),
            (2, everything, combine.shape, f32),
            (3, everything, expand.shape, f32),
            (4, everything, compress_sum.shape, f32),
            (5, everything, input_grad.shape, f32),
            (6, everything, layer_output.shape, bf16),
            (7, slice(0, expert_total), (expert_total, col_width), f32),
            (7, slice(expert_total, expert_total + 1), (1, col_width), f32),
            (7, slice(expert_total + 1, expert_total + 2), (1, col_width), f32),
            (7, (slice(expert_total + 2, expert_total + 3), slice(0, RANK)), (1, RANK), f32),
        ),
    )
    return (
        layer_output,
        input_grad,
        scaling_grad.reshape(col_width),
        queries_grad,
        compress_grad.T,
        rescale_grad.reshape(RANK),
        expand_grad,
        combine_grad,
        premix_grad.reshape(col_width),
        router_grad.T,
        widening_grad.transpose(0, 2, 1),
        narrowing_grad,
        fanout_grad.transpose(0, 2, 1)[None],
        funnel_grad,
    )


def local(
    activations,
    cotangent,
    routing,
    segments,
    scaling,
    queries,
    compress,
    rescale,
    expand,
    combine,
    premix,
    router,
    widening,
    narrowing,
    fanout,
    funnel,
):
    dp_count = lax.axis_size("dp")
    row_count = lax.axis_size("row")
    col_count = lax.axis_size("col")
    dp_index = lax.axis_index("dp")
    row_index = lax.axis_index("row")
    col_index = lax.axis_index("col")
    local_rows = activations.shape[0]
    col_width = activations.shape[1]
    seq_length = local_rows * row_count
    half_length = seq_length // col_count
    head_width = NOPE + ROPE
    pair_width = NOPE + HEADV
    local_heads = queries.shape[1] // head_width
    slice_width = compress.shape[1]
    expert_total = router.shape[1]
    capacity = local_rows * TOP * 4 // (3 * expert_total)
    slots = capacity * row_count
    slot_total = slots * dp_count
    block_rows = min(512, half_length)
    block_count = half_length // block_rows
    score_scale = head_width ** (-0.5)

    inputs = activations.astype(f32)
    scale_one = norm_scale(inputs)
    normed_one = (inputs * scale_one[:, None] * scaling).astype(bf16)
    gathered_one = row_gather(normed_one)
    compress_all = lax.all_gather(compress, "row", axis=1, tiled=True)

    routing_all = row_gather(routing)
    cotangent_all = row_gather(after(cotangent, gathered_one))
    offsets = jnp.arange(dp_count, dtype=jnp.int32)
    my_experts = ((dp_index + offsets) % dp_count) * row_count + row_index
    goes = jnp.any(routing_all[None, :, :] == my_experts[:, None, None], axis=2)
    token_range = jnp.arange(seq_length, dtype=jnp.int32)
    earlier = (token_range[:, None] < token_range[None, :]).astype(bf16)
    rank = dot(goes.astype(bf16), earlier).astype(jnp.int32)
    slot_range = jnp.arange(slots, dtype=jnp.int32)
    pick = (
        ((rank[:, None, :] == slot_range[None, :, None]) & goes[:, None, :])
        .astype(bf16)
        .reshape(slot_total, seq_length)
    )

    def dispatch(tokens):
        rows = dot(pick, tokens).astype(bf16).reshape(dp_count, slots, col_width)
        arrived = send_out([rows[k] for k in range(dp_count)])
        return col_gather(jnp.concatenate(arrived, axis=0), axis=1)

    def bring_back(part):
        summed = col_scatter(part.astype(bf16), axis=1).reshape(dp_count, slots, col_width)
        arrived = send_back([summed[k] for k in range(dp_count)])
        return dot_tn(pick, jnp.concatenate(arrived, axis=0))

    query_part = dot(gathered_one, queries)
    latent_part = dot(gathered_one, compress_all)
    query_raw, latent_raw = col_scatter((query_part, latent_part))
    latent_plain = latent_raw[:, :RANK]
    latent_scale = lax.rsqrt(jnp.mean(latent_plain * latent_plain, axis=1) + epsilon)
    latent_normed = (latent_plain * latent_scale[:, None] * rescale).astype(bf16)
    expanded = dot(latent_normed, expand).reshape(half_length, local_heads, pair_width)
    positions = col_index * half_length + jnp.arange(half_length, dtype=jnp.int32)
    cosine, sine_table = rotation(positions, ROPE)
    key_shared = rotate(latent_raw[:, RANK:], cosine, sine_table, 1.0)
    query_heads = query_raw.reshape(half_length, local_heads, head_width)
    query_local = jnp.concatenate(
        [
            query_heads[..., :NOPE],
            rotate(query_heads[..., NOPE:], cosine[:, None, :], sine_table[:, None, :], 1.0),
        ],
        axis=2,
    ).astype(bf16)
    key_local = jnp.concatenate(
        [
            expanded[..., :NOPE],
            jnp.broadcast_to(key_shared[:, None, :], (half_length, local_heads, ROPE)),
        ],
        axis=2,
    ).astype(bf16)
    value_local = expanded[..., NOPE:].astype(bf16)
    key_flat, value_flat = (
        col_gather(key_local.reshape(half_length, local_heads * head_width)),
        col_gather(value_local.reshape(half_length, local_heads * HEADV)),
    )
    key_heads = key_flat.reshape(seq_length, local_heads, head_width)
    value_heads = value_flat.reshape(seq_length, local_heads, HEADV)
    own_segments = lax.dynamic_slice_in_dim(
        segments, col_index * half_length, half_length, 0
    ).reshape(block_count, block_rows)
    query_blocks = query_local.reshape(block_count, block_rows, local_heads, head_width)

    def attend_block(inputs_block):
        query_block, segment_block = inputs_block
        scores = (
            jnp.einsum("qhd,khd->hqk", query_block, key_heads, preferred_element_type=f32)
            * score_scale
        )
        visible = segments[None, None, :] <= segment_block[None, :, None]
        scores = jnp.where(visible, scores, masked_score)
        largest = jnp.max(scores, axis=2, keepdims=True)
        weight = jnp.exp(scores - largest)
        totals = jnp.sum(weight, axis=2, keepdims=True)
        probability = (weight / totals).astype(bf16)
        result = jnp.einsum("hqk,khd->qhd", probability, value_heads, preferred_element_type=f32)
        return (result.astype(bf16), (largest + jnp.log(totals))[..., 0])

    attended_blocks, log_totals = lax.map(attend_block, (query_blocks, own_segments))
    attended = attended_blocks.reshape(half_length, local_heads * HEADV)
    attended_all = col_gather(attended)
    branch = row_scatter(dot(attended_all, combine))

    reply_grad_rows = dispatch(cotangent_all)
    inner_weight = fanout[0]
    outer_weight = funnel[0]
    hidden_raw = dot_nt(reply_grad_rows, outer_weight)
    shared_hidden_grad = col_scatter(dot_nt(cotangent_all, narrowing))

    residual = inputs + branch
    scale_two = norm_scale(residual)
    normed_two = (residual * scale_two[:, None] * premix).astype(bf16)
    gathered_two = row_gather(normed_two)

    expert_rows = dispatch(gathered_two)
    expert_range = jnp.arange(expert_total, dtype=jnp.int32)
    router_all = lax.all_gather(router, "col", axis=0, tiled=True)
    own_expert = dp_index * row_count + row_index
    slot_probs = jax.nn.softmax(dot(expert_rows, router_all), axis=1)
    slot_gates = jnp.sum(jnp.where(expert_range == own_expert, slot_probs, 0.0), axis=1)
    gate_up = jnp.einsum("rd,gdf->grf", expert_rows, inner_weight, preferred_element_type=f32)
    gate_input, up_input = gate_up[0], gate_up[1]
    hidden = jax.nn.silu(gate_input) * up_input
    expert_hidden = hidden.astype(bf16)
    slot_gate_grad = col_totals(jnp.sum(hidden * hidden_raw, axis=1))
    hidden_grad = hidden_raw * slot_gates[:, None]
    expert_gu_grad = jnp.stack(
        [hidden_grad * up_input * silu_slope(gate_input), hidden_grad * jax.nn.silu(gate_input)]
    ).astype(bf16)
    input_part = jnp.einsum(
        "grf,gdf->rd", expert_gu_grad, inner_weight, preferred_element_type=f32
    )
    routed_grad = bring_back(input_part)
    gate_grad_parts = send_back(
        [slot_gate_grad.reshape(dp_count, slots)[k] for k in range(dp_count)]
    )

    logits = col_totals(dot(gathered_two, router))
    router_probs = jax.nn.softmax(logits, axis=1)
    gate_grad = jnp.sum(
        pick.reshape(dp_count, slots, seq_length).astype(f32)
        * jnp.stack(gate_grad_parts)[:, :, None],
        axis=1,
    )
    mine = (my_experts[:, None] == expert_range[None, :]).astype(f32)
    probs_grad = jnp.sum(gate_grad[:, :, None] * mine[:, None, :], axis=0)
    logit_grad = router_probs * (
        probs_grad - jnp.sum(router_probs * probs_grad, axis=1, keepdims=True)
    )
    router_part = dot_tn(gathered_two, logit_grad)

    shared_gate_up = col_scatter(
        jnp.einsum("td,gdf->tgf", gathered_two, widening, preferred_element_type=f32)
    )
    shared_hidden = (jax.nn.silu(shared_gate_up[:, 0]) * shared_gate_up[:, 1]).astype(bf16)
    hidden_all = col_gather(shared_hidden)
    narrowing_grad = dot_tn(hidden_all, cotangent_all)
    shared_gu_grad = jnp.stack(
        [
            shared_hidden_grad * shared_gate_up[:, 1] * silu_slope(shared_gate_up[:, 0]),
            shared_hidden_grad * jax.nn.silu(shared_gate_up[:, 0]),
        ],
        axis=1,
    ).astype(bf16)
    gu_grad_all = col_gather(shared_gu_grad)
    widening_grad = jnp.einsum(
        "td,tgf->gdf", gathered_two, gu_grad_all, preferred_element_type=f32
    )
    shared_input_part = jnp.einsum(
        "tgf,gdf->td", gu_grad_all, widening, preferred_element_type=f32
    )
    shared_sums = lax.psum((narrowing_grad.astype(bf16), widening_grad.astype(bf16)), "dp")

    grad_part = routed_grad + shared_input_part + dot_nt(logit_grad, router)
    premix_part = jnp.sum(grad_part * gathered_two.astype(f32), axis=0) / premix
    normed_grad = row_scatter(grad_part)

    upstream = cotangent.astype(f32)
    residual_grad = upstream + norm_back(residual, scale_two, premix, normed_grad)
    branch_all = row_gather(residual_grad.astype(bf16))

    funnel_grad = dot_tn((hidden * slot_gates[:, None]).astype(bf16), reply_grad_rows)[None]
    fanout_grad = jnp.einsum(
        "rd,grf->gdf", expert_rows, expert_gu_grad, preferred_element_type=f32
    )[None]
    reply_part = dot(expert_hidden, outer_weight) * slot_gates[:, None]
    routed = bring_back(reply_part)
    shared_out = row_scatter(routed + dot(hidden_all, narrowing))
    layer_output = (residual + shared_out).astype(bf16)

    combine_grad = dot_tn(attended_all, branch_all)
    combine_sum = lax.psum(after(combine_grad.astype(bf16), *shared_sums), "dp")
    attended_grad = col_scatter(dot_nt(branch_all, combine))
    attended_grad_blocks = attended_grad.astype(bf16).reshape(
        block_count, block_rows, local_heads, HEADV
    )

    def attend_back(carried, inputs_block):
        key_sum, value_sum = carried
        query_block, grad_block, log_block, segment_block = inputs_block
        scores = (
            jnp.einsum("qhd,khd->hqk", query_block, key_heads, preferred_element_type=f32)
            * score_scale
        )
        visible = segments[None, None, :] <= segment_block[None, :, None]
        probability = jnp.where(visible, jnp.exp(scores - log_block[..., None]), 0.0)
        weight_grad = jnp.einsum(
            "qhd,khd->hqk", grad_block, value_heads, preferred_element_type=f32
        )
        inner_sum = jnp.sum(probability * weight_grad, axis=2, keepdims=True)
        score_grad = (probability * (weight_grad - inner_sum)).astype(bf16)
        query_grad_block = (
            jnp.einsum("hqk,khd->qhd", score_grad, key_heads, preferred_element_type=f32)
            * score_scale
        )
        key_sum = (
            key_sum
            + jnp.einsum("hqk,qhd->khd", score_grad, query_block, preferred_element_type=f32)
            * score_scale
        )
        value_sum = value_sum + jnp.einsum(
            "hqk,qhd->khd", probability.astype(bf16), grad_block, preferred_element_type=f32
        )
        return ((key_sum, value_sum), query_grad_block)

    key_start = jnp.zeros((seq_length, local_heads, head_width), f32)
    value_start = jnp.zeros((seq_length, local_heads, HEADV), f32)
    (key_grad_all, value_grad_all), query_grad_blocks = lax.scan(
        attend_back,
        (key_start, value_start),
        (query_blocks, attended_grad_blocks, log_totals, own_segments),
    )
    key_grad, value_grad = col_scatter(
        (
            key_grad_all.reshape(seq_length, local_heads * head_width),
            value_grad_all.reshape(seq_length, local_heads * HEADV),
        )
    )
    key_grad = key_grad.reshape(half_length, local_heads, head_width)
    value_grad = value_grad.reshape(half_length, local_heads, HEADV)
    query_grad = query_grad_blocks.reshape(half_length, local_heads, head_width)
    query_raw_grad = (
        jnp.concatenate(
            [
                query_grad[..., :NOPE],
                rotate(query_grad[..., NOPE:], cosine[:, None, :], sine_table[:, None, :], -1.0),
            ],
            axis=2,
        )
        .astype(bf16)
        .reshape(half_length, local_heads * head_width)
    )
    expanded_grad = (
        jnp.concatenate([key_grad[..., :NOPE], value_grad], axis=2)
        .astype(bf16)
        .reshape(half_length, local_heads * pair_width)
    )
    shared_rope_grad = rotate(jnp.sum(key_grad[..., NOPE:], axis=1), cosine, sine_table, -1.0)

    latent_grad = dot_nt(expanded_grad, expand)
    latent_weighted = latent_grad * rescale
    latent_inner = jnp.mean(latent_weighted * latent_plain, axis=1)
    rescale_part = jnp.sum(latent_grad * latent_plain * latent_scale[:, None], axis=0)
    plain_grad = (
        latent_weighted * latent_scale[:, None]
        - latent_plain * (latent_scale**3 * latent_inner)[:, None]
    )
    latent_raw_grad = jnp.concatenate([plain_grad, shared_rope_grad], axis=1).astype(bf16)
    query_grad_all = col_gather(query_raw_grad)
    latent_grad_all = col_gather(latent_raw_grad)
    first_part = dot_nt(query_grad_all, queries) + dot_nt(latent_grad_all, compress_all)
    first_grad = row_scatter(first_part)
    input_grad = residual_grad + norm_back(inputs, scale_one, scaling, first_grad)

    queries_part = dot_tn(gathered_one, query_grad_all)
    own_latent_grad = lax.psum_scatter(
        latent_raw_grad, "row", scatter_dimension=1, tiled=True
    )
    compress_part = dot_tn(gathered_one, col_gather(own_latent_grad))
    half_rank = RANK // col_count
    latent_normed_all = col_gather(latent_normed)
    expanded_grad_all = col_gather(expanded_grad)
    expand_half = dot_tn(
        lax.dynamic_slice_in_dim(latent_normed_all, col_index * half_rank, half_rank, 1),
        expanded_grad_all,
    )
    scaling_part = jnp.sum(first_part * gathered_one.astype(f32), axis=0) / scaling
    queries_sum, expand_sum, compress_sum = lax.psum(
        (
            after(queries_part.astype(bf16), combine_sum),
            expand_half.astype(bf16),
            compress_part.astype(bf16),
        ),
        "dp",
    )
    premix_sum, router_sum = lax.psum((premix_part, router_part), ("dp", "row"))
    rescale_sum = lax.psum(rescale_part, ("dp", "row", "col"))
    scaling_sum = lax.psum(scaling_part, ("dp", "row"))
    return (
        layer_output,
        input_grad,
        scaling_sum,
        queries_sum.astype(f32),
        compress_sum.astype(f32),
        rescale_sum,
        col_gather(expand_sum).astype(f32),
        combine_sum.astype(f32),
        premix_sum,
        router_sum,
        shared_sums[1].astype(f32),
        shared_sums[0].astype(f32),
        fanout_grad,
        funnel_grad,
    )


def solution(mesh):
    placed = (
        P(("dp", "row"), "col"),
        P(("dp", "row"), "col"),
        P(("dp", "row"), None),
        P("dp"),
        P("col"),
        P("col", "row"),
        P("col", "row"),
        P(),
        P(None, "row"),
        P("row", "col"),
        P("col"),
        P("col", None),
        P(None, "col", "row"),
        P("row", "col"),
        P(("dp", "row"), None, None, "col"),
        P(("dp", "row"), "col", None),
    )
    squared = mesh.shape["dp"] == SQUARE and mesh.shape["row"] == ROWS
    return jax.shard_map(
        local_square if squared else local,
        mesh=mesh,
        in_specs=placed,
        out_specs=(
            P(("dp", "row"), "col"),
            P(("dp", "row"), "col"),
            P("col"),
            P("col", "row"),
            P("col", "row"),
            P(),
            P(None, "row"),
            P("row", "col"),
            P("col"),
            P("col", None),
            P(None, "col", "row"),
            P("row", "col"),
            P(("dp", "row"), None, None, "col"),
            P(("dp", "row"), "col", None),
        ),
        check_vma=False,
    )
```

```python
import functools

import jax
import jax.numpy as jnp
import numpy as np
from jax import lax
from jax.experimental import pallas as pl
from jax.experimental.pallas import tpu as pltpu
from jax.sharding import PartitionSpec as P

D = 2048
NOPE = 128
ROPE = 64
HEADV = 128
RANK = 512
TOP = 6


epsilon = 1e-06
masked_score = -1e30
f32 = jnp.float32
bf16 = jnp.bfloat16


def after(value, *earlier):
    return lax.optimization_barrier((value,) + earlier)[0]


def silu_slope(values):
    sigmoid = jax.nn.sigmoid(values)
    return sigmoid * (1.0 + values * (1.0 - sigmoid))


def rotation(positions, rope_width):
    half_width = rope_width // 2
    frequency = 10000.0 ** (-jnp.arange(half_width, dtype=jnp.float32) * 2.0 / rope_width)
    angles = positions.astype(jnp.float32)[:, None] * frequency[None, :]
    return (jnp.cos(angles), jnp.sin(angles))


def rotate(values, cosine, sine_table, direction):
    half_width = values.shape[-1] // 2
    first_half = values[..., :half_width]
    second_half = values[..., half_width:]
    return jnp.concatenate(
        [
            first_half * cosine - direction * second_half * sine_table,
            second_half * cosine + direction * first_half * sine_table,
        ],
        axis=-1,
    )


def dot(left, right):
    return jnp.dot(left, right, preferred_element_type=f32)


def dot_tn(left, right):
    return lax.dot_general(left, right, (((0,), (0,)), ((), ())), preferred_element_type=f32)


def dot_nt(left, right):
    return lax.dot_general(left, right, (((1,), (1,)), ((), ())), preferred_element_type=f32)


def col_totals(values):
    return lax.psum(values, "col")


def row_gather(values):
    return lax.all_gather(values, "row", axis=0, tiled=True)


def col_gather(values, axis=0):
    return lax.all_gather(values, "col", axis=axis, tiled=True)


def col_scatter(values, axis=0):
    return lax.psum_scatter(values, "col", scatter_dimension=axis, tiled=True)


def row_scatter(values):
    return lax.psum_scatter(
        values.astype(bf16), "row", scatter_dimension=0, tiled=True
    ).astype(f32)


def send_out(parts):
    count = len(parts)
    return [parts[0]] + [
        lax.ppermute(parts[k], "dp", [(i, (i + k) % count) for i in range(count)])
        for k in range(1, count)
    ]


def send_back(parts):
    count = len(parts)
    return [parts[0]] + [
        lax.ppermute(parts[k], "dp", [(i, (i - k) % count) for i in range(count)])
        for k in range(1, count)
    ]


def norm_scale(values):
    square_sum = col_totals(jnp.sum(values * values, axis=1))
    return lax.rsqrt(square_sum / D + epsilon)


def norm_back(values, row_scale, gain_vector, upstream):
    weighted = upstream * gain_vector
    inner_mean = col_totals(jnp.sum(weighted * values, axis=1)) / D
    return weighted * row_scale[:, None] - values * (row_scale**3 * inner_mean)[:, None]


MESH = pl.DeviceIdType.MESH
VMEM = pltpu.VMEM
DMA = pltpu.SemaphoreType.DMA
MIB = 1024 * 1024
ROWS = 4
SQUARE = 4
COLS = 2
SPLIT = 2


def nn(left, right):
    return lax.dot_general(left, right, (((1,), (0,)), ((), ())), preferred_element_type=f32)


def tn(left, right):
    return lax.dot_general(left, right, (((0,), (0,)), ((), ())), preferred_element_type=f32)


def nt(left, right):
    return lax.dot_general(left, right, (((1,), (1,)), ((), ())), preferred_element_type=f32)


def block_at(row, turn):
    swapped = jnp.where(turn < 2, 1 - turn, turn)
    inner = jnp.logical_or(row == 1, row == 2)
    near = jnp.where(inner, swapped, turn)
    return jnp.where(row < 2, near, ROWS - 1 - near)


def partner(place, step):
    across, along = lax.rem(place, 2), lax.div(place, 2)
    across = lax.rem(across + step % 2, 2)
    along = lax.rem(along + step // 2, 2)
    return along * 2 + across


def remote(source, target, sent, arrived, where):
    return pltpu.make_async_remote_copy(
        src_ref=source,
        dst_ref=target,
        send_sem=sent,
        recv_sem=arrived,
        device_id=where,
        device_id_type=MESH,
    )


def greet(row, place, col, line=False, square=True):
    barrier = pltpu.get_barrier_semaphore()
    met = 1
    if line:
        for step in range(1, ROWS):
            pl.semaphore_signal(
                barrier,
                inc=1,
                device_id={"row": lax.rem(row + step, ROWS)},
                device_id_type=MESH,
            )
        met = met + ROWS - 1
    else:

        @pl.when(row > 0)
        def _():
            pl.semaphore_signal(barrier, inc=1, device_id={"row": row - 1}, device_id_type=MESH)

        @pl.when(row < ROWS - 1)
        def _():
            pl.semaphore_signal(barrier, inc=1, device_id={"row": row + 1}, device_id_type=MESH)

        met = met + (row > 0).astype(jnp.int32) + (row < ROWS - 1).astype(jnp.int32)
    if square:
        for step in range(1, SQUARE):
            pl.semaphore_signal(
                barrier, inc=1, device_id={"dp": partner(place, step)}, device_id_type=MESH
            )
        met = met + SQUARE - 1
    pl.semaphore_signal(barrier, inc=1, device_id={"col": 1 - col}, device_id_type=MESH)
    return met


def meet(met):
    pl.semaphore_wait(pltpu.get_barrier_semaphore(), met)


class Line:
    def __init__(self, row, buffer, sent, arrived):
        self.row, self.buffer, self.sent, self.arrived = row, buffer, sent, arrived

    def copy(self, block, way):
        to = self.row + 1 if way == 0 else self.row - 1
        here = self.buffer.at[block]
        return remote(here, here, self.sent.at[block, way], self.arrived.at[block], {"row": to})

    def each(self, block, act):
        @pl.when(jnp.logical_and(block <= self.row, self.row < ROWS - 1))
        def _():
            act(self.copy(block, 0))

        @pl.when(jnp.logical_and(block >= self.row, self.row > 0))
        def _():
            act(self.copy(block, 1))

    def wait(self, block):
        self.copy(block, 0).wait_recv()

    def pass_on(self, block):
        self.each(block, lambda copy: copy.start())

    def finish(self):
        def one(block, carried):
            self.each(block, lambda copy: copy.wait_send())
            return carried

        lax.fori_loop(0, ROWS, one, 0)


class SquareRest:
    def __init__(self, place, which, kept, got, middle, second, result, sent, arrived):
        self.x, self.y, self.which = lax.rem(place, 2), lax.div(place, 2), which
        self.to_x, self.to_y = {"dp": partner(place, 1)}, {"dp": partner(place, 2)}
        self.kept, self.got = kept, got
        self.middle, self.second, self.result = middle, second, result
        self.sent, self.arrived = sent.at[which], arrived.at[which]

    def copies(self, phase):
        x, y, which = self.x, self.y, self.which
        if phase == 1:
            plan = (
                (self.middle.at[0, which], self.second.at[0, which], self.to_y),
                (self.middle.at[1, which], self.second.at[1, which], self.to_x),
            )
        elif phase == 2:
            one = self.result.at[2 * x + y, which]
            two = self.result.at[4 + 2 * y + x, which]
            plan = ((one, one, self.to_y), (two, two, self.to_x))
        else:
            one = self.result.at[pl.ds(2 * x, 2), which]
            two = self.result.at[pl.ds(4 + 2 * y, 2), which]
            plan = ((one, one, self.to_x), (two, two, self.to_y))
        return [
            remote(source, target, self.sent.at[2 * phase + i], self.arrived.at[2 * phase + i], to)
            for i, (source, target, to) in enumerate(plan)
        ]

    def sum_of(self, half, side):
        wide = self.middle.shape[3]
        lanes = pl.ds(pl.multiple_of(side * wide, 128), wide)
        which = self.which
        kept, got = self.kept[half, which, :, lanes], self.got[half, which, :, lanes]
        return kept.astype(f32) + got.astype(f32)

    def prepare(self):
        self.middle[0, self.which] = self.sum_of(0, 1 - self.y).astype(bf16)
        self.middle[1, self.which] = self.sum_of(1, 1 - self.x).astype(bf16)

    def run(self, phase):
        x, y, which = self.x, self.y, self.which
        if phase > 1:
            for copy in self.copies(phase - 1):
                copy.wait_recv()
        if phase == 2:
            self.result[2 * x + y, which] = (
                self.sum_of(0, y) + self.second[0, which].astype(f32)
            ).astype(bf16)
            self.result[4 + 2 * y + x, which] = (
                self.sum_of(1, x) + self.second[1, which].astype(f32)
            ).astype(bf16)
        if phase < 4:
            for copy in self.copies(phase):
                copy.start()

    def finish(self):
        for phase in (1, 2, 3):
            for copy in self.copies(phase):
                copy.wait_send()


class SumLine:
    def __init__(self, row, part, leaving, coming, sent, arrived):
        self.row, self.part, self.leaving, self.coming = row, part, leaving, coming
        self.sent, self.arrived = sent, arrived
        self.lines = part.shape[1] // SPLIT

    def piece(self, index):
        return pl.ds(index * self.lines, self.lines)

    def copy(self, block, index, way):
        return remote(
            self.leaving.at[block, self.piece(index)],
            self.coming.at[way, block, self.piece(index)],
            self.sent.at[block, index],
            self.arrived.at[way, block, index],
            {"row": self.row + 1 - 2 * way},
        )

    def send(self, block, index):
        @pl.when(block > self.row)
        def _():
            self.copy(block, index, 0).start()

        @pl.when(block < self.row)
        def _():
            self.copy(block, index, 1).start()

    def chained(self, block):
        return jnp.logical_or(
            jnp.logical_and(block > self.row, self.row > 0),
            jnp.logical_and(block < self.row, self.row < ROWS - 1),
        )

    def begin(self, block):
        @pl.when(jnp.logical_and(block != self.row, jnp.logical_not(self.chained(block))))
        def _():
            self.leaving[block] = self.part[block].astype(bf16)
            for index in range(SPLIT):
                self.send(block, index)

    def pass_on(self, block):
        @pl.when(self.chained(block))
        def _():
            way = (block < self.row).astype(jnp.int32)
            for index in range(SPLIT):
                self.copy(block, index, way).wait_recv()
                piece = self.piece(index)
                self.leaving[block, piece] = (
                    self.part[block, piece].astype(f32)
                    + self.coming[way, block, piece].astype(f32)
                ).astype(bf16)
                self.send(block, index)

    def total(self, target):
        target[...] = self.part[self.row].astype(f32)
        for way, there in ((0, self.row > 0), (1, self.row < ROWS - 1)):

            @pl.when(there)
            def _(way=way):
                for index in range(SPLIT):
                    self.copy(self.row, index, way).wait_recv()
                    target[self.piece(index)] += self.coming[
                        way, self.row, self.piece(index)
                    ].astype(f32)

    def finish(self):
        def one(block, carried):
            @pl.when(block != self.row)
            def _():
                for index in range(SPLIT):
                    self.copy(block, index, 0).wait_send()

            return carried

        lax.fori_loop(0, ROWS, one, 0)


def swap_halves(values):
    lanes = values.shape[1]
    lane = lax.broadcasted_iota(jnp.int32, values.shape, 1)
    return jnp.where(
        lane % ROPE < ROPE // 2,
        pltpu.roll(values, lanes - ROPE // 2, 1),
        pltpu.roll(values, ROPE // 2, 1),
    )


def attend_kernel(
    act_ref,
    scaling_ref,
    compress_ref,
    rescale_ref,
    premix_ref,
    mark_ref,
    cot_ref,
    route_ref,
    router_ref,
    queries_ref,
    expand_ref,
    combine_ref,
    cos_far,
    sin_far,
    key_cos_far,
    key_sin_far,
    one_out,
    query_out,
    key_out,
    value_out,
    probs_out,
    latent_out,
    normed_latent_out,
    attended_out,
    compress_out,
    cot_out,
    pick_out,
    back_out,
    rows_out,
    residual_ref,
    two_ref,
    scale_one_ref,
    scale_two_ref,
    router_all,
    one_ref,
    query_ref,
    key_ref,
    value_ref,
    probs_ref,
    latent_ref,
    normed_latent_ref,
    attended_ref,
    compress_all,
    cot_all,
    pick_ref,
    back_ref,
    rows_ref,
    queries,
    expand,
    combine,
    cos_ref,
    sin_ref,
    key_cos_ref,
    key_sin_ref,
    stat_to,
    stat_from,
    query_own,
    query_to,
    query_from,
    latent_to,
    latent_from,
    part,
    leaving,
    coming,
    routes,
    staged,
    marks,
    raw,
    scales,
    load_sem,
    store_sem,
    rows_sem,
    stat_sent,
    stat_arrived,
    line_sent,
    line_arrived,
    comp_sent,
    comp_arrived,
    comp_out_sent,
    comp_out_arrived,
    query_sent,
    query_arrived,
    latent_sent,
    latent_arrived,
    att_sent,
    att_arrived,
    sum_sent,
    sum_arrived,
    cot_sent,
    cot_arrived,
    route_sent,
    route_arrived,
    out_sent,
    out_arrived,
    pair_sent,
    pair_arrived,
    router_sent,
    router_arrived,
    scale_sent,
    scale_arrived,
):
    place, row, col = lax.axis_index("dp"), lax.axis_index("row"), lax.axis_index("col")
    other = 1 - col
    inner = jnp.logical_and(row > 0, row < ROWS - 1)
    sibling = {"col": other}
    tokens, width = act_ref.shape
    slots = pick_ref.shape[1] // SQUARE
    mine = query_own.shape[2]
    sliced = compress_ref.shape[0]
    quarter = width // SQUARE
    score_scale = (NOPE + ROPE) ** (-0.5)
    loads = [
        pltpu.make_async_copy(source, target, load_sem.at[i])
        for i, (source, target) in enumerate(
            [
                (queries_ref, queries),
                (expand_ref, expand),
                (combine_ref, combine),
                (cos_far, cos_ref),
                (sin_far, sin_ref),
                (key_cos_far, key_cos_ref),
                (key_sin_far, key_sin_ref),
            ]
        )
    ]
    for load in loads:
        load.start()
    stores = [
        pltpu.make_async_copy(source, target, store_sem.at[i])
        for i, (source, target) in enumerate(
            [
                (one_ref, one_out),
                (query_ref, query_out),
                (key_ref, key_out),
                (value_ref, value_out),
                (latent_ref, latent_out),
                (normed_latent_ref, normed_latent_out),
                (compress_all, compress_out),
                (probs_ref, probs_out),
                (attended_ref, attended_out),
                (cot_all, cot_out),
                (pick_ref, pick_out),
                (back_ref, back_out),
            ]
        )
    ]

    def rows_store(block):
        return pltpu.make_async_copy(
            rows_ref.at[:, block], rows_out.at[:, block], rows_sem.at[block]
        )

    def stat_copy(index):
        return remote(
            stat_to.at[index],
            stat_from.at[index],
            stat_sent.at[index],
            stat_arrived.at[index],
            sibling,
        )

    def scale_of(values, index):
        own = jnp.sum(values * values, axis=1, keepdims=True)
        stat_to[index] = jnp.broadcast_to(own, (tokens, 128))
        stat_copy(index).start()
        stat_copy(index).wait_recv()
        return lax.rsqrt((own + stat_from[index][:, 0:1]) / D + epsilon)

    def comp_piece(block, member):
        return compress_all.at[
            pl.ds(pl.multiple_of(block * sliced, 16), sliced),
            pl.ds(pl.multiple_of(member * quarter, 128), quarter),
        ]

    def comp_copy(block, way):
        here = comp_piece(block, place)
        return remote(
            here,
            here,
            comp_sent.at[block, way],
            comp_arrived.at[block],
            {"row": row + 1 - 2 * way},
        )

    def comp_each(block, act):
        @pl.when(jnp.logical_and(block <= row, row < ROWS - 1))
        def _():
            act(comp_copy(block, 0))

        @pl.when(jnp.logical_and(block >= row, row > 0))
        def _():
            act(comp_copy(block, 1))

    def comp_out(block, step, member):
        here = comp_piece(block, member)
        return remote(
            here,
            here,
            comp_out_sent.at[block, step],
            comp_out_arrived.at[block, step],
            {"dp": partner(place, step)},
        )

    line = Line(row, raw, line_sent, line_arrived)
    scale_line = Line(row, scales, scale_sent, scale_arrived)
    cot_line = Line(row, cot_all, cot_sent, cot_arrived)
    route_line = Line(row, routes, route_sent, route_arrived)
    sums = SumLine(row, part, leaving, coming, sum_sent, sum_arrived)

    met = greet(row, place, col)
    compress_all[pl.ds(pl.multiple_of(row * sliced, 16), sliced)] = compress_ref[...]
    compress_all[ROWS * sliced :] = jnp.zeros(
        (compress_all.shape[0] - ROWS * sliced, width), bf16
    )
    raw[pl.ds(row, 1)] = act_ref[...].reshape(1, tokens, width)
    meet(met)
    comp_each(row, lambda copy: copy.start())
    line.pass_on(row)

    def router_copy(half):
        here = router_all.at[:, pl.ds(pl.multiple_of(half * width, width), width)]
        return remote(here, here, router_sent.at[0], router_arrived.at[0], sibling)

    inputs = act_ref[...].astype(f32)
    scale_one = scale_of(inputs, 0)
    scale_one_ref[...] = scale_one
    scales[pl.ds(row, 1)] = jnp.broadcast_to(scale_one, (tokens, 128)).T[0:8].reshape(1, 8, tokens)
    scale_line.pass_on(row)
    router_all[:, pl.ds(pl.multiple_of(col * width, width), width)] = router_ref[...]
    router_copy(col).start()
    cot_all[pl.ds(row, 1)] = cot_ref[...].reshape(1, tokens, width)
    routes[pl.ds(row, 1)] = route_ref[...].reshape((1,) + route_ref.shape)

    @pl.when(jnp.logical_not(inner))
    def _():
        route_line.pass_on(row)
        cot_line.pass_on(row)

    for block in range(ROWS):
        mark = mark_ref[:, block * tokens : (block + 1) * tokens].astype(f32)
        marks[block] = jnp.broadcast_to(mark, (8, tokens)).T
    loads[0].wait()

    def query_copy(block):
        return remote(
            query_to.at[block],
            query_from.at[block],
            query_sent.at[block],
            query_arrived.at[block],
            sibling,
        )

    def latent_copy(block):
        return remote(
            latent_to.at[block],
            latent_from.at[block],
            latent_sent.at[block],
            latent_arrived.at[block],
            sibling,
        )

    def att_copy(block, half):
        here = attended_ref.at[block, :, pl.ds(pl.multiple_of(half * 2 * HEADV, 128), 2 * HEADV)]
        return remote(here, here, att_sent.at[block], att_arrived.at[block], sibling)

    def comp_relay(step):
        block = block_at(row, step)
        comp_copy(block, 0).wait_recv()
        comp_each(block, lambda copy: copy.start())
        for shift in (3, 2, 1):
            comp_out(block, shift, place).start()

    def relay_one(step):
        block = block_at(row, step)
        line.wait(block)
        line.pass_on(block)
        scale_line.wait(block)
        scale_line.pass_on(block)

    def normalise(step):
        block = block_at(row, step)
        scale = scales[block].T[:, 0:1]
        normed = (raw[block].astype(f32) * scale * scaling_ref[...]).astype(bf16)
        one_ref[block] = normed
        query_to[block] = nn(
            normed, queries[:, pl.ds(pl.multiple_of(other * mine, 128), mine)]
        ).astype(bf16)
        query_copy(block).start()
        query_own[block] = nn(normed, queries[:, pl.ds(pl.multiple_of(col * mine, 128), mine)])

    def latents(step):
        block = block_at(row, step)
        value = nt(one_ref[block], compress_all[...])
        latent_to[block] = value
        latent_copy(block).start()
        latent_ref[block] = value

    def keys(step):
        block = block_at(row, step)
        latent_copy(block).wait_recv()
        latent = latent_ref[block] + latent_from[block]
        latent_ref[block] = latent
        plain = latent[:, :RANK]
        scale = lax.rsqrt(jnp.mean(plain * plain, axis=1, keepdims=True) + epsilon)
        normed = (plain * scale * rescale_ref[...]).astype(bf16)
        normed_latent_ref[block] = normed
        own = 2 * (NOPE + HEADV)
        expanded = nn(normed, expand[:, pl.ds(pl.multiple_of(col * own, 128), own)])
        rope = latent[:, RANK:]
        rope = rope * key_cos_ref[block] + swap_halves(rope) * key_sin_ref[block]
        first = jnp.concatenate([expanded[:, :NOPE], rope], axis=1)
        second = jnp.concatenate([expanded[:, 2 * NOPE : 3 * NOPE], rope], axis=1)
        key_ref[0, block] = first.astype(bf16)
        key_ref[1, block] = pltpu.roll(second, ROPE, 1).astype(bf16)
        value_ref[0, block] = expanded[:, NOPE : 2 * NOPE].astype(bf16)
        value_ref[1, block] = expanded[:, 3 * NOPE :].astype(bf16)
        query_copy(block).wait_recv()
        query = query_own[block] + query_from[block].astype(f32)
        query_ref[block] = (
            query * cos_ref[block] + swap_halves(query) * sin_ref[block]
        ).astype(bf16)

    def gather(step, carried):
        @pl.when(step > 0)
        def _():
            relay_one(step)

        normalise(step)

        @pl.when(step < 2)
        def _():
            comp_relay(step + 1)

        @pl.when(step == 1)
        def _():
            comp_relay(3)

        return carried

    lax.fori_loop(0, ROWS - 1, gather, 0)

    @pl.when(inner)
    def _():
        relay_one(ROWS - 1)

    def comp_arrive(block, carried):
        @pl.when(block != row)
        def _():
            for shift in range(1, SQUARE):
                comp_out(block, shift, partner(place, shift)).wait_recv()

        return carried

    lax.fori_loop(0, ROWS, comp_arrive, 0)
    for load in loads[1:2] + loads[3:]:
        load.wait()

    def middle(step, carried):
        @pl.when(jnp.logical_and(step == ROWS - 1, jnp.logical_not(inner)))
        def _():
            relay_one(step)

        @pl.when(step == ROWS - 1)
        def _():
            normalise(step)

        @pl.when(step < ROWS)
        def _():
            latents(step)

        @pl.when(step > 0)
        def _():
            keys(step - 1)

        return carried

    lax.fori_loop(0, ROWS - 1, middle, 0)

    @pl.when(inner)
    def _():
        route_line.pass_on(row)
        cot_line.pass_on(row)

    def relay(step):
        block = block_at(row, step)
        route_line.wait(block)
        route_line.pass_on(block)
        cot_line.wait(block)
        cot_line.pass_on(block)

    def out_copy(block, step):
        piece = pl.ds(step * slots, slots)
        return remote(
            staged.at[block, piece],
            rows_ref.at[col, block, piece],
            out_sent.at[block, step],
            out_arrived.at[block, step],
            {"dp": partner(place, step)},
        )

    def pair_copy(block, half):
        here = rows_ref.at[half, block]
        return remote(here, here, pair_sent.at[block], pair_arrived.at[block], sibling)

    def take(step):
        block = block_at(row, step)

        @pl.when(jnp.logical_and(step > 0, jnp.logical_not(inner)))
        def _():
            relay(step)

        before = (
            lax.broadcasted_iota(jnp.int32, (tokens, tokens), 0)
            < lax.broadcasted_iota(jnp.int32, (tokens, tokens), 1)
        ).astype(bf16)
        routing = routes[block]
        chosen = []
        for shift in range(SQUARE):
            expert = partner(place, shift) * ROWS + row
            hit = (routing == expert).astype(f32)
            chosen.append(jnp.max(hit, axis=0, keepdims=True))
        goes = jnp.concatenate(chosen + chosen, axis=0)
        rank = nn(goes.astype(bf16), before)
        for shift in range(SQUARE):
            slot = lax.broadcasted_iota(jnp.int32, (slots, tokens), 0).astype(f32)
            here = jnp.logical_and(slot == rank[shift : shift + 1], goes[shift : shift + 1] > 0.5)
            pick = here.astype(f32)
            pick_ref[block, shift * slots : (shift + 1) * slots] = pick.astype(bf16)
            back_ref[block, :, shift * slots : (shift + 1) * slots] = pick.T.astype(bf16)
        staged[block] = nn(pick_ref[block], cot_all[block]).astype(bf16)
        for shift in (3, 2, 1):
            out_copy(block, shift).start()
        rows_ref[col, block, 0:slots] = staged[block, 0:slots]

    def forward(step):
        block = block_at(row, step)
        for shift in range(1, SQUARE):
            out_copy(block, shift).wait_recv()
        pair_copy(block, col).start()

    take(0)

    @pl.when(inner)
    def _():
        relay(1)
        relay(2)

    lax.fori_loop(ROWS - 1, ROWS + 1, middle, 0)

    for index in range(7):
        stores[index].start()
    seq = ROWS * tokens
    lanes = NOPE + 2 * ROPE

    def attend(turn, carried):
        block = block_at(row, ROWS - 1 - turn)
        visible = mark_ref[...].astype(f32) <= marks[block][:, 0:1]
        for head in range(2):
            query = query_ref[block, :, head * NOPE : head * NOPE + lanes]
            scores = nt(query, key_ref[head].reshape(seq, lanes)) * score_scale
            scores = jnp.where(visible, scores, masked_score)
            weight = jnp.exp(scores - jnp.max(scores, axis=1, keepdims=True))
            probs = (weight / jnp.sum(weight, axis=1, keepdims=True)).astype(bf16)
            probs_ref[head, block] = probs
            result = nn(probs, value_ref[head].reshape(seq, HEADV)).astype(bf16)
            at = pl.multiple_of((col * 2 + head) * HEADV, 128)
            attended_ref[block, :, pl.ds(at, HEADV)] = result
        att_copy(block, col).start()

        @pl.when(jnp.logical_and(turn == 0, inner))
        def _():
            relay(3)

        @pl.when(turn > 0)
        def _():
            mix(turn - 1)
            take(turn)

        return carried

    def mix(turn):
        block = block_at(row, ROWS - 1 - turn)
        att_copy(block, other).wait_recv()
        part[block] = nn(attended_ref[block], combine[...])
        sums.begin(block)

    loads[2].wait()
    lax.fori_loop(0, ROWS, attend, 0)
    mix(ROWS - 1)
    for index in range(7, 12):
        stores[index].start()

    def hand_on(turn, carried):
        sums.pass_on(block_at(row, jnp.where(turn == 0, 3, turn)))
        forward(turn)
        return carried

    lax.fori_loop(0, 3, hand_on, 0)
    sums.total(residual_ref)
    residual = residual_ref[...] + inputs
    residual_ref[...] = residual
    scale_two = scale_of(residual, 1)
    scale_two_ref[...] = scale_two
    two_ref[...] = (residual * scale_two * premix_ref[...]).astype(bf16)
    forward(3)

    def ended(block, carried):
        pair_copy(block, other).wait_recv()
        rows_store(block).start()
        pair_copy(block, col).wait_send()
        for shift in range(1, SQUARE):
            out_copy(block, shift).wait_send()

            @pl.when(block != row)
            def _(shift=shift):
                comp_out(block, shift, place).wait_send()

        comp_each(block, lambda copy: copy.wait_send())
        query_copy(block).wait_send()
        latent_copy(block).wait_send()
        att_copy(block, col).wait_send()
        return carried

    lax.fori_loop(0, ROWS, ended, 0)
    for store in stores:
        store.wait()

    def stored(block, carried):
        rows_store(block).wait()
        return carried

    lax.fori_loop(0, ROWS, stored, 0)
    router_copy(other).wait_recv()
    router_copy(col).wait_send()
    stat_copy(0).wait_send()
    stat_copy(1).wait_send()
    sums.finish()
    line.finish()
    scale_line.finish()
    cot_line.finish()
    route_line.finish()


def turning_tables(length):
    half = ROPE // 2
    frequency = 10000.0 ** (-np.arange(half, dtype=np.float32) * 2.0 / ROPE)
    angles = np.arange(length, dtype=np.float32)[:, None] * frequency[None, :].astype(np.float32)
    cosine, sine = np.cos(angles), np.sin(angles)
    cosine, sine = np.concatenate([cosine, cosine], 1), np.concatenate([-sine, sine], 1)
    ones, zeros = np.ones((length, NOPE)), np.zeros((length, NOPE))
    gap = np.zeros((length, 128 - ROPE))
    tables = (
        np.concatenate([ones, cosine, ones, cosine], 1),
        np.concatenate([zeros, sine, zeros, sine], 1),
        np.concatenate([cosine, gap], 1),
        np.concatenate([sine, gap], 1),
    )
    return [
        jnp.asarray(table.reshape(ROWS, length // ROWS, -1).astype(np.float32))
        for table in tables
    ]


def pair_sems():
    return [DMA((ROWS,)), DMA((ROWS,))]


def line_sems():
    return [DMA((ROWS, 2)), DMA((ROWS,))]


def square_sems():
    return [DMA((ROWS, SQUARE)), DMA((ROWS, SQUARE))]


def sum_sems():
    return [DMA((ROWS, SPLIT)), DMA((2, ROWS, SPLIT))]


def run_attention(
    activations,
    scaling,
    queries,
    compress,
    rescale,
    expand,
    combine,
    premix,
    segments,
    cotangent,
    routing,
    router,
    tables,
    slots,
):
    tokens, width = activations.shape
    seq = ROWS * tokens
    mine = queries.shape[1] // COLS
    sliced = compress.shape[1]
    latent_width = RANK + 128
    picked = SQUARE * slots
    lanes = NOPE + 2 * ROPE
    routes = routing.T
    whole = pl.BlockSpec(memory_space=VMEM)
    far = pl.BlockSpec(memory_space=pl.ANY)

    def shape(*dims, dtype=bf16):
        return jax.ShapeDtypeStruct(dims, dtype)

    kept = [
        shape(ROWS, tokens, width),
        shape(ROWS, tokens, mine),
        shape(2, ROWS, tokens, lanes),
        shape(2, ROWS, tokens, HEADV),
        shape(2, ROWS, tokens, seq),
        shape(ROWS, tokens, latent_width, dtype=f32),
        shape(ROWS, tokens, RANK),
        shape(ROWS, tokens, COLS * 2 * HEADV),
        shape(latent_width, width),
        shape(ROWS, tokens, width),
        shape(ROWS, picked, tokens),
        shape(ROWS, tokens, picked),
        shape(COLS, ROWS, picked, width),
    ]
    return pl.pallas_call(
        attend_kernel,
        name="attend",
        out_shape=(
            *kept,
            shape(tokens, width, dtype=f32),
            shape(tokens, width),
            shape(tokens, 1, dtype=f32),
            shape(tokens, 1, dtype=f32),
            shape(router.shape[1], COLS * width),
        ),
        in_specs=[whole] * 9 + [far] * 7,
        out_specs=(far,) * 13 + (whole,) * 5,
        scratch_shapes=[
            *[VMEM(value.shape, value.dtype) for value in kept],
            VMEM(queries.shape, bf16),
            VMEM(expand.shape, bf16),
            VMEM(combine.shape, bf16),
            *[VMEM(table.shape, f32) for table in tables],
            VMEM((2, tokens, 128), f32),
            VMEM((2, tokens, 128), f32),
            VMEM((ROWS, tokens, mine), f32),
            VMEM((ROWS, tokens, mine), bf16),
            VMEM((ROWS, tokens, mine), bf16),
            VMEM((ROWS, tokens, latent_width), f32),
            VMEM((ROWS, tokens, latent_width), f32),
            VMEM((ROWS, tokens, width), f32),
            VMEM((ROWS, tokens, width), bf16),
            VMEM((2, ROWS, tokens, width), bf16),
            VMEM((ROWS,) + routes.shape, jnp.int32),
            VMEM((ROWS, picked, width), bf16),
            VMEM((ROWS, tokens, 8), f32),
            VMEM((ROWS, tokens, width), bf16),
            VMEM((ROWS, 8, tokens), f32),
            DMA((7,)),
            DMA((12,)),
            DMA((ROWS,)),
            DMA((2,)),
            DMA((2,)),
            *line_sems(),
            *line_sems(),
            *square_sems(),
            *pair_sems(),
            *pair_sems(),
            *pair_sems(),
            *sum_sems(),
            *line_sems(),
            *line_sems(),
            *square_sems(),
            *pair_sems(),
            DMA((1,)),
            DMA((1,)),
            *line_sems(),
        ],
        compiler_params=pltpu.CompilerParams(
            collective_id=1, has_side_effects=True, vmem_limit_bytes=56 * MIB
        ),
        cost_estimate=pl.CostEstimate(
            flops=40 * 1024**3, bytes_accessed=32 * MIB, transcendentals=0
        ),
    )(
        activations,
        scaling.reshape(1, width),
        compress.T,
        rescale.reshape(1, RANK),
        premix.reshape(1, width),
        segments.reshape(1, seq),
        cotangent,
        routes,
        router.T,
        queries,
        expand,
        combine,
        *tables,
    )


def attend_back_kernel(
    normed_grad_ref,
    residual_ref,
    scale_two_ref,
    premix_ref,
    cot_ref,
    act_ref,
    scale_one_ref,
    scaling_ref,
    rescale_ref,
    combine_far,
    query_far,
    key_far,
    value_far,
    probs_far,
    cos_far,
    sin_far,
    queries_far,
    expand_far,
    latent_far,
    key_cos_far,
    key_sin_far,
    compress_far,
    one_far,
    kept_far,
    got_x_far,
    got_y_far,
    attended_far,
    normed_latent_far,
    narrow_far,
    home_far,
    back_far,
    shared_far,
    premix_far,
    router_far,
    input_grad_ref,
    output_ref,
    small_ref,
    shared_sum,
    queries_out,
    combine_out,
    expand_out,
    compress_out,
    branch_ref,
    query_grad_ref,
    expanded_ref,
    own_latent_ref,
    scaling_rows,
    rescale_rows,
    combine,
    query_ref,
    key_ref,
    value_ref,
    probs_ref,
    cos_ref,
    sin_ref,
    queries,
    expand,
    latent_ref,
    key_cos_ref,
    key_sin_ref,
    compress_all,
    one_ref,
    kept,
    got,
    middle,
    second,
    result,
    attended,
    normed_latent,
    narrow,
    home,
    back_ref,
    shared_ref,
    premix_rows,
    router_rows,
    stat_to,
    stat_from,
    grad_own,
    grad_to,
    grad_from,
    key_grad,
    value_grad,
    latent_own,
    latent_to,
    latent_from,
    turned,
    turned_from,
    part,
    leaving,
    coming,
    total,
    load_sem,
    stat_sent,
    stat_arrived,
    line_sent,
    line_arrived,
    grad_sent,
    grad_arrived,
    query_sent,
    query_arrived,
    latent_sent,
    latent_arrived,
    turned_sent,
    turned_arrived,
    own_sent,
    own_arrived,
    sum_sent,
    sum_arrived,
    rest_sent,
    rest_arrived,
    rest_sem,
    reply_part,
    reply_leaving,
    reply_coming,
    small_to,
    small_from,
    small_line,
    small_square,
    small_own,
    expand_other,
    store_sem,
    reply_sent,
    reply_arrived,
    pair_sent,
    pair_arrived,
    small_sent,
    small_arrived,
    *sums_scratch,
):
    place, row, col = lax.axis_index("dp"), lax.axis_index("row"), lax.axis_index("col")
    other = 1 - col
    sibling = {"col": other}
    tokens, width = act_ref.shape
    seq = ROWS * tokens
    mine = query_ref.shape[2]
    lanes = key_ref.shape[3]
    both = 2 * HEADV
    sliced = own_latent_ref.shape[0]
    score_scale = (NOPE + ROPE) ** (-0.5)
    loads = [
        pltpu.make_async_copy(source, target, load_sem.at[i])
        for i, (source, target) in enumerate(
            [
                (kept_far, kept),
                (got_x_far, got.at[0]),
                (got_y_far, got.at[1]),
                (combine_far, combine),
                (query_far, query_ref),
                (key_far, key_ref),
                (value_far, value_ref),
                (probs_far, probs_ref),
                (cos_far, cos_ref),
                (sin_far, sin_ref),
                (queries_far, queries),
                (expand_far, expand),
                (latent_far, latent_ref),
                (key_cos_far, key_cos_ref),
                (key_sin_far, key_sin_ref),
                (compress_far, compress_all),
                (one_far, one_ref),
                (attended_far, attended),
                (normed_latent_far, normed_latent),
                (narrow_far, narrow),
                (home_far, home),
                (back_far, back_ref),
                (shared_far, shared_ref),
                (premix_far, premix_rows),
                (router_far, router_rows),
            ]
        )
    ]
    for load in loads:
        load.start()
    line = Line(row, branch_ref, line_sent, line_arrived)
    sums = SumLine(row, part, leaving, coming, sum_sent, sum_arrived)
    met = greet(row, place, col, line=True)

    def stat_copy(index):
        return remote(
            stat_to.at[index],
            stat_from.at[index],
            stat_sent.at[index],
            stat_arrived.at[index],
            sibling,
        )

    def norm_begin(values, gain, upstream, index):
        weighted = upstream * gain
        own = jnp.sum(weighted * values, axis=1, keepdims=True)
        stat_to[index] = jnp.broadcast_to(own, (tokens, 128))
        stat_copy(index).start()

    def norm_grad(values, scale, gain, upstream, index):
        stat_copy(index).wait_recv()
        inner = (stat_to[index][:, 0:1] + stat_from[index][:, 0:1]) / D
        return upstream * gain * scale - values * (scale * scale * scale * inner)

    for load in loads[0:3]:
        load.wait()
    rests = [
        SquareRest(place, which, kept, got, middle, second, result, rest_sent, rest_arrived)
        for which in range(kept.shape[1])
    ]
    for rest in rests:
        rest.prepare()
    meet(met)
    norm_begin(residual_ref[...], premix_ref[...], normed_grad_ref[...], 0)
    for rest in rests:
        rest.run(1)
    residual_grad = cot_ref[...].astype(f32) + norm_grad(
        residual_ref[...], scale_two_ref[...], premix_ref[...], normed_grad_ref[...], 0
    )
    input_grad_ref[...] = residual_grad
    branch_ref[pl.ds(row, 1)] = residual_grad.astype(bf16).reshape(1, tokens, width)
    line.pass_on(row)
    key_grad[...] = jnp.zeros_like(key_grad)
    value_grad[...] = jnp.zeros_like(value_grad)
    scaling_rows[...] = jnp.zeros_like(scaling_rows)
    rescale_rows[...] = jnp.zeros_like(rescale_rows)

    line_sums = SumLine(
        row, reply_part, reply_leaving, reply_coming, reply_sent, reply_arrived
    )
    experts = router_rows.shape[0]
    kinds = [sums_scratch[7 * i : 7 * i + 7] for i in range(4)]
    parts = [scratch[0] for scratch in kinds]
    plan = [(kind, chunk) for kind in range(4) for chunk in range(parts[kind].shape[0])]
    pieces_of = [
        SquareSum(place, *[ref.at[chunk] for ref in kinds[kind]]) for kind, chunk in plan
    ]
    count = len(plan)

    def begin(index):
        kind, chunk = plan[index]
        part_ref = parts[kind]
        if kind == 0 and chunk == 0:
            loads[17].wait()
        if kind == 2:
            loads[18].wait()
        if kind < 2:
            left, right = ((attended, branch_ref), (one_ref, query_grad_ref))[kind]
            height = 8 * part_ref.shape[2]
            piece = left[:, :, chunk * height : (chunk + 1) * height].reshape(seq, height)
            grad = tn(piece, right[...].reshape(seq, right.shape[2]))
        elif kind == 2:
            grad = tn(
                normed_latent[...].reshape(seq, RANK),
                expanded_ref[...].reshape(seq, expanded_ref.shape[2]),
            )
        else:
            grad = nn(own_latent_ref[...], one_ref[...].reshape(seq, width)).astype(bf16)
            for piece in range(8):
                part_ref[0, piece] = grad[:, piece * (width // 8) : (piece + 1) * (width // 8)]
        if kind < 3:
            part_ref[chunk] = grad.astype(bf16).reshape(part_ref.shape[1:])
        pieces_of[index].run(0)

    stores = []

    def store(source, target):
        copy = pltpu.make_async_copy(source, target, store_sem.at[len(stores)])
        copy.start()
        stores.append(copy)

    def pair_copy():
        return remote(kinds[2][4].at[0], expand_other, pair_sent.at[0], pair_arrived.at[0], sibling)

    def expand_lanes(half):
        wide = expand_other.shape[2]
        return expand_out.at[:, :, pl.ds(pl.multiple_of(half * wide, 128), wide)]

    def put(index):
        kind, chunk = plan[index]
        done = kinds[kind][4]
        if kind < 2:
            store(done.at[chunk], (combine_out, queries_out)[kind].at[chunk])
        elif kind == 2:
            store(done.at[0], expand_lanes(col))
            pair_copy().start()
        else:
            lanes = width // 8
            for piece in range(8):
                store(done.at[0, piece], compress_out.at[:, piece * lanes : (piece + 1) * lanes])

    def advance(turn):
        for phase in (1, 2, 3, 4):
            index = turn - phase
            if 0 <= index < count:
                pieces_of[index].run(phase)
                if phase == 4:
                    put(index)
        if 2 <= turn < count:
            begin(turn)

    def reply_add(turn, carried):
        block = block_at(row, ROWS - 1 - turn)
        reply_part[block] = (
            nn(back_ref[block], home[block]) + nn(shared_ref[block], narrow[...])
        ).astype(bf16)
        line_sums.begin(block)
        return carried

    def small_copy(step):
        if step == 0:
            return remote(small_to, small_from, small_sent.at[0], small_arrived.at[0], sibling)
        if step < ROWS:
            return remote(
                small_own,
                small_line.at[step],
                small_sent.at[step],
                small_arrived.at[step],
                {"row": lax.rem(row + step, ROWS)},
            )
        shift = step - ROWS + 1
        return remote(
            small_ref,
            small_square.at[shift],
            small_sent.at[step],
            small_arrived.at[step],
            {"dp": partner(place, shift)},
        )

    def small_begin():
        loads[23].wait()
        loads[24].wait()
        rescale_row = jnp.sum(rescale_rows[...], axis=0, keepdims=True)
        empty = jnp.zeros((small_own.shape[0] - experts, width), f32)
        small_to[0:experts] = router_rows[:, pl.ds(pl.multiple_of(other * width, width), width)]
        small_to[experts:] = empty
        small_to[experts + 2 : experts + 3, 0:RANK] = rescale_row
        small_copy(0).start()
        small_own[0:experts] = router_rows[:, pl.ds(pl.multiple_of(col * width, width), width)]
        small_own[experts:] = empty
        small_own[experts : experts + 1] = (
            jnp.sum(premix_rows[...], axis=0, keepdims=True) / premix_ref[...]
        )
        small_own[experts + 1 : experts + 2] = (
            jnp.sum(scaling_rows[...], axis=0, keepdims=True) / scaling_ref[...]
        )
        small_own[experts + 2 : experts + 3, 0:RANK] = rescale_row

    def small_line_begin():
        small_copy(0).wait_recv()
        small_own[...] += small_from[...]
        for step in range(1, ROWS):
            small_copy(step).start()

    def small_square_begin():
        for step in range(1, ROWS):
            small_copy(step).wait_recv()
        small_ref[...] = small_own[...] + small_line[1] + small_line[2] + small_line[3]
        for step in range(ROWS, ROWS + SQUARE - 1):
            small_copy(step).start()

    def small_end():
        for step in range(ROWS, ROWS + SQUARE - 1):
            small_copy(step).wait_recv()
        for step in range(ROWS, ROWS + SQUARE - 1):
            small_copy(step).wait_send()
        small_ref[...] += small_square[1] + small_square[2] + small_square[3]

    def reply_begin():
        for load in loads[19:23]:
            load.wait()
        lax.fori_loop(0, ROWS, reply_add, 0)

    def reply_pass():
        lax.fori_loop(0, 3, line_pass, 0)

    def reply_end():
        line_sums.total(total)
        output_ref[...] = (total[...] + residual_ref[...]).astype(bf16)

    def line_pass(turn, carried):
        line_sums.pass_on(block_at(row, jnp.where(turn == 0, 3, turn)))
        return carried

    def grad_copy(block):
        return remote(
            grad_to.at[block],
            grad_from.at[block],
            grad_sent.at[block],
            grad_arrived.at[block],
            sibling,
        )

    def query_copy(block, half):
        here = query_grad_ref.at[block, :, pl.ds(pl.multiple_of(half * mine, 128), mine)]
        return remote(here, here, query_sent.at[block], query_arrived.at[block], sibling)

    def latent_copy(block):
        return remote(
            latent_to.at[block],
            latent_from.at[block],
            latent_sent.at[block],
            latent_arrived.at[block],
            sibling,
        )

    def arrive(step):
        block = block_at(row, step)

        @pl.when(step > 0)
        def _():
            line.wait(block)
            line.pass_on(block)

        @pl.when(step == 0)
        def _():
            loads[3].wait()

        grads = branch_ref[block]
        grad_to[block] = nt(
            grads, combine[pl.ds(pl.multiple_of(other * both, 16), both)]
        ).astype(bf16)
        grad_copy(block).start()
        grad_own[block] = nt(grads, combine[pl.ds(pl.multiple_of(col * both, 16), both)])

    def heads(step):
        block = block_at(row, step)

        @pl.when(step == 0)
        def _():
            for load in loads[4:10]:
                load.wait()

        grad_copy(block).wait_recv()
        grads = (grad_own[block] + grad_from[block].astype(f32)).astype(bf16)
        pieces = []
        for head in range(2):
            upstream = grads[:, head * HEADV : (head + 1) * HEADV]
            query = query_ref[block, :, head * NOPE : head * NOPE + lanes]
            probs = probs_ref[head, block]
            weight = probs.astype(f32)
            probs_back = nt(upstream, value_ref[head].reshape(seq, HEADV))
            inner = jnp.sum(weight * probs_back, axis=1, keepdims=True)
            score_grad = (weight * (probs_back - inner)).astype(bf16)
            pieces.append(nn(score_grad, key_ref[head].reshape(seq, lanes)) * score_scale)
            key_grad[head] += tn(score_grad, query)
            value_grad[head] += tn(probs, upstream)
        first, second = pieces
        grad = jnp.concatenate(
            [first[:, :NOPE], first[:, NOPE:] + second[:, :NOPE], second[:, NOPE:]], axis=1
        )
        grad = grad * cos_ref[block] - swap_halves(grad) * sin_ref[block]
        query_grad_ref[block, :, pl.ds(pl.multiple_of(col * mine, 128), mine)] = grad.astype(bf16)
        query_copy(block, col).start()

    def project(step):
        block = block_at(row, step)

        @pl.when(step == 0)
        def _():
            loads[10].wait()

        query_copy(block, other).wait_recv()
        part[block] = nt(query_grad_ref[block], queries[...])

    def turn(step, carried):
        @pl.when(step < ROWS)
        def _():
            arrive(step)

        @pl.when(step == 1)
        def _():
            for rest in rests:
                rest.run(2)

        @pl.when(step == 2)
        def _():
            rests[0].run(3)

        @pl.when(step == 3)
        def _():
            rests[1].run(3)
            rests[2].run(3)

        @pl.when(step >= 1)
        def _():
            heads(step - 1)

        @pl.when(step >= 2)
        def _():
            project(step - 2)

        return carried

    lax.fori_loop(0, ROWS + 1, turn, 0)
    for load in loads[11:17]:
        load.wait()
    begin(0)
    begin(1)
    reply_begin()

    def latents(turn, carried):
        block = block_at(row, ROWS - 1 - turn)
        here = pl.ds(pl.multiple_of(block * tokens, 128), tokens)
        first = key_grad[0, here] * score_scale
        second = pltpu.roll(key_grad[1, here] * score_scale, lanes - ROPE, 1)
        grad = jnp.concatenate(
            [first[:, :NOPE], value_grad[0, here], second[:, :NOPE], value_grad[1, here]], axis=1
        ).astype(bf16)
        expanded_ref[block] = grad
        own = 2 * (NOPE + HEADV)
        upstream = nt(grad, expand[:, pl.ds(pl.multiple_of(col * own, 128), own)])
        plain = latent_ref[block][:, :RANK]
        scale = lax.rsqrt(jnp.mean(plain * plain, axis=1, keepdims=True) + epsilon)
        rescale_rows[...] += jnp.sum(
            (upstream * plain * scale).reshape(tokens // 8, 8, RANK), axis=0
        )
        weighted = upstream * rescale_ref[...]
        inner = jnp.mean(weighted * plain, axis=1, keepdims=True)
        plain_grad = weighted * scale - plain * (scale * scale * scale * inner)
        rope = first[:, NOPE:] + second[:, NOPE:]
        lane = lax.broadcasted_iota(jnp.int32, rope.shape, 1)
        rope = jnp.where(lane < ROPE, rope, 0.0)
        rope = rope * key_cos_ref[block] - swap_halves(rope) * key_sin_ref[block]
        value = jnp.concatenate([plain_grad, rope], axis=1)
        latent_own[block] = value
        latent_to[block] = value.astype(bf16)
        latent_copy(block).start()
        return carried

    lax.fori_loop(0, ROWS, latents, 0)
    project(ROWS - 1)

    def turned_piece(member):
        return turned.at[
            pl.ds(pl.multiple_of(member * sliced, 16), sliced),
            pl.ds(pl.multiple_of(col * (seq // COLS), 128), seq // COLS),
        ]

    def turned_copy(step):
        to = lax.rem(row + step, ROWS)
        return remote(
            turned_piece(to),
            turned_from.at[step],
            turned_sent.at[step],
            turned_arrived.at[step],
            {"row": to},
        )

    def mix(turn, carried):
        block = block_at(row, ROWS - 1 - turn)
        latent_copy(block).wait_recv()
        latent = latent_own[block] + latent_from[block].astype(f32)
        here = pl.ds(pl.multiple_of(block * tokens, 128), tokens)
        total_here = part[block] + nn(latent.astype(bf16), compress_all[...])
        part[block] = total_here
        sums.begin(block)
        turned[:, here] = latent.T.astype(bf16)
        scaling_rows[...] += jnp.sum(
            (total_here * one_ref[block].astype(f32)).reshape(tokens // 8, 8, width), axis=0
        )
        return carried

    lax.fori_loop(0, ROWS, mix, 0)
    for step in range(1, ROWS):
        turned_copy(step).start()

    advance(1)
    small_begin()
    for turn in range(3):
        sums.pass_on(block_at(row, 3 if turn == 0 else turn))
        advance(turn + 2)
        if turn == 0:
            small_line_begin()
    for step in range(1, ROWS):
        turned_copy(step).wait_recv()
    half = pl.ds(pl.multiple_of(col * (seq // COLS), 128), seq // COLS)
    own_sum = turned[pl.ds(pl.multiple_of(row * sliced, 16), sliced), half].astype(f32)
    for step in range(1, ROWS):
        own_sum = own_sum + turned_from[step].astype(f32)
    own_latent_ref[:, half] = own_sum.astype(bf16)

    def own_copy(part_of):
        here = own_latent_ref.at[
            :, pl.ds(pl.multiple_of(part_of * (seq // COLS), 128), seq // COLS)
        ]
        return remote(here, here, own_sent.at[0], own_arrived.at[0], sibling)

    own_copy(col).start()
    advance(5)
    sums.total(total)
    norm_begin(act_ref[...].astype(f32), scaling_ref[...], total[...], 1)
    input_grad_ref[...] += norm_grad(
        act_ref[...].astype(f32), scale_one_ref[...], scaling_ref[...], total[...], 1
    )
    advance(6)
    reply_pass()
    for rest in rests:
        rest.run(4)
    pieces = [
        pltpu.make_async_copy(
            result.at[i], shared_sum.at[:, :, i * 128 : (i + 1) * 128], rest_sem.at[i]
        )
        for i in range(8)
    ]
    for piece in pieces:
        piece.start()
    own_copy(other).wait_recv()
    own_copy(col).wait_send()
    advance(7)
    small_square_begin()
    advance(8)
    reply_end()
    for turn in range(9, count + 5):
        advance(turn)
    small_end()
    pair_copy().wait_recv()
    store(expand_other, expand_lanes(other))

    def ended(block, carried):
        grad_copy(block).wait_send()
        query_copy(block, col).wait_send()
        latent_copy(block).wait_send()
        return carried

    lax.fori_loop(0, ROWS, ended, 0)
    for step in range(1, ROWS):
        turned_copy(step).wait_send()
    stat_copy(0).wait_send()
    stat_copy(1).wait_send()
    for piece in pieces:
        piece.wait()
    for copy in stores:
        copy.wait()
    pair_copy().wait_send()
    for step in range(ROWS):
        small_copy(step).wait_send()
    for one_sum in pieces_of:
        one_sum.finish()
    line_sums.finish()
    for rest in rests:
        rest.finish()
    sums.finish()
    line.finish()


def run_attention_back(
    normed_grad,
    residual,
    scale_two,
    premix,
    cotangent,
    activations,
    scale_one,
    scaling,
    one,
    query,
    key,
    value,
    probs,
    latent,
    rescale,
    tables,
    compress_all,
    queries,
    expand,
    combine,
    shared,
    more,
):
    tokens, width = activations.shape
    seq = ROWS * tokens
    mine = query.shape[2]
    lanes = key.shape[3]
    latent_width = latent.shape[2]
    sliced = (RANK + ROPE) // ROWS
    whole = pl.BlockSpec(memory_space=VMEM)
    far = pl.BlockSpec(memory_space=pl.ANY)

    def shape(*dims, dtype=bf16):
        return jax.ShapeDtypeStruct(dims, dtype)

    kept, got_x, got_y = shared
    heads = more[0].shape[2]
    own_heads = 2 * (NOPE + HEADV)
    small = (24, width)
    piece = kept.shape[1:3] + (kept.shape[3] // 2,)
    loaded = (
        combine,
        query,
        key,
        value,
        probs,
        tables[0],
        tables[1],
        queries,
        expand,
        latent,
        tables[2],
        tables[3],
        compress_all,
        one,
    )
    return pl.pallas_call(
        attend_back_kernel,
        name="attend_back",
        out_shape=(
            shape(tokens, width, dtype=f32),
            shape(tokens, width),
            shape(*small, dtype=f32),
            shape(*kept.shape[1:3], width),
            shape(4, 8, width // 32, COLS * mine),
            shape(2, 8, heads // 16, width),
            shape(8, RANK // 8, COLS * own_heads),
            shape(sliced, width),
        ),
        in_specs=[whole] * 9 + [far] * 25,
        out_specs=(whole,) * 3 + (far,) * 5,
        scratch_shapes=[
            VMEM((ROWS, tokens, width), bf16),
            VMEM((ROWS, tokens, COLS * mine), bf16),
            VMEM((ROWS, tokens, own_heads), bf16),
            VMEM((sliced, seq), bf16),
            VMEM((8, width), f32),
            VMEM((8, RANK), f32),
            *[VMEM(value.shape, value.dtype) for value in loaded],
            VMEM(kept.shape, bf16),
            VMEM(kept.shape, bf16),
            VMEM((2,) + piece, bf16),
            VMEM((2,) + piece, bf16),
            VMEM((8,) + piece, bf16),
            *[VMEM(value.shape, value.dtype) for value in more],
            VMEM((2, tokens, 128), f32),
            VMEM((2, tokens, 128), f32),
            VMEM((ROWS, tokens, 2 * HEADV), f32),
            VMEM((ROWS, tokens, 2 * HEADV), bf16),
            VMEM((ROWS, tokens, 2 * HEADV), bf16),
            VMEM((2, seq, lanes), f32),
            VMEM((2, seq, HEADV), f32),
            VMEM((ROWS, tokens, latent_width), f32),
            VMEM((ROWS, tokens, latent_width), bf16),
            VMEM((ROWS, tokens, latent_width), bf16),
            VMEM((latent_width, seq), bf16),
            VMEM((ROWS, sliced, seq // COLS), bf16),
            VMEM((ROWS, tokens, width), f32),
            VMEM((ROWS, tokens, width), bf16),
            VMEM((2, ROWS, tokens, width), bf16),
            VMEM((tokens, width), f32),
            DMA((25,)),
            DMA((2,)),
            DMA((2,)),
            *line_sems(),
            *pair_sems(),
            *pair_sems(),
            *pair_sems(),
            *pair_sems(),
            *pair_sems(),
            *sum_sems(),
            DMA((kept.shape[1], 8)),
            DMA((kept.shape[1], 8)),
            DMA((8,)),
            VMEM((ROWS, tokens, width), bf16),
            VMEM((ROWS, tokens, width), bf16),
            VMEM((2, ROWS, tokens, width), bf16),
            VMEM(small, f32),
            VMEM(small, f32),
            VMEM((ROWS,) + small, f32),
            VMEM((SQUARE,) + small, f32),
            VMEM(small, f32),
            VMEM((8, RANK // 8, own_heads), bf16),
            DMA((16,)),
            *sum_sems(),
            DMA((1,)),
            DMA((1,)),
            DMA((ROWS + SQUARE - 1,)),
            DMA((ROWS + SQUARE - 1,)),
            *square_scratch((2, heads // 16, width)),
            *square_scratch((4, width // 32, COLS * mine)),
            *square_scratch((1, RANK // 8, own_heads)),
            *square_scratch((1, sliced, width // 8)),
        ],
        compiler_params=pltpu.CompilerParams(
            collective_id=3, has_side_effects=True, vmem_limit_bytes=62 * MIB
        ),
        cost_estimate=pl.CostEstimate(
            flops=40 * 1024**3, bytes_accessed=32 * MIB, transcendentals=0
        ),
    )(
        normed_grad,
        residual,
        scale_two,
        premix.reshape(1, width),
        cotangent,
        activations,
        scale_one,
        scaling.reshape(1, width),
        rescale.reshape(1, RANK),
        *loaded,
        kept,
        got_x,
        got_y,
        *more,
    )


def silu_pair(values):
    sigmoid = 1.0 / (1.0 + jnp.exp(-values))
    return values * sigmoid, sigmoid * (1.0 + values * (1.0 - sigmoid))


def expert_kernel(
    normed_ref,
    pick_ref,
    router_ref,
    back_far,
    cot_far,
    cot_rows_ref,
    fan_ref,
    fun_ref,
    wide_ref,
    narrow_ref,
    sum_ref,
    rows_out,
    gu_out,
    hidden_out,
    shared_x,
    shared_y,
    shared_kept,
    shared_far,
    reply_ref,
    premix_ref,
    router_rows,
    gathered_ref,
    shared_out,
    back_ref,
    cot_ref,
    fan,
    fun,
    wide,
    narrow,
    cot_rows,
    rows,
    staged,
    gu,
    hidden,
    pair_own,
    pair_to,
    pair_from,
    home,
    shared_to,
    shared_from,
    part,
    passed_to,
    passed_from,
    shared_gu,
    shared_grad,
    load_sem,
    store_sem,
    line_sent,
    line_arrived,
    out_sent,
    out_arrived,
    fwd_sent,
    fwd_arrived,
    shared_sent,
    shared_arrived,
    half_sent,
    half_arrived,
    home_sent,
    home_arrived,
    sum_sent,
    sum_arrived,
    other_sent,
    other_arrived,
    reply_sent,
    reply_arrived,
    grad_sem,
    late_sem,
):
    place, row, col = lax.axis_index("dp"), lax.axis_index("row"), lax.axis_index("col")
    other = 1 - col
    inner = jnp.logical_and(row > 0, row < ROWS - 1)
    tokens, width = normed_ref.shape
    picked = pick_ref.shape[1]
    slots = picked // SQUARE
    experts = router_ref.shape[0]
    share = narrow.shape[0]
    loads = [
        pltpu.make_async_copy(source, target, load_sem.at[i])
        for i, (source, target) in enumerate(
            [
                (wide_ref, wide),
                (narrow_ref, narrow),
                (fan_ref, fan),
                (cot_rows_ref, cot_rows),
                (fun_ref, fun),
                (cot_far, cot_ref),
                (back_far, back_ref),
            ]
        )
    ]
    for load in loads:
        load.start()
    met = greet(row, place, col)
    gathered_ref[pl.ds(row, 1)] = normed_ref[...].reshape(1, tokens, width)
    staged[pl.ds(row, 1)] = (
        nn(pick_ref[row], normed_ref[...]).astype(bf16).reshape(1, picked, width)
    )
    meet(met)
    line = Line(row, gathered_ref, line_sent, line_arrived)
    line.pass_on(row)
    premix_ref[...] = jnp.zeros_like(premix_ref)
    router_rows[...] = jnp.zeros_like(router_rows)
    sums = SumLine(row, part, passed_to, passed_from, sum_sent, sum_arrived)
    sibling = {"col": other}

    def half_lines(half):
        return pl.ds(pl.multiple_of(half * width, width), width)

    def square_copy(source, target, sent, arrived, block, step):
        piece = pl.ds(step * slots, slots)
        return remote(
            source.at[block, piece],
            target.at[block, piece],
            sent.at[block, step],
            arrived.at[block, step],
            {"dp": partner(place, step)},
        )

    def out_copy(block, step):
        return square_copy(staged, rows.at[col], out_sent, out_arrived, block, step)

    def home_copy(block, step):
        return square_copy(staged, home, home_sent, home_arrived, block, step)

    def reply_copy(block, step):
        return square_copy(staged, reply_ref, reply_sent, reply_arrived, block, step)

    def keep_copy(block):
        own = pl.ds(0, slots)
        return pltpu.make_async_copy(
            staged.at[block, own], reply_ref.at[block, own], reply_arrived.at[block, 0]
        )

    def fwd_copy(block, half):
        here = rows.at[half, block]
        return remote(here, here, fwd_sent.at[block], fwd_arrived.at[block], sibling)

    def shared_copy(block):
        return remote(
            shared_to.at[block],
            shared_from.at[block],
            shared_sent.at[block],
            shared_arrived.at[block],
            sibling,
        )

    def half_copy(step):
        return remote(
            pair_to.at[lax.rem(step, 2)],
            pair_from.at[step],
            half_sent.at[step],
            half_arrived.at[step],
            sibling,
        )

    def other_copy(step):
        return remote(
            pair_to.at[lax.rem(step, 2)],
            pair_from.at[jnp.where(step == ROWS - 1, ROWS, step)],
            other_sent.at[step],
            other_arrived.at[step],
            sibling,
        )

    def stores(step):
        block = block_at(row, step)
        return [
            pltpu.make_async_copy(source, target, store_sem.at[index, step])
            for index, (source, target) in enumerate(
                [
                    (rows.at[:, block], rows_out.at[:, block]),
                    (gu.at[:, lax.rem(step, 2)], gu_out.at[:, block]),
                    (hidden.at[block], hidden_out.at[block]),
                ]
            )
        ]

    def relay(step):
        block = block_at(row, step)
        line.wait(block)
        line.pass_on(block)

    def take(step):
        block = block_at(row, step)

        @pl.when(jnp.logical_and(step > 0, jnp.logical_not(inner)))
        def _():
            relay(step)

        @pl.when(step > 0)
        def _():
            staged[block] = nn(pick_ref[block], gathered_ref[block]).astype(bf16)

        for shift in (3, 2, 1):
            out_copy(block, shift).start()
        rows[col, block, 0:slots] = staged[block, 0:slots]

    def shared_begin(step):
        block = block_at(row, step)

        @pl.when(step == 0)
        def _():
            loads[0].wait()
            loads[1].wait()
            loads[5].wait()

        for index, value in enumerate(
            (
                nt(gathered_ref[block], wide[0]),
                nt(gathered_ref[block], wide[1]),
                nt(cot_ref[block], narrow[...]),
            )
        ):
            shared_to[block, index] = value.astype(bf16)
        shared_copy(block).start()

    def forward(step):
        block = block_at(row, step)
        for shift in range(1, SQUARE):
            out_copy(block, shift).wait_recv()
        fwd_copy(block, col).start()

    def shared(step):
        block = block_at(row, step)
        shared_copy(block).wait_recv()
        gate, up, grad = [
            shared_to[block, index].astype(f32) + shared_from[block, index].astype(f32)
            for index in range(3)
        ]
        act, slope = silu_pair(gate)
        shared_out[block] = (act * up).astype(bf16)
        gate_grad = (grad * up * slope).astype(bf16)
        up_grad = (grad * act).astype(bf16)
        shared_gu[0, block] = gate_grad
        shared_gu[1, block] = up_grad
        part[block] = nn(gate_grad, wide[0]) + nn(up_grad, wide[1])

    def experts_of(step):
        block = block_at(row, step)

        @pl.when(step == 0)
        def _():
            for load in loads[2:5] + loads[6:]:
                load.wait()

        @pl.when(step > 1)
        def _():
            stores(step - 2)[1].wait()
            half_copy(step - 2).wait_send()

        fwd_copy(block, other).wait_recv()
        left, right = rows[0, block], rows[1, block]
        logits = nt(left, router_ref[:, 0:width]) + nt(right, router_ref[:, width:])
        logits = logits - jnp.max(logits, axis=1, keepdims=True)
        weight = jnp.exp(logits)
        probs = weight / jnp.sum(weight, axis=1, keepdims=True)
        own = (
            lax.broadcasted_iota(jnp.int32, (picked, experts), 1) == place * ROWS + row
        ).astype(f32)
        gates = jnp.sum(probs * own, axis=1, keepdims=True)
        raw = nt(cot_rows[0, block], fun[:, 0:width]) + nt(cot_rows[1, block], fun[:, width:])
        gate = nt(left, fan[0, :, 0:width]) + nt(right, fan[0, :, width:])
        up = nt(left, fan[1, :, 0:width]) + nt(right, fan[1, :, width:])
        act, slope = silu_pair(gate)
        value = act * up
        hidden[block] = (value * gates).astype(bf16)
        gate_sum = gates * jnp.sum(value * raw, axis=1, keepdims=True)
        logit_grad = (gate_sum * (own - probs)).astype(bf16)
        raw = raw * gates
        slot = lax.rem(step, 2)
        gu[0, slot] = (raw * up * slope).astype(bf16)
        gu[1, slot] = (raw * act).astype(bf16)

        def half_of(half):
            lines = half_lines(half)
            return (
                nn(gu[0, slot], fan[0, :, lines])
                + nn(gu[1, slot], fan[1, :, lines])
                + nn(logit_grad, router_ref[:, lines])
            )

        pair_to[slot] = half_of(other).astype(bf16)
        half_copy(step).start()
        pair_own[...] = half_of(col)
        router_rows[:, 0:width] += tn(logit_grad, left)
        router_rows[:, width:] += tn(logit_grad, right)
        for copy in stores(step):
            copy.start()

    def send_home(step):
        block = block_at(row, step)
        for shift in range(1, SQUARE):
            out_copy(block, shift).wait_send()
        half_copy(step).wait_recv()
        staged[block] = (pair_own[...] + pair_from[step].astype(f32)).astype(bf16)
        for shift in (3, 2, 1):
            home_copy(block, shift).start()
        home[block, 0:slots] = staged[block, 0:slots]

    def add_up(step):
        block = block_at(row, step)
        for shift in range(1, SQUARE):
            home_copy(block, shift).wait_recv()
        total = part[block] + nn(back_ref[block], home[block])
        part[block] = total
        premix_ref[...] += jnp.sum(
            (total * gathered_ref[block].astype(f32)).reshape(tokens // 8, 8, width), axis=0
        )
        sums.begin(block)

    def reply(step):
        block = block_at(row, step)
        slot = lax.rem(step, 2)

        @pl.when(step < 2)
        def _():
            half_copy(step + 2).wait_send()

        @pl.when(step > 1)
        def _():
            other_copy(step - 2).wait_send()

        pair_to[slot] = nn(hidden[block], fun[:, half_lines(other)]).astype(bf16)
        other_copy(step).start()

    def reply_home(step):
        block = block_at(row, step)
        own = nn(hidden[block], fun[:, half_lines(col)])
        for shift in range(1, SQUARE):
            home_copy(block, shift).wait_send()
        came = jnp.where(step == ROWS - 1, ROWS, step)
        other_copy(step).wait_recv()
        staged[block] = (own + pair_from[came].astype(f32)).astype(bf16)
        for shift in (3, 2, 1):
            reply_copy(block, shift).start()
        keep_copy(block).start()

    def turn(step, carried):
        @pl.when(jnp.logical_and(step == 2, inner))
        def _():
            relay(3)

        @pl.when(step < ROWS)
        def _():
            take(step)

        @pl.when(jnp.logical_and(step >= 1, step <= ROWS))
        def _():
            forward(step - 1)

        @pl.when(step < ROWS)
        def _():
            shared_begin(step)

        @pl.when(jnp.logical_and(step == 0, inner))
        def _():
            relay(1)
            relay(2)

        @pl.when(step >= 2)
        def _():
            shared(step - 2)
            send_home(step - 2)

        @pl.when(step == ROWS)
        def _():
            reply(0)

        @pl.when(step == ROWS + 1)
        def _():
            reply_home(0)

        @pl.when(step >= ROWS)
        def _():
            add_up(2 * step - 2 * ROWS)

        @pl.when(step == ROWS)
        def _():
            add_up(1)

        @pl.when(jnp.logical_and(step >= 1, step <= ROWS))
        def _():
            experts_of(step - 1)

        return carried

    lax.fori_loop(0, ROWS + 2, turn, 0)

    def replies(step, carried):
        @pl.when(step < ROWS)
        def _():
            reply(step)

        @pl.when(step > 1)
        def _():
            reply_home(step - 1)

        return carried

    late = [
        pltpu.make_async_copy(source, target, late_sem.at[i])
        for i, (source, target) in enumerate(
            [(shared_out, shared_far)]
        )
    ]
    for copy in late:
        copy.start()
    lax.fori_loop(1, ROWS + 1, replies, 0)
    add_up(ROWS - 1)

    def hand_on(turn, carried):
        sums.pass_on(block_at(row, jnp.where(turn == 2, 1, turn + 2)))
        return carried

    lax.fori_loop(0, ROWS - 1, hand_on, 0)

    seq = ROWS * tokens
    for index, (left, right) in enumerate(
        (
            (shared_out, cot_ref),
            (shared_gu.at[0], gathered_ref),
            (shared_gu.at[1], gathered_ref),
        )
    ):
        grad = tn(left[...].reshape(seq, share), right[...].reshape(seq, width))
        shared_grad[index] = grad.astype(bf16)
    x, y = lax.rem(place, 2), lax.div(place, 2)
    quarter = width // SQUARE
    grad_copies = []
    for index, (half, side, target) in enumerate(
        (
            (0, 1 - x, shared_x),
            (1, 1 - y, shared_y),
            (0, x, shared_kept.at[0]),
            (1, y, shared_kept.at[1]),
        )
    ):
        lanes = pl.ds(pl.multiple_of((2 * half + side) * quarter, 128), quarter)
        grad_copies.append(
            pltpu.make_async_copy(shared_grad.at[:, :, lanes], target, grad_sem.at[index])
        )
        grad_copies[index].start()
    sums.total(sum_ref)

    def ended(step, carried):
        block = block_at(row, step)
        shared_copy(block).wait_send()
        fwd_copy(block, col).wait_send()
        for shift in range(1, SQUARE):
            reply_copy(block, shift).wait_recv()
            reply_copy(block, shift).wait_send()
        keep_copy(block).wait()
        copies = stores(step)
        copies[0].wait()
        copies[2].wait()

        @pl.when(step >= ROWS - 2)
        def _():
            copies[1].wait()
            other_copy(step).wait_send()

        return carried

    lax.fori_loop(0, ROWS, ended, 0)
    for copy in grad_copies + late:
        copy.wait()
    sums.finish()
    line.finish()


def run_experts(
    normed, pick, back, cot_rows, cot_all, fan, fun, wide, narrow, router_all
):
    tokens, width = normed.shape
    picked = pick.shape[1]
    hid = fun.shape[0]
    share = narrow.shape[0]
    experts = router_all.shape[0]
    whole = pl.BlockSpec(memory_space=VMEM)
    far = pl.BlockSpec(memory_space=pl.ANY)

    def shape(*dims, dtype=bf16):
        return jax.ShapeDtypeStruct(dims, dtype)

    return pl.pallas_call(
        expert_kernel,
        name="experts",
        out_shape=(
            shape(tokens, width, dtype=f32),
            shape(COLS, ROWS, picked, width),
            shape(2, ROWS, picked, hid),
            shape(ROWS, picked, hid),
            shape(3, share, width // SQUARE),
            shape(3, share, width // SQUARE),
            shape(2, 3, share, width // SQUARE),
            shape(ROWS, tokens, share),
            shape(ROWS, picked, width),
            shape(8, width, dtype=f32),
            shape(experts, COLS * width, dtype=f32),
        ),
        in_specs=[whole] * 3 + [far] * 7,
        out_specs=(whole,) + (far,) * 8 + (whole,) * 2,
        scratch_shapes=[
            VMEM((ROWS, tokens, width), bf16),
            VMEM((ROWS, tokens, share), bf16),
            VMEM(back.shape, bf16),
            VMEM(cot_all.shape, bf16),
            VMEM(fan.shape, bf16),
            VMEM(fun.shape, bf16),
            VMEM(wide.shape, bf16),
            VMEM(narrow.shape, bf16),
            VMEM(cot_rows.shape, bf16),
            VMEM((COLS, ROWS, picked, width), bf16),
            VMEM((ROWS, picked, width), bf16),
            VMEM((2, 2, picked, hid), bf16),
            VMEM((ROWS, picked, hid), bf16),
            VMEM((picked, width), f32),
            VMEM((2, picked, width), bf16),
            VMEM((ROWS + 1, picked, width), bf16),
            VMEM((ROWS, picked, width), bf16),
            VMEM((ROWS, 3, tokens, share), bf16),
            VMEM((ROWS, 3, tokens, share), bf16),
            VMEM((ROWS, tokens, width), f32),
            VMEM((ROWS, tokens, width), bf16),
            VMEM((2, ROWS, tokens, width), bf16),
            VMEM((2, ROWS, tokens, share), bf16),
            VMEM((3, share, width), bf16),
            DMA((7,)),
            DMA((3, ROWS)),
            *line_sems(),
            *square_sems(),
            *pair_sems(),
            *pair_sems(),
            *pair_sems(),
            *square_sems(),
            *sum_sems(),
            *pair_sems(),
            *square_sems(),
            DMA((4,)),
            DMA((1,)),
        ],
        compiler_params=pltpu.CompilerParams(
            collective_id=2, has_side_effects=True, vmem_limit_bytes=62 * MIB
        ),
        cost_estimate=pl.CostEstimate(
            flops=60 * 1024**3, bytes_accessed=64 * MIB, transcendentals=0
        ),
    )(normed, pick, router_all, back, cot_all, cot_rows, fan, fun, wide, narrow)


class SquareSum:
    def __init__(self, place, part, first, second, middle, result, sent, arrived):
        self.x, self.y = lax.rem(place, 2), lax.div(place, 2)
        self.to_x, self.to_y = {"dp": partner(place, 1)}, {"dp": partner(place, 2)}
        self.part, self.first, self.second = part, first, second
        self.middle, self.result = middle, result
        self.sent, self.arrived = sent, arrived

    def copies(self, phase):
        x, y = self.x, self.y
        if phase == 0:
            plan = (
                (self.part.at[pl.ds(2 - 2 * x, 2)], self.first.at[0:2], self.to_x),
                (self.part.at[pl.ds(6 - 2 * y, 2)], self.first.at[2:4], self.to_y),
            )
        elif phase == 1:
            plan = (
                (self.middle.at[0], self.second.at[0], self.to_y),
                (self.middle.at[1], self.second.at[1], self.to_x),
            )
        elif phase == 2:
            one, two = self.result.at[2 * x + y], self.result.at[4 + 2 * y + x]
            plan = ((one, one, self.to_y), (two, two, self.to_x))
        else:
            one, two = self.result.at[pl.ds(2 * x, 2)], self.result.at[pl.ds(4 + 2 * y, 2)]
            plan = ((one, one, self.to_x), (two, two, self.to_y))
        return [
            remote(source, target, self.sent.at[2 * phase + i], self.arrived.at[2 * phase + i], to)
            for i, (source, target, to) in enumerate(plan)
        ]

    def start(self, phase):
        for copy in self.copies(phase):
            copy.start()

    def arrive(self, phase):
        for copy in self.copies(phase):
            copy.wait_recv()

    def run(self, phase):
        x, y = self.x, self.y
        if phase > 0:
            self.arrive(phase - 1)
        if phase == 1:
            for slot, piece, came in (
                (0, 2 * x + 1 - y, 1 - y),
                (1, 4 + 2 * y + 1 - x, 3 - x),
            ):
                self.middle[slot] = (
                    self.part[piece].astype(f32) + self.first[came].astype(f32)
                ).astype(bf16)
        if phase == 2:
            for slot, piece, came in ((0, 2 * x + y, y), (1, 4 + 2 * y + x, 2 + x)):
                self.result[piece] = (
                    self.part[piece].astype(f32)
                    + self.first[came].astype(f32)
                    + self.second[slot].astype(f32)
                ).astype(bf16)
        if phase < 4:
            self.start(phase)

    def finish(self):
        for phase in range(4):
            for copy in self.copies(phase):
                copy.wait_send()


def square_scratch(dims):
    count, rows, lanes = dims
    return [
        VMEM((count, 8, rows, lanes), bf16),
        VMEM((count, 4, rows, lanes), bf16),
        VMEM((count, 2, rows, lanes), bf16),
        VMEM((count, 2, rows, lanes), bf16),
        VMEM((count, 8, rows, lanes), bf16),
        DMA((count, 8)),
        DMA((count, 8)),
    ]


def write_kernel(count, plan, *refs):
    sources, targets = refs[:count], refs[count : count + len(plan)]
    rest = refs[count + len(plan) :]
    held, wide = rest[:count], rest[count : count + len(plan)]
    load_sem, store_sem = rest[count + len(plan) :]
    loads = [
        pltpu.make_async_copy(sources[i], held[i], load_sem.at[i]) for i in range(count)
    ]
    stores = [
        pltpu.make_async_copy(wide[i], targets[i], store_sem.at[i]) for i in range(len(plan))
    ]
    for load in loads:
        load.start()
    waited = set()
    for i, (source, where) in enumerate(plan):
        if source not in waited:
            loads[source].wait()
            waited.add(source)
        wide[i][...] = held[source][where].astype(wide[i].dtype)
        stores[i].start()
    for store in stores:
        store.wait()


def write_out(arrays, plan):
    far = pl.BlockSpec(memory_space=pl.ANY)
    shapes = [jax.ShapeDtypeStruct(shape, dtype) for _, _, shape, dtype in plan]
    return pl.pallas_call(
        functools.partial(
            write_kernel, len(arrays), [(source, where) for source, where, _, _ in plan]
        ),
        name="write_out",
        out_shape=shapes,
        in_specs=[far] * len(arrays),
        out_specs=[far] * len(plan),
        scratch_shapes=[
            *[VMEM(array.shape, array.dtype) for array in arrays],
            *[VMEM(shape.shape, shape.dtype) for shape in shapes],
            DMA((len(arrays),)),
            DMA((len(plan),)),
        ],
        compiler_params=pltpu.CompilerParams(vmem_limit_bytes=62 * MIB),
        cost_estimate=pl.CostEstimate(flops=0, bytes_accessed=24 * MIB, transcendentals=0),
    )(*arrays)


def product_kernel(left_ref, right_ref, out_ref, turned):
    wide = 256

    @pl.when(pl.program_id(1) == 0)
    def _():
        turned[...] = left_ref[0].T

    def one(index, carried):
        lanes = pl.ds(pl.multiple_of(index * wide, 128), wide)
        out_ref[0, :, lanes] = nn(turned[...], right_ref[0, :, lanes])
        return carried

    lax.fori_loop(0, right_ref.shape[2] // wide, one, 0)


def slot_products(left, right):
    kinds, slots, tall = left.shape
    halves, _, wide = right.shape
    return pl.pallas_call(
        product_kernel,
        name="slot_products",
        grid=(kinds, halves),
        out_shape=jax.ShapeDtypeStruct((kinds, tall, halves * wide), f32),
        in_specs=[
            pl.BlockSpec((1, slots, tall), lambda kind, half: (kind, 0, 0)),
            pl.BlockSpec((1, slots, wide), lambda kind, half: (half, 0, 0)),
        ],
        out_specs=pl.BlockSpec((1, tall, wide), lambda kind, half: (kind, 0, half)),
        scratch_shapes=[VMEM((tall, slots), bf16)],
        compiler_params=pltpu.CompilerParams(vmem_limit_bytes=40 * MIB),
        cost_estimate=pl.CostEstimate(
            flops=2 * kinds * halves * slots * tall * wide,
            bytes_accessed=4 * kinds * halves * tall * wide,
            transcendentals=0,
        ),
    )(left, right)


def local_square(
    activations,
    cotangent,
    routing,
    segments,
    scaling,
    queries,
    compress,
    rescale,
    expand,
    combine,
    premix,
    router,
    widening,
    narrowing,
    fanout,
    funnel,
):
    dp_count = lax.axis_size("dp")
    row_count = lax.axis_size("row")
    col_count = lax.axis_size("col")
    col_index = lax.axis_index("col")
    local_rows, col_width = activations.shape
    seq_length = local_rows * row_count
    expert_total = router.shape[1]
    capacity = local_rows * TOP * 4 // (3 * expert_total)
    slot_total = capacity * row_count * dp_count
    tables = turning_tables(seq_length)
    (
        one,
        query,
        key,
        value,
        probs,
        latent,
        latent_normed,
        attended,
        compress_all,
        cot_blocks,
        pick,
        back,
        cot_rows,
        residual,
        normed_two,
        scale_one,
        scale_two,
        router_all,
    ) = run_attention(
        activations,
        scaling,
        queries,
        compress,
        rescale,
        expand,
        combine,
        premix,
        segments,
        cotangent,
        routing,
        router,
        tables,
        capacity,
    )
    (
        normed_grad,
        expert_rows,
        expert_gu_grad,
        expert_hidden,
        shared_x,
        shared_y,
        shared_kept,
        hidden_blocks,
        reply_blocks,
        premix_rows,
        router_rows,
    ) = run_experts(
        normed_two,
        pick,
        back,
        cot_rows,
        cot_blocks,
        fanout[0].transpose(0, 2, 1),
        funnel[0],
        widening.transpose(0, 2, 1),
        narrowing,
        router_all,
    )
    slot_rows = expert_rows.reshape(col_count, slot_total, col_width)
    reply_grad_rows = cot_rows.reshape(col_count, slot_total, col_width)
    slot_hidden = expert_hidden.reshape(slot_total, -1)
    slot_gu_grad = expert_gu_grad.reshape(2, slot_total, -1)
    got_x = lax.ppermute(shared_x, "dp", [(i, i ^ 1) for i in range(SQUARE)])
    got_y = lax.ppermute(shared_y, "dp", [(i, i ^ 2) for i in range(SQUARE)])
    fanout_grad = slot_products(slot_gu_grad, slot_rows)
    funnel_grad = slot_products(slot_hidden[None], reply_grad_rows)
    normed_grad, fanout_grad, funnel_grad = lax.optimization_barrier(
        (normed_grad, fanout_grad, funnel_grad)
    )
    (
        input_grad,
        layer_output,
        small,
        shared_sum,
        queries_sum,
        combine_sum,
        expand_sum,
        compress_sum,
    ) = run_attention_back(
        normed_grad,
        residual,
        scale_two,
        premix,
        cotangent,
        activations,
        scale_one,
        scaling,
        one,
        query,
        key,
        value,
        probs,
        latent,
        rescale,
        tables,
        compress_all,
        queries,
        expand,
        combine,
        (shared_kept, got_x, got_y),
        (
            attended,
            latent_normed,
            narrowing,
            reply_blocks,
            back,
            hidden_blocks,
            premix_rows,
            router_rows,
        ),
    )
    everything = slice(None)
    share = narrowing.shape[0]
    (
        widening_grad,
        narrowing_grad,
        queries_grad,
        combine_grad,
        expand_grad,
        compress_grad,
        input_grad,
        layer_output,
        router_grad,
        premix_grad,
        scaling_grad,
        rescale_grad,
    ) = write_out(
        (
            shared_sum,
            queries_sum.reshape(queries.shape),
            combine_sum.reshape(combine.shape),
            expand_sum.reshape(expand.shape),
            compress_sum,
            input_grad,
            layer_output,
            small,
        ),
        (
            (0, slice(1, 3), (2, share, col_width), f32),
            (0, 0, (share, col_width), f32),
            (1, everything, queries.shape, f32),
            (2, everything, combine.shape, f32),
            (3, everything, expand.shape, f32),
            (4, everything, compress_sum.shape, f32),
            (5, everything, input_grad.shape, f32),
            (6, everything, layer_output.shape, bf16),
            (7, slice(0, expert_total), (expert_total, col_width), f32),
            (7, slice(expert_total, expert_total + 1), (1, col_width), f32),
            (7, slice(expert_total + 1, expert_total + 2), (1, col_width), f32),
            (7, (slice(expert_total + 2, expert_total + 3), slice(0, RANK)), (1, RANK), f32),
        ),
    )
    return (
        layer_output,
        input_grad,
        scaling_grad.reshape(col_width),
        queries_grad,
        compress_grad.T,
        rescale_grad.reshape(RANK),
        expand_grad,
        combine_grad,
        premix_grad.reshape(col_width),
        router_grad.T,
        widening_grad.transpose(0, 2, 1),
        narrowing_grad,
        fanout_grad.transpose(0, 2, 1)[None],
        funnel_grad,
    )


def local(
    activations,
    cotangent,
    routing,
    segments,
    scaling,
    queries,
    compress,
    rescale,
    expand,
    combine,
    premix,
    router,
    widening,
    narrowing,
    fanout,
    funnel,
):
    dp_count = lax.axis_size("dp")
    row_count = lax.axis_size("row")
    col_count = lax.axis_size("col")
    dp_index = lax.axis_index("dp")
    row_index = lax.axis_index("row")
    col_index = lax.axis_index("col")
    local_rows = activations.shape[0]
    col_width = activations.shape[1]
    seq_length = local_rows * row_count
    half_length = seq_length // col_count
    head_width = NOPE + ROPE
    pair_width = NOPE + HEADV
    local_heads = queries.shape[1] // head_width
    slice_width = compress.shape[1]
    expert_total = router.shape[1]
    capacity = local_rows * TOP * 4 // (3 * expert_total)
    slots = capacity * row_count
    slot_total = slots * dp_count
    block_rows = min(512, half_length)
    block_count = half_length // block_rows
    score_scale = head_width ** (-0.5)

    inputs = activations.astype(f32)
    scale_one = norm_scale(inputs)
    normed_one = (inputs * scale_one[:, None] * scaling).astype(bf16)
    gathered_one = row_gather(normed_one)
    compress_all = lax.all_gather(compress, "row", axis=1, tiled=True)

    routing_all = row_gather(routing)
    cotangent_all = row_gather(after(cotangent, gathered_one))
    offsets = jnp.arange(dp_count, dtype=jnp.int32)
    my_experts = ((dp_index + offsets) % dp_count) * row_count + row_index
    goes = jnp.any(routing_all[None, :, :] == my_experts[:, None, None], axis=2)
    token_range = jnp.arange(seq_length, dtype=jnp.int32)
    earlier = (token_range[:, None] < token_range[None, :]).astype(bf16)
    rank = dot(goes.astype(bf16), earlier).astype(jnp.int32)
    slot_range = jnp.arange(slots, dtype=jnp.int32)
    pick = (
        ((rank[:, None, :] == slot_range[None, :, None]) & goes[:, None, :])
        .astype(bf16)
        .reshape(slot_total, seq_length)
    )

    def dispatch(tokens):
        rows = dot(pick, tokens).astype(bf16).reshape(dp_count, slots, col_width)
        arrived = send_out([rows[k] for k in range(dp_count)])
        return col_gather(jnp.concatenate(arrived, axis=0), axis=1)

    def bring_back(part):
        summed = col_scatter(part.astype(bf16), axis=1).reshape(dp_count, slots, col_width)
        arrived = send_back([summed[k] for k in range(dp_count)])
        return dot_tn(pick, jnp.concatenate(arrived, axis=0))

    query_part = dot(gathered_one, queries)
    latent_part = dot(gathered_one, compress_all)
    query_raw, latent_raw = col_scatter((query_part, latent_part))
    latent_plain = latent_raw[:, :RANK]
    latent_scale = lax.rsqrt(jnp.mean(latent_plain * latent_plain, axis=1) + epsilon)
    latent_normed = (latent_plain * latent_scale[:, None] * rescale).astype(bf16)
    expanded = dot(latent_normed, expand).reshape(half_length, local_heads, pair_width)
    positions = col_index * half_length + jnp.arange(half_length, dtype=jnp.int32)
    cosine, sine_table = rotation(positions, ROPE)
    key_shared = rotate(latent_raw[:, RANK:], cosine, sine_table, 1.0)
    query_heads = query_raw.reshape(half_length, local_heads, head_width)
    query_local = jnp.concatenate(
        [
            query_heads[..., :NOPE],
            rotate(query_heads[..., NOPE:], cosine[:, None, :], sine_table[:, None, :], 1.0),
        ],
        axis=2,
    ).astype(bf16)
    key_local = jnp.concatenate(
        [
            expanded[..., :NOPE],
            jnp.broadcast_to(key_shared[:, None, :], (half_length, local_heads, ROPE)),
        ],
        axis=2,
    ).astype(bf16)
    value_local = expanded[..., NOPE:].astype(bf16)
    key_flat, value_flat = (
        col_gather(key_local.reshape(half_length, local_heads * head_width)),
        col_gather(value_local.reshape(half_length, local_heads * HEADV)),
    )
    key_heads = key_flat.reshape(seq_length, local_heads, head_width)
    value_heads = value_flat.reshape(seq_length, local_heads, HEADV)
    own_segments = lax.dynamic_slice_in_dim(
        segments, col_index * half_length, half_length, 0
    ).reshape(block_count, block_rows)
    query_blocks = query_local.reshape(block_count, block_rows, local_heads, head_width)

    def attend_block(inputs_block):
        query_block, segment_block = inputs_block
        scores = (
            jnp.einsum("qhd,khd->hqk", query_block, key_heads, preferred_element_type=f32)
            * score_scale
        )
        visible = segments[None, None, :] <= segment_block[None, :, None]
        scores = jnp.where(visible, scores, masked_score)
        largest = jnp.max(scores, axis=2, keepdims=True)
        weight = jnp.exp(scores - largest)
        totals = jnp.sum(weight, axis=2, keepdims=True)
        probability = (weight / totals).astype(bf16)
        result = jnp.einsum("hqk,khd->qhd", probability, value_heads, preferred_element_type=f32)
        return (result.astype(bf16), (largest + jnp.log(totals))[..., 0])

    attended_blocks, log_totals = lax.map(attend_block, (query_blocks, own_segments))
    attended = attended_blocks.reshape(half_length, local_heads * HEADV)
    attended_all = col_gather(attended)
    branch = row_scatter(dot(attended_all, combine))

    reply_grad_rows = dispatch(cotangent_all)
    inner_weight = fanout[0]
    outer_weight = funnel[0]
    hidden_raw = dot_nt(reply_grad_rows, outer_weight)
    shared_hidden_grad = col_scatter(dot_nt(cotangent_all, narrowing))

    residual = inputs + branch
    scale_two = norm_scale(residual)
    normed_two = (residual * scale_two[:, None] * premix).astype(bf16)
    gathered_two = row_gather(normed_two)

    expert_rows = dispatch(gathered_two)
    expert_range = jnp.arange(expert_total, dtype=jnp.int32)
    router_all = lax.all_gather(router, "col", axis=0, tiled=True)
    own_expert = dp_index * row_count + row_index
    slot_probs = jax.nn.softmax(dot(expert_rows, router_all), axis=1)
    slot_gates = jnp.sum(jnp.where(expert_range == own_expert, slot_probs, 0.0), axis=1)
    gate_up = jnp.einsum("rd,gdf->grf", expert_rows, inner_weight, preferred_element_type=f32)
    gate_input, up_input = gate_up[0], gate_up[1]
    hidden = jax.nn.silu(gate_input) * up_input
    expert_hidden = hidden.astype(bf16)
    slot_gate_grad = col_totals(jnp.sum(hidden * hidden_raw, axis=1))
    hidden_grad = hidden_raw * slot_gates[:, None]
    expert_gu_grad = jnp.stack(
        [hidden_grad * up_input * silu_slope(gate_input), hidden_grad * jax.nn.silu(gate_input)]
    ).astype(bf16)
    input_part = jnp.einsum(
        "grf,gdf->rd", expert_gu_grad, inner_weight, preferred_element_type=f32
    )
    routed_grad = bring_back(input_part)
    gate_grad_parts = send_back(
        [slot_gate_grad.reshape(dp_count, slots)[k] for k in range(dp_count)]
    )

    logits = col_totals(dot(gathered_two, router))
    router_probs = jax.nn.softmax(logits, axis=1)
    gate_grad = jnp.sum(
        pick.reshape(dp_count, slots, seq_length).astype(f32)
        * jnp.stack(gate_grad_parts)[:, :, None],
        axis=1,
    )
    mine = (my_experts[:, None] == expert_range[None, :]).astype(f32)
    probs_grad = jnp.sum(gate_grad[:, :, None] * mine[:, None, :], axis=0)
    logit_grad = router_probs * (
        probs_grad - jnp.sum(router_probs * probs_grad, axis=1, keepdims=True)
    )
    router_part = dot_tn(gathered_two, logit_grad)

    shared_gate_up = col_scatter(
        jnp.einsum("td,gdf->tgf", gathered_two, widening, preferred_element_type=f32)
    )
    shared_hidden = (jax.nn.silu(shared_gate_up[:, 0]) * shared_gate_up[:, 1]).astype(bf16)
    hidden_all = col_gather(shared_hidden)
    narrowing_grad = dot_tn(hidden_all, cotangent_all)
    shared_gu_grad = jnp.stack(
        [
            shared_hidden_grad * shared_gate_up[:, 1] * silu_slope(shared_gate_up[:, 0]),
            shared_hidden_grad * jax.nn.silu(shared_gate_up[:, 0]),
        ],
        axis=1,
    ).astype(bf16)
    gu_grad_all = col_gather(shared_gu_grad)
    widening_grad = jnp.einsum(
        "td,tgf->gdf", gathered_two, gu_grad_all, preferred_element_type=f32
    )
    shared_input_part = jnp.einsum(
        "tgf,gdf->td", gu_grad_all, widening, preferred_element_type=f32
    )
    shared_sums = lax.psum((narrowing_grad.astype(bf16), widening_grad.astype(bf16)), "dp")

    grad_part = routed_grad + shared_input_part + dot_nt(logit_grad, router)
    premix_part = jnp.sum(grad_part * gathered_two.astype(f32), axis=0) / premix
    normed_grad = row_scatter(grad_part)

    upstream = cotangent.astype(f32)
    residual_grad = upstream + norm_back(residual, scale_two, premix, normed_grad)
    branch_all = row_gather(residual_grad.astype(bf16))

    funnel_grad = dot_tn((hidden * slot_gates[:, None]).astype(bf16), reply_grad_rows)[None]
    fanout_grad = jnp.einsum(
        "rd,grf->gdf", expert_rows, expert_gu_grad, preferred_element_type=f32
    )[None]
    reply_part = dot(expert_hidden, outer_weight) * slot_gates[:, None]
    routed = bring_back(reply_part)
    shared_out = row_scatter(routed + dot(hidden_all, narrowing))
    layer_output = (residual + shared_out).astype(bf16)

    combine_grad = dot_tn(attended_all, branch_all)
    combine_sum = lax.psum(after(combine_grad.astype(bf16), *shared_sums), "dp")
    attended_grad = col_scatter(dot_nt(branch_all, combine))
    attended_grad_blocks = attended_grad.astype(bf16).reshape(
        block_count, block_rows, local_heads, HEADV
    )

    def attend_back(carried, inputs_block):
        key_sum, value_sum = carried
        query_block, grad_block, log_block, segment_block = inputs_block
        scores = (
            jnp.einsum("qhd,khd->hqk", query_block, key_heads, preferred_element_type=f32)
            * score_scale
        )
        visible = segments[None, None, :] <= segment_block[None, :, None]
        probability = jnp.where(visible, jnp.exp(scores - log_block[..., None]), 0.0)
        weight_grad = jnp.einsum(
            "qhd,khd->hqk", grad_block, value_heads, preferred_element_type=f32
        )
        inner_sum = jnp.sum(probability * weight_grad, axis=2, keepdims=True)
        score_grad = (probability * (weight_grad - inner_sum)).astype(bf16)
        query_grad_block = (
            jnp.einsum("hqk,khd->qhd", score_grad, key_heads, preferred_element_type=f32)
            * score_scale
        )
        key_sum = (
            key_sum
            + jnp.einsum("hqk,qhd->khd", score_grad, query_block, preferred_element_type=f32)
            * score_scale
        )
        value_sum = value_sum + jnp.einsum(
            "hqk,qhd->khd", probability.astype(bf16), grad_block, preferred_element_type=f32
        )
        return ((key_sum, value_sum), query_grad_block)

    key_start = jnp.zeros((seq_length, local_heads, head_width), f32)
    value_start = jnp.zeros((seq_length, local_heads, HEADV), f32)
    (key_grad_all, value_grad_all), query_grad_blocks = lax.scan(
        attend_back,
        (key_start, value_start),
        (query_blocks, attended_grad_blocks, log_totals, own_segments),
    )
    key_grad, value_grad = col_scatter(
        (
            key_grad_all.reshape(seq_length, local_heads * head_width),
            value_grad_all.reshape(seq_length, local_heads * HEADV),
        )
    )
    key_grad = key_grad.reshape(half_length, local_heads, head_width)
    value_grad = value_grad.reshape(half_length, local_heads, HEADV)
    query_grad = query_grad_blocks.reshape(half_length, local_heads, head_width)
    query_raw_grad = (
        jnp.concatenate(
            [
                query_grad[..., :NOPE],
                rotate(query_grad[..., NOPE:], cosine[:, None, :], sine_table[:, None, :], -1.0),
            ],
            axis=2,
        )
        .astype(bf16)
        .reshape(half_length, local_heads * head_width)
    )
    expanded_grad = (
        jnp.concatenate([key_grad[..., :NOPE], value_grad], axis=2)
        .astype(bf16)
        .reshape(half_length, local_heads * pair_width)
    )
    shared_rope_grad = rotate(jnp.sum(key_grad[..., NOPE:], axis=1), cosine, sine_table, -1.0)

    latent_grad = dot_nt(expanded_grad, expand)
    latent_weighted = latent_grad * rescale
    latent_inner = jnp.mean(latent_weighted * latent_plain, axis=1)
    rescale_part = jnp.sum(latent_grad * latent_plain * latent_scale[:, None], axis=0)
    plain_grad = (
        latent_weighted * latent_scale[:, None]
        - latent_plain * (latent_scale**3 * latent_inner)[:, None]
    )
    latent_raw_grad = jnp.concatenate([plain_grad, shared_rope_grad], axis=1).astype(bf16)
    query_grad_all = col_gather(query_raw_grad)
    latent_grad_all = col_gather(latent_raw_grad)
    first_part = dot_nt(query_grad_all, queries) + dot_nt(latent_grad_all, compress_all)
    first_grad = row_scatter(first_part)
    input_grad = residual_grad + norm_back(inputs, scale_one, scaling, first_grad)

    queries_part = dot_tn(gathered_one, query_grad_all)
    own_latent_grad = lax.psum_scatter(
        latent_raw_grad, "row", scatter_dimension=1, tiled=True
    )
    compress_part = dot_tn(gathered_one, col_gather(own_latent_grad))
    half_rank = RANK // col_count
    latent_normed_all = col_gather(latent_normed)
    expanded_grad_all = col_gather(expanded_grad)
    expand_half = dot_tn(
        lax.dynamic_slice_in_dim(latent_normed_all, col_index * half_rank, half_rank, 1),
        expanded_grad_all,
    )
    scaling_part = jnp.sum(first_part * gathered_one.astype(f32), axis=0) / scaling
    queries_sum, expand_sum, compress_sum = lax.psum(
        (
            after(queries_part.astype(bf16), combine_sum),
            expand_half.astype(bf16),
            compress_part.astype(bf16),
        ),
        "dp",
    )
    premix_sum, router_sum = lax.psum((premix_part, router_part), ("dp", "row"))
    rescale_sum = lax.psum(rescale_part, ("dp", "row", "col"))
    scaling_sum = lax.psum(scaling_part, ("dp", "row"))
    return (
        layer_output,
        input_grad,
        scaling_sum,
        queries_sum.astype(f32),
        compress_sum.astype(f32),
        rescale_sum,
        col_gather(expand_sum).astype(f32),
        combine_sum.astype(f32),
        premix_sum,
        router_sum,
        shared_sums[1].astype(f32),
        shared_sums[0].astype(f32),
        fanout_grad,
        funnel_grad,
    )


def solution(mesh):
    placed = (
        P(("dp", "row"), "col"),
        P(("dp", "row"), "col"),
        P(("dp", "row"), None),
        P("dp"),
        P("col"),
        P("col", "row"),
        P("col", "row"),
        P(),
        P(None, "row"),
        P("row", "col"),
        P("col"),
        P("col", None),
        P(None, "col", "row"),
        P("row", "col"),
        P(("dp", "row"), None, None, "col"),
        P(("dp", "row"), "col", None),
    )
    squared = mesh.shape["dp"] == SQUARE and mesh.shape["row"] == ROWS
    return jax.shard_map(
        local_square if squared else local,
        mesh=mesh,
        in_specs=placed,
        out_specs=(
            P(("dp", "row"), "col"),
            P(("dp", "row"), "col"),
            P("col"),
            P("col", "row"),
            P("col", "row"),
            P(),
            P(None, "row"),
            P("row", "col"),
            P("col"),
            P("col", None),
            P(None, "col", "row"),
            P("row", "col"),
            P(("dp", "row"), None, None, "col"),
            P(("dp", "row"), "col", None),
        ),
        check_vma=False,
    )
```

```python
import functools

import jax
import jax.numpy as jnp
import numpy as np
from jax import lax
from jax.experimental import pallas as pl
from jax.experimental.pallas import tpu as pltpu
from jax.sharding import PartitionSpec as P

D = 2048
NOPE = 128
ROPE = 64
HEADV = 128
RANK = 512
TOP = 6


epsilon = 1e-06
masked_score = -1e30
f32 = jnp.float32
bf16 = jnp.bfloat16


def after(value, *earlier):
    return lax.optimization_barrier((value,) + earlier)[0]


def silu_slope(values):
    sigmoid = jax.nn.sigmoid(values)
    return sigmoid * (1.0 + values * (1.0 - sigmoid))


def rotation(positions, rope_width):
    half_width = rope_width // 2
    frequency = 10000.0 ** (-jnp.arange(half_width, dtype=jnp.float32) * 2.0 / rope_width)
    angles = positions.astype(jnp.float32)[:, None] * frequency[None, :]
    return (jnp.cos(angles), jnp.sin(angles))


def rotate(values, cosine, sine_table, direction):
    half_width = values.shape[-1] // 2
    first_half = values[..., :half_width]
    second_half = values[..., half_width:]
    return jnp.concatenate(
        [
            first_half * cosine - direction * second_half * sine_table,
            second_half * cosine + direction * first_half * sine_table,
        ],
        axis=-1,
    )


def dot(left, right):
    return jnp.dot(left, right, preferred_element_type=f32)


def dot_tn(left, right):
    return lax.dot_general(left, right, (((0,), (0,)), ((), ())), preferred_element_type=f32)


def dot_nt(left, right):
    return lax.dot_general(left, right, (((1,), (1,)), ((), ())), preferred_element_type=f32)


def col_totals(values):
    return lax.psum(values, "col")


def row_gather(values):
    return lax.all_gather(values, "row", axis=0, tiled=True)


def col_gather(values, axis=0):
    return lax.all_gather(values, "col", axis=axis, tiled=True)


def col_scatter(values, axis=0):
    return lax.psum_scatter(values, "col", scatter_dimension=axis, tiled=True)


def row_scatter(values):
    return lax.psum_scatter(
        values.astype(bf16), "row", scatter_dimension=0, tiled=True
    ).astype(f32)


def send_out(parts):
    count = len(parts)
    return [parts[0]] + [
        lax.ppermute(parts[k], "dp", [(i, (i + k) % count) for i in range(count)])
        for k in range(1, count)
    ]


def send_back(parts):
    count = len(parts)
    return [parts[0]] + [
        lax.ppermute(parts[k], "dp", [(i, (i - k) % count) for i in range(count)])
        for k in range(1, count)
    ]


def norm_scale(values):
    square_sum = col_totals(jnp.sum(values * values, axis=1))
    return lax.rsqrt(square_sum / D + epsilon)


def norm_back(values, row_scale, gain_vector, upstream):
    weighted = upstream * gain_vector
    inner_mean = col_totals(jnp.sum(weighted * values, axis=1)) / D
    return weighted * row_scale[:, None] - values * (row_scale**3 * inner_mean)[:, None]


MESH = pl.DeviceIdType.MESH
VMEM = pltpu.VMEM
DMA = pltpu.SemaphoreType.DMA
MIB = 1024 * 1024
ROWS = 4
SQUARE = 4
COLS = 2
SPLIT = 2


def nn(left, right):
    return lax.dot_general(left, right, (((1,), (0,)), ((), ())), preferred_element_type=f32)


def tn(left, right):
    return lax.dot_general(left, right, (((0,), (0,)), ((), ())), preferred_element_type=f32)


def nt(left, right):
    return lax.dot_general(left, right, (((1,), (1,)), ((), ())), preferred_element_type=f32)


def block_at(row, turn):
    swapped = jnp.where(turn < 2, 1 - turn, turn)
    inner = jnp.logical_or(row == 1, row == 2)
    near = jnp.where(inner, swapped, turn)
    return jnp.where(row < 2, near, ROWS - 1 - near)


def partner(place, step):
    across, along = lax.rem(place, 2), lax.div(place, 2)
    across = lax.rem(across + step % 2, 2)
    along = lax.rem(along + step // 2, 2)
    return along * 2 + across


def beside(row, way):
    return lax.rem(row + ROWS + 1 - 2 * way, ROWS)


def remote(source, target, sent, arrived, where):
    return pltpu.make_async_remote_copy(
        src_ref=source,
        dst_ref=target,
        send_sem=sent,
        recv_sem=arrived,
        device_id=where,
        device_id_type=MESH,
    )


def greet(row, place, col, line=False, square=True):
    barrier = pltpu.get_barrier_semaphore()
    met = 1
    if line:
        for step in range(1, ROWS):
            pl.semaphore_signal(
                barrier,
                inc=1,
                device_id={"row": lax.rem(row + step, ROWS)},
                device_id_type=MESH,
            )
        met = met + ROWS - 1
    else:

        @pl.when(row > 0)
        def _():
            pl.semaphore_signal(barrier, inc=1, device_id={"row": row - 1}, device_id_type=MESH)

        @pl.when(row < ROWS - 1)
        def _():
            pl.semaphore_signal(barrier, inc=1, device_id={"row": row + 1}, device_id_type=MESH)

        met = met + (row > 0).astype(jnp.int32) + (row < ROWS - 1).astype(jnp.int32)
    if square:
        for step in range(1, SQUARE):
            pl.semaphore_signal(
                barrier, inc=1, device_id={"dp": partner(place, step)}, device_id_type=MESH
            )
        met = met + SQUARE - 1
    pl.semaphore_signal(barrier, inc=1, device_id={"col": 1 - col}, device_id_type=MESH)
    return met


def meet(met):
    pl.semaphore_wait(pltpu.get_barrier_semaphore(), met)


class Line:
    def __init__(self, row, buffer, sent, arrived):
        self.row, self.buffer, self.sent, self.arrived = row, buffer, sent, arrived

    def copy(self, block, way):
        here = self.buffer.at[block]
        to = {"row": beside(self.row, way)}
        return remote(here, here, self.sent.at[block, way], self.arrived.at[block], to)

    def each(self, block, act):
        @pl.when(jnp.logical_and(block <= self.row, self.row < ROWS - 1))
        def _():
            act(self.copy(block, 0))

        @pl.when(jnp.logical_and(block >= self.row, self.row > 0))
        def _():
            act(self.copy(block, 1))

    def wait(self, block):
        self.copy(block, 0).wait_recv()

    def pass_on(self, block):
        self.each(block, lambda copy: copy.start())

    def finish(self):
        def one(block, carried):
            self.each(block, lambda copy: copy.wait_send())
            return carried

        lax.fori_loop(0, ROWS, one, 0)


class SquareRest:
    def __init__(self, place, which, kept, got, middle, second, result, sent, arrived):
        self.x, self.y, self.which = lax.rem(place, 2), lax.div(place, 2), which
        self.to_x, self.to_y = {"dp": partner(place, 1)}, {"dp": partner(place, 2)}
        self.kept, self.got = kept, got
        self.middle, self.second, self.result = middle, second, result
        self.sent, self.arrived = sent.at[which], arrived.at[which]

    def copies(self, phase):
        x, y, which = self.x, self.y, self.which
        if phase == 1:
            plan = (
                (self.middle.at[0, which], self.second.at[0, which], self.to_y),
                (self.middle.at[1, which], self.second.at[1, which], self.to_x),
            )
        elif phase == 2:
            one = self.result.at[2 * x + y, which]
            two = self.result.at[4 + 2 * y + x, which]
            plan = ((one, one, self.to_y), (two, two, self.to_x))
        else:
            one = self.result.at[pl.ds(2 * x, 2), which]
            two = self.result.at[pl.ds(4 + 2 * y, 2), which]
            plan = ((one, one, self.to_x), (two, two, self.to_y))
        return [
            remote(source, target, self.sent.at[2 * phase + i], self.arrived.at[2 * phase + i], to)
            for i, (source, target, to) in enumerate(plan)
        ]

    def sum_of(self, half, side):
        wide = self.middle.shape[3]
        lanes = pl.ds(pl.multiple_of(side * wide, 128), wide)
        which = self.which
        kept, got = self.kept[half, which, :, lanes], self.got[half, which, :, lanes]
        return kept.astype(f32) + got.astype(f32)

    def prepare(self):
        self.middle[0, self.which] = self.sum_of(0, 1 - self.y).astype(bf16)
        self.middle[1, self.which] = self.sum_of(1, 1 - self.x).astype(bf16)

    def run(self, phase):
        x, y, which = self.x, self.y, self.which
        if phase > 1:
            for copy in self.copies(phase - 1):
                copy.wait_recv()
        if phase == 2:
            self.result[2 * x + y, which] = (
                self.sum_of(0, y) + self.second[0, which].astype(f32)
            ).astype(bf16)
            self.result[4 + 2 * y + x, which] = (
                self.sum_of(1, x) + self.second[1, which].astype(f32)
            ).astype(bf16)
        if phase < 4:
            for copy in self.copies(phase):
                copy.start()

    def finish(self):
        for phase in (1, 2, 3):
            for copy in self.copies(phase):
                copy.wait_send()


class SumLine:
    def __init__(self, row, part, leaving, coming, sent, arrived):
        self.row, self.part, self.leaving, self.coming = row, part, leaving, coming
        self.sent, self.arrived = sent, arrived
        self.lines = part.shape[1] // SPLIT

    def piece(self, index):
        return pl.ds(index * self.lines, self.lines)

    def copy(self, block, index, way):
        return remote(
            self.leaving.at[block, self.piece(index)],
            self.coming.at[way, block, self.piece(index)],
            self.sent.at[block, index],
            self.arrived.at[way, block, index],
            {"row": beside(self.row, way)},
        )

    def send(self, block, index):
        @pl.when(block > self.row)
        def _():
            self.copy(block, index, 0).start()

        @pl.when(block < self.row)
        def _():
            self.copy(block, index, 1).start()

    def chained(self, block):
        return jnp.logical_or(
            jnp.logical_and(block > self.row, self.row > 0),
            jnp.logical_and(block < self.row, self.row < ROWS - 1),
        )

    def begin(self, block):
        @pl.when(jnp.logical_and(block != self.row, jnp.logical_not(self.chained(block))))
        def _():
            self.leaving[block] = self.part[block].astype(bf16)
            for index in range(SPLIT):
                self.send(block, index)

    def pass_on(self, block):
        @pl.when(self.chained(block))
        def _():
            way = (block < self.row).astype(jnp.int32)
            for index in range(SPLIT):
                self.copy(block, index, way).wait_recv()
                piece = self.piece(index)
                self.leaving[block, piece] = (
                    self.part[block, piece].astype(f32)
                    + self.coming[way, block, piece].astype(f32)
                ).astype(bf16)
                self.send(block, index)

    def total(self, target):
        target[...] = self.part[self.row].astype(f32)
        for way, there in ((0, self.row > 0), (1, self.row < ROWS - 1)):

            @pl.when(there)
            def _(way=way):
                for index in range(SPLIT):
                    self.copy(self.row, index, way).wait_recv()
                    target[self.piece(index)] += self.coming[
                        way, self.row, self.piece(index)
                    ].astype(f32)

    def finish(self):
        def one(block, carried):
            @pl.when(block != self.row)
            def _():
                for index in range(SPLIT):
                    self.copy(block, index, 0).wait_send()

            return carried

        lax.fori_loop(0, ROWS, one, 0)


def swap_halves(values):
    lanes = values.shape[1]
    lane = lax.broadcasted_iota(jnp.int32, values.shape, 1)
    return jnp.where(
        lane % ROPE < ROPE // 2,
        pltpu.roll(values, lanes - ROPE // 2, 1),
        pltpu.roll(values, ROPE // 2, 1),
    )


def attend_kernel(
    act_ref,
    scaling_ref,
    compress_ref,
    rescale_ref,
    premix_ref,
    mark_ref,
    cot_ref,
    route_ref,
    router_ref,
    queries_ref,
    expand_ref,
    combine_ref,
    cos_far,
    sin_far,
    key_cos_far,
    key_sin_far,
    one_out,
    query_out,
    key_out,
    value_out,
    probs_out,
    latent_out,
    normed_latent_out,
    attended_out,
    compress_out,
    cot_out,
    pick_out,
    back_out,
    rows_out,
    residual_ref,
    two_ref,
    scale_one_ref,
    scale_two_ref,
    router_all,
    one_ref,
    query_ref,
    key_ref,
    value_ref,
    probs_ref,
    latent_ref,
    normed_latent_ref,
    attended_ref,
    compress_all,
    cot_all,
    pick_ref,
    back_ref,
    rows_ref,
    queries,
    expand,
    combine,
    cos_ref,
    sin_ref,
    key_cos_ref,
    key_sin_ref,
    stat_to,
    stat_from,
    query_own,
    query_to,
    query_from,
    latent_to,
    latent_from,
    part,
    leaving,
    coming,
    routes,
    staged,
    marks,
    raw,
    scales,
    load_sem,
    store_sem,
    rows_sem,
    stat_sent,
    stat_arrived,
    line_sent,
    line_arrived,
    comp_sent,
    comp_arrived,
    comp_out_sent,
    comp_out_arrived,
    query_sent,
    query_arrived,
    latent_sent,
    latent_arrived,
    att_sent,
    att_arrived,
    sum_sent,
    sum_arrived,
    cot_sent,
    cot_arrived,
    route_sent,
    route_arrived,
    out_sent,
    out_arrived,
    pair_sent,
    pair_arrived,
    router_sent,
    router_arrived,
    scale_sent,
    scale_arrived,
):
    place, row, col = lax.axis_index("dp"), lax.axis_index("row"), lax.axis_index("col")
    other = 1 - col
    inner = jnp.logical_and(row > 0, row < ROWS - 1)
    sibling = {"col": other}
    tokens, width = act_ref.shape
    slots = pick_ref.shape[1] // SQUARE
    mine = query_own.shape[2]
    sliced = compress_ref.shape[0]
    quarter = width // SQUARE
    score_scale = (NOPE + ROPE) ** (-0.5)
    loads = [
        pltpu.make_async_copy(source, target, load_sem.at[i])
        for i, (source, target) in enumerate(
            [
                (queries_ref, queries),
                (expand_ref, expand),
                (combine_ref, combine),
                (cos_far, cos_ref),
                (sin_far, sin_ref),
                (key_cos_far, key_cos_ref),
                (key_sin_far, key_sin_ref),
            ]
        )
    ]
    for load in loads:
        load.start()
    stores = [
        pltpu.make_async_copy(source, target, store_sem.at[i])
        for i, (source, target) in enumerate(
            [
                (one_ref, one_out),
                (query_ref, query_out),
                (key_ref, key_out),
                (value_ref, value_out),
                (latent_ref, latent_out),
                (normed_latent_ref, normed_latent_out),
                (compress_all, compress_out),
                (probs_ref, probs_out),
                (attended_ref, attended_out),
                (cot_all, cot_out),
                (pick_ref, pick_out),
                (back_ref, back_out),
            ]
        )
    ]

    def rows_store(block):
        return pltpu.make_async_copy(
            rows_ref.at[:, block], rows_out.at[:, block], rows_sem.at[block]
        )

    def stat_copy(index):
        return remote(
            stat_to.at[index],
            stat_from.at[index],
            stat_sent.at[index],
            stat_arrived.at[index],
            sibling,
        )

    def scale_of(values, index):
        own = jnp.sum(values * values, axis=1, keepdims=True)
        stat_to[index] = jnp.broadcast_to(own, (tokens, 128))
        stat_copy(index).start()
        stat_copy(index).wait_recv()
        return lax.rsqrt((own + stat_from[index][:, 0:1]) / D + epsilon)

    def comp_piece(block, member):
        return compress_all.at[
            pl.ds(pl.multiple_of(block * sliced, 16), sliced),
            pl.ds(pl.multiple_of(member * quarter, 128), quarter),
        ]

    def comp_copy(block, way):
        here = comp_piece(block, place)
        return remote(
            here,
            here,
            comp_sent.at[block, way],
            comp_arrived.at[block],
            {"row": beside(row, way)},
        )

    def comp_each(block, act):
        @pl.when(jnp.logical_and(block <= row, row < ROWS - 1))
        def _():
            act(comp_copy(block, 0))

        @pl.when(jnp.logical_and(block >= row, row > 0))
        def _():
            act(comp_copy(block, 1))

    def comp_out(block, step, member):
        here = comp_piece(block, member)
        return remote(
            here,
            here,
            comp_out_sent.at[block, step],
            comp_out_arrived.at[block, step],
            {"dp": partner(place, step)},
        )

    line = Line(row, raw, line_sent, line_arrived)
    scale_line = Line(row, scales, scale_sent, scale_arrived)
    cot_line = Line(row, cot_all, cot_sent, cot_arrived)
    route_line = Line(row, routes, route_sent, route_arrived)
    sums = SumLine(row, part, leaving, coming, sum_sent, sum_arrived)

    met = greet(row, place, col)
    compress_all[pl.ds(pl.multiple_of(row * sliced, 16), sliced)] = compress_ref[...]
    compress_all[ROWS * sliced :] = jnp.zeros(
        (compress_all.shape[0] - ROWS * sliced, width), bf16
    )
    raw[pl.ds(row, 1)] = act_ref[...].reshape(1, tokens, width)
    meet(met)
    comp_each(row, lambda copy: copy.start())
    line.pass_on(row)

    def router_copy(half):
        here = router_all.at[:, pl.ds(pl.multiple_of(half * width, width), width)]
        return remote(here, here, router_sent.at[0], router_arrived.at[0], sibling)

    inputs = act_ref[...].astype(f32)
    scale_one = scale_of(inputs, 0)
    scale_one_ref[...] = scale_one
    scales[pl.ds(row, 1)] = jnp.broadcast_to(scale_one, (tokens, 128)).T[0:8].reshape(1, 8, tokens)
    scale_line.pass_on(row)
    router_all[:, pl.ds(pl.multiple_of(col * width, width), width)] = router_ref[...]
    router_copy(col).start()
    cot_all[pl.ds(row, 1)] = cot_ref[...].reshape(1, tokens, width)
    routes[pl.ds(row, 1)] = route_ref[...].reshape((1,) + route_ref.shape)

    @pl.when(jnp.logical_not(inner))
    def _():
        route_line.pass_on(row)
        cot_line.pass_on(row)

    for block in range(ROWS):
        mark = mark_ref[:, block * tokens : (block + 1) * tokens].astype(f32)
        marks[block] = jnp.broadcast_to(mark, (8, tokens)).T
    loads[0].wait()

    def query_copy(block):
        return remote(
            query_to.at[block],
            query_from.at[block],
            query_sent.at[block],
            query_arrived.at[block],
            sibling,
        )

    def latent_copy(block):
        return remote(
            latent_to.at[block],
            latent_from.at[block],
            latent_sent.at[block],
            latent_arrived.at[block],
            sibling,
        )

    def att_copy(block, half):
        here = attended_ref.at[block, :, pl.ds(pl.multiple_of(half * 2 * HEADV, 128), 2 * HEADV)]
        return remote(here, here, att_sent.at[block], att_arrived.at[block], sibling)

    def comp_relay(step):
        block = block_at(row, step)
        comp_copy(block, 0).wait_recv()
        comp_each(block, lambda copy: copy.start())
        for shift in (3, 2, 1):
            comp_out(block, shift, place).start()

    def relay_one(step):
        block = block_at(row, step)
        line.wait(block)
        line.pass_on(block)
        scale_line.wait(block)
        scale_line.pass_on(block)

    def normalise(step):
        block = block_at(row, step)
        scale = scales[block].T[:, 0:1]
        normed = (raw[block].astype(f32) * scale * scaling_ref[...]).astype(bf16)
        one_ref[block] = normed
        query_to[block] = nn(
            normed, queries[:, pl.ds(pl.multiple_of(other * mine, 128), mine)]
        ).astype(bf16)
        query_copy(block).start()
        query_own[block] = nn(normed, queries[:, pl.ds(pl.multiple_of(col * mine, 128), mine)])

    def latents(step):
        block = block_at(row, step)
        value = nt(one_ref[block], compress_all[...])
        latent_to[block] = value
        latent_copy(block).start()
        latent_ref[block] = value

    def keys(step):
        block = block_at(row, step)
        latent_copy(block).wait_recv()
        latent = latent_ref[block] + latent_from[block]
        latent_ref[block] = latent
        plain = latent[:, :RANK]
        scale = lax.rsqrt(jnp.mean(plain * plain, axis=1, keepdims=True) + epsilon)
        normed = (plain * scale * rescale_ref[...]).astype(bf16)
        normed_latent_ref[block] = normed
        own = 2 * (NOPE + HEADV)
        expanded = nn(normed, expand[:, pl.ds(pl.multiple_of(col * own, 128), own)])
        rope = latent[:, RANK:]
        rope = rope * key_cos_ref[block] + swap_halves(rope) * key_sin_ref[block]
        first = jnp.concatenate([expanded[:, :NOPE], rope], axis=1)
        second = jnp.concatenate([expanded[:, 2 * NOPE : 3 * NOPE], rope], axis=1)
        key_ref[0, block] = first.astype(bf16)
        key_ref[1, block] = pltpu.roll(second, ROPE, 1).astype(bf16)
        value_ref[0, block] = expanded[:, NOPE : 2 * NOPE].astype(bf16)
        value_ref[1, block] = expanded[:, 3 * NOPE :].astype(bf16)
        query_copy(block).wait_recv()
        query = query_own[block] + query_from[block].astype(f32)
        query_ref[block] = (
            query * cos_ref[block] + swap_halves(query) * sin_ref[block]
        ).astype(bf16)

    def gather(step, carried):
        @pl.when(step > 0)
        def _():
            relay_one(step)

        normalise(step)

        @pl.when(step < 2)
        def _():
            comp_relay(step + 1)

        @pl.when(step == 1)
        def _():
            comp_relay(3)

        return carried

    lax.fori_loop(0, ROWS - 1, gather, 0)

    @pl.when(inner)
    def _():
        relay_one(ROWS - 1)

    def comp_arrive(block, carried):
        @pl.when(block != row)
        def _():
            for shift in range(1, SQUARE):
                comp_out(block, shift, partner(place, shift)).wait_recv()

        return carried

    lax.fori_loop(0, ROWS, comp_arrive, 0)
    for load in loads[1:2] + loads[3:]:
        load.wait()

    def middle(step, carried):
        @pl.when(jnp.logical_and(step == ROWS - 1, jnp.logical_not(inner)))
        def _():
            relay_one(step)

        @pl.when(step == ROWS - 1)
        def _():
            normalise(step)

        @pl.when(step < ROWS)
        def _():
            latents(step)

        @pl.when(step > 0)
        def _():
            keys(step - 1)

        return carried

    lax.fori_loop(0, ROWS - 1, middle, 0)

    @pl.when(inner)
    def _():
        route_line.pass_on(row)
        cot_line.pass_on(row)

    def relay(step):
        block = block_at(row, step)
        route_line.wait(block)
        route_line.pass_on(block)
        cot_line.wait(block)
        cot_line.pass_on(block)

    def out_copy(block, step):
        piece = pl.ds(step * slots, slots)
        return remote(
            staged.at[block, piece],
            rows_ref.at[col, block, piece],
            out_sent.at[block, step],
            out_arrived.at[block, step],
            {"dp": partner(place, step)},
        )

    def pair_copy(block, half):
        here = rows_ref.at[half, block]
        return remote(here, here, pair_sent.at[block], pair_arrived.at[block], sibling)

    def take(step):
        block = block_at(row, step)

        @pl.when(jnp.logical_and(step > 0, jnp.logical_not(inner)))
        def _():
            relay(step)

        before = (
            lax.broadcasted_iota(jnp.int32, (tokens, tokens), 0)
            < lax.broadcasted_iota(jnp.int32, (tokens, tokens), 1)
        ).astype(bf16)
        routing = routes[block]
        chosen = []
        for shift in range(SQUARE):
            expert = partner(place, shift) * ROWS + row
            hit = (routing == expert).astype(f32)
            chosen.append(jnp.max(hit, axis=0, keepdims=True))
        goes = jnp.concatenate(chosen + chosen, axis=0)
        rank = nn(goes.astype(bf16), before)
        for shift in range(SQUARE):
            slot = lax.broadcasted_iota(jnp.int32, (slots, tokens), 0).astype(f32)
            here = jnp.logical_and(slot == rank[shift : shift + 1], goes[shift : shift + 1] > 0.5)
            pick = here.astype(f32)
            pick_ref[block, shift * slots : (shift + 1) * slots] = pick.astype(bf16)
            back_ref[block, :, shift * slots : (shift + 1) * slots] = pick.T.astype(bf16)
        staged[block] = nn(pick_ref[block], cot_all[block]).astype(bf16)
        for shift in (3, 2, 1):
            out_copy(block, shift).start()
        rows_ref[col, block, 0:slots] = staged[block, 0:slots]

    def forward(step):
        block = block_at(row, step)
        for shift in range(1, SQUARE):
            out_copy(block, shift).wait_recv()
        pair_copy(block, col).start()

    take(0)

    @pl.when(inner)
    def _():
        relay(1)
        relay(2)

    lax.fori_loop(ROWS - 1, ROWS + 1, middle, 0)

    for index in range(7):
        stores[index].start()
    seq = ROWS * tokens
    lanes = NOPE + 2 * ROPE

    def attend(turn, carried):
        block = block_at(row, ROWS - 1 - turn)
        visible = mark_ref[...].astype(f32) <= marks[block][:, 0:1]
        for head in range(2):
            query = query_ref[block, :, head * NOPE : head * NOPE + lanes]
            scores = nt(query, key_ref[head].reshape(seq, lanes)) * score_scale
            scores = jnp.where(visible, scores, masked_score)
            weight = jnp.exp(scores - jnp.max(scores, axis=1, keepdims=True))
            probs = (weight / jnp.sum(weight, axis=1, keepdims=True)).astype(bf16)
            probs_ref[head, block] = probs
            result = nn(probs, value_ref[head].reshape(seq, HEADV)).astype(bf16)
            at = pl.multiple_of((col * 2 + head) * HEADV, 128)
            attended_ref[block, :, pl.ds(at, HEADV)] = result
        att_copy(block, col).start()

        @pl.when(jnp.logical_and(turn == 0, inner))
        def _():
            relay(3)

        @pl.when(turn > 0)
        def _():
            mix(turn - 1)
            take(turn)

        return carried

    def mix(turn):
        block = block_at(row, ROWS - 1 - turn)
        att_copy(block, other).wait_recv()
        part[block] = nn(attended_ref[block], combine[...])
        sums.begin(block)

    loads[2].wait()
    lax.fori_loop(0, ROWS, attend, 0)
    mix(ROWS - 1)
    for index in range(7, 12):
        stores[index].start()

    def hand_on(turn, carried):
        sums.pass_on(block_at(row, jnp.where(turn == 0, 3, turn)))
        forward(turn)
        return carried

    lax.fori_loop(0, 3, hand_on, 0)
    sums.total(residual_ref)
    residual = residual_ref[...] + inputs
    residual_ref[...] = residual
    scale_two = scale_of(residual, 1)
    scale_two_ref[...] = scale_two
    two_ref[...] = (residual * scale_two * premix_ref[...]).astype(bf16)
    forward(3)

    def ended(block, carried):
        pair_copy(block, other).wait_recv()
        rows_store(block).start()
        pair_copy(block, col).wait_send()
        for shift in range(1, SQUARE):
            out_copy(block, shift).wait_send()

            @pl.when(block != row)
            def _(shift=shift):
                comp_out(block, shift, place).wait_send()

        comp_each(block, lambda copy: copy.wait_send())
        query_copy(block).wait_send()
        latent_copy(block).wait_send()
        att_copy(block, col).wait_send()
        return carried

    lax.fori_loop(0, ROWS, ended, 0)
    for store in stores:
        store.wait()

    def stored(block, carried):
        rows_store(block).wait()
        return carried

    lax.fori_loop(0, ROWS, stored, 0)
    router_copy(other).wait_recv()
    router_copy(col).wait_send()
    stat_copy(0).wait_send()
    stat_copy(1).wait_send()
    sums.finish()
    line.finish()
    scale_line.finish()
    cot_line.finish()
    route_line.finish()


def turning_tables(length):
    half = ROPE // 2
    frequency = 10000.0 ** (-np.arange(half, dtype=np.float32) * 2.0 / ROPE)
    angles = np.arange(length, dtype=np.float32)[:, None] * frequency[None, :].astype(np.float32)
    cosine, sine = np.cos(angles), np.sin(angles)
    cosine, sine = np.concatenate([cosine, cosine], 1), np.concatenate([-sine, sine], 1)
    ones, zeros = np.ones((length, NOPE)), np.zeros((length, NOPE))
    gap = np.zeros((length, 128 - ROPE))
    tables = (
        np.concatenate([ones, cosine, ones, cosine], 1),
        np.concatenate([zeros, sine, zeros, sine], 1),
        np.concatenate([cosine, gap], 1),
        np.concatenate([sine, gap], 1),
    )
    return [
        jnp.asarray(table.reshape(ROWS, length // ROWS, -1).astype(np.float32))
        for table in tables
    ]


def pair_sems():
    return [DMA((ROWS,)), DMA((ROWS,))]


def line_sems():
    return [DMA((ROWS, 2)), DMA((ROWS,))]


def square_sems():
    return [DMA((ROWS, SQUARE)), DMA((ROWS, SQUARE))]


def sum_sems():
    return [DMA((ROWS, SPLIT)), DMA((2, ROWS, SPLIT))]


def run_attention(
    activations,
    scaling,
    queries,
    compress,
    rescale,
    expand,
    combine,
    premix,
    segments,
    cotangent,
    routing,
    router,
    tables,
    slots,
):
    tokens, width = activations.shape
    seq = ROWS * tokens
    mine = queries.shape[1] // COLS
    sliced = compress.shape[1]
    latent_width = RANK + 128
    picked = SQUARE * slots
    lanes = NOPE + 2 * ROPE
    routes = routing.T
    whole = pl.BlockSpec(memory_space=VMEM)
    far = pl.BlockSpec(memory_space=pl.ANY)

    def shape(*dims, dtype=bf16):
        return jax.ShapeDtypeStruct(dims, dtype)

    kept = [
        shape(ROWS, tokens, width),
        shape(ROWS, tokens, mine),
        shape(2, ROWS, tokens, lanes),
        shape(2, ROWS, tokens, HEADV),
        shape(2, ROWS, tokens, seq),
        shape(ROWS, tokens, latent_width, dtype=f32),
        shape(ROWS, tokens, RANK),
        shape(ROWS, tokens, COLS * 2 * HEADV),
        shape(latent_width, width),
        shape(ROWS, tokens, width),
        shape(ROWS, picked, tokens),
        shape(ROWS, tokens, picked),
        shape(COLS, ROWS, picked, width),
    ]
    return pl.pallas_call(
        attend_kernel,
        name="attend",
        out_shape=(
            *kept,
            shape(tokens, width, dtype=f32),
            shape(tokens, width),
            shape(tokens, 1, dtype=f32),
            shape(tokens, 1, dtype=f32),
            shape(router.shape[1], COLS * width),
        ),
        in_specs=[whole] * 9 + [far] * 7,
        out_specs=(far,) * 13 + (whole,) * 5,
        scratch_shapes=[
            *[VMEM(value.shape, value.dtype) for value in kept],
            VMEM(queries.shape, bf16),
            VMEM(expand.shape, bf16),
            VMEM(combine.shape, bf16),
            *[VMEM(table.shape, f32) for table in tables],
            VMEM((2, tokens, 128), f32),
            VMEM((2, tokens, 128), f32),
            VMEM((ROWS, tokens, mine), f32),
            VMEM((ROWS, tokens, mine), bf16),
            VMEM((ROWS, tokens, mine), bf16),
            VMEM((ROWS, tokens, latent_width), f32),
            VMEM((ROWS, tokens, latent_width), f32),
            VMEM((ROWS, tokens, width), f32),
            VMEM((ROWS, tokens, width), bf16),
            VMEM((2, ROWS, tokens, width), bf16),
            VMEM((ROWS,) + routes.shape, jnp.int32),
            VMEM((ROWS, picked, width), bf16),
            VMEM((ROWS, tokens, 8), f32),
            VMEM((ROWS, tokens, width), bf16),
            VMEM((ROWS, 8, tokens), f32),
            DMA((7,)),
            DMA((12,)),
            DMA((ROWS,)),
            DMA((2,)),
            DMA((2,)),
            *line_sems(),
            *line_sems(),
            *square_sems(),
            *pair_sems(),
            *pair_sems(),
            *pair_sems(),
            *sum_sems(),
            *line_sems(),
            *line_sems(),
            *square_sems(),
            *pair_sems(),
            DMA((1,)),
            DMA((1,)),
            *line_sems(),
        ],
        compiler_params=pltpu.CompilerParams(
            collective_id=1, has_side_effects=True, vmem_limit_bytes=56 * MIB
        ),
        cost_estimate=pl.CostEstimate(
            flops=40 * 1024**3, bytes_accessed=32 * MIB, transcendentals=0
        ),
    )(
        activations,
        scaling.reshape(1, width),
        compress.T,
        rescale.reshape(1, RANK),
        premix.reshape(1, width),
        segments.reshape(1, seq),
        cotangent,
        routes,
        router.T,
        queries,
        expand,
        combine,
        *tables,
    )


def attend_back_kernel(
    normed_grad_ref,
    residual_ref,
    scale_two_ref,
    premix_ref,
    cot_ref,
    act_ref,
    scale_one_ref,
    scaling_ref,
    rescale_ref,
    combine_far,
    query_far,
    key_far,
    value_far,
    probs_far,
    cos_far,
    sin_far,
    queries_far,
    expand_far,
    latent_far,
    key_cos_far,
    key_sin_far,
    compress_far,
    one_far,
    kept_far,
    got_x_far,
    got_y_far,
    attended_far,
    normed_latent_far,
    narrow_far,
    home_far,
    back_far,
    shared_far,
    premix_far,
    router_far,
    input_grad_ref,
    output_ref,
    small_ref,
    shared_sum,
    queries_out,
    combine_out,
    expand_out,
    compress_out,
    branch_ref,
    query_grad_ref,
    expanded_ref,
    own_latent_ref,
    scaling_rows,
    rescale_rows,
    combine,
    query_ref,
    key_ref,
    value_ref,
    probs_ref,
    cos_ref,
    sin_ref,
    queries,
    expand,
    latent_ref,
    key_cos_ref,
    key_sin_ref,
    compress_all,
    one_ref,
    kept,
    got,
    middle,
    second,
    result,
    attended,
    normed_latent,
    narrow,
    home,
    back_ref,
    shared_ref,
    premix_rows,
    router_rows,
    stat_to,
    stat_from,
    grad_own,
    grad_to,
    grad_from,
    key_grad,
    value_grad,
    latent_own,
    latent_to,
    latent_from,
    turned,
    turned_from,
    part,
    leaving,
    coming,
    total,
    load_sem,
    stat_sent,
    stat_arrived,
    line_sent,
    line_arrived,
    grad_sent,
    grad_arrived,
    query_sent,
    query_arrived,
    latent_sent,
    latent_arrived,
    turned_sent,
    turned_arrived,
    own_sent,
    own_arrived,
    sum_sent,
    sum_arrived,
    rest_sent,
    rest_arrived,
    rest_sem,
    reply_part,
    reply_leaving,
    reply_coming,
    small_to,
    small_from,
    small_line,
    small_square,
    small_own,
    expand_other,
    store_sem,
    reply_sent,
    reply_arrived,
    pair_sent,
    pair_arrived,
    small_sent,
    small_arrived,
    *sums_scratch,
):
    place, row, col = lax.axis_index("dp"), lax.axis_index("row"), lax.axis_index("col")
    other = 1 - col
    sibling = {"col": other}
    tokens, width = act_ref.shape
    seq = ROWS * tokens
    mine = query_ref.shape[2]
    lanes = key_ref.shape[3]
    both = 2 * HEADV
    sliced = own_latent_ref.shape[0]
    score_scale = (NOPE + ROPE) ** (-0.5)
    loads = [
        pltpu.make_async_copy(source, target, load_sem.at[i])
        for i, (source, target) in enumerate(
            [
                (kept_far, kept),
                (got_x_far, got.at[0]),
                (got_y_far, got.at[1]),
                (combine_far, combine),
                (query_far, query_ref),
                (key_far, key_ref),
                (value_far, value_ref),
                (probs_far, probs_ref),
                (cos_far, cos_ref),
                (sin_far, sin_ref),
                (queries_far, queries),
                (expand_far, expand),
                (latent_far, latent_ref),
                (key_cos_far, key_cos_ref),
                (key_sin_far, key_sin_ref),
                (compress_far, compress_all),
                (one_far, one_ref),
                (attended_far, attended),
                (normed_latent_far, normed_latent),
                (narrow_far, narrow),
                (home_far, home),
                (back_far, back_ref),
                (shared_far, shared_ref),
                (premix_far, premix_rows),
                (router_far, router_rows),
            ]
        )
    ]
    for load in loads:
        load.start()
    line = Line(row, branch_ref, line_sent, line_arrived)
    sums = SumLine(row, part, leaving, coming, sum_sent, sum_arrived)
    met = greet(row, place, col, line=True)

    def stat_copy(index):
        return remote(
            stat_to.at[index],
            stat_from.at[index],
            stat_sent.at[index],
            stat_arrived.at[index],
            sibling,
        )

    def norm_begin(values, gain, upstream, index):
        weighted = upstream * gain
        own = jnp.sum(weighted * values, axis=1, keepdims=True)
        stat_to[index] = jnp.broadcast_to(own, (tokens, 128))
        stat_copy(index).start()

    def norm_grad(values, scale, gain, upstream, index):
        stat_copy(index).wait_recv()
        inner = (stat_to[index][:, 0:1] + stat_from[index][:, 0:1]) / D
        return upstream * gain * scale - values * (scale * scale * scale * inner)

    for load in loads[0:3]:
        load.wait()
    rests = [
        SquareRest(place, which, kept, got, middle, second, result, rest_sent, rest_arrived)
        for which in range(kept.shape[1])
    ]
    for rest in rests:
        rest.prepare()
    meet(met)
    norm_begin(residual_ref[...], premix_ref[...], normed_grad_ref[...], 0)
    for rest in rests:
        rest.run(1)
    residual_grad = cot_ref[...].astype(f32) + norm_grad(
        residual_ref[...], scale_two_ref[...], premix_ref[...], normed_grad_ref[...], 0
    )
    input_grad_ref[...] = residual_grad
    branch_ref[pl.ds(row, 1)] = residual_grad.astype(bf16).reshape(1, tokens, width)
    line.pass_on(row)
    key_grad[...] = jnp.zeros_like(key_grad)
    value_grad[...] = jnp.zeros_like(value_grad)
    scaling_rows[...] = jnp.zeros_like(scaling_rows)
    rescale_rows[...] = jnp.zeros_like(rescale_rows)

    line_sums = SumLine(
        row, reply_part, reply_leaving, reply_coming, reply_sent, reply_arrived
    )
    experts = router_rows.shape[0]
    kinds = [sums_scratch[7 * i : 7 * i + 7] for i in range(4)]
    parts = [scratch[0] for scratch in kinds]
    plan = [(kind, chunk) for kind in range(4) for chunk in range(parts[kind].shape[0])]
    pieces_of = [
        SquareSum(place, *[ref.at[chunk] for ref in kinds[kind]]) for kind, chunk in plan
    ]
    count = len(plan)

    def begin(index):
        kind, chunk = plan[index]
        part_ref = parts[kind]
        if kind == 0 and chunk == 0:
            loads[17].wait()
        if kind == 2:
            loads[18].wait()
        if kind < 2:
            left, right = ((attended, branch_ref), (one_ref, query_grad_ref))[kind]
            height = 8 * part_ref.shape[2]
            piece = left[:, :, chunk * height : (chunk + 1) * height].reshape(seq, height)
            grad = tn(piece, right[...].reshape(seq, right.shape[2]))
        elif kind == 2:
            grad = tn(
                normed_latent[...].reshape(seq, RANK),
                expanded_ref[...].reshape(seq, expanded_ref.shape[2]),
            )
        else:
            grad = nn(own_latent_ref[...], one_ref[...].reshape(seq, width)).astype(bf16)
            for piece in range(8):
                part_ref[0, piece] = grad[:, piece * (width // 8) : (piece + 1) * (width // 8)]
        if kind < 3:
            part_ref[chunk] = grad.astype(bf16).reshape(part_ref.shape[1:])
        pieces_of[index].run(0)

    stores = []

    def store(source, target):
        copy = pltpu.make_async_copy(source, target, store_sem.at[len(stores)])
        copy.start()
        stores.append(copy)

    def pair_copy():
        return remote(kinds[2][4].at[0], expand_other, pair_sent.at[0], pair_arrived.at[0], sibling)

    def expand_lanes(half):
        wide = expand_other.shape[2]
        return expand_out.at[:, :, pl.ds(pl.multiple_of(half * wide, 128), wide)]

    def put(index):
        kind, chunk = plan[index]
        done = kinds[kind][4]
        if kind < 2:
            store(done.at[chunk], (combine_out, queries_out)[kind].at[chunk])
        elif kind == 2:
            store(done.at[0], expand_lanes(col))
            pair_copy().start()
        else:
            lanes = width // 8
            for piece in range(8):
                store(done.at[0, piece], compress_out.at[:, piece * lanes : (piece + 1) * lanes])

    def advance(turn):
        for phase in (1, 2, 3, 4):
            index = turn - phase
            if 0 <= index < count:
                pieces_of[index].run(phase)
                if phase == 4:
                    put(index)
        if 2 <= turn < count:
            begin(turn)

    def reply_add(turn, carried):
        block = block_at(row, ROWS - 1 - turn)
        reply_part[block] = (
            nn(back_ref[block], home[block]) + nn(shared_ref[block], narrow[...])
        ).astype(bf16)
        line_sums.begin(block)
        return carried

    def small_copy(step):
        if step == 0:
            return remote(small_to, small_from, small_sent.at[0], small_arrived.at[0], sibling)
        if step < ROWS:
            return remote(
                small_own,
                small_line.at[step],
                small_sent.at[step],
                small_arrived.at[step],
                {"row": lax.rem(row + step, ROWS)},
            )
        shift = step - ROWS + 1
        return remote(
            small_ref,
            small_square.at[shift],
            small_sent.at[step],
            small_arrived.at[step],
            {"dp": partner(place, shift)},
        )

    def small_begin():
        loads[23].wait()
        loads[24].wait()
        rescale_row = jnp.sum(rescale_rows[...], axis=0, keepdims=True)
        empty = jnp.zeros((small_own.shape[0] - experts, width), f32)
        small_to[0:experts] = router_rows[:, pl.ds(pl.multiple_of(other * width, width), width)]
        small_to[experts:] = empty
        small_to[experts + 2 : experts + 3, 0:RANK] = rescale_row
        small_copy(0).start()
        small_own[0:experts] = router_rows[:, pl.ds(pl.multiple_of(col * width, width), width)]
        small_own[experts:] = empty
        small_own[experts : experts + 1] = (
            jnp.sum(premix_rows[...], axis=0, keepdims=True) / premix_ref[...]
        )
        small_own[experts + 1 : experts + 2] = (
            jnp.sum(scaling_rows[...], axis=0, keepdims=True) / scaling_ref[...]
        )
        small_own[experts + 2 : experts + 3, 0:RANK] = rescale_row

    def small_line_begin():
        small_copy(0).wait_recv()
        small_own[...] += small_from[...]
        for step in range(1, ROWS):
            small_copy(step).start()

    def small_square_begin():
        for step in range(1, ROWS):
            small_copy(step).wait_recv()
        small_ref[...] = small_own[...] + small_line[1] + small_line[2] + small_line[3]
        for step in range(ROWS, ROWS + SQUARE - 1):
            small_copy(step).start()

    def small_end():
        for step in range(ROWS, ROWS + SQUARE - 1):
            small_copy(step).wait_recv()
        for step in range(ROWS, ROWS + SQUARE - 1):
            small_copy(step).wait_send()
        small_ref[...] += small_square[1] + small_square[2] + small_square[3]

    def reply_begin():
        for load in loads[19:23]:
            load.wait()
        lax.fori_loop(0, ROWS, reply_add, 0)

    def reply_pass():
        lax.fori_loop(0, 3, line_pass, 0)

    def reply_end():
        line_sums.total(total)
        output_ref[...] = (total[...] + residual_ref[...]).astype(bf16)

    def line_pass(turn, carried):
        line_sums.pass_on(block_at(row, jnp.where(turn == 0, 3, turn)))
        return carried

    def grad_copy(block):
        return remote(
            grad_to.at[block],
            grad_from.at[block],
            grad_sent.at[block],
            grad_arrived.at[block],
            sibling,
        )

    def query_copy(block, half):
        here = query_grad_ref.at[block, :, pl.ds(pl.multiple_of(half * mine, 128), mine)]
        return remote(here, here, query_sent.at[block], query_arrived.at[block], sibling)

    def latent_copy(block):
        return remote(
            latent_to.at[block],
            latent_from.at[block],
            latent_sent.at[block],
            latent_arrived.at[block],
            sibling,
        )

    def arrive(step):
        block = block_at(row, step)

        @pl.when(step > 0)
        def _():
            line.wait(block)
            line.pass_on(block)

        @pl.when(step == 0)
        def _():
            loads[3].wait()

        grads = branch_ref[block]
        grad_to[block] = nt(
            grads, combine[pl.ds(pl.multiple_of(other * both, 16), both)]
        ).astype(bf16)
        grad_copy(block).start()
        grad_own[block] = nt(grads, combine[pl.ds(pl.multiple_of(col * both, 16), both)])

    def heads(step):
        block = block_at(row, step)

        @pl.when(step == 0)
        def _():
            for load in loads[4:10]:
                load.wait()

        grad_copy(block).wait_recv()
        grads = (grad_own[block] + grad_from[block].astype(f32)).astype(bf16)
        pieces = []
        for head in range(2):
            upstream = grads[:, head * HEADV : (head + 1) * HEADV]
            query = query_ref[block, :, head * NOPE : head * NOPE + lanes]
            probs = probs_ref[head, block]
            weight = probs.astype(f32)
            probs_back = nt(upstream, value_ref[head].reshape(seq, HEADV))
            inner = jnp.sum(weight * probs_back, axis=1, keepdims=True)
            score_grad = (weight * (probs_back - inner)).astype(bf16)
            pieces.append(nn(score_grad, key_ref[head].reshape(seq, lanes)) * score_scale)
            key_grad[head] += tn(score_grad, query)
            value_grad[head] += tn(probs, upstream)
        first, second = pieces
        grad = jnp.concatenate(
            [first[:, :NOPE], first[:, NOPE:] + second[:, :NOPE], second[:, NOPE:]], axis=1
        )
        grad = grad * cos_ref[block] - swap_halves(grad) * sin_ref[block]
        query_grad_ref[block, :, pl.ds(pl.multiple_of(col * mine, 128), mine)] = grad.astype(bf16)
        query_copy(block, col).start()

    def project(step):
        block = block_at(row, step)

        @pl.when(step == 0)
        def _():
            loads[10].wait()

        query_copy(block, other).wait_recv()
        part[block] = nt(query_grad_ref[block], queries[...])

    def turn(step, carried):
        @pl.when(step < ROWS)
        def _():
            arrive(step)

        @pl.when(step == 1)
        def _():
            for rest in rests:
                rest.run(2)

        @pl.when(step == 2)
        def _():
            rests[0].run(3)

        @pl.when(step == 3)
        def _():
            rests[1].run(3)
            rests[2].run(3)

        @pl.when(step >= 1)
        def _():
            heads(step - 1)

        @pl.when(step >= 2)
        def _():
            project(step - 2)

        return carried

    lax.fori_loop(0, ROWS + 1, turn, 0)
    for load in loads[11:17]:
        load.wait()
    begin(0)
    begin(1)
    reply_begin()

    def latents(turn, carried):
        block = block_at(row, ROWS - 1 - turn)
        here = pl.ds(pl.multiple_of(block * tokens, 128), tokens)
        first = key_grad[0, here] * score_scale
        second = pltpu.roll(key_grad[1, here] * score_scale, lanes - ROPE, 1)
        grad = jnp.concatenate(
            [first[:, :NOPE], value_grad[0, here], second[:, :NOPE], value_grad[1, here]], axis=1
        ).astype(bf16)
        expanded_ref[block] = grad
        own = 2 * (NOPE + HEADV)
        upstream = nt(grad, expand[:, pl.ds(pl.multiple_of(col * own, 128), own)])
        plain = latent_ref[block][:, :RANK]
        scale = lax.rsqrt(jnp.mean(plain * plain, axis=1, keepdims=True) + epsilon)
        rescale_rows[...] += jnp.sum(
            (upstream * plain * scale).reshape(tokens // 8, 8, RANK), axis=0
        )
        weighted = upstream * rescale_ref[...]
        inner = jnp.mean(weighted * plain, axis=1, keepdims=True)
        plain_grad = weighted * scale - plain * (scale * scale * scale * inner)
        rope = first[:, NOPE:] + second[:, NOPE:]
        lane = lax.broadcasted_iota(jnp.int32, rope.shape, 1)
        rope = jnp.where(lane < ROPE, rope, 0.0)
        rope = rope * key_cos_ref[block] - swap_halves(rope) * key_sin_ref[block]
        value = jnp.concatenate([plain_grad, rope], axis=1)
        latent_own[block] = value
        latent_to[block] = value.astype(bf16)
        latent_copy(block).start()
        return carried

    lax.fori_loop(0, ROWS, latents, 0)
    project(ROWS - 1)

    def turned_piece(member):
        return turned.at[
            pl.ds(pl.multiple_of(member * sliced, 16), sliced),
            pl.ds(pl.multiple_of(col * (seq // COLS), 128), seq // COLS),
        ]

    def turned_copy(step):
        to = lax.rem(row + step, ROWS)
        return remote(
            turned_piece(to),
            turned_from.at[step],
            turned_sent.at[step],
            turned_arrived.at[step],
            {"row": to},
        )

    def mix(turn, carried):
        block = block_at(row, ROWS - 1 - turn)
        latent_copy(block).wait_recv()
        latent = latent_own[block] + latent_from[block].astype(f32)
        here = pl.ds(pl.multiple_of(block * tokens, 128), tokens)
        total_here = part[block] + nn(latent.astype(bf16), compress_all[...])
        part[block] = total_here
        sums.begin(block)
        turned[:, here] = latent.T.astype(bf16)
        scaling_rows[...] += jnp.sum(
            (total_here * one_ref[block].astype(f32)).reshape(tokens // 8, 8, width), axis=0
        )
        return carried

    lax.fori_loop(0, ROWS, mix, 0)
    for step in range(1, ROWS):
        turned_copy(step).start()

    advance(1)
    small_begin()
    for turn in range(3):
        sums.pass_on(block_at(row, 3 if turn == 0 else turn))
        advance(turn + 2)
        if turn == 0:
            small_line_begin()
    for step in range(1, ROWS):
        turned_copy(step).wait_recv()
    half = pl.ds(pl.multiple_of(col * (seq // COLS), 128), seq // COLS)
    own_sum = turned[pl.ds(pl.multiple_of(row * sliced, 16), sliced), half].astype(f32)
    for step in range(1, ROWS):
        own_sum = own_sum + turned_from[step].astype(f32)
    own_latent_ref[:, half] = own_sum.astype(bf16)

    def own_copy(part_of):
        here = own_latent_ref.at[
            :, pl.ds(pl.multiple_of(part_of * (seq // COLS), 128), seq // COLS)
        ]
        return remote(here, here, own_sent.at[0], own_arrived.at[0], sibling)

    own_copy(col).start()
    advance(5)
    sums.total(total)
    norm_begin(act_ref[...].astype(f32), scaling_ref[...], total[...], 1)
    input_grad_ref[...] += norm_grad(
        act_ref[...].astype(f32), scale_one_ref[...], scaling_ref[...], total[...], 1
    )
    advance(6)
    reply_pass()
    for rest in rests:
        rest.run(4)
    pieces = [
        pltpu.make_async_copy(
            result.at[i], shared_sum.at[:, :, i * 128 : (i + 1) * 128], rest_sem.at[i]
        )
        for i in range(8)
    ]
    for piece in pieces:
        piece.start()
    own_copy(other).wait_recv()
    own_copy(col).wait_send()
    advance(7)
    small_square_begin()
    advance(8)
    reply_end()
    for turn in range(9, count + 5):
        advance(turn)
    small_end()
    pair_copy().wait_recv()
    store(expand_other, expand_lanes(other))

    def ended(block, carried):
        grad_copy(block).wait_send()
        query_copy(block, col).wait_send()
        latent_copy(block).wait_send()
        return carried

    lax.fori_loop(0, ROWS, ended, 0)
    for step in range(1, ROWS):
        turned_copy(step).wait_send()
    stat_copy(0).wait_send()
    stat_copy(1).wait_send()
    for piece in pieces:
        piece.wait()
    for copy in stores:
        copy.wait()
    pair_copy().wait_send()
    for step in range(ROWS):
        small_copy(step).wait_send()
    for one_sum in pieces_of:
        one_sum.finish()
    line_sums.finish()
    for rest in rests:
        rest.finish()
    sums.finish()
    line.finish()


def run_attention_back(
    normed_grad,
    residual,
    scale_two,
    premix,
    cotangent,
    activations,
    scale_one,
    scaling,
    one,
    query,
    key,
    value,
    probs,
    latent,
    rescale,
    tables,
    compress_all,
    queries,
    expand,
    combine,
    shared,
    more,
):
    tokens, width = activations.shape
    seq = ROWS * tokens
    mine = query.shape[2]
    lanes = key.shape[3]
    latent_width = latent.shape[2]
    sliced = (RANK + ROPE) // ROWS
    whole = pl.BlockSpec(memory_space=VMEM)
    far = pl.BlockSpec(memory_space=pl.ANY)

    def shape(*dims, dtype=bf16):
        return jax.ShapeDtypeStruct(dims, dtype)

    kept, got_x, got_y = shared
    heads = more[0].shape[2]
    own_heads = 2 * (NOPE + HEADV)
    small = (24, width)
    piece = kept.shape[1:3] + (kept.shape[3] // 2,)
    loaded = (
        combine,
        query,
        key,
        value,
        probs,
        tables[0],
        tables[1],
        queries,
        expand,
        latent,
        tables[2],
        tables[3],
        compress_all,
        one,
    )
    return pl.pallas_call(
        attend_back_kernel,
        name="attend_back",
        out_shape=(
            shape(tokens, width, dtype=f32),
            shape(tokens, width),
            shape(*small, dtype=f32),
            shape(*kept.shape[1:3], width),
            shape(4, 8, width // 32, COLS * mine),
            shape(2, 8, heads // 16, width),
            shape(8, RANK // 8, COLS * own_heads),
            shape(sliced, width),
        ),
        in_specs=[whole] * 9 + [far] * 25,
        out_specs=(whole,) * 3 + (far,) * 5,
        scratch_shapes=[
            VMEM((ROWS, tokens, width), bf16),
            VMEM((ROWS, tokens, COLS * mine), bf16),
            VMEM((ROWS, tokens, own_heads), bf16),
            VMEM((sliced, seq), bf16),
            VMEM((8, width), f32),
            VMEM((8, RANK), f32),
            *[VMEM(value.shape, value.dtype) for value in loaded],
            VMEM(kept.shape, bf16),
            VMEM(kept.shape, bf16),
            VMEM((2,) + piece, bf16),
            VMEM((2,) + piece, bf16),
            VMEM((8,) + piece, bf16),
            *[VMEM(value.shape, value.dtype) for value in more],
            VMEM((2, tokens, 128), f32),
            VMEM((2, tokens, 128), f32),
            VMEM((ROWS, tokens, 2 * HEADV), f32),
            VMEM((ROWS, tokens, 2 * HEADV), bf16),
            VMEM((ROWS, tokens, 2 * HEADV), bf16),
            VMEM((2, seq, lanes), f32),
            VMEM((2, seq, HEADV), f32),
            VMEM((ROWS, tokens, latent_width), f32),
            VMEM((ROWS, tokens, latent_width), bf16),
            VMEM((ROWS, tokens, latent_width), bf16),
            VMEM((latent_width, seq), bf16),
            VMEM((ROWS, sliced, seq // COLS), bf16),
            VMEM((ROWS, tokens, width), f32),
            VMEM((ROWS, tokens, width), bf16),
            VMEM((2, ROWS, tokens, width), bf16),
            VMEM((tokens, width), f32),
            DMA((25,)),
            DMA((2,)),
            DMA((2,)),
            *line_sems(),
            *pair_sems(),
            *pair_sems(),
            *pair_sems(),
            *pair_sems(),
            *pair_sems(),
            *sum_sems(),
            DMA((kept.shape[1], 8)),
            DMA((kept.shape[1], 8)),
            DMA((8,)),
            VMEM((ROWS, tokens, width), bf16),
            VMEM((ROWS, tokens, width), bf16),
            VMEM((2, ROWS, tokens, width), bf16),
            VMEM(small, f32),
            VMEM(small, f32),
            VMEM((ROWS,) + small, f32),
            VMEM((SQUARE,) + small, f32),
            VMEM(small, f32),
            VMEM((8, RANK // 8, own_heads), bf16),
            DMA((16,)),
            *sum_sems(),
            DMA((1,)),
            DMA((1,)),
            DMA((ROWS + SQUARE - 1,)),
            DMA((ROWS + SQUARE - 1,)),
            *square_scratch((2, heads // 16, width)),
            *square_scratch((4, width // 32, COLS * mine)),
            *square_scratch((1, RANK // 8, own_heads)),
            *square_scratch((1, sliced, width // 8)),
        ],
        compiler_params=pltpu.CompilerParams(
            collective_id=3, has_side_effects=True, vmem_limit_bytes=62 * MIB
        ),
        cost_estimate=pl.CostEstimate(
            flops=40 * 1024**3, bytes_accessed=32 * MIB, transcendentals=0
        ),
    )(
        normed_grad,
        residual,
        scale_two,
        premix.reshape(1, width),
        cotangent,
        activations,
        scale_one,
        scaling.reshape(1, width),
        rescale.reshape(1, RANK),
        *loaded,
        kept,
        got_x,
        got_y,
        *more,
    )


def silu_pair(values):
    sigmoid = 1.0 / (1.0 + jnp.exp(-values))
    return values * sigmoid, sigmoid * (1.0 + values * (1.0 - sigmoid))


def expert_kernel(
    normed_ref,
    pick_ref,
    router_ref,
    back_far,
    cot_far,
    cot_rows_ref,
    fan_ref,
    fun_ref,
    wide_ref,
    narrow_ref,
    sum_ref,
    rows_out,
    gu_out,
    hidden_out,
    shared_x,
    shared_y,
    shared_kept,
    shared_far,
    reply_ref,
    premix_ref,
    router_rows,
    gathered_ref,
    shared_out,
    back_ref,
    cot_ref,
    fan,
    fun,
    wide,
    narrow,
    cot_rows,
    rows,
    staged,
    gu,
    hidden,
    pair_own,
    pair_to,
    pair_from,
    home,
    shared_to,
    shared_from,
    part,
    passed_to,
    passed_from,
    shared_gu,
    shared_grad,
    load_sem,
    store_sem,
    line_sent,
    line_arrived,
    out_sent,
    out_arrived,
    fwd_sent,
    fwd_arrived,
    shared_sent,
    shared_arrived,
    half_sent,
    half_arrived,
    home_sent,
    home_arrived,
    sum_sent,
    sum_arrived,
    other_sent,
    other_arrived,
    reply_sent,
    reply_arrived,
    grad_sem,
    late_sem,
):
    place, row, col = lax.axis_index("dp"), lax.axis_index("row"), lax.axis_index("col")
    other = 1 - col
    inner = jnp.logical_and(row > 0, row < ROWS - 1)
    tokens, width = normed_ref.shape
    picked = pick_ref.shape[1]
    slots = picked // SQUARE
    experts = router_ref.shape[0]
    share = narrow.shape[0]
    loads = [
        pltpu.make_async_copy(source, target, load_sem.at[i])
        for i, (source, target) in enumerate(
            [
                (wide_ref, wide),
                (narrow_ref, narrow),
                (fan_ref, fan),
                (cot_rows_ref, cot_rows),
                (fun_ref, fun),
                (cot_far, cot_ref),
                (back_far, back_ref),
            ]
        )
    ]
    for load in loads:
        load.start()
    met = greet(row, place, col)
    gathered_ref[pl.ds(row, 1)] = normed_ref[...].reshape(1, tokens, width)
    staged[pl.ds(row, 1)] = (
        nn(pick_ref[row], normed_ref[...]).astype(bf16).reshape(1, picked, width)
    )
    meet(met)
    line = Line(row, gathered_ref, line_sent, line_arrived)
    line.pass_on(row)
    premix_ref[...] = jnp.zeros_like(premix_ref)
    router_rows[...] = jnp.zeros_like(router_rows)
    sums = SumLine(row, part, passed_to, passed_from, sum_sent, sum_arrived)
    sibling = {"col": other}

    def half_lines(half):
        return pl.ds(pl.multiple_of(half * width, width), width)

    def square_copy(source, target, sent, arrived, block, step):
        piece = pl.ds(step * slots, slots)
        return remote(
            source.at[block, piece],
            target.at[block, piece],
            sent.at[block, step],
            arrived.at[block, step],
            {"dp": partner(place, step)},
        )

    def out_copy(block, step):
        return square_copy(staged, rows.at[col], out_sent, out_arrived, block, step)

    def home_copy(block, step):
        return square_copy(staged, home, home_sent, home_arrived, block, step)

    def reply_copy(block, step):
        return square_copy(staged, reply_ref, reply_sent, reply_arrived, block, step)

    def keep_copy(block):
        own = pl.ds(0, slots)
        return pltpu.make_async_copy(
            staged.at[block, own], reply_ref.at[block, own], reply_arrived.at[block, 0]
        )

    def fwd_copy(block, half):
        here = rows.at[half, block]
        return remote(here, here, fwd_sent.at[block], fwd_arrived.at[block], sibling)

    def shared_copy(block):
        return remote(
            shared_to.at[block],
            shared_from.at[block],
            shared_sent.at[block],
            shared_arrived.at[block],
            sibling,
        )

    def half_copy(step):
        return remote(
            pair_to.at[lax.rem(step, 2)],
            pair_from.at[step],
            half_sent.at[step],
            half_arrived.at[step],
            sibling,
        )

    def other_copy(step):
        return remote(
            pair_to.at[lax.rem(step, 2)],
            pair_from.at[jnp.where(step == ROWS - 1, ROWS, step)],
            other_sent.at[step],
            other_arrived.at[step],
            sibling,
        )

    def stores(step):
        block = block_at(row, step)
        return [
            pltpu.make_async_copy(source, target, store_sem.at[index, step])
            for index, (source, target) in enumerate(
                [
                    (rows.at[:, block], rows_out.at[:, block]),
                    (gu.at[:, lax.rem(step, 2)], gu_out.at[:, block]),
                    (hidden.at[block], hidden_out.at[block]),
                ]
            )
        ]

    def relay(step):
        block = block_at(row, step)
        line.wait(block)
        line.pass_on(block)

    def take(step):
        block = block_at(row, step)

        @pl.when(jnp.logical_and(step > 0, jnp.logical_not(inner)))
        def _():
            relay(step)

        @pl.when(step > 0)
        def _():
            staged[block] = nn(pick_ref[block], gathered_ref[block]).astype(bf16)

        for shift in (3, 2, 1):
            out_copy(block, shift).start()
        rows[col, block, 0:slots] = staged[block, 0:slots]

    def shared_begin(step):
        block = block_at(row, step)

        @pl.when(step == 0)
        def _():
            loads[0].wait()
            loads[1].wait()
            loads[5].wait()

        for index, value in enumerate(
            (
                nt(gathered_ref[block], wide[0]),
                nt(gathered_ref[block], wide[1]),
                nt(cot_ref[block], narrow[...]),
            )
        ):
            shared_to[block, index] = value.astype(bf16)
        shared_copy(block).start()

    def forward(step):
        block = block_at(row, step)
        for shift in range(1, SQUARE):
            out_copy(block, shift).wait_recv()
        fwd_copy(block, col).start()

    def shared(step):
        block = block_at(row, step)
        shared_copy(block).wait_recv()
        gate, up, grad = [
            shared_to[block, index].astype(f32) + shared_from[block, index].astype(f32)
            for index in range(3)
        ]
        act, slope = silu_pair(gate)
        shared_out[block] = (act * up).astype(bf16)
        gate_grad = (grad * up * slope).astype(bf16)
        up_grad = (grad * act).astype(bf16)
        shared_gu[0, block] = gate_grad
        shared_gu[1, block] = up_grad
        part[block] = nn(gate_grad, wide[0]) + nn(up_grad, wide[1])

    def experts_of(step):
        block = block_at(row, step)

        @pl.when(step == 0)
        def _():
            for load in loads[2:5] + loads[6:]:
                load.wait()

        @pl.when(step > 1)
        def _():
            stores(step - 2)[1].wait()
            half_copy(step - 2).wait_send()

        fwd_copy(block, other).wait_recv()
        left, right = rows[0, block], rows[1, block]
        logits = nt(left, router_ref[:, 0:width]) + nt(right, router_ref[:, width:])
        logits = logits - jnp.max(logits, axis=1, keepdims=True)
        weight = jnp.exp(logits)
        probs = weight / jnp.sum(weight, axis=1, keepdims=True)
        own = (
            lax.broadcasted_iota(jnp.int32, (picked, experts), 1) == place * ROWS + row
        ).astype(f32)
        gates = jnp.sum(probs * own, axis=1, keepdims=True)
        raw = nt(cot_rows[0, block], fun[:, 0:width]) + nt(cot_rows[1, block], fun[:, width:])
        gate = nt(left, fan[0, :, 0:width]) + nt(right, fan[0, :, width:])
        up = nt(left, fan[1, :, 0:width]) + nt(right, fan[1, :, width:])
        act, slope = silu_pair(gate)
        value = act * up
        hidden[block] = (value * gates).astype(bf16)
        gate_sum = gates * jnp.sum(value * raw, axis=1, keepdims=True)
        logit_grad = (gate_sum * (own - probs)).astype(bf16)
        raw = raw * gates
        slot = lax.rem(step, 2)
        gu[0, slot] = (raw * up * slope).astype(bf16)
        gu[1, slot] = (raw * act).astype(bf16)

        def half_of(half):
            lines = half_lines(half)
            return (
                nn(gu[0, slot], fan[0, :, lines])
                + nn(gu[1, slot], fan[1, :, lines])
                + nn(logit_grad, router_ref[:, lines])
            )

        pair_to[slot] = half_of(other).astype(bf16)
        half_copy(step).start()
        pair_own[...] = half_of(col)
        router_rows[:, 0:width] += tn(logit_grad, left)
        router_rows[:, width:] += tn(logit_grad, right)
        for copy in stores(step):
            copy.start()

    def send_home(step):
        block = block_at(row, step)
        for shift in range(1, SQUARE):
            out_copy(block, shift).wait_send()
        half_copy(step).wait_recv()
        staged[block] = (pair_own[...] + pair_from[step].astype(f32)).astype(bf16)
        for shift in (3, 2, 1):
            home_copy(block, shift).start()
        home[block, 0:slots] = staged[block, 0:slots]

    def add_up(step):
        block = block_at(row, step)
        for shift in range(1, SQUARE):
            home_copy(block, shift).wait_recv()
        total = part[block] + nn(back_ref[block], home[block])
        part[block] = total
        premix_ref[...] += jnp.sum(
            (total * gathered_ref[block].astype(f32)).reshape(tokens // 8, 8, width), axis=0
        )
        sums.begin(block)

    def reply(step):
        block = block_at(row, step)
        slot = lax.rem(step, 2)

        @pl.when(step < 2)
        def _():
            half_copy(step + 2).wait_send()

        @pl.when(step > 1)
        def _():
            other_copy(step - 2).wait_send()

        pair_to[slot] = nn(hidden[block], fun[:, half_lines(other)]).astype(bf16)
        other_copy(step).start()

    def reply_home(step):
        block = block_at(row, step)
        own = nn(hidden[block], fun[:, half_lines(col)])
        for shift in range(1, SQUARE):
            home_copy(block, shift).wait_send()
        came = jnp.where(step == ROWS - 1, ROWS, step)
        other_copy(step).wait_recv()
        staged[block] = (own + pair_from[came].astype(f32)).astype(bf16)
        for shift in (3, 2, 1):
            reply_copy(block, shift).start()
        keep_copy(block).start()

    def turn(step, carried):
        @pl.when(jnp.logical_and(step == 2, inner))
        def _():
            relay(3)

        @pl.when(step < ROWS)
        def _():
            take(step)

        @pl.when(jnp.logical_and(step >= 1, step <= ROWS))
        def _():
            forward(step - 1)

        @pl.when(step < ROWS)
        def _():
            shared_begin(step)

        @pl.when(jnp.logical_and(step == 0, inner))
        def _():
            relay(1)
            relay(2)

        @pl.when(step >= 2)
        def _():
            shared(step - 2)
            send_home(step - 2)

        @pl.when(step == ROWS)
        def _():
            reply(0)

        @pl.when(step == ROWS + 1)
        def _():
            reply_home(0)

        @pl.when(step >= ROWS)
        def _():
            add_up(2 * step - 2 * ROWS)

        @pl.when(step == ROWS)
        def _():
            add_up(1)

        @pl.when(jnp.logical_and(step >= 1, step <= ROWS))
        def _():
            experts_of(step - 1)

        return carried

    lax.fori_loop(0, ROWS + 2, turn, 0)

    def replies(step, carried):
        @pl.when(step < ROWS)
        def _():
            reply(step)

        @pl.when(step > 1)
        def _():
            reply_home(step - 1)

        return carried

    late = [
        pltpu.make_async_copy(source, target, late_sem.at[i])
        for i, (source, target) in enumerate(
            [(shared_out, shared_far)]
        )
    ]
    for copy in late:
        copy.start()
    lax.fori_loop(1, ROWS + 1, replies, 0)
    add_up(ROWS - 1)

    def hand_on(turn, carried):
        sums.pass_on(block_at(row, jnp.where(turn == 2, 1, turn + 2)))
        return carried

    lax.fori_loop(0, ROWS - 1, hand_on, 0)

    seq = ROWS * tokens
    for index, (left, right) in enumerate(
        (
            (shared_out, cot_ref),
            (shared_gu.at[0], gathered_ref),
            (shared_gu.at[1], gathered_ref),
        )
    ):
        grad = tn(left[...].reshape(seq, share), right[...].reshape(seq, width))
        shared_grad[index] = grad.astype(bf16)
    x, y = lax.rem(place, 2), lax.div(place, 2)
    quarter = width // SQUARE
    grad_copies = []
    for index, (half, side, target) in enumerate(
        (
            (0, 1 - x, shared_x),
            (1, 1 - y, shared_y),
            (0, x, shared_kept.at[0]),
            (1, y, shared_kept.at[1]),
        )
    ):
        lanes = pl.ds(pl.multiple_of((2 * half + side) * quarter, 128), quarter)
        grad_copies.append(
            pltpu.make_async_copy(shared_grad.at[:, :, lanes], target, grad_sem.at[index])
        )
        grad_copies[index].start()
    sums.total(sum_ref)

    def ended(step, carried):
        block = block_at(row, step)
        shared_copy(block).wait_send()
        fwd_copy(block, col).wait_send()
        for shift in range(1, SQUARE):
            reply_copy(block, shift).wait_recv()
            reply_copy(block, shift).wait_send()
        keep_copy(block).wait()
        copies = stores(step)
        copies[0].wait()
        copies[2].wait()

        @pl.when(step >= ROWS - 2)
        def _():
            copies[1].wait()
            other_copy(step).wait_send()

        return carried

    lax.fori_loop(0, ROWS, ended, 0)
    for copy in grad_copies + late:
        copy.wait()
    sums.finish()
    line.finish()


def run_experts(
    normed, pick, back, cot_rows, cot_all, fan, fun, wide, narrow, router_all
):
    tokens, width = normed.shape
    picked = pick.shape[1]
    hid = fun.shape[0]
    share = narrow.shape[0]
    experts = router_all.shape[0]
    whole = pl.BlockSpec(memory_space=VMEM)
    far = pl.BlockSpec(memory_space=pl.ANY)

    def shape(*dims, dtype=bf16):
        return jax.ShapeDtypeStruct(dims, dtype)

    return pl.pallas_call(
        expert_kernel,
        name="experts",
        out_shape=(
            shape(tokens, width, dtype=f32),
            shape(COLS, ROWS, picked, width),
            shape(2, ROWS, picked, hid),
            shape(ROWS, picked, hid),
            shape(3, share, width // SQUARE),
            shape(3, share, width // SQUARE),
            shape(2, 3, share, width // SQUARE),
            shape(ROWS, tokens, share),
            shape(ROWS, picked, width),
            shape(8, width, dtype=f32),
            shape(experts, COLS * width, dtype=f32),
        ),
        in_specs=[whole] * 3 + [far] * 7,
        out_specs=(whole,) + (far,) * 8 + (whole,) * 2,
        scratch_shapes=[
            VMEM((ROWS, tokens, width), bf16),
            VMEM((ROWS, tokens, share), bf16),
            VMEM(back.shape, bf16),
            VMEM(cot_all.shape, bf16),
            VMEM(fan.shape, bf16),
            VMEM(fun.shape, bf16),
            VMEM(wide.shape, bf16),
            VMEM(narrow.shape, bf16),
            VMEM(cot_rows.shape, bf16),
            VMEM((COLS, ROWS, picked, width), bf16),
            VMEM((ROWS, picked, width), bf16),
            VMEM((2, 2, picked, hid), bf16),
            VMEM((ROWS, picked, hid), bf16),
            VMEM((picked, width), f32),
            VMEM((2, picked, width), bf16),
            VMEM((ROWS + 1, picked, width), bf16),
            VMEM((ROWS, picked, width), bf16),
            VMEM((ROWS, 3, tokens, share), bf16),
            VMEM((ROWS, 3, tokens, share), bf16),
            VMEM((ROWS, tokens, width), f32),
            VMEM((ROWS, tokens, width), bf16),
            VMEM((2, ROWS, tokens, width), bf16),
            VMEM((2, ROWS, tokens, share), bf16),
            VMEM((3, share, width), bf16),
            DMA((7,)),
            DMA((3, ROWS)),
            *line_sems(),
            *square_sems(),
            *pair_sems(),
            *pair_sems(),
            *pair_sems(),
            *square_sems(),
            *sum_sems(),
            *pair_sems(),
            *square_sems(),
            DMA((4,)),
            DMA((1,)),
        ],
        compiler_params=pltpu.CompilerParams(
            collective_id=2, has_side_effects=True, vmem_limit_bytes=62 * MIB
        ),
        cost_estimate=pl.CostEstimate(
            flops=60 * 1024**3, bytes_accessed=64 * MIB, transcendentals=0
        ),
    )(normed, pick, router_all, back, cot_all, cot_rows, fan, fun, wide, narrow)


class SquareSum:
    def __init__(self, place, part, first, second, middle, result, sent, arrived):
        self.x, self.y = lax.rem(place, 2), lax.div(place, 2)
        self.to_x, self.to_y = {"dp": partner(place, 1)}, {"dp": partner(place, 2)}
        self.part, self.first, self.second = part, first, second
        self.middle, self.result = middle, result
        self.sent, self.arrived = sent, arrived

    def copies(self, phase):
        x, y = self.x, self.y
        if phase == 0:
            plan = (
                (self.part.at[pl.ds(2 - 2 * x, 2)], self.first.at[0:2], self.to_x),
                (self.part.at[pl.ds(6 - 2 * y, 2)], self.first.at[2:4], self.to_y),
            )
        elif phase == 1:
            plan = (
                (self.middle.at[0], self.second.at[0], self.to_y),
                (self.middle.at[1], self.second.at[1], self.to_x),
            )
        elif phase == 2:
            one, two = self.result.at[2 * x + y], self.result.at[4 + 2 * y + x]
            plan = ((one, one, self.to_y), (two, two, self.to_x))
        else:
            one, two = self.result.at[pl.ds(2 * x, 2)], self.result.at[pl.ds(4 + 2 * y, 2)]
            plan = ((one, one, self.to_x), (two, two, self.to_y))
        return [
            remote(source, target, self.sent.at[2 * phase + i], self.arrived.at[2 * phase + i], to)
            for i, (source, target, to) in enumerate(plan)
        ]

    def start(self, phase):
        for copy in self.copies(phase):
            copy.start()

    def arrive(self, phase):
        for copy in self.copies(phase):
            copy.wait_recv()

    def run(self, phase):
        x, y = self.x, self.y
        if phase > 0:
            self.arrive(phase - 1)
        if phase == 1:
            for slot, piece, came in (
                (0, 2 * x + 1 - y, 1 - y),
                (1, 4 + 2 * y + 1 - x, 3 - x),
            ):
                self.middle[slot] = (
                    self.part[piece].astype(f32) + self.first[came].astype(f32)
                ).astype(bf16)
        if phase == 2:
            for slot, piece, came in ((0, 2 * x + y, y), (1, 4 + 2 * y + x, 2 + x)):
                self.result[piece] = (
                    self.part[piece].astype(f32)
                    + self.first[came].astype(f32)
                    + self.second[slot].astype(f32)
                ).astype(bf16)
        if phase < 4:
            self.start(phase)

    def finish(self):
        for phase in range(4):
            for copy in self.copies(phase):
                copy.wait_send()


def square_scratch(dims):
    count, rows, lanes = dims
    return [
        VMEM((count, 8, rows, lanes), bf16),
        VMEM((count, 4, rows, lanes), bf16),
        VMEM((count, 2, rows, lanes), bf16),
        VMEM((count, 2, rows, lanes), bf16),
        VMEM((count, 8, rows, lanes), bf16),
        DMA((count, 8)),
        DMA((count, 8)),
    ]


def write_kernel(count, plan, *refs):
    sources, targets = refs[:count], refs[count : count + len(plan)]
    rest = refs[count + len(plan) :]
    held, wide = rest[:count], rest[count : count + len(plan)]
    load_sem, store_sem = rest[count + len(plan) :]
    loads = [
        pltpu.make_async_copy(sources[i], held[i], load_sem.at[i]) for i in range(count)
    ]
    stores = [
        pltpu.make_async_copy(wide[i], targets[i], store_sem.at[i]) for i in range(len(plan))
    ]
    for load in loads:
        load.start()
    waited = set()
    for i, (source, where) in enumerate(plan):
        if source not in waited:
            loads[source].wait()
            waited.add(source)
        wide[i][...] = held[source][where].astype(wide[i].dtype)
        stores[i].start()
    for store in stores:
        store.wait()


def write_out(arrays, plan):
    far = pl.BlockSpec(memory_space=pl.ANY)
    shapes = [jax.ShapeDtypeStruct(shape, dtype) for _, _, shape, dtype in plan]
    return pl.pallas_call(
        functools.partial(
            write_kernel, len(arrays), [(source, where) for source, where, _, _ in plan]
        ),
        name="write_out",
        out_shape=shapes,
        in_specs=[far] * len(arrays),
        out_specs=[far] * len(plan),
        scratch_shapes=[
            *[VMEM(array.shape, array.dtype) for array in arrays],
            *[VMEM(shape.shape, shape.dtype) for shape in shapes],
            DMA((len(arrays),)),
            DMA((len(plan),)),
        ],
        compiler_params=pltpu.CompilerParams(vmem_limit_bytes=62 * MIB),
        cost_estimate=pl.CostEstimate(flops=0, bytes_accessed=24 * MIB, transcendentals=0),
    )(*arrays)


def product_kernel(left_ref, right_ref, out_ref, turned):
    wide = 256

    @pl.when(pl.program_id(1) == 0)
    def _():
        turned[...] = left_ref[0].T

    def one(index, carried):
        lanes = pl.ds(pl.multiple_of(index * wide, 128), wide)
        out_ref[0, :, lanes] = nn(turned[...], right_ref[0, :, lanes])
        return carried

    lax.fori_loop(0, right_ref.shape[2] // wide, one, 0)


def slot_products(left, right):
    kinds, slots, tall = left.shape
    halves, _, wide = right.shape
    return pl.pallas_call(
        product_kernel,
        name="slot_products",
        grid=(kinds, halves),
        out_shape=jax.ShapeDtypeStruct((kinds, tall, halves * wide), f32),
        in_specs=[
            pl.BlockSpec((1, slots, tall), lambda kind, half: (kind, 0, 0)),
            pl.BlockSpec((1, slots, wide), lambda kind, half: (half, 0, 0)),
        ],
        out_specs=pl.BlockSpec((1, tall, wide), lambda kind, half: (kind, 0, half)),
        scratch_shapes=[VMEM((tall, slots), bf16)],
        compiler_params=pltpu.CompilerParams(vmem_limit_bytes=40 * MIB),
        cost_estimate=pl.CostEstimate(
            flops=2 * kinds * halves * slots * tall * wide,
            bytes_accessed=4 * kinds * halves * tall * wide,
            transcendentals=0,
        ),
    )(left, right)


def local_square(
    activations,
    cotangent,
    routing,
    segments,
    scaling,
    queries,
    compress,
    rescale,
    expand,
    combine,
    premix,
    router,
    widening,
    narrowing,
    fanout,
    funnel,
):
    dp_count = lax.axis_size("dp")
    row_count = lax.axis_size("row")
    col_count = lax.axis_size("col")
    col_index = lax.axis_index("col")
    local_rows, col_width = activations.shape
    seq_length = local_rows * row_count
    expert_total = router.shape[1]
    capacity = local_rows * TOP * 4 // (3 * expert_total)
    slot_total = capacity * row_count * dp_count
    tables = turning_tables(seq_length)
    (
        one,
        query,
        key,
        value,
        probs,
        latent,
        latent_normed,
        attended,
        compress_all,
        cot_blocks,
        pick,
        back,
        cot_rows,
        residual,
        normed_two,
        scale_one,
        scale_two,
        router_all,
    ) = run_attention(
        activations,
        scaling,
        queries,
        compress,
        rescale,
        expand,
        combine,
        premix,
        segments,
        cotangent,
        routing,
        router,
        tables,
        capacity,
    )
    (
        normed_grad,
        expert_rows,
        expert_gu_grad,
        expert_hidden,
        shared_x,
        shared_y,
        shared_kept,
        hidden_blocks,
        reply_blocks,
        premix_rows,
        router_rows,
    ) = run_experts(
        normed_two,
        pick,
        back,
        cot_rows,
        cot_blocks,
        fanout[0].transpose(0, 2, 1),
        funnel[0],
        widening.transpose(0, 2, 1),
        narrowing,
        router_all,
    )
    slot_rows = expert_rows.reshape(col_count, slot_total, col_width)
    reply_grad_rows = cot_rows.reshape(col_count, slot_total, col_width)
    slot_hidden = expert_hidden.reshape(slot_total, -1)
    slot_gu_grad = expert_gu_grad.reshape(2, slot_total, -1)
    got_x = lax.ppermute(shared_x, "dp", [(i, i ^ 1) for i in range(SQUARE)])
    got_y = lax.ppermute(shared_y, "dp", [(i, i ^ 2) for i in range(SQUARE)])
    fanout_grad = slot_products(slot_gu_grad, slot_rows)
    funnel_grad = slot_products(slot_hidden[None], reply_grad_rows)
    normed_grad, fanout_grad, funnel_grad = lax.optimization_barrier(
        (normed_grad, fanout_grad, funnel_grad)
    )
    (
        input_grad,
        layer_output,
        small,
        shared_sum,
        queries_sum,
        combine_sum,
        expand_sum,
        compress_sum,
    ) = run_attention_back(
        normed_grad,
        residual,
        scale_two,
        premix,
        cotangent,
        activations,
        scale_one,
        scaling,
        one,
        query,
        key,
        value,
        probs,
        latent,
        rescale,
        tables,
        compress_all,
        queries,
        expand,
        combine,
        (shared_kept, got_x, got_y),
        (
            attended,
            latent_normed,
            narrowing,
            reply_blocks,
            back,
            hidden_blocks,
            premix_rows,
            router_rows,
        ),
    )
    everything = slice(None)
    share = narrowing.shape[0]
    (
        widening_grad,
        narrowing_grad,
        queries_grad,
        combine_grad,
        expand_grad,
        compress_grad,
        input_grad,
        layer_output,
        router_grad,
        premix_grad,
        scaling_grad,
        rescale_grad,
    ) = write_out(
        (
            shared_sum,
            queries_sum.reshape(queries.shape),
            combine_sum.reshape(combine.shape),
            expand_sum.reshape(expand.shape),
            compress_sum,
            input_grad,
            layer_output,
            small,
        ),
        (
            (0, slice(1, 3), (2, share, col_width), f32),
            (0, 0, (share, col_width), f32),
            (1, everything, queries.shape, f32),
            (2, everything, combine.shape, f32),
            (3, everything, expand.shape, f32),
            (4, everything, compress_sum.shape, f32),
            (5, everything, input_grad.shape, f32),
            (6, everything, layer_output.shape, bf16),
            (7, slice(0, expert_total), (expert_total, col_width), f32),
            (7, slice(expert_total, expert_total + 1), (1, col_width), f32),
            (7, slice(expert_total + 1, expert_total + 2), (1, col_width), f32),
            (7, (slice(expert_total + 2, expert_total + 3), slice(0, RANK)), (1, RANK), f32),
        ),
    )
    return (
        layer_output,
        input_grad,
        scaling_grad.reshape(col_width),
        queries_grad,
        compress_grad.T,
        rescale_grad.reshape(RANK),
        expand_grad,
        combine_grad,
        premix_grad.reshape(col_width),
        router_grad.T,
        widening_grad.transpose(0, 2, 1),
        narrowing_grad,
        fanout_grad.transpose(0, 2, 1)[None],
        funnel_grad,
    )


def local(
    activations,
    cotangent,
    routing,
    segments,
    scaling,
    queries,
    compress,
    rescale,
    expand,
    combine,
    premix,
    router,
    widening,
    narrowing,
    fanout,
    funnel,
):
    dp_count = lax.axis_size("dp")
    row_count = lax.axis_size("row")
    col_count = lax.axis_size("col")
    dp_index = lax.axis_index("dp")
    row_index = lax.axis_index("row")
    col_index = lax.axis_index("col")
    local_rows = activations.shape[0]
    col_width = activations.shape[1]
    seq_length = local_rows * row_count
    half_length = seq_length // col_count
    head_width = NOPE + ROPE
    pair_width = NOPE + HEADV
    local_heads = queries.shape[1] // head_width
    slice_width = compress.shape[1]
    expert_total = router.shape[1]
    capacity = local_rows * TOP * 4 // (3 * expert_total)
    slots = capacity * row_count
    slot_total = slots * dp_count
    block_rows = min(512, half_length)
    block_count = half_length // block_rows
    score_scale = head_width ** (-0.5)

    inputs = activations.astype(f32)
    scale_one = norm_scale(inputs)
    normed_one = (inputs * scale_one[:, None] * scaling).astype(bf16)
    gathered_one = row_gather(normed_one)
    compress_all = lax.all_gather(compress, "row", axis=1, tiled=True)

    routing_all = row_gather(routing)
    cotangent_all = row_gather(after(cotangent, gathered_one))
    offsets = jnp.arange(dp_count, dtype=jnp.int32)
    my_experts = ((dp_index + offsets) % dp_count) * row_count + row_index
    goes = jnp.any(routing_all[None, :, :] == my_experts[:, None, None], axis=2)
    token_range = jnp.arange(seq_length, dtype=jnp.int32)
    earlier = (token_range[:, None] < token_range[None, :]).astype(bf16)
    rank = dot(goes.astype(bf16), earlier).astype(jnp.int32)
    slot_range = jnp.arange(slots, dtype=jnp.int32)
    pick = (
        ((rank[:, None, :] == slot_range[None, :, None]) & goes[:, None, :])
        .astype(bf16)
        .reshape(slot_total, seq_length)
    )

    def dispatch(tokens):
        rows = dot(pick, tokens).astype(bf16).reshape(dp_count, slots, col_width)
        arrived = send_out([rows[k] for k in range(dp_count)])
        return col_gather(jnp.concatenate(arrived, axis=0), axis=1)

    def bring_back(part):
        summed = col_scatter(part.astype(bf16), axis=1).reshape(dp_count, slots, col_width)
        arrived = send_back([summed[k] for k in range(dp_count)])
        return dot_tn(pick, jnp.concatenate(arrived, axis=0))

    query_part = dot(gathered_one, queries)
    latent_part = dot(gathered_one, compress_all)
    query_raw, latent_raw = col_scatter((query_part, latent_part))
    latent_plain = latent_raw[:, :RANK]
    latent_scale = lax.rsqrt(jnp.mean(latent_plain * latent_plain, axis=1) + epsilon)
    latent_normed = (latent_plain * latent_scale[:, None] * rescale).astype(bf16)
    expanded = dot(latent_normed, expand).reshape(half_length, local_heads, pair_width)
    positions = col_index * half_length + jnp.arange(half_length, dtype=jnp.int32)
    cosine, sine_table = rotation(positions, ROPE)
    key_shared = rotate(latent_raw[:, RANK:], cosine, sine_table, 1.0)
    query_heads = query_raw.reshape(half_length, local_heads, head_width)
    query_local = jnp.concatenate(
        [
            query_heads[..., :NOPE],
            rotate(query_heads[..., NOPE:], cosine[:, None, :], sine_table[:, None, :], 1.0),
        ],
        axis=2,
    ).astype(bf16)
    key_local = jnp.concatenate(
        [
            expanded[..., :NOPE],
            jnp.broadcast_to(key_shared[:, None, :], (half_length, local_heads, ROPE)),
        ],
        axis=2,
    ).astype(bf16)
    value_local = expanded[..., NOPE:].astype(bf16)
    key_flat, value_flat = (
        col_gather(key_local.reshape(half_length, local_heads * head_width)),
        col_gather(value_local.reshape(half_length, local_heads * HEADV)),
    )
    key_heads = key_flat.reshape(seq_length, local_heads, head_width)
    value_heads = value_flat.reshape(seq_length, local_heads, HEADV)
    own_segments = lax.dynamic_slice_in_dim(
        segments, col_index * half_length, half_length, 0
    ).reshape(block_count, block_rows)
    query_blocks = query_local.reshape(block_count, block_rows, local_heads, head_width)

    def attend_block(inputs_block):
        query_block, segment_block = inputs_block
        scores = (
            jnp.einsum("qhd,khd->hqk", query_block, key_heads, preferred_element_type=f32)
            * score_scale
        )
        visible = segments[None, None, :] <= segment_block[None, :, None]
        scores = jnp.where(visible, scores, masked_score)
        largest = jnp.max(scores, axis=2, keepdims=True)
        weight = jnp.exp(scores - largest)
        totals = jnp.sum(weight, axis=2, keepdims=True)
        probability = (weight / totals).astype(bf16)
        result = jnp.einsum("hqk,khd->qhd", probability, value_heads, preferred_element_type=f32)
        return (result.astype(bf16), (largest + jnp.log(totals))[..., 0])

    attended_blocks, log_totals = lax.map(attend_block, (query_blocks, own_segments))
    attended = attended_blocks.reshape(half_length, local_heads * HEADV)
    attended_all = col_gather(attended)
    branch = row_scatter(dot(attended_all, combine))

    reply_grad_rows = dispatch(cotangent_all)
    inner_weight = fanout[0]
    outer_weight = funnel[0]
    hidden_raw = dot_nt(reply_grad_rows, outer_weight)
    shared_hidden_grad = col_scatter(dot_nt(cotangent_all, narrowing))

    residual = inputs + branch
    scale_two = norm_scale(residual)
    normed_two = (residual * scale_two[:, None] * premix).astype(bf16)
    gathered_two = row_gather(normed_two)

    expert_rows = dispatch(gathered_two)
    expert_range = jnp.arange(expert_total, dtype=jnp.int32)
    router_all = lax.all_gather(router, "col", axis=0, tiled=True)
    own_expert = dp_index * row_count + row_index
    slot_probs = jax.nn.softmax(dot(expert_rows, router_all), axis=1)
    slot_gates = jnp.sum(jnp.where(expert_range == own_expert, slot_probs, 0.0), axis=1)
    gate_up = jnp.einsum("rd,gdf->grf", expert_rows, inner_weight, preferred_element_type=f32)
    gate_input, up_input = gate_up[0], gate_up[1]
    hidden = jax.nn.silu(gate_input) * up_input
    expert_hidden = hidden.astype(bf16)
    slot_gate_grad = col_totals(jnp.sum(hidden * hidden_raw, axis=1))
    hidden_grad = hidden_raw * slot_gates[:, None]
    expert_gu_grad = jnp.stack(
        [hidden_grad * up_input * silu_slope(gate_input), hidden_grad * jax.nn.silu(gate_input)]
    ).astype(bf16)
    input_part = jnp.einsum(
        "grf,gdf->rd", expert_gu_grad, inner_weight, preferred_element_type=f32
    )
    routed_grad = bring_back(input_part)
    gate_grad_parts = send_back(
        [slot_gate_grad.reshape(dp_count, slots)[k] for k in range(dp_count)]
    )

    logits = col_totals(dot(gathered_two, router))
    router_probs = jax.nn.softmax(logits, axis=1)
    gate_grad = jnp.sum(
        pick.reshape(dp_count, slots, seq_length).astype(f32)
        * jnp.stack(gate_grad_parts)[:, :, None],
        axis=1,
    )
    mine = (my_experts[:, None] == expert_range[None, :]).astype(f32)
    probs_grad = jnp.sum(gate_grad[:, :, None] * mine[:, None, :], axis=0)
    logit_grad = router_probs * (
        probs_grad - jnp.sum(router_probs * probs_grad, axis=1, keepdims=True)
    )
    router_part = dot_tn(gathered_two, logit_grad)

    shared_gate_up = col_scatter(
        jnp.einsum("td,gdf->tgf", gathered_two, widening, preferred_element_type=f32)
    )
    shared_hidden = (jax.nn.silu(shared_gate_up[:, 0]) * shared_gate_up[:, 1]).astype(bf16)
    hidden_all = col_gather(shared_hidden)
    narrowing_grad = dot_tn(hidden_all, cotangent_all)
    shared_gu_grad = jnp.stack(
        [
            shared_hidden_grad * shared_gate_up[:, 1] * silu_slope(shared_gate_up[:, 0]),
            shared_hidden_grad * jax.nn.silu(shared_gate_up[:, 0]),
        ],
        axis=1,
    ).astype(bf16)
    gu_grad_all = col_gather(shared_gu_grad)
    widening_grad = jnp.einsum(
        "td,tgf->gdf", gathered_two, gu_grad_all, preferred_element_type=f32
    )
    shared_input_part = jnp.einsum(
        "tgf,gdf->td", gu_grad_all, widening, preferred_element_type=f32
    )
    shared_sums = lax.psum((narrowing_grad.astype(bf16), widening_grad.astype(bf16)), "dp")

    grad_part = routed_grad + shared_input_part + dot_nt(logit_grad, router)
    premix_part = jnp.sum(grad_part * gathered_two.astype(f32), axis=0) / premix
    normed_grad = row_scatter(grad_part)

    upstream = cotangent.astype(f32)
    residual_grad = upstream + norm_back(residual, scale_two, premix, normed_grad)
    branch_all = row_gather(residual_grad.astype(bf16))

    funnel_grad = dot_tn((hidden * slot_gates[:, None]).astype(bf16), reply_grad_rows)[None]
    fanout_grad = jnp.einsum(
        "rd,grf->gdf", expert_rows, expert_gu_grad, preferred_element_type=f32
    )[None]
    reply_part = dot(expert_hidden, outer_weight) * slot_gates[:, None]
    routed = bring_back(reply_part)
    shared_out = row_scatter(routed + dot(hidden_all, narrowing))
    layer_output = (residual + shared_out).astype(bf16)

    combine_grad = dot_tn(attended_all, branch_all)
    combine_sum = lax.psum(after(combine_grad.astype(bf16), *shared_sums), "dp")
    attended_grad = col_scatter(dot_nt(branch_all, combine))
    attended_grad_blocks = attended_grad.astype(bf16).reshape(
        block_count, block_rows, local_heads, HEADV
    )

    def attend_back(carried, inputs_block):
        key_sum, value_sum = carried
        query_block, grad_block, log_block, segment_block = inputs_block
        scores = (
            jnp.einsum("qhd,khd->hqk", query_block, key_heads, preferred_element_type=f32)
            * score_scale
        )
        visible = segments[None, None, :] <= segment_block[None, :, None]
        probability = jnp.where(visible, jnp.exp(scores - log_block[..., None]), 0.0)
        weight_grad = jnp.einsum(
            "qhd,khd->hqk", grad_block, value_heads, preferred_element_type=f32
        )
        inner_sum = jnp.sum(probability * weight_grad, axis=2, keepdims=True)
        score_grad = (probability * (weight_grad - inner_sum)).astype(bf16)
        query_grad_block = (
            jnp.einsum("hqk,khd->qhd", score_grad, key_heads, preferred_element_type=f32)
            * score_scale
        )
        key_sum = (
            key_sum
            + jnp.einsum("hqk,qhd->khd", score_grad, query_block, preferred_element_type=f32)
            * score_scale
        )
        value_sum = value_sum + jnp.einsum(
            "hqk,qhd->khd", probability.astype(bf16), grad_block, preferred_element_type=f32
        )
        return ((key_sum, value_sum), query_grad_block)

    key_start = jnp.zeros((seq_length, local_heads, head_width), f32)
    value_start = jnp.zeros((seq_length, local_heads, HEADV), f32)
    (key_grad_all, value_grad_all), query_grad_blocks = lax.scan(
        attend_back,
        (key_start, value_start),
        (query_blocks, attended_grad_blocks, log_totals, own_segments),
    )
    key_grad, value_grad = col_scatter(
        (
            key_grad_all.reshape(seq_length, local_heads * head_width),
            value_grad_all.reshape(seq_length, local_heads * HEADV),
        )
    )
    key_grad = key_grad.reshape(half_length, local_heads, head_width)
    value_grad = value_grad.reshape(half_length, local_heads, HEADV)
    query_grad = query_grad_blocks.reshape(half_length, local_heads, head_width)
    query_raw_grad = (
        jnp.concatenate(
            [
                query_grad[..., :NOPE],
                rotate(query_grad[..., NOPE:], cosine[:, None, :], sine_table[:, None, :], -1.0),
            ],
            axis=2,
        )
        .astype(bf16)
        .reshape(half_length, local_heads * head_width)
    )
    expanded_grad = (
        jnp.concatenate([key_grad[..., :NOPE], value_grad], axis=2)
        .astype(bf16)
        .reshape(half_length, local_heads * pair_width)
    )
    shared_rope_grad = rotate(jnp.sum(key_grad[..., NOPE:], axis=1), cosine, sine_table, -1.0)

    latent_grad = dot_nt(expanded_grad, expand)
    latent_weighted = latent_grad * rescale
    latent_inner = jnp.mean(latent_weighted * latent_plain, axis=1)
    rescale_part = jnp.sum(latent_grad * latent_plain * latent_scale[:, None], axis=0)
    plain_grad = (
        latent_weighted * latent_scale[:, None]
        - latent_plain * (latent_scale**3 * latent_inner)[:, None]
    )
    latent_raw_grad = jnp.concatenate([plain_grad, shared_rope_grad], axis=1).astype(bf16)
    query_grad_all = col_gather(query_raw_grad)
    latent_grad_all = col_gather(latent_raw_grad)
    first_part = dot_nt(query_grad_all, queries) + dot_nt(latent_grad_all, compress_all)
    first_grad = row_scatter(first_part)
    input_grad = residual_grad + norm_back(inputs, scale_one, scaling, first_grad)

    queries_part = dot_tn(gathered_one, query_grad_all)
    own_latent_grad = lax.psum_scatter(
        latent_raw_grad, "row", scatter_dimension=1, tiled=True
    )
    compress_part = dot_tn(gathered_one, col_gather(own_latent_grad))
    half_rank = RANK // col_count
    latent_normed_all = col_gather(latent_normed)
    expanded_grad_all = col_gather(expanded_grad)
    expand_half = dot_tn(
        lax.dynamic_slice_in_dim(latent_normed_all, col_index * half_rank, half_rank, 1),
        expanded_grad_all,
    )
    scaling_part = jnp.sum(first_part * gathered_one.astype(f32), axis=0) / scaling
    queries_sum, expand_sum, compress_sum = lax.psum(
        (
            after(queries_part.astype(bf16), combine_sum),
            expand_half.astype(bf16),
            compress_part.astype(bf16),
        ),
        "dp",
    )
    premix_sum, router_sum = lax.psum((premix_part, router_part), ("dp", "row"))
    rescale_sum = lax.psum(rescale_part, ("dp", "row", "col"))
    scaling_sum = lax.psum(scaling_part, ("dp", "row"))
    return (
        layer_output,
        input_grad,
        scaling_sum,
        queries_sum.astype(f32),
        compress_sum.astype(f32),
        rescale_sum,
        col_gather(expand_sum).astype(f32),
        combine_sum.astype(f32),
        premix_sum,
        router_sum,
        shared_sums[1].astype(f32),
        shared_sums[0].astype(f32),
        fanout_grad,
        funnel_grad,
    )


def solution(mesh):
    placed = (
        P(("dp", "row"), "col"),
        P(("dp", "row"), "col"),
        P(("dp", "row"), None),
        P("dp"),
        P("col"),
        P("col", "row"),
        P("col", "row"),
        P(),
        P(None, "row"),
        P("row", "col"),
        P("col"),
        P("col", None),
        P(None, "col", "row"),
        P("row", "col"),
        P(("dp", "row"), None, None, "col"),
        P(("dp", "row"), "col", None),
    )
    squared = mesh.shape["dp"] == SQUARE and mesh.shape["row"] == ROWS
    return jax.shard_map(
        local_square if squared else local,
        mesh=mesh,
        in_specs=placed,
        out_specs=(
            P(("dp", "row"), "col"),
            P(("dp", "row"), "col"),
            P("col"),
            P("col", "row"),
            P("col", "row"),
            P(),
            P(None, "row"),
            P("row", "col"),
            P("col"),
            P("col", None),
            P(None, "col", "row"),
            P("row", "col"),
            P(("dp", "row"), None, None, "col"),
            P(("dp", "row"), "col", None),
        ),
        check_vma=False,
    )
```

```python
import functools

import jax
import jax.numpy as jnp
import numpy as np
from jax import lax
from jax.experimental import pallas as pl
from jax.experimental.pallas import tpu as pltpu
from jax.sharding import PartitionSpec as P

D = 2048
NOPE = 128
ROPE = 64
HEADV = 128
RANK = 512
TOP = 6


epsilon = 1e-06
masked_score = -1e30
f32 = jnp.float32
bf16 = jnp.bfloat16


def after(value, *earlier):
    return lax.optimization_barrier((value,) + earlier)[0]


def silu_slope(values):
    sigmoid = jax.nn.sigmoid(values)
    return sigmoid * (1.0 + values * (1.0 - sigmoid))


def rotation(positions, rope_width):
    half_width = rope_width // 2
    frequency = 10000.0 ** (-jnp.arange(half_width, dtype=jnp.float32) * 2.0 / rope_width)
    angles = positions.astype(jnp.float32)[:, None] * frequency[None, :]
    return (jnp.cos(angles), jnp.sin(angles))


def rotate(values, cosine, sine_table, direction):
    half_width = values.shape[-1] // 2
    first_half = values[..., :half_width]
    second_half = values[..., half_width:]
    return jnp.concatenate(
        [
            first_half * cosine - direction * second_half * sine_table,
            second_half * cosine + direction * first_half * sine_table,
        ],
        axis=-1,
    )


def dot(left, right):
    return jnp.dot(left, right, preferred_element_type=f32)


def dot_tn(left, right):
    return lax.dot_general(left, right, (((0,), (0,)), ((), ())), preferred_element_type=f32)


def dot_nt(left, right):
    return lax.dot_general(left, right, (((1,), (1,)), ((), ())), preferred_element_type=f32)


def col_totals(values):
    return lax.psum(values, "col")


def row_gather(values):
    return lax.all_gather(values, "row", axis=0, tiled=True)


def col_gather(values, axis=0):
    return lax.all_gather(values, "col", axis=axis, tiled=True)


def col_scatter(values, axis=0):
    return lax.psum_scatter(values, "col", scatter_dimension=axis, tiled=True)


def row_scatter(values):
    return lax.psum_scatter(
        values.astype(bf16), "row", scatter_dimension=0, tiled=True
    ).astype(f32)


def send_out(parts):
    count = len(parts)
    return [parts[0]] + [
        lax.ppermute(parts[k], "dp", [(i, (i + k) % count) for i in range(count)])
        for k in range(1, count)
    ]


def send_back(parts):
    count = len(parts)
    return [parts[0]] + [
        lax.ppermute(parts[k], "dp", [(i, (i - k) % count) for i in range(count)])
        for k in range(1, count)
    ]


def norm_scale(values):
    square_sum = col_totals(jnp.sum(values * values, axis=1))
    return lax.rsqrt(square_sum / D + epsilon)


def norm_back(values, row_scale, gain_vector, upstream):
    weighted = upstream * gain_vector
    inner_mean = col_totals(jnp.sum(weighted * values, axis=1)) / D
    return weighted * row_scale[:, None] - values * (row_scale**3 * inner_mean)[:, None]


MESH = pl.DeviceIdType.MESH
VMEM = pltpu.VMEM
DMA = pltpu.SemaphoreType.DMA
MIB = 1024 * 1024
ROWS = 4
SQUARE = 4
COLS = 2
SPLIT = 2


def nn(left, right):
    return lax.dot_general(left, right, (((1,), (0,)), ((), ())), preferred_element_type=f32)


def tn(left, right):
    return lax.dot_general(left, right, (((0,), (0,)), ((), ())), preferred_element_type=f32)


def nt(left, right):
    return lax.dot_general(left, right, (((1,), (1,)), ((), ())), preferred_element_type=f32)


def block_at(row, turn):
    swapped = jnp.where(turn < 2, 1 - turn, turn)
    inner = jnp.logical_or(row == 1, row == 2)
    near = jnp.where(inner, swapped, turn)
    return jnp.where(row < 2, near, ROWS - 1 - near)


def partner(place, step):
    across, along = lax.rem(place, 2), lax.div(place, 2)
    across = lax.rem(across + step % 2, 2)
    along = lax.rem(along + step // 2, 2)
    return along * 2 + across


def beside(row, way):
    return lax.rem(row + ROWS + 1 - 2 * way, ROWS)


def remote(source, target, sent, arrived, where):
    return pltpu.make_async_remote_copy(
        src_ref=source,
        dst_ref=target,
        send_sem=sent,
        recv_sem=arrived,
        device_id=where,
        device_id_type=MESH,
    )


def greet(row, place, col, line=False, square=True):
    barrier = pltpu.get_barrier_semaphore()
    met = 1
    if line:
        for step in range(1, ROWS):
            pl.semaphore_signal(
                barrier,
                inc=1,
                device_id={"row": lax.rem(row + step, ROWS)},
                device_id_type=MESH,
            )
        met = met + ROWS - 1
    else:

        @pl.when(row > 0)
        def _():
            pl.semaphore_signal(barrier, inc=1, device_id={"row": row - 1}, device_id_type=MESH)

        @pl.when(row < ROWS - 1)
        def _():
            pl.semaphore_signal(barrier, inc=1, device_id={"row": row + 1}, device_id_type=MESH)

        met = met + (row > 0).astype(jnp.int32) + (row < ROWS - 1).astype(jnp.int32)
    if square:
        for step in range(1, SQUARE):
            pl.semaphore_signal(
                barrier, inc=1, device_id={"dp": partner(place, step)}, device_id_type=MESH
            )
        met = met + SQUARE - 1
    pl.semaphore_signal(barrier, inc=1, device_id={"col": 1 - col}, device_id_type=MESH)
    return met


def meet(met):
    pl.semaphore_wait(pltpu.get_barrier_semaphore(), met)


class Line:
    def __init__(self, row, buffer, sent, arrived):
        self.row, self.buffer, self.sent, self.arrived = row, buffer, sent, arrived

    def copy(self, block, way):
        here = self.buffer.at[block]
        to = {"row": beside(self.row, way)}
        return remote(here, here, self.sent.at[block, way], self.arrived.at[block], to)

    def each(self, block, act):
        @pl.when(jnp.logical_and(block <= self.row, self.row < ROWS - 1))
        def _():
            act(self.copy(block, 0))

        @pl.when(jnp.logical_and(block >= self.row, self.row > 0))
        def _():
            act(self.copy(block, 1))

    def wait(self, block):
        self.copy(block, 0).wait_recv()

    def pass_on(self, block):
        self.each(block, lambda copy: copy.start())

    def finish(self):
        def one(block, carried):
            self.each(block, lambda copy: copy.wait_send())
            return carried

        lax.fori_loop(0, ROWS, one, 0)


class SquareRest:
    def __init__(self, place, which, kept, got, middle, second, result, sent, arrived):
        self.x, self.y, self.which = lax.rem(place, 2), lax.div(place, 2), which
        self.to_x, self.to_y = {"dp": partner(place, 1)}, {"dp": partner(place, 2)}
        self.kept, self.got = kept, got
        self.middle, self.second, self.result = middle, second, result
        self.sent, self.arrived = sent.at[which], arrived.at[which]

    def copies(self, phase):
        x, y, which = self.x, self.y, self.which
        if phase == 1:
            plan = (
                (self.middle.at[0, which], self.second.at[0, which], self.to_y),
                (self.middle.at[1, which], self.second.at[1, which], self.to_x),
            )
        elif phase == 2:
            one = self.result.at[2 * x + y, which]
            two = self.result.at[4 + 2 * y + x, which]
            plan = ((one, one, self.to_y), (two, two, self.to_x))
        else:
            one = self.result.at[pl.ds(2 * x, 2), which]
            two = self.result.at[pl.ds(4 + 2 * y, 2), which]
            plan = ((one, one, self.to_x), (two, two, self.to_y))
        return [
            remote(source, target, self.sent.at[2 * phase + i], self.arrived.at[2 * phase + i], to)
            for i, (source, target, to) in enumerate(plan)
        ]

    def sum_of(self, half, side):
        wide = self.middle.shape[3]
        lanes = pl.ds(pl.multiple_of(side * wide, 128), wide)
        which = self.which
        kept, got = self.kept[half, which, :, lanes], self.got[half, which, :, lanes]
        return kept.astype(f32) + got.astype(f32)

    def prepare(self):
        self.middle[0, self.which] = self.sum_of(0, 1 - self.y).astype(bf16)
        self.middle[1, self.which] = self.sum_of(1, 1 - self.x).astype(bf16)

    def run(self, phase):
        x, y, which = self.x, self.y, self.which
        if phase > 1:
            for copy in self.copies(phase - 1):
                copy.wait_recv()
        if phase == 2:
            self.result[2 * x + y, which] = (
                self.sum_of(0, y) + self.second[0, which].astype(f32)
            ).astype(bf16)
            self.result[4 + 2 * y + x, which] = (
                self.sum_of(1, x) + self.second[1, which].astype(f32)
            ).astype(bf16)
        if phase < 4:
            for copy in self.copies(phase):
                copy.start()

    def finish(self):
        for phase in (1, 2, 3):
            for copy in self.copies(phase):
                copy.wait_send()


class SumLine:
    def __init__(self, row, part, leaving, coming, sent, arrived):
        self.row, self.part, self.leaving, self.coming = row, part, leaving, coming
        self.sent, self.arrived = sent, arrived
        self.lines = part.shape[1] // SPLIT

    def piece(self, index):
        return pl.ds(index * self.lines, self.lines)

    def copy(self, block, index, way):
        return remote(
            self.leaving.at[block, self.piece(index)],
            self.coming.at[way, block, self.piece(index)],
            self.sent.at[block, index],
            self.arrived.at[way, block, index],
            {"row": beside(self.row, way)},
        )

    def send(self, block, index):
        @pl.when(block > self.row)
        def _():
            self.copy(block, index, 0).start()

        @pl.when(block < self.row)
        def _():
            self.copy(block, index, 1).start()

    def chained(self, block):
        return jnp.logical_or(
            jnp.logical_and(block > self.row, self.row > 0),
            jnp.logical_and(block < self.row, self.row < ROWS - 1),
        )

    def begin(self, block):
        @pl.when(jnp.logical_and(block != self.row, jnp.logical_not(self.chained(block))))
        def _():
            self.leaving[block] = self.part[block].astype(bf16)
            for index in range(SPLIT):
                self.send(block, index)

    def pass_on(self, block):
        @pl.when(self.chained(block))
        def _():
            way = (block < self.row).astype(jnp.int32)
            for index in range(SPLIT):
                self.copy(block, index, way).wait_recv()
                piece = self.piece(index)
                self.leaving[block, piece] = (
                    self.part[block, piece].astype(f32)
                    + self.coming[way, block, piece].astype(f32)
                ).astype(bf16)
                self.send(block, index)

    def total(self, target):
        target[...] = self.part[self.row].astype(f32)
        for way, there in ((0, self.row > 0), (1, self.row < ROWS - 1)):

            @pl.when(there)
            def _(way=way):
                for index in range(SPLIT):
                    self.copy(self.row, index, way).wait_recv()
                    target[self.piece(index)] += self.coming[
                        way, self.row, self.piece(index)
                    ].astype(f32)

    def finish(self):
        def one(block, carried):
            @pl.when(block != self.row)
            def _():
                for index in range(SPLIT):
                    self.copy(block, index, 0).wait_send()

            return carried

        lax.fori_loop(0, ROWS, one, 0)


def swap_halves(values):
    lanes = values.shape[1]
    lane = lax.broadcasted_iota(jnp.int32, values.shape, 1)
    return jnp.where(
        lane % ROPE < ROPE // 2,
        pltpu.roll(values, lanes - ROPE // 2, 1),
        pltpu.roll(values, ROPE // 2, 1),
    )


def attend_kernel(
    act_ref,
    scaling_ref,
    compress_ref,
    rescale_ref,
    premix_ref,
    mark_ref,
    cot_ref,
    route_ref,
    router_ref,
    queries_ref,
    expand_ref,
    combine_ref,
    cos_far,
    sin_far,
    key_cos_far,
    key_sin_far,
    one_out,
    query_out,
    key_out,
    value_out,
    probs_out,
    latent_out,
    normed_latent_out,
    attended_out,
    compress_out,
    cot_out,
    pick_out,
    back_out,
    rows_out,
    residual_ref,
    two_ref,
    scale_one_ref,
    scale_two_ref,
    router_all,
    one_ref,
    query_ref,
    key_ref,
    value_ref,
    probs_ref,
    latent_ref,
    normed_latent_ref,
    attended_ref,
    compress_all,
    cot_all,
    pick_ref,
    back_ref,
    rows_ref,
    queries,
    expand,
    combine,
    cos_ref,
    sin_ref,
    key_cos_ref,
    key_sin_ref,
    stat_to,
    stat_from,
    query_own,
    query_to,
    query_from,
    latent_to,
    latent_from,
    part,
    leaving,
    coming,
    routes,
    staged,
    marks,
    raw,
    scales,
    load_sem,
    store_sem,
    rows_sem,
    stat_sent,
    stat_arrived,
    line_sent,
    line_arrived,
    comp_sent,
    comp_arrived,
    comp_out_sent,
    comp_out_arrived,
    query_sent,
    query_arrived,
    latent_sent,
    latent_arrived,
    att_sent,
    att_arrived,
    sum_sent,
    sum_arrived,
    cot_sent,
    cot_arrived,
    route_sent,
    route_arrived,
    out_sent,
    out_arrived,
    pair_sent,
    pair_arrived,
    router_sent,
    router_arrived,
    scale_sent,
    scale_arrived,
):
    place, row, col = lax.axis_index("dp"), lax.axis_index("row"), lax.axis_index("col")
    other = 1 - col
    inner = jnp.logical_and(row > 0, row < ROWS - 1)
    sibling = {"col": other}
    tokens, width = act_ref.shape
    slots = pick_ref.shape[1] // SQUARE
    mine = query_own.shape[2]
    sliced = compress_ref.shape[0]
    quarter = width // SQUARE
    score_scale = (NOPE + ROPE) ** (-0.5)
    loads = [
        pltpu.make_async_copy(source, target, load_sem.at[i])
        for i, (source, target) in enumerate(
            [
                (queries_ref, queries),
                (expand_ref, expand),
                (combine_ref, combine),
                (cos_far, cos_ref),
                (sin_far, sin_ref),
                (key_cos_far, key_cos_ref),
                (key_sin_far, key_sin_ref),
            ]
        )
    ]
    for load in loads:
        load.start()
    stores = [
        pltpu.make_async_copy(source, target, store_sem.at[i])
        for i, (source, target) in enumerate(
            [
                (one_ref, one_out),
                (query_ref, query_out),
                (key_ref, key_out),
                (value_ref, value_out),
                (latent_ref, latent_out),
                (normed_latent_ref, normed_latent_out),
                (compress_all, compress_out),
                (probs_ref, probs_out),
                (attended_ref, attended_out),
                (cot_all, cot_out),
                (pick_ref, pick_out),
                (back_ref, back_out),
            ]
        )
    ]

    def rows_store(block):
        return pltpu.make_async_copy(
            rows_ref.at[:, block], rows_out.at[:, block], rows_sem.at[block]
        )

    def stat_copy(index):
        return remote(
            stat_to.at[index],
            stat_from.at[index],
            stat_sent.at[index],
            stat_arrived.at[index],
            sibling,
        )

    def scale_of(values, index):
        own = jnp.sum(values * values, axis=1, keepdims=True)
        stat_to[index] = jnp.broadcast_to(own, (tokens, 128))
        stat_copy(index).start()
        stat_copy(index).wait_recv()
        return lax.rsqrt((own + stat_from[index][:, 0:1]) / D + epsilon)

    def comp_piece(block, member):
        return compress_all.at[
            pl.ds(pl.multiple_of(block * sliced, 16), sliced),
            pl.ds(pl.multiple_of(member * quarter, 128), quarter),
        ]

    def comp_copy(block, way):
        here = comp_piece(block, place)
        return remote(
            here,
            here,
            comp_sent.at[block, way],
            comp_arrived.at[block],
            {"row": beside(row, way)},
        )

    def comp_each(block, act):
        @pl.when(jnp.logical_and(block <= row, row < ROWS - 1))
        def _():
            act(comp_copy(block, 0))

        @pl.when(jnp.logical_and(block >= row, row > 0))
        def _():
            act(comp_copy(block, 1))

    def comp_out(block, step, member):
        here = comp_piece(block, member)
        return remote(
            here,
            here,
            comp_out_sent.at[block, step],
            comp_out_arrived.at[block, step],
            {"dp": partner(place, step)},
        )

    line = Line(row, raw, line_sent, line_arrived)
    scale_line = Line(row, scales, scale_sent, scale_arrived)
    cot_line = Line(row, cot_all, cot_sent, cot_arrived)
    route_line = Line(row, routes, route_sent, route_arrived)
    sums = SumLine(row, part, leaving, coming, sum_sent, sum_arrived)

    met = greet(row, place, col)
    compress_all[pl.ds(pl.multiple_of(row * sliced, 16), sliced)] = compress_ref[...]
    compress_all[ROWS * sliced :] = jnp.zeros(
        (compress_all.shape[0] - ROWS * sliced, width), bf16
    )
    raw[pl.ds(row, 1)] = act_ref[...].reshape(1, tokens, width)
    meet(met)
    comp_each(row, lambda copy: copy.start())
    line.pass_on(row)

    def router_copy(half):
        here = router_all.at[:, pl.ds(pl.multiple_of(half * width, width), width)]
        return remote(here, here, router_sent.at[0], router_arrived.at[0], sibling)

    inputs = act_ref[...].astype(f32)
    scale_one = scale_of(inputs, 0)
    scale_one_ref[...] = scale_one
    scales[pl.ds(row, 1)] = jnp.broadcast_to(scale_one, (tokens, 128)).T[0:8].reshape(1, 8, tokens)
    scale_line.pass_on(row)
    router_all[:, pl.ds(pl.multiple_of(col * width, width), width)] = router_ref[...]
    router_copy(col).start()
    cot_all[pl.ds(row, 1)] = cot_ref[...].reshape(1, tokens, width)
    routes[pl.ds(row, 1)] = route_ref[...].reshape((1,) + route_ref.shape)

    @pl.when(jnp.logical_not(inner))
    def _():
        route_line.pass_on(row)
        cot_line.pass_on(row)

    for block in range(ROWS):
        mark = mark_ref[:, block * tokens : (block + 1) * tokens].astype(f32)
        marks[block] = jnp.broadcast_to(mark, (8, tokens)).T
    loads[0].wait()

    def query_copy(block):
        return remote(
            query_to.at[block],
            query_from.at[block],
            query_sent.at[block],
            query_arrived.at[block],
            sibling,
        )

    def latent_copy(block):
        return remote(
            latent_to.at[block],
            latent_from.at[block],
            latent_sent.at[block],
            latent_arrived.at[block],
            sibling,
        )

    def att_copy(block, half):
        here = attended_ref.at[block, :, pl.ds(pl.multiple_of(half * 2 * HEADV, 128), 2 * HEADV)]
        return remote(here, here, att_sent.at[block], att_arrived.at[block], sibling)

    def comp_relay(step):
        block = block_at(row, step)
        comp_copy(block, 0).wait_recv()
        comp_each(block, lambda copy: copy.start())
        for shift in (3, 2, 1):
            comp_out(block, shift, place).start()

    def relay_one(step):
        block = block_at(row, step)
        line.wait(block)
        line.pass_on(block)
        scale_line.wait(block)
        scale_line.pass_on(block)

    def normalise(step):
        block = block_at(row, step)
        scale = scales[block].T[:, 0:1]
        normed = (raw[block].astype(f32) * scale * scaling_ref[...]).astype(bf16)
        one_ref[block] = normed
        query_to[block] = nn(
            normed, queries[:, pl.ds(pl.multiple_of(other * mine, 128), mine)]
        ).astype(bf16)
        query_copy(block).start()
        query_own[block] = nn(normed, queries[:, pl.ds(pl.multiple_of(col * mine, 128), mine)])

    def latents(step):
        block = block_at(row, step)
        value = nt(one_ref[block], compress_all[...])
        latent_to[block] = value
        latent_copy(block).start()
        latent_ref[block] = value

    def keys(step):
        block = block_at(row, step)
        latent_copy(block).wait_recv()
        latent = latent_ref[block] + latent_from[block]
        latent_ref[block] = latent
        plain = latent[:, :RANK]
        scale = lax.rsqrt(jnp.mean(plain * plain, axis=1, keepdims=True) + epsilon)
        normed = (plain * scale * rescale_ref[...]).astype(bf16)
        normed_latent_ref[block] = normed
        own = 2 * (NOPE + HEADV)
        expanded = nn(normed, expand[:, pl.ds(pl.multiple_of(col * own, 128), own)])
        rope = latent[:, RANK:]
        rope = rope * key_cos_ref[block] + swap_halves(rope) * key_sin_ref[block]
        first = jnp.concatenate([expanded[:, :NOPE], rope], axis=1)
        second = jnp.concatenate([expanded[:, 2 * NOPE : 3 * NOPE], rope], axis=1)
        key_ref[0, block] = first.astype(bf16)
        key_ref[1, block] = pltpu.roll(second, ROPE, 1).astype(bf16)
        value_ref[0, block] = expanded[:, NOPE : 2 * NOPE].astype(bf16)
        value_ref[1, block] = expanded[:, 3 * NOPE :].astype(bf16)
        query_copy(block).wait_recv()
        query = query_own[block] + query_from[block].astype(f32)
        query_ref[block] = (
            query * cos_ref[block] + swap_halves(query) * sin_ref[block]
        ).astype(bf16)

    def gather(step, carried):
        @pl.when(step > 0)
        def _():
            relay_one(step)

        normalise(step)

        @pl.when(step < 2)
        def _():
            comp_relay(step + 1)

        @pl.when(step == 1)
        def _():
            comp_relay(3)

        return carried

    lax.fori_loop(0, ROWS - 1, gather, 0)

    @pl.when(inner)
    def _():
        relay_one(ROWS - 1)

    def comp_arrive(block, carried):
        @pl.when(block != row)
        def _():
            for shift in range(1, SQUARE):
                comp_out(block, shift, partner(place, shift)).wait_recv()

        return carried

    lax.fori_loop(0, ROWS, comp_arrive, 0)
    for load in loads[1:2] + loads[3:]:
        load.wait()

    def middle(step, carried):
        @pl.when(jnp.logical_and(step == ROWS - 1, jnp.logical_not(inner)))
        def _():
            relay_one(step)

        @pl.when(step == ROWS - 1)
        def _():
            normalise(step)

        @pl.when(step < ROWS)
        def _():
            latents(step)

        @pl.when(step > 0)
        def _():
            keys(step - 1)

        return carried

    lax.fori_loop(0, ROWS - 1, middle, 0)

    @pl.when(inner)
    def _():
        route_line.pass_on(row)
        cot_line.pass_on(row)

    def relay(step):
        block = block_at(row, step)
        route_line.wait(block)
        route_line.pass_on(block)
        cot_line.wait(block)
        cot_line.pass_on(block)

    def out_copy(block, step):
        piece = pl.ds(step * slots, slots)
        return remote(
            staged.at[block, piece],
            rows_ref.at[col, block, piece],
            out_sent.at[block, step],
            out_arrived.at[block, step],
            {"dp": partner(place, step)},
        )

    def pair_copy(block, half):
        here = rows_ref.at[half, block]
        return remote(here, here, pair_sent.at[block], pair_arrived.at[block], sibling)

    def take(step):
        block = block_at(row, step)

        @pl.when(jnp.logical_and(step > 0, jnp.logical_not(inner)))
        def _():
            relay(step)

        before = (
            lax.broadcasted_iota(jnp.int32, (tokens, tokens), 0)
            < lax.broadcasted_iota(jnp.int32, (tokens, tokens), 1)
        ).astype(bf16)
        routing = routes[block]
        chosen = []
        for shift in range(SQUARE):
            expert = partner(place, shift) * ROWS + row
            hit = (routing == expert).astype(f32)
            chosen.append(jnp.max(hit, axis=0, keepdims=True))
        goes = jnp.concatenate(chosen + chosen, axis=0)
        rank = nn(goes.astype(bf16), before)
        for shift in range(SQUARE):
            slot = lax.broadcasted_iota(jnp.int32, (slots, tokens), 0).astype(f32)
            here = jnp.logical_and(slot == rank[shift : shift + 1], goes[shift : shift + 1] > 0.5)
            pick = here.astype(f32)
            pick_ref[block, shift * slots : (shift + 1) * slots] = pick.astype(bf16)
            back_ref[block, :, shift * slots : (shift + 1) * slots] = pick.T.astype(bf16)
        staged[block] = nn(pick_ref[block], cot_all[block]).astype(bf16)
        for shift in (3, 2, 1):
            out_copy(block, shift).start()
        rows_ref[col, block, 0:slots] = staged[block, 0:slots]

    def forward(step):
        block = block_at(row, step)
        for shift in range(1, SQUARE):
            out_copy(block, shift).wait_recv()
        pair_copy(block, col).start()

    take(0)

    @pl.when(inner)
    def _():
        relay(1)
        relay(2)

    lax.fori_loop(ROWS - 1, ROWS + 1, middle, 0)

    for index in range(7):
        stores[index].start()
    seq = ROWS * tokens
    lanes = NOPE + 2 * ROPE

    def attend(turn, carried):
        block = block_at(row, ROWS - 1 - turn)
        visible = mark_ref[...].astype(f32) <= marks[block][:, 0:1]
        for head in range(2):
            query = query_ref[block, :, head * NOPE : head * NOPE + lanes]
            scores = nt(query, key_ref[head].reshape(seq, lanes)) * score_scale
            scores = jnp.where(visible, scores, masked_score)
            weight = jnp.exp(scores - jnp.max(scores, axis=1, keepdims=True))
            probs = (weight / jnp.sum(weight, axis=1, keepdims=True)).astype(bf16)
            probs_ref[head, block] = probs
            result = nn(probs, value_ref[head].reshape(seq, HEADV)).astype(bf16)
            at = pl.multiple_of((col * 2 + head) * HEADV, 128)
            attended_ref[block, :, pl.ds(at, HEADV)] = result
        att_copy(block, col).start()

        @pl.when(jnp.logical_and(turn == 0, inner))
        def _():
            relay(3)

        @pl.when(turn > 0)
        def _():
            mix(turn - 1)
            take(turn)

        return carried

    def mix(turn):
        block = block_at(row, ROWS - 1 - turn)
        att_copy(block, other).wait_recv()
        part[block] = nn(attended_ref[block], combine[...])
        sums.begin(block)

    loads[2].wait()
    lax.fori_loop(0, ROWS, attend, 0)
    mix(ROWS - 1)
    for index in range(7, 12):
        stores[index].start()

    def hand_on(turn, carried):
        sums.pass_on(block_at(row, jnp.where(turn == 0, 3, turn)))
        forward(turn)
        return carried

    lax.fori_loop(0, 3, hand_on, 0)
    sums.total(residual_ref)
    residual = residual_ref[...] + inputs
    residual_ref[...] = residual
    scale_two = scale_of(residual, 1)
    scale_two_ref[...] = scale_two
    two_ref[...] = (residual * scale_two * premix_ref[...]).astype(bf16)
    forward(3)

    def ended(block, carried):
        pair_copy(block, other).wait_recv()
        rows_store(block).start()
        pair_copy(block, col).wait_send()
        for shift in range(1, SQUARE):
            out_copy(block, shift).wait_send()

            @pl.when(block != row)
            def _(shift=shift):
                comp_out(block, shift, place).wait_send()

        comp_each(block, lambda copy: copy.wait_send())
        query_copy(block).wait_send()
        latent_copy(block).wait_send()
        att_copy(block, col).wait_send()
        return carried

    lax.fori_loop(0, ROWS, ended, 0)
    for store in stores:
        store.wait()

    def stored(block, carried):
        rows_store(block).wait()
        return carried

    lax.fori_loop(0, ROWS, stored, 0)
    router_copy(other).wait_recv()
    router_copy(col).wait_send()
    stat_copy(0).wait_send()
    stat_copy(1).wait_send()
    sums.finish()
    line.finish()
    scale_line.finish()
    cot_line.finish()
    route_line.finish()


def turning_tables(length):
    half = ROPE // 2
    frequency = 10000.0 ** (-np.arange(half, dtype=np.float32) * 2.0 / ROPE)
    angles = np.arange(length, dtype=np.float32)[:, None] * frequency[None, :].astype(np.float32)
    cosine, sine = np.cos(angles), np.sin(angles)
    cosine, sine = np.concatenate([cosine, cosine], 1), np.concatenate([-sine, sine], 1)
    ones, zeros = np.ones((length, NOPE)), np.zeros((length, NOPE))
    gap = np.zeros((length, 128 - ROPE))
    tables = (
        np.concatenate([ones, cosine, ones, cosine], 1),
        np.concatenate([zeros, sine, zeros, sine], 1),
        np.concatenate([cosine, gap], 1),
        np.concatenate([sine, gap], 1),
    )
    return [
        jnp.asarray(table.reshape(ROWS, length // ROWS, -1).astype(np.float32))
        for table in tables
    ]


def pair_sems():
    return [DMA((ROWS,)), DMA((ROWS,))]


def line_sems():
    return [DMA((ROWS, 2)), DMA((ROWS,))]


def square_sems():
    return [DMA((ROWS, SQUARE)), DMA((ROWS, SQUARE))]


def sum_sems():
    return [DMA((ROWS, SPLIT)), DMA((2, ROWS, SPLIT))]


def run_attention(
    activations,
    scaling,
    queries,
    compress,
    rescale,
    expand,
    combine,
    premix,
    segments,
    cotangent,
    routing,
    router,
    tables,
    slots,
):
    tokens, width = activations.shape
    seq = ROWS * tokens
    mine = queries.shape[1] // COLS
    sliced = compress.shape[1]
    latent_width = RANK + 128
    picked = SQUARE * slots
    lanes = NOPE + 2 * ROPE
    routes = routing.T
    whole = pl.BlockSpec(memory_space=VMEM)
    far = pl.BlockSpec(memory_space=pl.ANY)

    def shape(*dims, dtype=bf16):
        return jax.ShapeDtypeStruct(dims, dtype)

    kept = [
        shape(ROWS, tokens, width),
        shape(ROWS, tokens, mine),
        shape(2, ROWS, tokens, lanes),
        shape(2, ROWS, tokens, HEADV),
        shape(2, ROWS, tokens, seq),
        shape(ROWS, tokens, latent_width, dtype=f32),
        shape(ROWS, tokens, RANK),
        shape(ROWS, tokens, COLS * 2 * HEADV),
        shape(latent_width, width),
        shape(ROWS, tokens, width),
        shape(ROWS, picked, tokens),
        shape(ROWS, tokens, picked),
        shape(COLS, ROWS, picked, width),
    ]
    return pl.pallas_call(
        attend_kernel,
        name="attend",
        out_shape=(
            *kept,
            shape(tokens, width, dtype=f32),
            shape(tokens, width),
            shape(tokens, 1, dtype=f32),
            shape(tokens, 1, dtype=f32),
            shape(router.shape[1], COLS * width),
        ),
        in_specs=[whole] * 9 + [far] * 7,
        out_specs=(far,) * 13 + (whole,) * 5,
        scratch_shapes=[
            *[VMEM(value.shape, value.dtype) for value in kept],
            VMEM(queries.shape, bf16),
            VMEM(expand.shape, bf16),
            VMEM(combine.shape, bf16),
            *[VMEM(table.shape, f32) for table in tables],
            VMEM((2, tokens, 128), f32),
            VMEM((2, tokens, 128), f32),
            VMEM((ROWS, tokens, mine), f32),
            VMEM((ROWS, tokens, mine), bf16),
            VMEM((ROWS, tokens, mine), bf16),
            VMEM((ROWS, tokens, latent_width), f32),
            VMEM((ROWS, tokens, latent_width), f32),
            VMEM((ROWS, tokens, width), f32),
            VMEM((ROWS, tokens, width), bf16),
            VMEM((2, ROWS, tokens, width), bf16),
            VMEM((ROWS,) + routes.shape, jnp.int32),
            VMEM((ROWS, picked, width), bf16),
            VMEM((ROWS, tokens, 8), f32),
            VMEM((ROWS, tokens, width), bf16),
            VMEM((ROWS, 8, tokens), f32),
            DMA((7,)),
            DMA((12,)),
            DMA((ROWS,)),
            DMA((2,)),
            DMA((2,)),
            *line_sems(),
            *line_sems(),
            *square_sems(),
            *pair_sems(),
            *pair_sems(),
            *pair_sems(),
            *sum_sems(),
            *line_sems(),
            *line_sems(),
            *square_sems(),
            *pair_sems(),
            DMA((1,)),
            DMA((1,)),
            *line_sems(),
        ],
        compiler_params=pltpu.CompilerParams(
            collective_id=1, has_side_effects=True, vmem_limit_bytes=56 * MIB
        ),
        cost_estimate=pl.CostEstimate(
            flops=40 * 1024**3, bytes_accessed=32 * MIB, transcendentals=0
        ),
    )(
        activations,
        scaling.reshape(1, width),
        compress.T,
        rescale.reshape(1, RANK),
        premix.reshape(1, width),
        segments.reshape(1, seq),
        cotangent,
        routes,
        router.T,
        queries,
        expand,
        combine,
        *tables,
    )


def attend_back_kernel(
    normed_grad_ref,
    residual_ref,
    scale_two_ref,
    premix_ref,
    cot_ref,
    act_ref,
    scale_one_ref,
    scaling_ref,
    rescale_ref,
    combine_far,
    query_far,
    key_far,
    value_far,
    probs_far,
    cos_far,
    sin_far,
    queries_far,
    expand_far,
    latent_far,
    key_cos_far,
    key_sin_far,
    compress_far,
    one_far,
    kept_far,
    got_x_far,
    got_y_far,
    attended_far,
    normed_latent_far,
    narrow_far,
    home_far,
    back_far,
    shared_far,
    premix_far,
    router_far,
    input_grad_ref,
    output_ref,
    small_ref,
    shared_sum,
    queries_out,
    combine_out,
    expand_out,
    compress_out,
    branch_ref,
    query_grad_ref,
    expanded_ref,
    own_latent_ref,
    scaling_rows,
    rescale_rows,
    combine,
    query_ref,
    key_ref,
    value_ref,
    probs_ref,
    cos_ref,
    sin_ref,
    queries,
    expand,
    latent_ref,
    key_cos_ref,
    key_sin_ref,
    compress_all,
    one_ref,
    kept,
    got,
    middle,
    second,
    result,
    attended,
    normed_latent,
    narrow,
    home,
    back_ref,
    shared_ref,
    premix_rows,
    router_rows,
    stat_to,
    stat_from,
    grad_own,
    grad_to,
    grad_from,
    key_grad,
    value_grad,
    latent_own,
    latent_to,
    latent_from,
    turned,
    turned_from,
    part,
    leaving,
    coming,
    total,
    load_sem,
    stat_sent,
    stat_arrived,
    line_sent,
    line_arrived,
    grad_sent,
    grad_arrived,
    query_sent,
    query_arrived,
    latent_sent,
    latent_arrived,
    turned_sent,
    turned_arrived,
    own_sent,
    own_arrived,
    sum_sent,
    sum_arrived,
    rest_sent,
    rest_arrived,
    rest_sem,
    reply_part,
    reply_leaving,
    reply_coming,
    small_to,
    small_from,
    small_line,
    small_square,
    small_own,
    expand_other,
    store_sem,
    reply_sent,
    reply_arrived,
    pair_sent,
    pair_arrived,
    small_sent,
    small_arrived,
    *sums_scratch,
):
    place, row, col = lax.axis_index("dp"), lax.axis_index("row"), lax.axis_index("col")
    other = 1 - col
    sibling = {"col": other}
    tokens, width = act_ref.shape
    seq = ROWS * tokens
    mine = query_ref.shape[2]
    lanes = key_ref.shape[3]
    both = 2 * HEADV
    sliced = own_latent_ref.shape[0]
    score_scale = (NOPE + ROPE) ** (-0.5)
    loads = [
        pltpu.make_async_copy(source, target, load_sem.at[i])
        for i, (source, target) in enumerate(
            [
                (kept_far, kept),
                (got_x_far, got.at[0]),
                (got_y_far, got.at[1]),
                (combine_far, combine),
                (query_far, query_ref),
                (key_far, key_ref),
                (value_far, value_ref),
                (probs_far, probs_ref),
                (cos_far, cos_ref),
                (sin_far, sin_ref),
                (queries_far, queries),
                (expand_far, expand),
                (latent_far, latent_ref),
                (key_cos_far, key_cos_ref),
                (key_sin_far, key_sin_ref),
                (compress_far, compress_all),
                (one_far, one_ref),
                (attended_far, attended),
                (normed_latent_far, normed_latent),
                (narrow_far, narrow),
                (home_far, home),
                (back_far, back_ref),
                (shared_far, shared_ref),
                (premix_far, premix_rows),
                (router_far, router_rows),
            ]
        )
    ]
    for load in loads:
        load.start()
    line = Line(row, branch_ref, line_sent, line_arrived)
    sums = SumLine(row, part, leaving, coming, sum_sent, sum_arrived)
    met = greet(row, place, col, line=True)

    def stat_copy(index):
        return remote(
            stat_to.at[index],
            stat_from.at[index],
            stat_sent.at[index],
            stat_arrived.at[index],
            sibling,
        )

    def norm_begin(values, gain, upstream, index):
        weighted = upstream * gain
        own = jnp.sum(weighted * values, axis=1, keepdims=True)
        stat_to[index] = jnp.broadcast_to(own, (tokens, 128))
        stat_copy(index).start()

    def norm_grad(values, scale, gain, upstream, index):
        stat_copy(index).wait_recv()
        inner = (stat_to[index][:, 0:1] + stat_from[index][:, 0:1]) / D
        return upstream * gain * scale - values * (scale * scale * scale * inner)

    for load in loads[0:3]:
        load.wait()
    rests = [
        SquareRest(place, which, kept, got, middle, second, result, rest_sent, rest_arrived)
        for which in range(kept.shape[1])
    ]
    rests[0].prepare()
    meet(met)
    rests[0].run(1)
    for rest in rests[1:]:
        rest.prepare()
        rest.run(1)
    norm_begin(residual_ref[...], premix_ref[...], normed_grad_ref[...], 0)
    residual_grad = cot_ref[...].astype(f32) + norm_grad(
        residual_ref[...], scale_two_ref[...], premix_ref[...], normed_grad_ref[...], 0
    )
    input_grad_ref[...] = residual_grad
    branch_ref[pl.ds(row, 1)] = residual_grad.astype(bf16).reshape(1, tokens, width)
    line.pass_on(row)
    key_grad[...] = jnp.zeros_like(key_grad)
    value_grad[...] = jnp.zeros_like(value_grad)
    scaling_rows[...] = jnp.zeros_like(scaling_rows)
    rescale_rows[...] = jnp.zeros_like(rescale_rows)

    line_sums = SumLine(
        row, reply_part, reply_leaving, reply_coming, reply_sent, reply_arrived
    )
    experts = router_rows.shape[0]
    kinds = [sums_scratch[7 * i : 7 * i + 7] for i in range(4)]
    parts = [scratch[0] for scratch in kinds]
    plan = [(kind, chunk) for kind in range(4) for chunk in range(parts[kind].shape[0])]
    pieces_of = [
        SquareSum(place, *[ref.at[chunk] for ref in kinds[kind]]) for kind, chunk in plan
    ]
    count = len(plan)

    def begin(index):
        kind, chunk = plan[index]
        part_ref = parts[kind]
        if kind == 0 and chunk == 0:
            loads[17].wait()
        if kind == 2:
            loads[18].wait()
        if kind < 2:
            left, right = ((attended, branch_ref), (one_ref, query_grad_ref))[kind]
            height = 8 * part_ref.shape[2]
            piece = left[:, :, chunk * height : (chunk + 1) * height].reshape(seq, height)
            grad = tn(piece, right[...].reshape(seq, right.shape[2]))
        elif kind == 2:
            grad = tn(
                normed_latent[...].reshape(seq, RANK),
                expanded_ref[...].reshape(seq, expanded_ref.shape[2]),
            )
        else:
            grad = nn(own_latent_ref[...], one_ref[...].reshape(seq, width)).astype(bf16)
            for piece in range(8):
                part_ref[0, piece] = grad[:, piece * (width // 8) : (piece + 1) * (width // 8)]
        if kind < 3:
            part_ref[chunk] = grad.astype(bf16).reshape(part_ref.shape[1:])
        pieces_of[index].run(0)

    stores = []

    def store(source, target):
        copy = pltpu.make_async_copy(source, target, store_sem.at[len(stores)])
        copy.start()
        stores.append(copy)

    def pair_copy():
        return remote(kinds[2][4].at[0], expand_other, pair_sent.at[0], pair_arrived.at[0], sibling)

    def expand_lanes(half):
        wide = expand_other.shape[2]
        return expand_out.at[:, :, pl.ds(pl.multiple_of(half * wide, 128), wide)]

    def put(index):
        kind, chunk = plan[index]
        done = kinds[kind][4]
        if kind < 2:
            store(done.at[chunk], (combine_out, queries_out)[kind].at[chunk])
        elif kind == 2:
            store(done.at[0], expand_lanes(col))
            pair_copy().start()
        else:
            lanes = width // 8
            for piece in range(8):
                store(done.at[0, piece], compress_out.at[:, piece * lanes : (piece + 1) * lanes])

    def advance(turn):
        for phase in (1, 2, 3, 4):
            index = turn - phase
            if 0 <= index < count:
                pieces_of[index].run(phase)
                if phase == 4:
                    put(index)
        if 2 <= turn < count:
            begin(turn)

    def reply_add(turn, carried):
        block = block_at(row, ROWS - 1 - turn)
        reply_part[block] = (
            nn(back_ref[block], home[block]) + nn(shared_ref[block], narrow[...])
        ).astype(bf16)
        line_sums.begin(block)
        return carried

    def small_copy(step):
        if step == 0:
            return remote(small_to, small_from, small_sent.at[0], small_arrived.at[0], sibling)
        if step < ROWS:
            return remote(
                small_own,
                small_line.at[step],
                small_sent.at[step],
                small_arrived.at[step],
                {"row": lax.rem(row + step, ROWS)},
            )
        shift = step - ROWS + 1
        return remote(
            small_ref,
            small_square.at[shift],
            small_sent.at[step],
            small_arrived.at[step],
            {"dp": partner(place, shift)},
        )

    def small_begin():
        loads[23].wait()
        loads[24].wait()
        rescale_row = jnp.sum(rescale_rows[...], axis=0, keepdims=True)
        empty = jnp.zeros((small_own.shape[0] - experts, width), f32)
        small_to[0:experts] = router_rows[:, pl.ds(pl.multiple_of(other * width, width), width)]
        small_to[experts:] = empty
        small_to[experts + 2 : experts + 3, 0:RANK] = rescale_row
        small_copy(0).start()
        small_own[0:experts] = router_rows[:, pl.ds(pl.multiple_of(col * width, width), width)]
        small_own[experts:] = empty
        small_own[experts : experts + 1] = (
            jnp.sum(premix_rows[...], axis=0, keepdims=True) / premix_ref[...]
        )
        small_own[experts + 1 : experts + 2] = (
            jnp.sum(scaling_rows[...], axis=0, keepdims=True) / scaling_ref[...]
        )
        small_own[experts + 2 : experts + 3, 0:RANK] = rescale_row

    def small_line_begin():
        small_copy(0).wait_recv()
        small_own[...] += small_from[...]
        for step in range(1, ROWS):
            small_copy(step).start()

    def small_square_begin():
        for step in range(1, ROWS):
            small_copy(step).wait_recv()
        small_ref[...] = small_own[...] + small_line[1] + small_line[2] + small_line[3]
        for step in range(ROWS, ROWS + SQUARE - 1):
            small_copy(step).start()

    def small_end():
        for step in range(ROWS, ROWS + SQUARE - 1):
            small_copy(step).wait_recv()
        for step in range(ROWS, ROWS + SQUARE - 1):
            small_copy(step).wait_send()
        small_ref[...] += small_square[1] + small_square[2] + small_square[3]

    def reply_begin():
        for load in loads[19:23]:
            load.wait()
        lax.fori_loop(0, ROWS, reply_add, 0)

    def reply_pass():
        lax.fori_loop(0, 3, line_pass, 0)

    def reply_end():
        line_sums.total(total)
        output_ref[...] = (total[...] + residual_ref[...]).astype(bf16)

    def line_pass(turn, carried):
        line_sums.pass_on(block_at(row, jnp.where(turn == 0, 3, turn)))
        return carried

    def grad_copy(block):
        return remote(
            grad_to.at[block],
            grad_from.at[block],
            grad_sent.at[block],
            grad_arrived.at[block],
            sibling,
        )

    def query_copy(block, half):
        here = query_grad_ref.at[block, :, pl.ds(pl.multiple_of(half * mine, 128), mine)]
        return remote(here, here, query_sent.at[block], query_arrived.at[block], sibling)

    def latent_copy(block):
        return remote(
            latent_to.at[block],
            latent_from.at[block],
            latent_sent.at[block],
            latent_arrived.at[block],
            sibling,
        )

    def arrive(step):
        block = block_at(row, step)

        @pl.when(step > 0)
        def _():
            line.wait(block)
            line.pass_on(block)

        @pl.when(step == 0)
        def _():
            loads[3].wait()

        grads = branch_ref[block]
        grad_to[block] = nt(
            grads, combine[pl.ds(pl.multiple_of(other * both, 16), both)]
        ).astype(bf16)
        grad_copy(block).start()
        grad_own[block] = nt(grads, combine[pl.ds(pl.multiple_of(col * both, 16), both)])

    def heads(step):
        block = block_at(row, step)

        @pl.when(step == 0)
        def _():
            for load in loads[4:10]:
                load.wait()

        grad_copy(block).wait_recv()
        grads = (grad_own[block] + grad_from[block].astype(f32)).astype(bf16)
        pieces = []
        for head in range(2):
            upstream = grads[:, head * HEADV : (head + 1) * HEADV]
            query = query_ref[block, :, head * NOPE : head * NOPE + lanes]
            probs = probs_ref[head, block]
            weight = probs.astype(f32)
            probs_back = nt(upstream, value_ref[head].reshape(seq, HEADV))
            inner = jnp.sum(weight * probs_back, axis=1, keepdims=True)
            score_grad = (weight * (probs_back - inner)).astype(bf16)
            pieces.append(nn(score_grad, key_ref[head].reshape(seq, lanes)) * score_scale)
            key_grad[head] += tn(score_grad, query)
            value_grad[head] += tn(probs, upstream)
        first, second = pieces
        grad = jnp.concatenate(
            [first[:, :NOPE], first[:, NOPE:] + second[:, :NOPE], second[:, NOPE:]], axis=1
        )
        grad = grad * cos_ref[block] - swap_halves(grad) * sin_ref[block]
        query_grad_ref[block, :, pl.ds(pl.multiple_of(col * mine, 128), mine)] = grad.astype(bf16)
        query_copy(block, col).start()

    def project(step):
        block = block_at(row, step)

        @pl.when(step == 0)
        def _():
            loads[10].wait()

        query_copy(block, other).wait_recv()
        part[block] = nt(query_grad_ref[block], queries[...])

    def turn(step, carried):
        @pl.when(step < ROWS)
        def _():
            arrive(step)

        @pl.when(step == 1)
        def _():
            for rest in rests:
                rest.run(2)

        @pl.when(step == 2)
        def _():
            rests[0].run(3)

        @pl.when(step == 3)
        def _():
            rests[1].run(3)
            rests[2].run(3)

        @pl.when(step >= 1)
        def _():
            heads(step - 1)

        @pl.when(step >= 2)
        def _():
            project(step - 2)

        return carried

    lax.fori_loop(0, ROWS + 1, turn, 0)
    for load in loads[11:17]:
        load.wait()
    begin(0)
    begin(1)
    reply_begin()

    def latents(turn, carried):
        block = block_at(row, ROWS - 1 - turn)
        here = pl.ds(pl.multiple_of(block * tokens, 128), tokens)
        first = key_grad[0, here] * score_scale
        second = pltpu.roll(key_grad[1, here] * score_scale, lanes - ROPE, 1)
        grad = jnp.concatenate(
            [first[:, :NOPE], value_grad[0, here], second[:, :NOPE], value_grad[1, here]], axis=1
        ).astype(bf16)
        expanded_ref[block] = grad
        own = 2 * (NOPE + HEADV)
        upstream = nt(grad, expand[:, pl.ds(pl.multiple_of(col * own, 128), own)])
        plain = latent_ref[block][:, :RANK]
        scale = lax.rsqrt(jnp.mean(plain * plain, axis=1, keepdims=True) + epsilon)
        rescale_rows[...] += jnp.sum(
            (upstream * plain * scale).reshape(tokens // 8, 8, RANK), axis=0
        )
        weighted = upstream * rescale_ref[...]
        inner = jnp.mean(weighted * plain, axis=1, keepdims=True)
        plain_grad = weighted * scale - plain * (scale * scale * scale * inner)
        rope = first[:, NOPE:] + second[:, NOPE:]
        lane = lax.broadcasted_iota(jnp.int32, rope.shape, 1)
        rope = jnp.where(lane < ROPE, rope, 0.0)
        rope = rope * key_cos_ref[block] - swap_halves(rope) * key_sin_ref[block]
        value = jnp.concatenate([plain_grad, rope], axis=1)
        latent_own[block] = value
        latent_to[block] = value.astype(bf16)
        latent_copy(block).start()
        return carried

    lax.fori_loop(0, ROWS, latents, 0)
    project(ROWS - 1)

    def turned_piece(member):
        return turned.at[
            pl.ds(pl.multiple_of(member * sliced, 16), sliced),
            pl.ds(pl.multiple_of(col * (seq // COLS), 128), seq // COLS),
        ]

    def turned_copy(step):
        to = lax.rem(row + step, ROWS)
        return remote(
            turned_piece(to),
            turned_from.at[step],
            turned_sent.at[step],
            turned_arrived.at[step],
            {"row": to},
        )

    def mix(turn, carried):
        block = block_at(row, ROWS - 1 - turn)
        latent_copy(block).wait_recv()
        latent = latent_own[block] + latent_from[block].astype(f32)
        here = pl.ds(pl.multiple_of(block * tokens, 128), tokens)
        total_here = part[block] + nn(latent.astype(bf16), compress_all[...])
        part[block] = total_here
        sums.begin(block)
        turned[:, here] = latent.T.astype(bf16)
        scaling_rows[...] += jnp.sum(
            (total_here * one_ref[block].astype(f32)).reshape(tokens // 8, 8, width), axis=0
        )
        return carried

    lax.fori_loop(0, ROWS, mix, 0)
    for step in range(1, ROWS):
        turned_copy(step).start()

    advance(1)
    small_begin()
    for turn in range(3):
        sums.pass_on(block_at(row, 3 if turn == 0 else turn))
        advance(turn + 2)
        if turn == 0:
            small_line_begin()
    for step in range(1, ROWS):
        turned_copy(step).wait_recv()
    half = pl.ds(pl.multiple_of(col * (seq // COLS), 128), seq // COLS)
    own_sum = turned[pl.ds(pl.multiple_of(row * sliced, 16), sliced), half].astype(f32)
    for step in range(1, ROWS):
        own_sum = own_sum + turned_from[step].astype(f32)
    own_latent_ref[:, half] = own_sum.astype(bf16)

    def own_copy(part_of):
        here = own_latent_ref.at[
            :, pl.ds(pl.multiple_of(part_of * (seq // COLS), 128), seq // COLS)
        ]
        return remote(here, here, own_sent.at[0], own_arrived.at[0], sibling)

    own_copy(col).start()
    advance(5)
    sums.total(total)
    norm_begin(act_ref[...].astype(f32), scaling_ref[...], total[...], 1)
    input_grad_ref[...] += norm_grad(
        act_ref[...].astype(f32), scale_one_ref[...], scaling_ref[...], total[...], 1
    )
    advance(6)
    reply_pass()
    for rest in rests:
        rest.run(4)
    pieces = [
        pltpu.make_async_copy(
            result.at[i], shared_sum.at[:, :, i * 128 : (i + 1) * 128], rest_sem.at[i]
        )
        for i in range(8)
    ]
    for piece in pieces:
        piece.start()
    own_copy(other).wait_recv()
    own_copy(col).wait_send()
    advance(7)
    small_square_begin()
    advance(8)
    reply_end()
    for turn in range(9, count + 5):
        advance(turn)
    small_end()
    pair_copy().wait_recv()
    store(expand_other, expand_lanes(other))

    def ended(block, carried):
        grad_copy(block).wait_send()
        query_copy(block, col).wait_send()
        latent_copy(block).wait_send()
        return carried

    lax.fori_loop(0, ROWS, ended, 0)
    for step in range(1, ROWS):
        turned_copy(step).wait_send()
    stat_copy(0).wait_send()
    stat_copy(1).wait_send()
    for piece in pieces:
        piece.wait()
    for copy in stores:
        copy.wait()
    pair_copy().wait_send()
    for step in range(ROWS):
        small_copy(step).wait_send()
    for one_sum in pieces_of:
        one_sum.finish()
    line_sums.finish()
    for rest in rests:
        rest.finish()
    sums.finish()
    line.finish()


def run_attention_back(
    normed_grad,
    residual,
    scale_two,
    premix,
    cotangent,
    activations,
    scale_one,
    scaling,
    one,
    query,
    key,
    value,
    probs,
    latent,
    rescale,
    tables,
    compress_all,
    queries,
    expand,
    combine,
    shared,
    more,
):
    tokens, width = activations.shape
    seq = ROWS * tokens
    mine = query.shape[2]
    lanes = key.shape[3]
    latent_width = latent.shape[2]
    sliced = (RANK + ROPE) // ROWS
    whole = pl.BlockSpec(memory_space=VMEM)
    far = pl.BlockSpec(memory_space=pl.ANY)

    def shape(*dims, dtype=bf16):
        return jax.ShapeDtypeStruct(dims, dtype)

    kept, got_x, got_y = shared
    heads = more[0].shape[2]
    own_heads = 2 * (NOPE + HEADV)
    small = (24, width)
    piece = kept.shape[1:3] + (kept.shape[3] // 2,)
    loaded = (
        combine,
        query,
        key,
        value,
        probs,
        tables[0],
        tables[1],
        queries,
        expand,
        latent,
        tables[2],
        tables[3],
        compress_all,
        one,
    )
    return pl.pallas_call(
        attend_back_kernel,
        name="attend_back",
        out_shape=(
            shape(tokens, width, dtype=f32),
            shape(tokens, width),
            shape(*small, dtype=f32),
            shape(*kept.shape[1:3], width),
            shape(4, 8, width // 32, COLS * mine),
            shape(2, 8, heads // 16, width),
            shape(8, RANK // 8, COLS * own_heads),
            shape(sliced, width),
        ),
        in_specs=[whole] * 9 + [far] * 25,
        out_specs=(whole,) * 3 + (far,) * 5,
        scratch_shapes=[
            VMEM((ROWS, tokens, width), bf16),
            VMEM((ROWS, tokens, COLS * mine), bf16),
            VMEM((ROWS, tokens, own_heads), bf16),
            VMEM((sliced, seq), bf16),
            VMEM((8, width), f32),
            VMEM((8, RANK), f32),
            *[VMEM(value.shape, value.dtype) for value in loaded],
            VMEM(kept.shape, bf16),
            VMEM(kept.shape, bf16),
            VMEM((2,) + piece, bf16),
            VMEM((2,) + piece, bf16),
            VMEM((8,) + piece, bf16),
            *[VMEM(value.shape, value.dtype) for value in more],
            VMEM((2, tokens, 128), f32),
            VMEM((2, tokens, 128), f32),
            VMEM((ROWS, tokens, 2 * HEADV), f32),
            VMEM((ROWS, tokens, 2 * HEADV), bf16),
            VMEM((ROWS, tokens, 2 * HEADV), bf16),
            VMEM((2, seq, lanes), f32),
            VMEM((2, seq, HEADV), f32),
            VMEM((ROWS, tokens, latent_width), f32),
            VMEM((ROWS, tokens, latent_width), bf16),
            VMEM((ROWS, tokens, latent_width), bf16),
            VMEM((latent_width, seq), bf16),
            VMEM((ROWS, sliced, seq // COLS), bf16),
            VMEM((ROWS, tokens, width), f32),
            VMEM((ROWS, tokens, width), bf16),
            VMEM((2, ROWS, tokens, width), bf16),
            VMEM((tokens, width), f32),
            DMA((25,)),
            DMA((2,)),
            DMA((2,)),
            *line_sems(),
            *pair_sems(),
            *pair_sems(),
            *pair_sems(),
            *pair_sems(),
            *pair_sems(),
            *sum_sems(),
            DMA((kept.shape[1], 8)),
            DMA((kept.shape[1], 8)),
            DMA((8,)),
            VMEM((ROWS, tokens, width), bf16),
            VMEM((ROWS, tokens, width), bf16),
            VMEM((2, ROWS, tokens, width), bf16),
            VMEM(small, f32),
            VMEM(small, f32),
            VMEM((ROWS,) + small, f32),
            VMEM((SQUARE,) + small, f32),
            VMEM(small, f32),
            VMEM((8, RANK // 8, own_heads), bf16),
            DMA((16,)),
            *sum_sems(),
            DMA((1,)),
            DMA((1,)),
            DMA((ROWS + SQUARE - 1,)),
            DMA((ROWS + SQUARE - 1,)),
            *square_scratch((2, heads // 16, width)),
            *square_scratch((4, width // 32, COLS * mine)),
            *square_scratch((1, RANK // 8, own_heads)),
            *square_scratch((1, sliced, width // 8)),
        ],
        compiler_params=pltpu.CompilerParams(
            collective_id=3, has_side_effects=True, vmem_limit_bytes=62 * MIB
        ),
        cost_estimate=pl.CostEstimate(
            flops=40 * 1024**3, bytes_accessed=32 * MIB, transcendentals=0
        ),
    )(
        normed_grad,
        residual,
        scale_two,
        premix.reshape(1, width),
        cotangent,
        activations,
        scale_one,
        scaling.reshape(1, width),
        rescale.reshape(1, RANK),
        *loaded,
        kept,
        got_x,
        got_y,
        *more,
    )


def silu_pair(values):
    sigmoid = 1.0 / (1.0 + jnp.exp(-values))
    return values * sigmoid, sigmoid * (1.0 + values * (1.0 - sigmoid))


def expert_kernel(
    normed_ref,
    pick_ref,
    router_ref,
    back_far,
    cot_far,
    cot_rows_ref,
    fan_ref,
    fun_ref,
    wide_ref,
    narrow_ref,
    sum_ref,
    rows_out,
    gu_out,
    hidden_out,
    shared_x,
    shared_y,
    shared_kept,
    shared_far,
    reply_ref,
    premix_ref,
    router_rows,
    gathered_ref,
    shared_out,
    back_ref,
    cot_ref,
    fan,
    fun,
    wide,
    narrow,
    cot_rows,
    rows,
    staged,
    gu,
    hidden,
    pair_own,
    pair_to,
    pair_from,
    home,
    shared_to,
    shared_from,
    part,
    passed_to,
    passed_from,
    shared_gu,
    shared_grad,
    load_sem,
    store_sem,
    line_sent,
    line_arrived,
    out_sent,
    out_arrived,
    fwd_sent,
    fwd_arrived,
    shared_sent,
    shared_arrived,
    half_sent,
    half_arrived,
    home_sent,
    home_arrived,
    sum_sent,
    sum_arrived,
    other_sent,
    other_arrived,
    reply_sent,
    reply_arrived,
    grad_sem,
    late_sem,
):
    place, row, col = lax.axis_index("dp"), lax.axis_index("row"), lax.axis_index("col")
    other = 1 - col
    inner = jnp.logical_and(row > 0, row < ROWS - 1)
    tokens, width = normed_ref.shape
    picked = pick_ref.shape[1]
    slots = picked // SQUARE
    experts = router_ref.shape[0]
    share = narrow.shape[0]
    loads = [
        pltpu.make_async_copy(source, target, load_sem.at[i])
        for i, (source, target) in enumerate(
            [
                (wide_ref, wide),
                (narrow_ref, narrow),
                (fan_ref, fan),
                (cot_rows_ref, cot_rows),
                (fun_ref, fun),
                (cot_far, cot_ref),
                (back_far, back_ref),
            ]
        )
    ]
    for load in loads:
        load.start()
    met = greet(row, place, col)
    gathered_ref[pl.ds(row, 1)] = normed_ref[...].reshape(1, tokens, width)
    staged[pl.ds(row, 1)] = (
        nn(pick_ref[row], normed_ref[...]).astype(bf16).reshape(1, picked, width)
    )
    meet(met)
    line = Line(row, gathered_ref, line_sent, line_arrived)
    line.pass_on(row)
    premix_ref[...] = jnp.zeros_like(premix_ref)
    router_rows[...] = jnp.zeros_like(router_rows)
    sums = SumLine(row, part, passed_to, passed_from, sum_sent, sum_arrived)
    sibling = {"col": other}

    def half_lines(half):
        return pl.ds(pl.multiple_of(half * width, width), width)

    def square_copy(source, target, sent, arrived, block, step):
        piece = pl.ds(step * slots, slots)
        return remote(
            source.at[block, piece],
            target.at[block, piece],
            sent.at[block, step],
            arrived.at[block, step],
            {"dp": partner(place, step)},
        )

    def out_copy(block, step):
        return square_copy(staged, rows.at[col], out_sent, out_arrived, block, step)

    def home_copy(block, step):
        return square_copy(staged, home, home_sent, home_arrived, block, step)

    def reply_copy(block, step):
        return square_copy(staged, reply_ref, reply_sent, reply_arrived, block, step)

    def keep_copy(block):
        own = pl.ds(0, slots)
        return pltpu.make_async_copy(
            staged.at[block, own], reply_ref.at[block, own], reply_arrived.at[block, 0]
        )

    def fwd_copy(block, half):
        here = rows.at[half, block]
        return remote(here, here, fwd_sent.at[block], fwd_arrived.at[block], sibling)

    def shared_copy(block):
        return remote(
            shared_to.at[block],
            shared_from.at[block],
            shared_sent.at[block],
            shared_arrived.at[block],
            sibling,
        )

    def half_copy(step):
        return remote(
            pair_to.at[lax.rem(step, 2)],
            pair_from.at[step],
            half_sent.at[step],
            half_arrived.at[step],
            sibling,
        )

    def other_copy(step):
        return remote(
            pair_to.at[lax.rem(step, 2)],
            pair_from.at[jnp.where(step == ROWS - 1, ROWS, step)],
            other_sent.at[step],
            other_arrived.at[step],
            sibling,
        )

    def stores(step):
        block = block_at(row, step)
        return [
            pltpu.make_async_copy(source, target, store_sem.at[index, step])
            for index, (source, target) in enumerate(
                [
                    (rows.at[:, block], rows_out.at[:, block]),
                    (gu.at[:, lax.rem(step, 2)], gu_out.at[:, block]),
                    (hidden.at[block], hidden_out.at[block]),
                ]
            )
        ]

    def relay(step):
        block = block_at(row, step)
        line.wait(block)
        line.pass_on(block)

    def take(step):
        block = block_at(row, step)

        @pl.when(jnp.logical_and(step > 0, jnp.logical_not(inner)))
        def _():
            relay(step)

        @pl.when(step > 0)
        def _():
            staged[block] = nn(pick_ref[block], gathered_ref[block]).astype(bf16)

        for shift in (3, 2, 1):
            out_copy(block, shift).start()
        rows[col, block, 0:slots] = staged[block, 0:slots]

    def shared_begin(step):
        block = block_at(row, step)

        @pl.when(step == 0)
        def _():
            loads[0].wait()
            loads[1].wait()
            loads[5].wait()

        for index, value in enumerate(
            (
                nt(gathered_ref[block], wide[0]),
                nt(gathered_ref[block], wide[1]),
                nt(cot_ref[block], narrow[...]),
            )
        ):
            shared_to[block, index] = value.astype(bf16)
        shared_copy(block).start()

    def forward(step):
        block = block_at(row, step)
        for shift in range(1, SQUARE):
            out_copy(block, shift).wait_recv()
        fwd_copy(block, col).start()

    def shared(step):
        block = block_at(row, step)
        shared_copy(block).wait_recv()
        gate, up, grad = [
            shared_to[block, index].astype(f32) + shared_from[block, index].astype(f32)
            for index in range(3)
        ]
        act, slope = silu_pair(gate)
        shared_out[block] = (act * up).astype(bf16)
        gate_grad = (grad * up * slope).astype(bf16)
        up_grad = (grad * act).astype(bf16)
        shared_gu[0, block] = gate_grad
        shared_gu[1, block] = up_grad
        part[block] = nn(gate_grad, wide[0]) + nn(up_grad, wide[1])

    def experts_of(step):
        block = block_at(row, step)

        @pl.when(step == 0)
        def _():
            for load in loads[2:5] + loads[6:]:
                load.wait()

        @pl.when(step > 1)
        def _():
            stores(step - 2)[1].wait()
            half_copy(step - 2).wait_send()

        fwd_copy(block, other).wait_recv()
        left, right = rows[0, block], rows[1, block]
        logits = nt(left, router_ref[:, 0:width]) + nt(right, router_ref[:, width:])
        logits = logits - jnp.max(logits, axis=1, keepdims=True)
        weight = jnp.exp(logits)
        probs = weight / jnp.sum(weight, axis=1, keepdims=True)
        own = (
            lax.broadcasted_iota(jnp.int32, (picked, experts), 1) == place * ROWS + row
        ).astype(f32)
        gates = jnp.sum(probs * own, axis=1, keepdims=True)
        raw = nt(cot_rows[0, block], fun[:, 0:width]) + nt(cot_rows[1, block], fun[:, width:])
        gate = nt(left, fan[0, :, 0:width]) + nt(right, fan[0, :, width:])
        up = nt(left, fan[1, :, 0:width]) + nt(right, fan[1, :, width:])
        act, slope = silu_pair(gate)
        value = act * up
        hidden[block] = (value * gates).astype(bf16)
        gate_sum = gates * jnp.sum(value * raw, axis=1, keepdims=True)
        logit_grad = (gate_sum * (own - probs)).astype(bf16)
        raw = raw * gates
        slot = lax.rem(step, 2)
        gu[0, slot] = (raw * up * slope).astype(bf16)
        gu[1, slot] = (raw * act).astype(bf16)

        def half_of(half):
            lines = half_lines(half)
            return (
                nn(gu[0, slot], fan[0, :, lines])
                + nn(gu[1, slot], fan[1, :, lines])
                + nn(logit_grad, router_ref[:, lines])
            )

        pair_to[slot] = half_of(other).astype(bf16)
        half_copy(step).start()
        pair_own[...] = half_of(col)
        router_rows[:, 0:width] += tn(logit_grad, left)
        router_rows[:, width:] += tn(logit_grad, right)
        for copy in stores(step):
            copy.start()

    def send_home(step):
        block = block_at(row, step)
        for shift in range(1, SQUARE):
            out_copy(block, shift).wait_send()
        half_copy(step).wait_recv()
        staged[block] = (pair_own[...] + pair_from[step].astype(f32)).astype(bf16)
        for shift in (3, 2, 1):
            home_copy(block, shift).start()
        home[block, 0:slots] = staged[block, 0:slots]

    def add_up(step):
        block = block_at(row, step)
        for shift in range(1, SQUARE):
            home_copy(block, shift).wait_recv()
        total = part[block] + nn(back_ref[block], home[block])
        part[block] = total
        premix_ref[...] += jnp.sum(
            (total * gathered_ref[block].astype(f32)).reshape(tokens // 8, 8, width), axis=0
        )
        sums.begin(block)

    def reply(step):
        block = block_at(row, step)
        slot = lax.rem(step, 2)

        @pl.when(step < 2)
        def _():
            half_copy(step + 2).wait_send()

        @pl.when(step > 1)
        def _():
            other_copy(step - 2).wait_send()

        pair_to[slot] = nn(hidden[block], fun[:, half_lines(other)]).astype(bf16)
        other_copy(step).start()

    def reply_home(step):
        block = block_at(row, step)
        own = nn(hidden[block], fun[:, half_lines(col)])
        for shift in range(1, SQUARE):
            home_copy(block, shift).wait_send()
        came = jnp.where(step == ROWS - 1, ROWS, step)
        other_copy(step).wait_recv()
        staged[block] = (own + pair_from[came].astype(f32)).astype(bf16)
        for shift in (3, 2, 1):
            reply_copy(block, shift).start()
        keep_copy(block).start()

    def turn(step, carried):
        @pl.when(jnp.logical_and(step == 2, inner))
        def _():
            relay(3)

        @pl.when(step < ROWS)
        def _():
            take(step)

        @pl.when(jnp.logical_and(step >= 1, step <= ROWS))
        def _():
            forward(step - 1)

        @pl.when(step < ROWS)
        def _():
            shared_begin(step)

        @pl.when(jnp.logical_and(step == 0, inner))
        def _():
            relay(1)
            relay(2)

        @pl.when(step >= 2)
        def _():
            shared(step - 2)
            send_home(step - 2)

        @pl.when(step == ROWS)
        def _():
            reply(0)

        @pl.when(step == ROWS + 1)
        def _():
            reply_home(0)

        @pl.when(step >= ROWS)
        def _():
            add_up(2 * step - 2 * ROWS)

        @pl.when(step == ROWS)
        def _():
            add_up(1)

        @pl.when(jnp.logical_and(step >= 1, step <= ROWS))
        def _():
            experts_of(step - 1)

        return carried

    lax.fori_loop(0, ROWS + 2, turn, 0)

    def replies(step, carried):
        @pl.when(step < ROWS)
        def _():
            reply(step)

        @pl.when(step > 1)
        def _():
            reply_home(step - 1)

        return carried

    late = [
        pltpu.make_async_copy(source, target, late_sem.at[i])
        for i, (source, target) in enumerate(
            [(shared_out, shared_far)]
        )
    ]
    for copy in late:
        copy.start()
    lax.fori_loop(1, ROWS + 1, replies, 0)
    add_up(ROWS - 1)

    def hand_on(turn, carried):
        sums.pass_on(block_at(row, jnp.where(turn == 2, 1, turn + 2)))
        return carried

    lax.fori_loop(0, ROWS - 1, hand_on, 0)

    seq = ROWS * tokens
    for index, (left, right) in enumerate(
        (
            (shared_out, cot_ref),
            (shared_gu.at[0], gathered_ref),
            (shared_gu.at[1], gathered_ref),
        )
    ):
        grad = tn(left[...].reshape(seq, share), right[...].reshape(seq, width))
        shared_grad[index] = grad.astype(bf16)
    x, y = lax.rem(place, 2), lax.div(place, 2)
    quarter = width // SQUARE
    grad_copies = []
    for index, (half, side, target) in enumerate(
        (
            (0, 1 - x, shared_x),
            (1, 1 - y, shared_y),
            (0, x, shared_kept.at[0]),
            (1, y, shared_kept.at[1]),
        )
    ):
        lanes = pl.ds(pl.multiple_of((2 * half + side) * quarter, 128), quarter)
        grad_copies.append(
            pltpu.make_async_copy(shared_grad.at[:, :, lanes], target, grad_sem.at[index])
        )
        grad_copies[index].start()
    sums.total(sum_ref)

    def ended(step, carried):
        block = block_at(row, step)
        shared_copy(block).wait_send()
        fwd_copy(block, col).wait_send()
        for shift in range(1, SQUARE):
            reply_copy(block, shift).wait_recv()
            reply_copy(block, shift).wait_send()
        keep_copy(block).wait()
        copies = stores(step)
        copies[0].wait()
        copies[2].wait()

        @pl.when(step >= ROWS - 2)
        def _():
            copies[1].wait()
            other_copy(step).wait_send()

        return carried

    lax.fori_loop(0, ROWS, ended, 0)
    for copy in grad_copies + late:
        copy.wait()
    sums.finish()
    line.finish()


def run_experts(
    normed, pick, back, cot_rows, cot_all, fan, fun, wide, narrow, router_all
):
    tokens, width = normed.shape
    picked = pick.shape[1]
    hid = fun.shape[0]
    share = narrow.shape[0]
    experts = router_all.shape[0]
    whole = pl.BlockSpec(memory_space=VMEM)
    far = pl.BlockSpec(memory_space=pl.ANY)

    def shape(*dims, dtype=bf16):
        return jax.ShapeDtypeStruct(dims, dtype)

    return pl.pallas_call(
        expert_kernel,
        name="experts",
        out_shape=(
            shape(tokens, width, dtype=f32),
            shape(COLS, ROWS, picked, width),
            shape(2, ROWS, picked, hid),
            shape(ROWS, picked, hid),
            shape(3, share, width // SQUARE),
            shape(3, share, width // SQUARE),
            shape(2, 3, share, width // SQUARE),
            shape(ROWS, tokens, share),
            shape(ROWS, picked, width),
            shape(8, width, dtype=f32),
            shape(experts, COLS * width, dtype=f32),
        ),
        in_specs=[whole] * 3 + [far] * 7,
        out_specs=(whole,) + (far,) * 8 + (whole,) * 2,
        scratch_shapes=[
            VMEM((ROWS, tokens, width), bf16),
            VMEM((ROWS, tokens, share), bf16),
            VMEM(back.shape, bf16),
            VMEM(cot_all.shape, bf16),
            VMEM(fan.shape, bf16),
            VMEM(fun.shape, bf16),
            VMEM(wide.shape, bf16),
            VMEM(narrow.shape, bf16),
            VMEM(cot_rows.shape, bf16),
            VMEM((COLS, ROWS, picked, width), bf16),
            VMEM((ROWS, picked, width), bf16),
            VMEM((2, 2, picked, hid), bf16),
            VMEM((ROWS, picked, hid), bf16),
            VMEM((picked, width), f32),
            VMEM((2, picked, width), bf16),
            VMEM((ROWS + 1, picked, width), bf16),
            VMEM((ROWS, picked, width), bf16),
            VMEM((ROWS, 3, tokens, share), bf16),
            VMEM((ROWS, 3, tokens, share), bf16),
            VMEM((ROWS, tokens, width), f32),
            VMEM((ROWS, tokens, width), bf16),
            VMEM((2, ROWS, tokens, width), bf16),
            VMEM((2, ROWS, tokens, share), bf16),
            VMEM((3, share, width), bf16),
            DMA((7,)),
            DMA((3, ROWS)),
            *line_sems(),
            *square_sems(),
            *pair_sems(),
            *pair_sems(),
            *pair_sems(),
            *square_sems(),
            *sum_sems(),
            *pair_sems(),
            *square_sems(),
            DMA((4,)),
            DMA((1,)),
        ],
        compiler_params=pltpu.CompilerParams(
            collective_id=2, has_side_effects=True, vmem_limit_bytes=62 * MIB
        ),
        cost_estimate=pl.CostEstimate(
            flops=60 * 1024**3, bytes_accessed=64 * MIB, transcendentals=0
        ),
    )(normed, pick, router_all, back, cot_all, cot_rows, fan, fun, wide, narrow)


class SquareSum:
    def __init__(self, place, part, first, second, middle, result, sent, arrived):
        self.x, self.y = lax.rem(place, 2), lax.div(place, 2)
        self.to_x, self.to_y = {"dp": partner(place, 1)}, {"dp": partner(place, 2)}
        self.part, self.first, self.second = part, first, second
        self.middle, self.result = middle, result
        self.sent, self.arrived = sent, arrived

    def copies(self, phase):
        x, y = self.x, self.y
        if phase == 0:
            plan = (
                (self.part.at[pl.ds(2 - 2 * x, 2)], self.first.at[0:2], self.to_x),
                (self.part.at[pl.ds(6 - 2 * y, 2)], self.first.at[2:4], self.to_y),
            )
        elif phase == 1:
            plan = (
                (self.middle.at[0], self.second.at[0], self.to_y),
                (self.middle.at[1], self.second.at[1], self.to_x),
            )
        elif phase == 2:
            one, two = self.result.at[2 * x + y], self.result.at[4 + 2 * y + x]
            plan = ((one, one, self.to_y), (two, two, self.to_x))
        else:
            one, two = self.result.at[pl.ds(2 * x, 2)], self.result.at[pl.ds(4 + 2 * y, 2)]
            plan = ((one, one, self.to_x), (two, two, self.to_y))
        return [
            remote(source, target, self.sent.at[2 * phase + i], self.arrived.at[2 * phase + i], to)
            for i, (source, target, to) in enumerate(plan)
        ]

    def start(self, phase):
        for copy in self.copies(phase):
            copy.start()

    def arrive(self, phase):
        for copy in self.copies(phase):
            copy.wait_recv()

    def run(self, phase):
        x, y = self.x, self.y
        if phase > 0:
            self.arrive(phase - 1)
        if phase == 1:
            for slot, piece, came in (
                (0, 2 * x + 1 - y, 1 - y),
                (1, 4 + 2 * y + 1 - x, 3 - x),
            ):
                self.middle[slot] = (
                    self.part[piece].astype(f32) + self.first[came].astype(f32)
                ).astype(bf16)
        if phase == 2:
            for slot, piece, came in ((0, 2 * x + y, y), (1, 4 + 2 * y + x, 2 + x)):
                self.result[piece] = (
                    self.part[piece].astype(f32)
                    + self.first[came].astype(f32)
                    + self.second[slot].astype(f32)
                ).astype(bf16)
        if phase < 4:
            self.start(phase)

    def finish(self):
        for phase in range(4):
            for copy in self.copies(phase):
                copy.wait_send()


def square_scratch(dims):
    count, rows, lanes = dims
    return [
        VMEM((count, 8, rows, lanes), bf16),
        VMEM((count, 4, rows, lanes), bf16),
        VMEM((count, 2, rows, lanes), bf16),
        VMEM((count, 2, rows, lanes), bf16),
        VMEM((count, 8, rows, lanes), bf16),
        DMA((count, 8)),
        DMA((count, 8)),
    ]


def write_kernel(count, plan, *refs):
    sources, targets = refs[:count], refs[count : count + len(plan)]
    rest = refs[count + len(plan) :]
    held, wide = rest[:count], rest[count : count + len(plan)]
    load_sem, store_sem = rest[count + len(plan) :]
    loads = [
        pltpu.make_async_copy(sources[i], held[i], load_sem.at[i]) for i in range(count)
    ]
    stores = [
        pltpu.make_async_copy(wide[i], targets[i], store_sem.at[i]) for i in range(len(plan))
    ]
    for load in loads:
        load.start()
    waited = set()
    for i, (source, where) in enumerate(plan):
        if source not in waited:
            loads[source].wait()
            waited.add(source)
        wide[i][...] = held[source][where].astype(wide[i].dtype)
        stores[i].start()
    for store in stores:
        store.wait()


def write_out(arrays, plan):
    far = pl.BlockSpec(memory_space=pl.ANY)
    shapes = [jax.ShapeDtypeStruct(shape, dtype) for _, _, shape, dtype in plan]
    return pl.pallas_call(
        functools.partial(
            write_kernel, len(arrays), [(source, where) for source, where, _, _ in plan]
        ),
        name="write_out",
        out_shape=shapes,
        in_specs=[far] * len(arrays),
        out_specs=[far] * len(plan),
        scratch_shapes=[
            *[VMEM(array.shape, array.dtype) for array in arrays],
            *[VMEM(shape.shape, shape.dtype) for shape in shapes],
            DMA((len(arrays),)),
            DMA((len(plan),)),
        ],
        compiler_params=pltpu.CompilerParams(vmem_limit_bytes=62 * MIB),
        cost_estimate=pl.CostEstimate(flops=0, bytes_accessed=24 * MIB, transcendentals=0),
    )(*arrays)


def product_kernel(left_ref, right_ref, out_ref, turned):
    wide = 256

    @pl.when(pl.program_id(1) == 0)
    def _():
        turned[...] = left_ref[0].T

    def one(index, carried):
        lanes = pl.ds(pl.multiple_of(index * wide, 128), wide)
        out_ref[0, :, lanes] = nn(turned[...], right_ref[0, :, lanes])
        return carried

    lax.fori_loop(0, right_ref.shape[2] // wide, one, 0)


def slot_products(left, right):
    kinds, slots, tall = left.shape
    halves, _, wide = right.shape
    return pl.pallas_call(
        product_kernel,
        name="slot_products",
        grid=(kinds, halves),
        out_shape=jax.ShapeDtypeStruct((kinds, tall, halves * wide), f32),
        in_specs=[
            pl.BlockSpec((1, slots, tall), lambda kind, half: (kind, 0, 0)),
            pl.BlockSpec((1, slots, wide), lambda kind, half: (half, 0, 0)),
        ],
        out_specs=pl.BlockSpec((1, tall, wide), lambda kind, half: (kind, 0, half)),
        scratch_shapes=[VMEM((tall, slots), bf16)],
        compiler_params=pltpu.CompilerParams(vmem_limit_bytes=40 * MIB),
        cost_estimate=pl.CostEstimate(
            flops=2 * kinds * halves * slots * tall * wide,
            bytes_accessed=4 * kinds * halves * tall * wide,
            transcendentals=0,
        ),
    )(left, right)


def local_square(
    activations,
    cotangent,
    routing,
    segments,
    scaling,
    queries,
    compress,
    rescale,
    expand,
    combine,
    premix,
    router,
    widening,
    narrowing,
    fanout,
    funnel,
):
    dp_count = lax.axis_size("dp")
    row_count = lax.axis_size("row")
    col_count = lax.axis_size("col")
    col_index = lax.axis_index("col")
    local_rows, col_width = activations.shape
    seq_length = local_rows * row_count
    expert_total = router.shape[1]
    capacity = local_rows * TOP * 4 // (3 * expert_total)
    slot_total = capacity * row_count * dp_count
    tables = turning_tables(seq_length)
    (
        one,
        query,
        key,
        value,
        probs,
        latent,
        latent_normed,
        attended,
        compress_all,
        cot_blocks,
        pick,
        back,
        cot_rows,
        residual,
        normed_two,
        scale_one,
        scale_two,
        router_all,
    ) = run_attention(
        activations,
        scaling,
        queries,
        compress,
        rescale,
        expand,
        combine,
        premix,
        segments,
        cotangent,
        routing,
        router,
        tables,
        capacity,
    )
    (
        normed_grad,
        expert_rows,
        expert_gu_grad,
        expert_hidden,
        shared_x,
        shared_y,
        shared_kept,
        hidden_blocks,
        reply_blocks,
        premix_rows,
        router_rows,
    ) = run_experts(
        normed_two,
        pick,
        back,
        cot_rows,
        cot_blocks,
        fanout[0].transpose(0, 2, 1),
        funnel[0],
        widening.transpose(0, 2, 1),
        narrowing,
        router_all,
    )
    slot_rows = expert_rows.reshape(col_count, slot_total, col_width)
    reply_grad_rows = cot_rows.reshape(col_count, slot_total, col_width)
    slot_hidden = expert_hidden.reshape(slot_total, -1)
    slot_gu_grad = expert_gu_grad.reshape(2, slot_total, -1)
    got_x = lax.ppermute(shared_x, "dp", [(i, i ^ 1) for i in range(SQUARE)])
    got_y = lax.ppermute(shared_y, "dp", [(i, i ^ 2) for i in range(SQUARE)])
    fanout_grad = slot_products(slot_gu_grad, slot_rows)
    funnel_grad = slot_products(slot_hidden[None], reply_grad_rows)
    normed_grad, fanout_grad, funnel_grad = lax.optimization_barrier(
        (normed_grad, fanout_grad, funnel_grad)
    )
    (
        input_grad,
        layer_output,
        small,
        shared_sum,
        queries_sum,
        combine_sum,
        expand_sum,
        compress_sum,
    ) = run_attention_back(
        normed_grad,
        residual,
        scale_two,
        premix,
        cotangent,
        activations,
        scale_one,
        scaling,
        one,
        query,
        key,
        value,
        probs,
        latent,
        rescale,
        tables,
        compress_all,
        queries,
        expand,
        combine,
        (shared_kept, got_x, got_y),
        (
            attended,
            latent_normed,
            narrowing,
            reply_blocks,
            back,
            hidden_blocks,
            premix_rows,
            router_rows,
        ),
    )
    everything = slice(None)
    share = narrowing.shape[0]
    (
        widening_grad,
        narrowing_grad,
        queries_grad,
        combine_grad,
        expand_grad,
        compress_grad,
        input_grad,
        layer_output,
        router_grad,
        premix_grad,
        scaling_grad,
        rescale_grad,
    ) = write_out(
        (
            shared_sum,
            queries_sum.reshape(queries.shape),
            combine_sum.reshape(combine.shape),
            expand_sum.reshape(expand.shape),
            compress_sum,
            input_grad,
            layer_output,
            small,
        ),
        (
            (0, slice(1, 3), (2, share, col_width), f32),
            (0, 0, (share, col_width), f32),
            (1, everything, queries.shape, f32),
            (2, everything, combine.shape, f32),
            (3, everything, expand.shape, f32),
            (4, everything, compress_sum.shape, f32),
            (5, everything, input_grad.shape, f32),
            (6, everything, layer_output.shape, bf16),
            (7, slice(0, expert_total), (expert_total, col_width), f32),
            (7, slice(expert_total, expert_total + 1), (1, col_width), f32),
            (7, slice(expert_total + 1, expert_total + 2), (1, col_width), f32),
            (7, (slice(expert_total + 2, expert_total + 3), slice(0, RANK)), (1, RANK), f32),
        ),
    )
    return (
        layer_output,
        input_grad,
        scaling_grad.reshape(col_width),
        queries_grad,
        compress_grad.T,
        rescale_grad.reshape(RANK),
        expand_grad,
        combine_grad,
        premix_grad.reshape(col_width),
        router_grad.T,
        widening_grad.transpose(0, 2, 1),
        narrowing_grad,
        fanout_grad.transpose(0, 2, 1)[None],
        funnel_grad,
    )


def local(
    activations,
    cotangent,
    routing,
    segments,
    scaling,
    queries,
    compress,
    rescale,
    expand,
    combine,
    premix,
    router,
    widening,
    narrowing,
    fanout,
    funnel,
):
    dp_count = lax.axis_size("dp")
    row_count = lax.axis_size("row")
    col_count = lax.axis_size("col")
    dp_index = lax.axis_index("dp")
    row_index = lax.axis_index("row")
    col_index = lax.axis_index("col")
    local_rows = activations.shape[0]
    col_width = activations.shape[1]
    seq_length = local_rows * row_count
    half_length = seq_length // col_count
    head_width = NOPE + ROPE
    pair_width = NOPE + HEADV
    local_heads = queries.shape[1] // head_width
    slice_width = compress.shape[1]
    expert_total = router.shape[1]
    capacity = local_rows * TOP * 4 // (3 * expert_total)
    slots = capacity * row_count
    slot_total = slots * dp_count
    block_rows = min(512, half_length)
    block_count = half_length // block_rows
    score_scale = head_width ** (-0.5)

    inputs = activations.astype(f32)
    scale_one = norm_scale(inputs)
    normed_one = (inputs * scale_one[:, None] * scaling).astype(bf16)
    gathered_one = row_gather(normed_one)
    compress_all = lax.all_gather(compress, "row", axis=1, tiled=True)

    routing_all = row_gather(routing)
    cotangent_all = row_gather(after(cotangent, gathered_one))
    offsets = jnp.arange(dp_count, dtype=jnp.int32)
    my_experts = ((dp_index + offsets) % dp_count) * row_count + row_index
    goes = jnp.any(routing_all[None, :, :] == my_experts[:, None, None], axis=2)
    token_range = jnp.arange(seq_length, dtype=jnp.int32)
    earlier = (token_range[:, None] < token_range[None, :]).astype(bf16)
    rank = dot(goes.astype(bf16), earlier).astype(jnp.int32)
    slot_range = jnp.arange(slots, dtype=jnp.int32)
    pick = (
        ((rank[:, None, :] == slot_range[None, :, None]) & goes[:, None, :])
        .astype(bf16)
        .reshape(slot_total, seq_length)
    )

    def dispatch(tokens):
        rows = dot(pick, tokens).astype(bf16).reshape(dp_count, slots, col_width)
        arrived = send_out([rows[k] for k in range(dp_count)])
        return col_gather(jnp.concatenate(arrived, axis=0), axis=1)

    def bring_back(part):
        summed = col_scatter(part.astype(bf16), axis=1).reshape(dp_count, slots, col_width)
        arrived = send_back([summed[k] for k in range(dp_count)])
        return dot_tn(pick, jnp.concatenate(arrived, axis=0))

    query_part = dot(gathered_one, queries)
    latent_part = dot(gathered_one, compress_all)
    query_raw, latent_raw = col_scatter((query_part, latent_part))
    latent_plain = latent_raw[:, :RANK]
    latent_scale = lax.rsqrt(jnp.mean(latent_plain * latent_plain, axis=1) + epsilon)
    latent_normed = (latent_plain * latent_scale[:, None] * rescale).astype(bf16)
    expanded = dot(latent_normed, expand).reshape(half_length, local_heads, pair_width)
    positions = col_index * half_length + jnp.arange(half_length, dtype=jnp.int32)
    cosine, sine_table = rotation(positions, ROPE)
    key_shared = rotate(latent_raw[:, RANK:], cosine, sine_table, 1.0)
    query_heads = query_raw.reshape(half_length, local_heads, head_width)
    query_local = jnp.concatenate(
        [
            query_heads[..., :NOPE],
            rotate(query_heads[..., NOPE:], cosine[:, None, :], sine_table[:, None, :], 1.0),
        ],
        axis=2,
    ).astype(bf16)
    key_local = jnp.concatenate(
        [
            expanded[..., :NOPE],
            jnp.broadcast_to(key_shared[:, None, :], (half_length, local_heads, ROPE)),
        ],
        axis=2,
    ).astype(bf16)
    value_local = expanded[..., NOPE:].astype(bf16)
    key_flat, value_flat = (
        col_gather(key_local.reshape(half_length, local_heads * head_width)),
        col_gather(value_local.reshape(half_length, local_heads * HEADV)),
    )
    key_heads = key_flat.reshape(seq_length, local_heads, head_width)
    value_heads = value_flat.reshape(seq_length, local_heads, HEADV)
    own_segments = lax.dynamic_slice_in_dim(
        segments, col_index * half_length, half_length, 0
    ).reshape(block_count, block_rows)
    query_blocks = query_local.reshape(block_count, block_rows, local_heads, head_width)

    def attend_block(inputs_block):
        query_block, segment_block = inputs_block
        scores = (
            jnp.einsum("qhd,khd->hqk", query_block, key_heads, preferred_element_type=f32)
            * score_scale
        )
        visible = segments[None, None, :] <= segment_block[None, :, None]
        scores = jnp.where(visible, scores, masked_score)
        largest = jnp.max(scores, axis=2, keepdims=True)
        weight = jnp.exp(scores - largest)
        totals = jnp.sum(weight, axis=2, keepdims=True)
        probability = (weight / totals).astype(bf16)
        result = jnp.einsum("hqk,khd->qhd", probability, value_heads, preferred_element_type=f32)
        return (result.astype(bf16), (largest + jnp.log(totals))[..., 0])

    attended_blocks, log_totals = lax.map(attend_block, (query_blocks, own_segments))
    attended = attended_blocks.reshape(half_length, local_heads * HEADV)
    attended_all = col_gather(attended)
    branch = row_scatter(dot(attended_all, combine))

    reply_grad_rows = dispatch(cotangent_all)
    inner_weight = fanout[0]
    outer_weight = funnel[0]
    hidden_raw = dot_nt(reply_grad_rows, outer_weight)
    shared_hidden_grad = col_scatter(dot_nt(cotangent_all, narrowing))

    residual = inputs + branch
    scale_two = norm_scale(residual)
    normed_two = (residual * scale_two[:, None] * premix).astype(bf16)
    gathered_two = row_gather(normed_two)

    expert_rows = dispatch(gathered_two)
    expert_range = jnp.arange(expert_total, dtype=jnp.int32)
    router_all = lax.all_gather(router, "col", axis=0, tiled=True)
    own_expert = dp_index * row_count + row_index
    slot_probs = jax.nn.softmax(dot(expert_rows, router_all), axis=1)
    slot_gates = jnp.sum(jnp.where(expert_range == own_expert, slot_probs, 0.0), axis=1)
    gate_up = jnp.einsum("rd,gdf->grf", expert_rows, inner_weight, preferred_element_type=f32)
    gate_input, up_input = gate_up[0], gate_up[1]
    hidden = jax.nn.silu(gate_input) * up_input
    expert_hidden = hidden.astype(bf16)
    slot_gate_grad = col_totals(jnp.sum(hidden * hidden_raw, axis=1))
    hidden_grad = hidden_raw * slot_gates[:, None]
    expert_gu_grad = jnp.stack(
        [hidden_grad * up_input * silu_slope(gate_input), hidden_grad * jax.nn.silu(gate_input)]
    ).astype(bf16)
    input_part = jnp.einsum(
        "grf,gdf->rd", expert_gu_grad, inner_weight, preferred_element_type=f32
    )
    routed_grad = bring_back(input_part)
    gate_grad_parts = send_back(
        [slot_gate_grad.reshape(dp_count, slots)[k] for k in range(dp_count)]
    )

    logits = col_totals(dot(gathered_two, router))
    router_probs = jax.nn.softmax(logits, axis=1)
    gate_grad = jnp.sum(
        pick.reshape(dp_count, slots, seq_length).astype(f32)
        * jnp.stack(gate_grad_parts)[:, :, None],
        axis=1,
    )
    mine = (my_experts[:, None] == expert_range[None, :]).astype(f32)
    probs_grad = jnp.sum(gate_grad[:, :, None] * mine[:, None, :], axis=0)
    logit_grad = router_probs * (
        probs_grad - jnp.sum(router_probs * probs_grad, axis=1, keepdims=True)
    )
    router_part = dot_tn(gathered_two, logit_grad)

    shared_gate_up = col_scatter(
        jnp.einsum("td,gdf->tgf", gathered_two, widening, preferred_element_type=f32)
    )
    shared_hidden = (jax.nn.silu(shared_gate_up[:, 0]) * shared_gate_up[:, 1]).astype(bf16)
    hidden_all = col_gather(shared_hidden)
    narrowing_grad = dot_tn(hidden_all, cotangent_all)
    shared_gu_grad = jnp.stack(
        [
            shared_hidden_grad * shared_gate_up[:, 1] * silu_slope(shared_gate_up[:, 0]),
            shared_hidden_grad * jax.nn.silu(shared_gate_up[:, 0]),
        ],
        axis=1,
    ).astype(bf16)
    gu_grad_all = col_gather(shared_gu_grad)
    widening_grad = jnp.einsum(
        "td,tgf->gdf", gathered_two, gu_grad_all, preferred_element_type=f32
    )
    shared_input_part = jnp.einsum(
        "tgf,gdf->td", gu_grad_all, widening, preferred_element_type=f32
    )
    shared_sums = lax.psum((narrowing_grad.astype(bf16), widening_grad.astype(bf16)), "dp")

    grad_part = routed_grad + shared_input_part + dot_nt(logit_grad, router)
    premix_part = jnp.sum(grad_part * gathered_two.astype(f32), axis=0) / premix
    normed_grad = row_scatter(grad_part)

    upstream = cotangent.astype(f32)
    residual_grad = upstream + norm_back(residual, scale_two, premix, normed_grad)
    branch_all = row_gather(residual_grad.astype(bf16))

    funnel_grad = dot_tn((hidden * slot_gates[:, None]).astype(bf16), reply_grad_rows)[None]
    fanout_grad = jnp.einsum(
        "rd,grf->gdf", expert_rows, expert_gu_grad, preferred_element_type=f32
    )[None]
    reply_part = dot(expert_hidden, outer_weight) * slot_gates[:, None]
    routed = bring_back(reply_part)
    shared_out = row_scatter(routed + dot(hidden_all, narrowing))
    layer_output = (residual + shared_out).astype(bf16)

    combine_grad = dot_tn(attended_all, branch_all)
    combine_sum = lax.psum(after(combine_grad.astype(bf16), *shared_sums), "dp")
    attended_grad = col_scatter(dot_nt(branch_all, combine))
    attended_grad_blocks = attended_grad.astype(bf16).reshape(
        block_count, block_rows, local_heads, HEADV
    )

    def attend_back(carried, inputs_block):
        key_sum, value_sum = carried
        query_block, grad_block, log_block, segment_block = inputs_block
        scores = (
            jnp.einsum("qhd,khd->hqk", query_block, key_heads, preferred_element_type=f32)
            * score_scale
        )
        visible = segments[None, None, :] <= segment_block[None, :, None]
        probability = jnp.where(visible, jnp.exp(scores - log_block[..., None]), 0.0)
        weight_grad = jnp.einsum(
            "qhd,khd->hqk", grad_block, value_heads, preferred_element_type=f32
        )
        inner_sum = jnp.sum(probability * weight_grad, axis=2, keepdims=True)
        score_grad = (probability * (weight_grad - inner_sum)).astype(bf16)
        query_grad_block = (
            jnp.einsum("hqk,khd->qhd", score_grad, key_heads, preferred_element_type=f32)
            * score_scale
        )
        key_sum = (
            key_sum
            + jnp.einsum("hqk,qhd->khd", score_grad, query_block, preferred_element_type=f32)
            * score_scale
        )
        value_sum = value_sum + jnp.einsum(
            "hqk,qhd->khd", probability.astype(bf16), grad_block, preferred_element_type=f32
        )
        return ((key_sum, value_sum), query_grad_block)

    key_start = jnp.zeros((seq_length, local_heads, head_width), f32)
    value_start = jnp.zeros((seq_length, local_heads, HEADV), f32)
    (key_grad_all, value_grad_all), query_grad_blocks = lax.scan(
        attend_back,
        (key_start, value_start),
        (query_blocks, attended_grad_blocks, log_totals, own_segments),
    )
    key_grad, value_grad = col_scatter(
        (
            key_grad_all.reshape(seq_length, local_heads * head_width),
            value_grad_all.reshape(seq_length, local_heads * HEADV),
        )
    )
    key_grad = key_grad.reshape(half_length, local_heads, head_width)
    value_grad = value_grad.reshape(half_length, local_heads, HEADV)
    query_grad = query_grad_blocks.reshape(half_length, local_heads, head_width)
    query_raw_grad = (
        jnp.concatenate(
            [
                query_grad[..., :NOPE],
                rotate(query_grad[..., NOPE:], cosine[:, None, :], sine_table[:, None, :], -1.0),
            ],
            axis=2,
        )
        .astype(bf16)
        .reshape(half_length, local_heads * head_width)
    )
    expanded_grad = (
        jnp.concatenate([key_grad[..., :NOPE], value_grad], axis=2)
        .astype(bf16)
        .reshape(half_length, local_heads * pair_width)
    )
    shared_rope_grad = rotate(jnp.sum(key_grad[..., NOPE:], axis=1), cosine, sine_table, -1.0)

    latent_grad = dot_nt(expanded_grad, expand)
    latent_weighted = latent_grad * rescale
    latent_inner = jnp.mean(latent_weighted * latent_plain, axis=1)
    rescale_part = jnp.sum(latent_grad * latent_plain * latent_scale[:, None], axis=0)
    plain_grad = (
        latent_weighted * latent_scale[:, None]
        - latent_plain * (latent_scale**3 * latent_inner)[:, None]
    )
    latent_raw_grad = jnp.concatenate([plain_grad, shared_rope_grad], axis=1).astype(bf16)
    query_grad_all = col_gather(query_raw_grad)
    latent_grad_all = col_gather(latent_raw_grad)
    first_part = dot_nt(query_grad_all, queries) + dot_nt(latent_grad_all, compress_all)
    first_grad = row_scatter(first_part)
    input_grad = residual_grad + norm_back(inputs, scale_one, scaling, first_grad)

    queries_part = dot_tn(gathered_one, query_grad_all)
    own_latent_grad = lax.psum_scatter(
        latent_raw_grad, "row", scatter_dimension=1, tiled=True
    )
    compress_part = dot_tn(gathered_one, col_gather(own_latent_grad))
    half_rank = RANK // col_count
    latent_normed_all = col_gather(latent_normed)
    expanded_grad_all = col_gather(expanded_grad)
    expand_half = dot_tn(
        lax.dynamic_slice_in_dim(latent_normed_all, col_index * half_rank, half_rank, 1),
        expanded_grad_all,
    )
    scaling_part = jnp.sum(first_part * gathered_one.astype(f32), axis=0) / scaling
    queries_sum, expand_sum, compress_sum = lax.psum(
        (
            after(queries_part.astype(bf16), combine_sum),
            expand_half.astype(bf16),
            compress_part.astype(bf16),
        ),
        "dp",
    )
    premix_sum, router_sum = lax.psum((premix_part, router_part), ("dp", "row"))
    rescale_sum = lax.psum(rescale_part, ("dp", "row", "col"))
    scaling_sum = lax.psum(scaling_part, ("dp", "row"))
    return (
        layer_output,
        input_grad,
        scaling_sum,
        queries_sum.astype(f32),
        compress_sum.astype(f32),
        rescale_sum,
        col_gather(expand_sum).astype(f32),
        combine_sum.astype(f32),
        premix_sum,
        router_sum,
        shared_sums[1].astype(f32),
        shared_sums[0].astype(f32),
        fanout_grad,
        funnel_grad,
    )


def solution(mesh):
    placed = (
        P(("dp", "row"), "col"),
        P(("dp", "row"), "col"),
        P(("dp", "row"), None),
        P("dp"),
        P("col"),
        P("col", "row"),
        P("col", "row"),
        P(),
        P(None, "row"),
        P("row", "col"),
        P("col"),
        P("col", None),
        P(None, "col", "row"),
        P("row", "col"),
        P(("dp", "row"), None, None, "col"),
        P(("dp", "row"), "col", None),
    )
    squared = mesh.shape["dp"] == SQUARE and mesh.shape["row"] == ROWS
    return jax.shard_map(
        local_square if squared else local,
        mesh=mesh,
        in_specs=placed,
        out_specs=(
            P(("dp", "row"), "col"),
            P(("dp", "row"), "col"),
            P("col"),
            P("col", "row"),
            P("col", "row"),
            P(),
            P(None, "row"),
            P("row", "col"),
            P("col"),
            P("col", None),
            P(None, "col", "row"),
            P("row", "col"),
            P(("dp", "row"), None, None, "col"),
            P(("dp", "row"), "col", None),
        ),
        check_vma=False,
    )
```
